32 devices in a mesh: experts: 4 (over y, core), context: 8 (over z, x).
Axes of the slice: x: 2, y: 2, z: 4, core: 2. Of those that a mesh axis runs over, the one named last changes fastest.
Arguments:
- tokens: bfloat16 [2, 2048, 1024], P(None, ('experts', 'context')), may hold values from -6 to 6
- lengths: int32 [2], replicated, may hold values from 512 to 2048, as said below
- expert_index: int32 [2, 2048, 2], P(None, ('experts', 'context')), may hold values from 0 to 3, all different within a row
- cotangent: bfloat16 [2, 2048, 1024], P(None, ('experts', 'context')), may hold values from -18 to 18
- norm_attn: float32 [1024], replicated, may hold values from 0.5 to 1.5
- w_query: bfloat16 [1024, 1024], replicated, may hold values from -0.1875 to 0.1875
- w_key: bfloat16 [1024, 1024], replicated, may hold values from -0.1875 to 0.1875
- w_value: bfloat16 [1024, 1024], replicated, may hold values from -0.1875 to 0.1875
- w_out: bfloat16 [1024, 1024], replicated, may hold values from -0.75 to 0.75
- rel_bias: float32 [32, 16], replicated, may hold values from -3 to 3
- norm_ffn: float32 [1024], replicated, may hold values from 0.5 to 1.5
- router: float32 [1024, 4], replicated, may hold values from -0.13125 to 0.13125
- w_gate: bfloat16 [4, 1024, 2816], P('experts'), may hold values from -0.1875 to 0.1875
- w_up: bfloat16 [4, 1024, 2816], P('experts'), may hold values from -0.1875 to 0.1875
- w_down: bfloat16 [4, 2816, 1024], P('experts'), may hold values from -0.67578125 to 0.67578125
Outputs:
- mixed_out: bfloat16 [2, 2048, 1024], P(None, ('experts', 'context'))
- grad_tokens: float32 [2, 2048, 1024], P(None, ('experts', 'context'))
- grad_norm_attn: float32 [1024], replicated
- grad_w_query: float32 [1024, 1024], replicated
- grad_w_key: float32 [1024, 1024], replicated
- grad_w_value: float32 [1024, 1024], replicated
- grad_w_out: float32 [1024, 1024], replicated
- grad_rel_bias: float32 [32, 16], replicated
- grad_norm_ffn: float32 [1024], replicated
- grad_router: float32 [1024, 4], replicated
- grad_w_gate: float32 [4, 1024, 2816], P('experts', 'context')
- grad_w_up: float32 [4, 1024, 2816], P('experts', 'context')
- grad_w_down: float32 [4, 2816, 1024], P('experts', 'context')
The draws below stay inside these ranges and needn't reach their ends.
Inputs may be any that keep to these rules, and one draw needn't show every extreme that they name: `lengths`: one sequence, drawn from the seed, is valid in all 2048 positions. `expert_index`: each token names two different experts.
All inputs are finite; a program needn't handle non-finite values.
Results may differ from the reference program's by a relative error of at most 0.03.
Values may be sent and summed in bfloat16 or wider, within the bound.
A program may use at most 384 MiB of HBM per device.

```python
import math
import jax
import jax.numpy as jnp
import numpy as np
from jax import lax

D = 1024
FF = 2816
HEADS = 16
HEAD_DIM = 64
NB = 32
MAXDIST = 128
SLOTS = 2
SPAN = 64
LEN = 2048
EXPERTS = 4
CAP = 80
N_EXPERTS = 4
N_CONTEXT = 8


def draw_lengths(key, part):
    key = jax.random.fold_in(key, 7)
    pick_key, size_key = jax.random.split(key)
    full_slot = jax.random.randint(pick_key, (), 0, SLOTS)
    others = jax.random.randint(size_key, (SLOTS,), LEN // 4, LEN + 1)
    return jnp.where(jnp.arange(SLOTS) == full_slot, LEN, others).astype(jnp.int32)


def draw_cotangent(key, part):
    key = jax.random.fold_in(key, 11)
    fraction = jnp.arange(LEN, dtype=jnp.float32) / (LEN - 1)
    row_scale = 0.5 * jnp.exp(fraction * jnp.log(6.0))
    noise = jnp.clip(jax.random.normal(key, (SLOTS, LEN, D), jnp.float32), -6.0, 6.0)
    return (noise * row_scale[None, :, None]).astype(jnp.bfloat16)


def shard_levels(rng, extent, cuts, least, largest):
    level, own = 1.0, jax.random.fold_in(rng, 6)
    for dim, parts in cuts:
        steps = jnp.exp(jax.random.uniform(jax.random.fold_in(own, dim), (parts,), jnp.float32, least / len(cuts), largest / len(cuts)))
        level = level * jnp.repeat(steps, extent[dim] // parts).reshape([-1 if axis == dim else 1 for axis in range(len(extent))])
    return level


def different_ones(own_key, rows, number_of, top, lift):
    ranking = jax.random.permutation(jax.random.fold_in(own_key, 1), number_of)
    favour = ranking
    for power in range(3):
        favour = favour * favour // number_of
    favour = favour * lift // number_of
    lots = jax.random.randint(jax.random.fold_in(own_key, 2), (rows, number_of), 0, 4096) + favour
    fixed_rows = jax.random.permutation(jax.random.fold_in(own_key, 3), rows)[jnp.arange(number_of) % rows]
    lots = jnp.where(jnp.arange(rows)[:, None] == fixed_rows[None, :], 1 << 14, lots)
    merit = lots * number_of + jnp.arange(number_of)
    return lax.top_k(merit.astype(jnp.int32), top)[1].astype(jnp.int32)


def gaussian(key, shape, deviation, most, cuts=(), kind=jnp.bfloat16):
    values = deviation * jax.random.normal(key, shape, jnp.float32)
    if cuts:
        values = values * shard_levels(key, shape, cuts, -0.22, 0.18)
    return jnp.clip(values, -most, most).astype(kind)


def setup_inputs(seed: int = 0) -> dict:
    key_of = jax.random.split(jax.random.key(seed), 16)
    return {
        "tokens": gaussian(key_of[0], (SLOTS, LEN, D), 1.0, 6.0, ((1, 32),)),
        "lengths": draw_lengths(jax.random.fold_in(key_of[15], 71), 0),
        "expert_index": different_ones(key_of[2], SLOTS * LEN, EXPERTS, 2, 4096).reshape((SLOTS, LEN, 2)),
        "cotangent": draw_cotangent(jax.random.fold_in(key_of[15], 71), 0),
        "norm_attn": jnp.clip(1.0 + 0.1 * jax.random.normal(key_of[4], (D,), jnp.float32), 0.5, 1.5),
        "w_query": gaussian(key_of[5], (D, D), D ** -0.5, 0.1875),
        "w_key": gaussian(key_of[6], (D, D), D ** -0.5, 0.1875),
        "w_value": gaussian(key_of[7], (D, D), D ** -0.5, 0.1875),
        "w_out": gaussian(key_of[8], (D, D), (D // 16) ** -0.5, 0.75),
        "rel_bias": gaussian(key_of[9], (NB, HEADS), 0.5, 3.0, (), jnp.float32),
        "norm_ffn": jnp.clip(1.0 + 0.1 * jax.random.normal(key_of[10], (D,), jnp.float32), 0.5, 1.5),
        "router": gaussian(key_of[11], (D, EXPERTS), (0.7 * D ** -0.5), 0.13125, (), jnp.float32),
        "w_gate": gaussian(key_of[12], (EXPERTS, D, FF), D ** -0.5, 0.1875, ((0, 4),)),
        "w_up": gaussian(key_of[13], (EXPERTS, D, FF), D ** -0.5, 0.1875, ((0, 4),)),
        "w_down": gaussian(key_of[14], (EXPERTS, FF, D), (1.5 * EXPERTS * FF ** -0.5), 0.67578125, ((0, 4),)),
    }


norm_epsilon = 1e-06
mask_fill = -1e+30
highest = lax.Precision.HIGHEST

@jax.custom_vjp
def low(v):
    return lax.optimization_barrier(v.astype(jnp.bfloat16)).astype(jnp.float32)

@jax.custom_vjp
def low_back(v):
    return v

def low_keep(v):
    return (low(v), None)

def low_pass(kept, grad):
    return (grad,)

def back_keep(v):
    return (v, None)

def back_low(kept, grad):
    return (low(grad),)
low.defvjp(low_keep, low_pass)
low_back.defvjp(back_keep, back_low)

def rounded(values):
    return low(low_back(values))

def bucket_of(distance, bucket_count, reach):
    exact = bucket_count // 2
    if distance < exact:
        return distance
    level = exact + int(math.log(distance / exact) / math.log(reach / exact) * (bucket_count - exact))
    return min(level, bucket_count - 1)

def bucket_bounds(bucket_count, reach):
    edges = []
    for level in range(1, bucket_count):
        distance = 0
        while bucket_of(distance, bucket_count, reach) < level:
            distance += 1
        edges.append(distance)
    lower_bounds = np.array([0] + edges, np.int32)
    upper_bounds = np.array(edges + [2 ** 30], np.int32)
    return (lower_bounds, upper_bounds)

def bucket_index(distance):
    lower_bounds, upper_bounds = bucket_bounds(NB, MAXDIST)
    inside = (distance[..., None] >= jnp.asarray(lower_bounds)) & (distance[..., None] < jnp.asarray(upper_bounds))
    return lax.optimization_barrier(jnp.sum(inside.astype(jnp.int32) * jnp.arange(NB, dtype=jnp.int32), -1))

def rms_norm(values, gain):
    inverse = lax.rsqrt(lax.optimization_barrier(jnp.mean(values * values, axis=-1, keepdims=True)) + norm_epsilon)
    return values * inverse * gain

def attend_slot(queries, key_rows, value_rows, rel_bias, length):
    positions = jnp.arange(LEN, dtype=jnp.int32)
    rows_block = math.gcd(LEN, 512)
    score_scale = HEAD_DIM ** (-0.5)

    def one_block(begin_at):
        query_rows = lax.dynamic_slice_in_dim(queries, begin_at, rows_block, 0)
        query_pos = begin_at + jnp.arange(rows_block, dtype=jnp.int32)
        scores = jnp.einsum('qhd,khd->qhk', query_rows, key_rows, precision=highest) * score_scale
        distance = jnp.maximum(query_pos[:, None] - positions[None, :], 0)
        bias_rows = jnp.take(rel_bias, bucket_index(distance), axis=0)
        scores = low_back(scores + jnp.transpose(bias_rows, (0, 2, 1)))
        allowed = (positions[None, :] <= query_pos[:, None]) & (positions[None, :] < length)
        scores = jnp.where(allowed[:, None, :], scores, mask_fill)
        weights = low(jax.nn.softmax(scores, axis=-1))
        return jnp.einsum('qhk,khd->qhd', weights, value_rows, precision=highest)
    starts = jnp.arange(0, LEN, rows_block, dtype=jnp.int32)
    blocks = lax.map(jax.checkpoint(one_block), starts)
    return blocks.reshape(LEN, HEADS, HEAD_DIM)

def to_groups(array, columns):
    groups = N_EXPERTS * N_CONTEXT
    shaped = array.reshape(SLOTS, groups, SPAN, columns)
    return jnp.transpose(shaped, (1, 0, 2, 3)).reshape(groups, SLOTS * SPAN, columns)

def from_groups(array, columns):
    groups = N_EXPERTS * N_CONTEXT
    shaped = array.reshape(groups, SLOTS, SPAN, columns)
    return jnp.transpose(shaped, (1, 0, 2, 3)).reshape(SLOTS * LEN, columns)

def dispatch_tables(expert_index, lengths):
    groups = N_EXPERTS * N_CONTEXT
    positions = jnp.arange(LEN, dtype=jnp.int32)
    valid = positions[None, :] < lengths[:, None]
    valid_groups = jnp.transpose(valid.reshape(SLOTS, groups, SPAN), (1, 0, 2)).reshape(groups, SLOTS * SPAN)
    picked = jnp.transpose(expert_index.reshape(SLOTS, groups, SPAN, 2), (1, 0, 2, 3)).reshape(groups, SLOTS * SPAN * 2)
    live_pairs = jnp.broadcast_to(valid_groups[:, :, None], (groups, SLOTS * SPAN, 2)).reshape(groups, SLOTS * SPAN * 2)
    chosen = ((picked[:, :, None] == jnp.arange(EXPERTS, dtype=jnp.int32)) & live_pairs[:, :, None]).astype(jnp.int32)
    earlier = jnp.cumsum(chosen, axis=1) - chosen
    position_in = lax.optimization_barrier(jnp.sum(earlier * chosen, -1))
    kept_pairs = live_pairs & (position_in < CAP)
    slot_of = jnp.where(kept_pairs, picked * CAP + position_in, -1)
    matches = slot_of[:, None, :] == jnp.arange(EXPERTS * CAP, dtype=jnp.int32)[None, :, None]
    table = jnp.any(matches.reshape(groups, EXPERTS * CAP, SLOTS * SPAN, 2), -1).astype(jnp.float32)
    return (table, valid)

def forward(tokens, norm_attn, w_query, w_key, w_value, w_out, rel_bias, norm_ffn, router, w_gate, w_up, w_down, table, valid, lengths):
    groups = N_EXPERTS * N_CONTEXT
    inputs = tokens.reshape(SLOTS * LEN, D)
    normed = low(rms_norm(inputs, norm_attn))
    queries = rounded(jnp.dot(normed, w_query, precision=highest)).reshape(SLOTS, LEN, HEADS, HEAD_DIM)
    key_rows = rounded(jnp.dot(normed, w_key, precision=highest)).reshape(SLOTS, LEN, HEADS, HEAD_DIM)
    value_rows = rounded(jnp.dot(normed, w_value, precision=highest)).reshape(SLOTS, LEN, HEADS, HEAD_DIM)
    attended = jnp.stack([attend_slot(queries[member], key_rows[member], value_rows[member], rel_bias, lengths[member]) for member in range(SLOTS)])
    attended = rounded(attended.reshape(SLOTS * LEN, D))
    branch = low_back(jnp.dot(attended, w_out, precision=highest))
    middle = inputs + branch
    second = low(rms_norm(middle, norm_ffn))
    logits = jnp.dot(second, router, precision=highest)
    gates = jax.nn.softmax(logits, axis=-1)
    second_groups = to_groups(second, D)
    gates_groups = to_groups(gates, EXPERTS)
    expert_rows = low_back(jnp.einsum('nmt,ntd->nmd', table, second_groups, precision=highest)).reshape(groups, EXPERTS, CAP, D)
    gate_pre = low_back(jnp.einsum('necd,edf->necf', expert_rows, w_gate, precision=highest))
    up_pre = low_back(jnp.einsum('necd,edf->necf', expert_rows, w_up, precision=highest))
    hidden = low(jax.nn.gelu(gate_pre, approximate=True) * up_pre)
    expert_out = rounded(jnp.einsum('necf,efd->necd', hidden, w_down, precision=highest)).reshape(groups, EXPERTS * CAP, D)
    slot_expert = ((jnp.arange(EXPERTS * CAP, dtype=jnp.int32) // CAP)[:, None] == jnp.arange(EXPERTS, dtype=jnp.int32)[None, :]).astype(jnp.float32)
    slot_weight = lax.optimization_barrier(jnp.sum(jnp.einsum('nmt,nte->nme', table, gates_groups, precision=highest) * slot_expert, -1))
    routed = jnp.einsum('nmt,nmd->ntd', table, slot_weight[..., None] * expert_out, precision=highest)
    routed = from_groups(routed, D)
    result = (middle + routed) * valid.reshape(SLOTS * LEN, 1).astype(jnp.float32)
    return result.reshape(SLOTS, LEN, D)

def reference(tokens, lengths, expert_index, cotangent, norm_attn, w_query, w_key, w_value, w_out, rel_bias, norm_ffn, router, w_gate, w_up, w_down):
    table, valid = dispatch_tables(expert_index, lengths)

    def wrapped(tokens_in, norm_attn_in, query_in, key_in, value_in, out_in, bias_in, norm_ffn_in, router_in, gate_in, up_in, down_in):
        return forward(tokens_in, norm_attn_in, query_in, key_in, value_in, out_in, bias_in, norm_ffn_in, router_in, gate_in, up_in, down_in, table, valid, lengths)
    result, backward = jax.vjp(wrapped, tokens.astype(jnp.float32), norm_attn.astype(jnp.float32), w_query.astype(jnp.float32), w_key.astype(jnp.float32), w_value.astype(jnp.float32), w_out.astype(jnp.float32), rel_bias.astype(jnp.float32), norm_ffn.astype(jnp.float32), router.astype(jnp.float32), w_gate.astype(jnp.float32), w_up.astype(jnp.float32), w_down.astype(jnp.float32))
    grads = backward(cotangent.astype(jnp.float32))
    return (result.astype(jnp.bfloat16), grads[0], grads[1], grads[2], grads[3], grads[4], grads[5], grads[6], grads[7], grads[8], grads[9], grads[10], grads[11])
```

```python
import math

import jax
import jax.numpy as jnp
import numpy as np
from jax import lax
from jax.experimental import pallas as pl
from jax.experimental.pallas import tpu as pltpu
from jax.sharding import PartitionSpec as P

MAXDIST = 128


norm_epsilon = 1e-06
mask_fill = -1e30
highest = lax.Precision.HIGHEST


def bucket_of(distance, bucket_count, reach):
    exact = bucket_count // 2
    if distance < exact:
        return distance
    level = exact + int(
        math.log(distance / exact) / math.log(reach / exact) * (bucket_count - exact)
    )
    return min(level, bucket_count - 1)


def bucket_edges(bucket_count, reach):
    edges = []
    for level in range(1, bucket_count):
        distance = 0
        while bucket_of(distance, bucket_count, reach) < level:
            distance += 1
        edges.append(distance)
    return edges


def relative_bucket(query_pos, key_pos, bucket_count):
    distance = jnp.maximum(query_pos[:, None] - key_pos[None, :], 0)
    bucket = jnp.zeros(distance.shape, jnp.int32)
    for edge in bucket_edges(bucket_count, MAXDIST):
        bucket = bucket + (distance >= edge).astype(jnp.int32)
    return bucket


def rms_norm(values, gain):
    inverse = lax.rsqrt(jnp.mean(values * values, axis=-1, keepdims=True) + norm_epsilon)
    return values * inverse * gain


def norm_back(values, gain, grad_in):
    inverse = lax.rsqrt(jnp.mean(values * values, axis=-1, keepdims=True) + norm_epsilon)
    normed = values * inverse
    grad_normed = grad_in * gain
    grad_values = inverse * (
        grad_normed - normed * jnp.mean(grad_normed * normed, axis=-1, keepdims=True)
    )
    return (grad_values, jnp.sum(grad_in * normed, 0))


def score_block(query_rows, key_rows, rel_bias, query_pos, key_pos, lengths, score_scale):
    raw_scores = (
        jnp.einsum("sqhd,skhd->sqhk", query_rows, key_rows, preferred_element_type=jnp.float32)
        * score_scale
    )
    bucket = relative_bucket(query_pos, key_pos, rel_bias.shape[0])
    onehot = (bucket[:, :, None] == jnp.arange(rel_bias.shape[0], dtype=jnp.int32)).astype(
        jnp.float32
    )
    bias_rows = jnp.einsum("qkb,bh->qhk", onehot, rel_bias, precision=highest)
    causal = (key_pos[None, :] <= query_pos[:, None])[None]
    inside = key_pos[None, None, :] < lengths[:, None, None]
    allowed = (causal & inside)[:, :, None, :]
    return (raw_scores + bias_rows[None], allowed, onehot)


def pair_grads(query_set, key_set, rel_bias, lengths, score_scale):
    query_rows, grad_rows, log_total, delta, query_pos = query_set
    key_rows, value_rows, key_pos = key_set
    scores, allowed, onehot = score_block(
        query_rows, key_rows, rel_bias, query_pos, key_pos, lengths, score_scale
    )
    weights = jnp.where(allowed, jnp.exp(scores - log_total[..., None]), 0.0)
    grad_value = jnp.einsum(
        "sqhk,sqhd->skhd",
        weights.astype(jnp.bfloat16),
        grad_rows,
        preferred_element_type=jnp.float32,
    )
    grad_weights = jnp.einsum(
        "sqhd,skhd->sqhk", grad_rows, value_rows, preferred_element_type=jnp.float32
    )
    grad_scores = (weights * (grad_weights - delta[..., None])).astype(jnp.bfloat16)
    grad_query = score_scale * jnp.einsum(
        "sqhk,skhd->sqhd", grad_scores, key_rows, preferred_element_type=jnp.float32
    )
    grad_key = score_scale * jnp.einsum(
        "sqhk,sqhd->skhd", grad_scores, query_rows, preferred_element_type=jnp.float32
    )
    grad_table = jnp.einsum(
        "sqhk,qkb->bh", grad_scores, onehot.astype(jnp.bfloat16), preferred_element_type=jnp.float32
    )
    return (grad_query, grad_key, grad_value, grad_table)


def dispatch_table(expert_index, live_rows, expert_count, capacity):
    picked = expert_index.reshape(-1)
    live_pairs = jnp.broadcast_to(live_rows[:, :, None], expert_index.shape).reshape(-1)
    chosen = (
        (picked[:, None] == jnp.arange(expert_count, dtype=jnp.int32)[None, :])
        & live_pairs[:, None]
    ).astype(jnp.int32)
    earlier = jnp.cumsum(chosen, axis=0) - chosen
    position_in = jnp.sum(earlier * chosen, -1)
    kept_pairs = live_pairs & (position_in < capacity)
    slot_of = jnp.where(kept_pairs, picked * capacity + position_in, -1)
    matches = slot_of[None, :] == jnp.arange(expert_count * capacity, dtype=jnp.int32)[:, None]
    table = jnp.any(matches.reshape(expert_count * capacity, -1, 2), -1).astype(jnp.float32)
    slot_ids = jnp.arange(expert_count * capacity, dtype=jnp.int32) // capacity
    slot_expert = (slot_ids[:, None] == jnp.arange(expert_count, dtype=jnp.int32)[None, :]).astype(
        jnp.float32
    )
    return (table, slot_expert)


def on_device(
    tokens,
    lengths,
    expert_index,
    cotangent,
    norm_attn,
    w_query,
    w_key,
    w_value,
    w_out,
    rel_bias,
    norm_ffn,
    router,
    w_gate,
    w_up,
    w_down,
):
    slot_count, per_slot, model_width = tokens.shape
    head_count = rel_bias.shape[1]
    head_size = model_width // head_count
    expert_count = router.shape[1]
    capacity = (10 * slot_count * per_slot + 4 * expert_count - 1) // (4 * expert_count)
    score_scale = head_size ** (-0.5)
    row_count = slot_count * per_slot
    shape_four = (slot_count, per_slot, head_count, head_size)
    shape_three = (slot_count, per_slot, model_width)
    device_at = lax.axis_index(("experts", "context"))
    positions = device_at * per_slot + jnp.arange(per_slot, dtype=jnp.int32)
    live_rows = positions[None, :] < lengths[:, None]
    keep_mask = live_rows.reshape(row_count, 1).astype(jnp.float32)
    inputs = tokens.reshape(row_count, model_width).astype(jnp.float32)
    normed = rms_norm(inputs, norm_attn).astype(jnp.bfloat16)
    query_flat = jnp.dot(normed, w_query, preferred_element_type=jnp.float32).astype(jnp.bfloat16)
    key_flat = jnp.dot(normed, w_key, preferred_element_type=jnp.float32).astype(jnp.bfloat16)
    value_flat = jnp.dot(normed, w_value, preferred_element_type=jnp.float32).astype(jnp.bfloat16)
    query_four = query_flat.reshape(shape_four)
    key_four = key_flat.reshape(shape_four)
    value_four = value_flat.reshape(shape_four)
    key_three = key_flat.reshape(shape_three)
    value_three = value_flat.reshape(shape_three)
    start_state = (
        jnp.zeros(shape_four, jnp.float32),
        jnp.full((slot_count, per_slot, head_count), mask_fill, jnp.float32),
        jnp.zeros((slot_count, per_slot, head_count), jnp.float32),
    )
    offset = jnp.int32(0)
    key_all = lax.all_gather(key_three, ("experts", "context"), axis=1, tiled=True)
    value_all = lax.all_gather(value_three, ("experts", "context"), axis=1, tiled=True)
    piece_rows = key_all.shape[1]
    block_rows = math.gcd(piece_rows, 8 * per_slot)

    def forward_visit(carried, block_id):
        running, running_max, denominator = carried
        local_at = block_id * block_rows
        key_rows = lax.dynamic_slice_in_dim(key_all, local_at, block_rows, 1).reshape(
            slot_count, block_rows, head_count, head_size
        )
        value_rows = lax.dynamic_slice_in_dim(value_all, local_at, block_rows, 1).reshape(
            slot_count, block_rows, head_count, head_size
        )
        key_pos = offset + local_at + jnp.arange(block_rows, dtype=jnp.int32)
        scores, allowed, _ = score_block(
            query_four, key_rows, rel_bias, positions, key_pos, lengths, score_scale
        )
        scores = jnp.where(allowed, scores, mask_fill)
        new_max = jnp.maximum(running_max, jnp.max(scores, -1))
        factor = jnp.exp(running_max - new_max)
        weights = jnp.where(allowed, jnp.exp(scores - new_max[..., None]), 0.0)
        denominator = denominator * factor + jnp.sum(weights, -1)
        running = running * factor[..., None] + jnp.einsum(
            "sqhk,skhd->sqhd",
            weights.astype(jnp.bfloat16),
            value_rows,
            preferred_element_type=jnp.float32,
        )
        return ((running, new_max, denominator), None)

    carried, _ = lax.scan(
        forward_visit, start_state, jnp.arange(piece_rows // block_rows, dtype=jnp.int32)
    )
    running, running_max, denominator = carried
    attended = running / denominator[..., None]
    log_total = running_max + jnp.log(denominator)
    attended_low = attended.reshape(row_count, model_width).astype(jnp.bfloat16)
    middle = inputs + jnp.dot(attended_low, w_out, preferred_element_type=jnp.float32)
    second_low = rms_norm(middle, norm_ffn).astype(jnp.bfloat16)
    second_wide = second_low.astype(jnp.float32)
    logits = jnp.dot(second_wide, router, precision=highest)
    gates = jax.nn.softmax(logits, axis=-1)
    table, slot_expert = dispatch_table(expert_index, live_rows, expert_count, capacity)
    table_low = table.astype(jnp.bfloat16)
    dispatched = jnp.dot(table_low, second_low, preferred_element_type=jnp.float32).astype(
        jnp.bfloat16
    )
    arrived = lax.all_to_all(
        dispatched.reshape(expert_count, capacity, model_width),
        "experts",
        split_axis=0,
        concat_axis=1,
        tiled=True,
    )[0]
    gate_pre = jnp.dot(arrived, w_gate[0], preferred_element_type=jnp.float32)
    up_pre = jnp.dot(arrived, w_up[0], preferred_element_type=jnp.float32)
    hidden_low = (jax.nn.gelu(gate_pre, approximate=True) * up_pre).astype(jnp.bfloat16)
    produced = jnp.dot(hidden_low, w_down[0], preferred_element_type=jnp.float32).astype(
        jnp.bfloat16
    )
    returned = lax.all_to_all(
        produced[None], "experts", split_axis=1, concat_axis=0, tiled=True
    ).reshape(expert_count * capacity, model_width)
    returned_wide = returned.astype(jnp.float32)
    slot_weight = jnp.sum(jnp.dot(table, gates, precision=highest) * slot_expert, -1)
    routed = jnp.dot(table.T, slot_weight[:, None] * returned_wide, precision=highest)
    result = ((middle + routed) * keep_mask).astype(jnp.bfloat16).reshape(shape_three)
    grad_result = cotangent.reshape(row_count, model_width).astype(jnp.float32) * keep_mask
    gathered_grad = jnp.dot(table, grad_result, precision=highest)
    grad_produced = (
        (slot_weight[:, None] * gathered_grad)
        .astype(jnp.bfloat16)
        .reshape(expert_count, capacity, model_width)
    )
    grad_arrived_out = lax.all_to_all(
        grad_produced, "experts", split_axis=0, concat_axis=1, tiled=True
    )[0]
    grad_slot_weight = jnp.sum(gathered_grad * returned_wide, -1)
    grad_hidden = jnp.dot(grad_arrived_out, w_down[0].T, preferred_element_type=jnp.float32)
    grad_w_down = jnp.dot(hidden_low.T, grad_arrived_out, preferred_element_type=jnp.float32)

    def activation(gate_in, up_in):
        return jax.nn.gelu(gate_in, approximate=True) * up_in

    _, activation_back = jax.vjp(activation, gate_pre, up_pre)
    grad_gate_pre, grad_up_pre = activation_back(grad_hidden)
    grad_gate_low = grad_gate_pre.astype(jnp.bfloat16)
    grad_up_low = grad_up_pre.astype(jnp.bfloat16)
    grad_w_gate = jnp.dot(arrived.T, grad_gate_low, preferred_element_type=jnp.float32)
    grad_w_up = jnp.dot(arrived.T, grad_up_low, preferred_element_type=jnp.float32)
    grad_arrived = (
        jnp.dot(grad_gate_low, w_gate[0].T, preferred_element_type=jnp.float32)
        + jnp.dot(grad_up_low, w_up[0].T, preferred_element_type=jnp.float32)
    ).astype(jnp.bfloat16)
    grad_returned = lax.all_to_all(
        grad_arrived[None], "experts", split_axis=1, concat_axis=0, tiled=True
    ).reshape(expert_count * capacity, model_width)
    expert_sums = (
        lax.psum_scatter(
            grad_w_gate[None].astype(jnp.bfloat16), "context", scatter_dimension=1, tiled=True
        ).astype(jnp.float32),
        lax.psum_scatter(
            grad_w_up[None].astype(jnp.bfloat16), "context", scatter_dimension=1, tiled=True
        ).astype(jnp.float32),
        lax.psum_scatter(
            grad_w_down[None].astype(jnp.bfloat16), "context", scatter_dimension=1, tiled=True
        ).astype(jnp.float32),
    )
    grad_second = jnp.dot(table_low.T, grad_returned, preferred_element_type=jnp.float32)
    grad_gates = jnp.dot(table.T, grad_slot_weight[:, None] * slot_expert, precision=highest)
    grad_logits = gates * (grad_gates - jnp.sum(gates * grad_gates, -1, keepdims=True))
    grad_router = jnp.dot(second_wide.T, grad_logits, precision=highest)
    grad_second = grad_second + jnp.dot(grad_logits, router.T, precision=highest)
    grad_middle_norm, grad_norm_ffn = norm_back(middle, norm_ffn, grad_second)
    grad_middle = grad_result + grad_middle_norm
    grad_middle_low = grad_middle.astype(jnp.bfloat16)
    grad_w_out = jnp.dot(attended_low.T, grad_middle_low, preferred_element_type=jnp.float32)
    grad_attended_low = jnp.dot(
        grad_middle_low, w_out.T, preferred_element_type=jnp.float32
    ).astype(jnp.bfloat16)
    grad_attended_four = grad_attended_low.reshape(shape_four)
    grad_attended_three = grad_attended_low.reshape(shape_three)
    delta = jnp.sum(grad_attended_four.astype(jnp.float32) * attended, -1)
    local_queries = (query_four, grad_attended_four, log_total, delta, positions)
    grad_start = (jnp.zeros(shape_four, jnp.float32), jnp.zeros(rel_bias.shape, jnp.float32))
    query_offset = jnp.int32(0)
    query_key_all = lax.all_gather(key_three, ("experts", "context"), axis=1, tiled=True)
    query_value_all = lax.all_gather(value_three, ("experts", "context"), axis=1, tiled=True)
    piece_rows = query_key_all.shape[1]
    query_block_rows = math.gcd(piece_rows, 8 * per_slot)

    def query_visit(carried, block_id):
        local_at = block_id * query_block_rows
        key_rows = lax.dynamic_slice_in_dim(query_key_all, local_at, query_block_rows, 1).reshape(
            slot_count, query_block_rows, head_count, head_size
        )
        value_rows = lax.dynamic_slice_in_dim(
            query_value_all, local_at, query_block_rows, 1
        ).reshape(slot_count, query_block_rows, head_count, head_size)
        key_pos = query_offset + local_at + jnp.arange(query_block_rows, dtype=jnp.int32)
        grad_query, _, _, grad_table = pair_grads(
            local_queries, (key_rows, value_rows, key_pos), rel_bias, lengths, score_scale
        )
        return ((carried[0] + grad_query, carried[1] + grad_table), None)

    carried, _ = lax.scan(
        query_visit, grad_start, jnp.arange(piece_rows // query_block_rows, dtype=jnp.int32)
    )
    grad_query_four, grad_table = carried
    log_whole, delta_whole = (
        lax.all_gather(log_total, ("experts", "context"), axis=1, tiled=True),
        lax.all_gather(delta, ("experts", "context"), axis=1, tiled=True),
    )
    local_keys = (key_four, value_four, positions)
    zero_four = jnp.zeros(shape_four, jnp.float32)
    key_offset = jnp.int32(0)
    query_all = lax.all_gather(
        query_flat.reshape(shape_three), ("experts", "context"), axis=1, tiled=True
    )
    grad_all = lax.all_gather(grad_attended_three, ("experts", "context"), axis=1, tiled=True)
    piece_rows = query_all.shape[1]
    key_block_rows = math.gcd(piece_rows, 8 * per_slot)

    def key_visit(carried, block_id):
        local_at = block_id * key_block_rows
        whole_at = key_offset + local_at
        query_rows = lax.dynamic_slice_in_dim(query_all, local_at, key_block_rows, 1).reshape(
            slot_count, key_block_rows, head_count, head_size
        )
        grad_rows = lax.dynamic_slice_in_dim(grad_all, local_at, key_block_rows, 1).reshape(
            slot_count, key_block_rows, head_count, head_size
        )
        log_rows = lax.dynamic_slice_in_dim(log_whole, whole_at, key_block_rows, 1)
        delta_rows = lax.dynamic_slice_in_dim(delta_whole, whole_at, key_block_rows, 1)
        query_pos = whole_at + jnp.arange(key_block_rows, dtype=jnp.int32)
        _, grad_key, grad_value, _ = pair_grads(
            (query_rows, grad_rows, log_rows, delta_rows, query_pos),
            local_keys,
            rel_bias,
            lengths,
            score_scale,
        )
        return ((carried[0] + grad_key, carried[1] + grad_value), None)

    carried, _ = lax.scan(
        key_visit, (zero_four, zero_four), jnp.arange(piece_rows // key_block_rows, dtype=jnp.int32)
    )
    grad_key_four, grad_value_four = carried
    grad_query_low = grad_query_four.reshape(row_count, model_width).astype(jnp.bfloat16)
    grad_key_low = grad_key_four.reshape(row_count, model_width).astype(jnp.bfloat16)
    grad_value_low = grad_value_four.reshape(row_count, model_width).astype(jnp.bfloat16)
    grad_w_query = jnp.dot(normed.T, grad_query_low, preferred_element_type=jnp.float32)
    grad_w_key = jnp.dot(normed.T, grad_key_low, preferred_element_type=jnp.float32)
    grad_w_value = jnp.dot(normed.T, grad_value_low, preferred_element_type=jnp.float32)
    grad_normed = (
        jnp.dot(grad_query_low, w_query.T, preferred_element_type=jnp.float32)
        + jnp.dot(grad_key_low, w_key.T, preferred_element_type=jnp.float32)
        + jnp.dot(grad_value_low, w_value.T, preferred_element_type=jnp.float32)
    )
    grad_input_norm, grad_norm_attn = norm_back(inputs, norm_attn, grad_normed)
    grad_tokens = (grad_middle + grad_input_norm).reshape(shape_three)
    dense = lax.psum(
        (
            grad_norm_attn,
            grad_w_query,
            grad_w_key,
            grad_w_value,
            grad_w_out,
            grad_table,
            grad_norm_ffn,
            grad_router,
        ),
        ("experts", "context"),
    )
    return (
        result,
        grad_tokens,
        dense[0],
        dense[1],
        dense[2],
        dense[3],
        dense[4],
        dense[5],
        dense[6],
        dense[7],
        expert_sums[0],
        expert_sums[1],
        expert_sums[2],
    )


MESH = pl.DeviceIdType.MESH
BF = jnp.bfloat16
F32 = jnp.float32
VMEM = pltpu.VMEM
ORDERS = (("x", "y", "l"), ("y", "l", "x"), ("l", "x", "y"))
COLUMNS = ((0, 384), (384, 384), (768, 256))
BIG = -1e30
TILE = 256
PLACES = 80
SHARE = 704
NT = (((1,), (1,)), ((), ()))
TN = (((0,), (0,)), ((), ()))
CUBE_SEMS = [pltpu.SemaphoreType.DMA((3, 8))] * 4


def spot():
    e = lax.axis_index("experts")
    c = lax.axis_index("context")
    return dict(k=lax.rem(e, 2), y=e // 2, x=lax.rem(c, 2), l=lax.rem(c // 2, 2), h=c // 4)


def flip(b, names):
    return {n: (1 - v if n in names else v) for n, v in b.items()}


def device(b):
    return {"experts": b["y"] * 2 + b["k"], "context": b["h"] * 4 + b["l"] * 2 + b["x"]}


def row_of(b):
    return b["y"] * 2 + b["k"]


def col_of(b):
    return b["l"] * 2 + b["x"]


def slot_of(b):
    return row_of(b) * 4 + col_of(b)


def greet(peers):
    barrier = pltpu.get_barrier_semaphore()
    for peer in peers:
        pl.semaphore_signal(barrier, inc=1, device_id=peer, device_id_type=MESH)
    pl.semaphore_wait(barrier, len(peers))


def cube_peers(b):
    return [device(flip(b, [n])) for n in ("x", "y", "l", "k")]


def cube_all(b):
    peers = []
    for step in range(1, 16):
        s = lax.rem(slot_of(b) + step, 16)
        peers.append({"experts": s // 4, "context": b["h"] * 4 + lax.rem(s, 4)})
    return peers


def world_all(b):
    me = row_of(b) * 8 + b["h"] * 4 + col_of(b)
    peers = []
    for step in range(1, 32):
        j = lax.rem(me + step, 32)
        peers.append((j, {"experts": j // 8, "context": lax.rem(j, 8)}))
    return me, peers


def remote(src, dst, ssem, rsem, peer):
    return pltpu.make_async_remote_copy(
        src_ref=src, dst_ref=dst, send_sem=ssem, recv_sem=rsem, device_id=peer, device_id_type=MESH
    )


def names_of(order, t):
    return [order[i] for i in range(3) if (t >> i) & 1]


def gather_cube(b, view, ss, rs, cs, cr):
    started = []
    core = device(flip(b, ["k"]))

    def link(p, t, i):
        ref = view(flip(b, names_of(ORDERS[p], t)), p)
        n = t | (1 << i)
        cp = remote(ref, ref, ss.at[p, n], rs.at[p, n], device(flip(b, [ORDERS[p][i]])))
        cp.start()
        started.append(cp)

    def across(p, t):
        ref = view(flip(b, names_of(ORDERS[p], t)), p)
        cp = remote(ref, ref, cs.at[p, t], cr.at[p, t], core)
        cp.start()
        started.append(cp)

    for i in range(3):
        for p in range(3):
            link(p, 0, i)
    for p in range(3):
        across(p, 0)
    for t in range(1, 8):
        for p in range(3):
            ref = view(flip(b, names_of(ORDERS[p], t)), p)
            remote(ref, ref, ss.at[p, t], rs.at[p, t], core).wait_recv()
            for i in range(t.bit_length(), 3):
                link(p, t, i)
            across(p, t)
    for cp in started:
        cp.wait_send()
    for p in range(3):
        for t in range(8):
            ref = view(flip(b, names_of(ORDERS[p], t) + ["k"]), p)
            remote(ref, ref, cs.at[p, t], cr.at[p, t], core).wait_recv()


def eighth(b):
    return b["y"] * 4 + b["l"] * 2 + b["x"]


def scatter_cube(b, parts, acc, landing, ss, rs, cs, cr):
    started = []
    core = device(flip(b, ["k"]))
    combos = [(y, l, x) for y in range(2) for l in range(2) for x in range(2)]
    order = sorted(range(8), key=lambda t: -bin(t).count("1"))

    def bits_t(t):
        return flip(b, [n for i, n in enumerate(("x", "y", "l")) if (t >> i) & 1])

    for t in order:
        there = flip(bits_t(t), ["k"])
        cp = remote(parts.at[slot_of(there)], acc.at[eighth(there)], cs.at[0, t], cr.at[0, t], core)
        cp.start()
        started.append(cp)
    for t in order:
        here = bits_t(t)
        n = eighth(here)
        remote(parts.at[slot_of(here)], acc.at[n], cs.at[0, t], cr.at[0, t], core).wait_recv()
        acc[n] = (acc[n].astype(F32) + parts[slot_of(here)].astype(F32)).astype(BF)
    for step in range(3):
        rest = 2 - step
        count = 1 << rest
        for p in range(3):
            c0, cn = COLUMNS[p]
            first = ORDERS[p][step]
            others = ORDERS[p][step + 1 :]
            for t in range(count - 1, -1, -1):
                there = flip(b, [first] + [others[i] for i in range(rest) if (t >> i) & 1])
                n = count + t
                cp = remote(
                    acc.at[eighth(there), :, pl.ds(c0, cn)],
                    landing.at[n, :, pl.ds(c0, cn)],
                    ss.at[p, n],
                    rs.at[p, n],
                    device(flip(b, [first])),
                )
                cp.start()
                started.append(cp)
        for p in range(3):
            c0, cn = COLUMNS[p]
            others = ORDERS[p][step + 1 :]
            for t in range(count - 1, -1, -1):
                here = flip(b, [others[i] for i in range(rest) if (t >> i) & 1])
                n = count + t
                target = eighth(here)
                ref = landing.at[n, :, pl.ds(c0, cn)]
                remote(ref, ref, ss.at[p, n], rs.at[p, n], core).wait_recv()
                acc[target, :, c0 : c0 + cn] = (
                    acc[target, :, c0 : c0 + cn].astype(F32)
                    + landing[n, :, c0 : c0 + cn].astype(F32)
                ).astype(BF)
    for cp in started:
        cp.wait_send()


def params(cid=None, mib=60):
    if cid is None:
        return pltpu.CompilerParams(vmem_limit_bytes=mib * 2**20)
    return pltpu.CompilerParams(
        collective_id=cid, has_side_effects=True, vmem_limit_bytes=mib * 2**20
    )


def call(body, outs, scratch, cid, *args, flops=0, data=0):
    return pl.pallas_call(
        body,
        out_shape=outs,
        in_specs=[pl.BlockSpec(memory_space=VMEM)] * len(args),
        out_specs=[pl.BlockSpec(memory_space=VMEM)] * len(outs),
        scratch_shapes=scratch,
        compiler_params=params(cid),
        cost_estimate=pl.CostEstimate(flops=flops, bytes_accessed=data, transcendentals=0),
    )(*args)


def shape(dims, kind=BF):
    return jax.ShapeDtypeStruct(dims, kind)


def gather_sequence(b, whole, staged, sems, hs, hr):
    partner = device(flip(b, ["h"]))
    mine = whole.at[row_of(b), b["h"], col_of(b)]
    cp = remote(staged.at[1 - b["h"]], mine, hs, hr, partner)
    cp.start()
    whole[row_of(b), b["h"], col_of(b)] = staged[b["h"]]
    theirs = whole.at[row_of(b), 1 - b["h"], col_of(b)]
    remote(theirs, theirs, hs, hr, partner).wait_recv()

    def view(v, p):
        c0, cn = COLUMNS[p]
        return whole.at[row_of(v), :, col_of(v), :, pl.ds(c0, cn)]

    gather_cube(b, view, *sems)
    cp.wait_send()


def group_view(ref):
    def view(v, p):
        c0, cn = COLUMNS[p]
        return ref.at[slot_of(v), :, pl.ds(c0, cn)]

    return view


def send_small(b, src, into, ss, rs):
    copies = []
    for step, peer in enumerate(cube_all(b)):
        cp = remote(src, into.at[slot_of(b)], ss.at[step], rs.at[step], peer)
        cp.start()
        copies.append(cp)
    return copies


def wait_small(b, into, ss, rs, copies):
    me = slot_of(b)
    for step in range(15):
        came = into.at[lax.rem(me + 15 - step, 16)]
        remote(came, came, ss.at[step], rs.at[step], device(b)).wait_recv()
    for cp in copies:
        cp.wait_send()


def inverse_rms(values):
    return lax.rsqrt(jnp.mean(values * values, axis=-1, keepdims=True) + norm_epsilon)


def first_body(tokens, cot, gain, picks, h1, dy, picks_all, staged, *sems):
    b = spot()
    greet([device(flip(b, ["h"]))] + cube_all(b))
    copies = send_small(b, picks, picks_all, sems[10], sems[11])
    picks_all[slot_of(b)] = picks[...]
    for s in range(2):
        rows = tokens[s].astype(F32)
        staged[s] = (rows * inverse_rms(rows) * gain[...]).astype(BF)
    gather_sequence(b, h1, staged, sems[0:4], sems[8], sems[9])
    dy[slot_of(b)] = cot[...]
    gather_cube(b, group_view(dy), *sems[4:8])
    wait_small(b, picks_all, sems[10], sems[11], copies)


def lane(shape_, dim=1):
    return lax.broadcasted_iota(jnp.int32, shape_, dim)


def near_tiles(row):
    wide = jnp.broadcast_to(row, (TILE, 2 * TILE))
    wide = pltpu.roll(wide, 0, 1, stride=1, stride_axis=0)
    later = lax.broadcasted_iota(jnp.int32, (TILE, TILE), 0) > lane((TILE, TILE))
    return [jnp.where(later, BIG, wide[:, :TILE]), wide[:, TILE:]]


def pack_halves(rows):
    n = rows.shape[0] // 64
    four = rows.reshape(n, 2, 32, 128)
    return jnp.where(
        lax.broadcasted_iota(jnp.int32, (n, 32, 128), 2) < 64,
        four[:, 0],
        pltpu.roll(four[:, 1].reshape(n * 32, 128), 64, 1).reshape(n, 32, 128),
    )


def attend_body(length, h1, w3, dist, packed, out_t, qs, ks, vs, lse, strip, v_t, weights):
    limit = length[0]
    for i in range(8):
        rows = slice(i * TILE, (i + 1) * TILE)
        p = jnp.dot(h1[rows], w3[...], preferred_element_type=F32)
        spot_lane = lane((TILE, 128))
        where_at = lax.broadcasted_iota(jnp.int32, (TILE, 128), 0) + i * TILE
        one = spot_lane == 64
        qs[rows] = jnp.where(one, 1.0, p[:, :128] * 0.125).astype(BF)
        ks[rows] = jnp.where(one & (where_at >= limit), BIG, p[:, 128:256]).astype(BF)
        v = jnp.where(one, 1.0, p[:, 256:]).astype(BF)
        vs[rows] = v
        v_t[:, rows] = v.astype(F32).T.astype(BF)
    near = near_tiles(dist[0:1])
    for i in range(8):
        cols = slice(i * TILE, (i + 1) * TILE)
        q = qs[cols]
        top = None
        for j in range(i + 1):
            rows = slice(j * TILE, (j + 1) * TILE)
            s = lax.dot_general(ks[rows], q, NT, preferred_element_type=F32)
            if i - j < 2:
                s = s + near[i - j]
            strip[rows] = s
            m = jnp.max(s, axis=0, keepdims=True)
            top = m if top is None else jnp.maximum(top, m)
        for j in range(i + 1):
            rows = slice(j * TILE, (j + 1) * TILE)
            weights[rows] = jnp.exp(strip[rows] - top).astype(BF)
        n = (i + 1) * TILE
        o = jnp.dot(v_t[:, :n], weights[:n], preferred_element_type=F32)
        total = o[64:65]
        o = o / total
        lse[:, cols] = jnp.broadcast_to(top + jnp.log(total), (8, TILE))
        out_t[:, cols] = o[:64]
        packed[4 * i : 4 * i + 4] = pack_halves(o.T).astype(BF)


def unpack_halves(first, second):
    a = first.astype(F32)
    c = second.astype(F32)
    left = lane((32, 128)) < 64
    top = jnp.where(left, a, pltpu.roll(c, 64, 1))
    bottom = jnp.where(left, pltpu.roll(a, 64, 1), c)
    return top.astype(BF), bottom.astype(BF)


def everyone(b, src, dst_at, ss, rs):
    me, peers = world_all(b)
    copies = []
    for step, (j, peer) in enumerate(peers):
        cp = remote(src.at[j], dst_at(me), ss.at[step], rs.at[step], peer)
        cp.start()
        copies.append(cp)
    return me, copies


def everyone_wait(b, me, dst_at, ss, rs, copies):
    for step in range(31):
        came = dst_at(lax.rem(me + 31 - step, 32))
        remote(came, came, ss.at[step], rs.at[step], device(b)).wait_recv()
    for cp in copies:
        cp.wait_send()


def middle_body(packed, tokens, w_out, gain, router3, middle, h2_all, gates_all, land, joined, gates, *sems):
    b = spot()
    greet([peer for _, peer in world_all(b)[1]])

    def at(j):
        return land.at[j]

    me, copies = everyone(b, packed, at, sems[4], sems[5])
    land[me] = packed[me]
    everyone_wait(b, me, at, sems[4], sems[5], copies)
    for s in range(2):
        for pair in range(8):
            first, second = 2 * pair, 2 * pair + 1
            j0 = (first // 4) * 8 + s * 4 + first % 4
            j1 = (second // 4) * 8 + s * 4 + second % 4
            top, bottom = unpack_halves(land[j0], land[j1])
            cols = slice(pair * 128, pair * 128 + 128)
            joined[s * 64 : s * 64 + 32, cols] = top
            joined[s * 64 + 32 : s * 64 + 64, cols] = bottom
    x = tokens[...].astype(F32)
    mid = x + jnp.dot(joined[...], w_out[...], preferred_element_type=F32)
    middle[...] = mid
    h2 = (mid * inverse_rms(mid) * gain[...]).astype(BF)
    h2_all[slot_of(b)] = h2
    gather_half = group_view(h2_all)
    logits = jnp.dot(h2, router3[...], preferred_element_type=F32).T
    logits = logits[0:8] + logits[8:16] + logits[16:24]
    real = lax.broadcasted_iota(jnp.int32, (8, 128), 0) < 4
    logits = jnp.where(real, logits, BIG)
    g = jnp.exp(logits - jnp.max(logits, axis=0, keepdims=True))
    gates[...] = g / jnp.sum(g, axis=0, keepdims=True)
    small = send_small(b, gates, gates_all, sems[6], sems[7])
    gates_all[slot_of(b)] = gates[...]
    gather_cube(b, gather_half, *sems[0:4])
    wait_small(b, gates_all, sems[6], sems[7], small)


def expert_body(
    h2, dy, gates, picks, wg, wu, wd, routed, dh2, dgates, gwg, gwu, gwd, rows, grad, dexp, weight, hid, dgs, dus, outs, drs, dws
):
    mine = lax.axis_index("experts")
    mine_f = mine.astype(F32)
    first = picks[:, 0, :]
    second = picks[:, 1, :]
    chosen = jnp.where((first == mine_f) | (second == mine_f), 1.0, 0.0)
    earlier = jnp.where(
        lax.broadcasted_iota(jnp.int32, (128, 128), 0) < lane((128, 128)), 1.0, 0.0
    )
    place = jnp.dot(chosen.astype(BF), earlier.astype(BF), preferred_element_type=F32)
    place = jnp.where((chosen > 0.5) & (place < PLACES), place, -1.0)
    place_t = jnp.concatenate([place, jnp.full((112, 128), -1.0, F32)], axis=0).T
    level = lax.broadcasted_iota(jnp.int32, (PLACES, 128), 0).astype(F32)
    level_t = lane((128, PLACES)).astype(F32)
    is_mine = lax.broadcasted_iota(jnp.int32, (8, 128), 0) == mine
    for m in range(16):
        at = slice(m * PLACES, (m + 1) * PLACES)
        hit = jnp.where(level == place[m : m + 1], 1.0, 0.0)
        hit_low = hit.astype(BF)
        rows[at] = jnp.dot(hit_low, h2[m], preferred_element_type=F32).astype(BF)
        g = jnp.dot(hit_low, dy[m], preferred_element_type=F32)
        gate_row = jnp.sum(jnp.where(is_mine, gates[m], 0.0), axis=0, keepdims=True)
        w = jnp.sum(hit * gate_row, axis=1, keepdims=True)
        grad[at] = g.astype(BF)
        dexp[at] = (w * g).astype(BF)
        weight[at] = jnp.broadcast_to(w, (PLACES, 128))
    c0 = math.sqrt(2.0 / math.pi)
    c1 = 0.044715
    for i in range(5):
        at = slice(i * TILE, (i + 1) * TILE)
        r = rows[at]
        gp = jnp.dot(r, wg[...], preferred_element_type=F32)
        up = jnp.dot(r, wu[...], preferred_element_type=F32)
        sq = gp * gp
        th = jnp.tanh(c0 * gp * (1.0 + c1 * sq))
        half = 0.5 * (1.0 + th)
        act = gp * half
        slope = half + 0.5 * gp * (1.0 - th * th) * (c0 * (1.0 + 3.0 * c1 * sq))
        h = (act * up).astype(BF)
        hid[at] = h
        o = jnp.dot(h, wd[...], preferred_element_type=F32)
        w = weight[at, 0:1]
        outs[at] = (w * o).astype(BF)
        dws[at] = jnp.broadcast_to(
            jnp.sum(grad[at].astype(F32) * o, axis=1, keepdims=True), (TILE, 128)
        )
        dh = lax.dot_general(dexp[at], wd[...], NT, preferred_element_type=F32)
        dg = (dh * up * slope).astype(BF)
        du = (dh * act).astype(BF)
        dgs[at] = dg
        dus[at] = du
        drs[at] = (
            lax.dot_general(dg, wg[...], NT, preferred_element_type=F32)
            + lax.dot_general(du, wu[...], NT, preferred_element_type=F32)
        ).astype(BF)
    for m in range(16):
        at = slice(m * PLACES, (m + 1) * PLACES)
        back = jnp.where(place_t[:, m : m + 1] == level_t, 1.0, 0.0).astype(BF)
        routed[m] = jnp.dot(back, outs[at], preferred_element_type=F32).astype(BF)
        dh2[m] = jnp.dot(back, drs[at], preferred_element_type=F32).astype(BF)
        hit = jnp.where(level == place[m : m + 1], 1.0, 0.0)
        dgates[m] = jnp.broadcast_to(
            jnp.sum(hit * dws[at], axis=0, keepdims=True), (8, 128)
        )
    gwd[...] = lax.dot_general(hid[...], dexp[...], TN, preferred_element_type=F32).astype(BF)
    gwg[...] = lax.dot_general(rows[...], dgs[...], TN, preferred_element_type=F32).astype(BF)
    gwu[...] = lax.dot_general(rows[...], dus[...], TN, preferred_element_type=F32).astype(BF)


def norm_back_rows(values, gain, grad_in):
    inverse = inverse_rms(values)
    normed = values * inverse
    scaled = grad_in * gain
    out = inverse * (scaled - normed * jnp.mean(scaled * normed, axis=-1, keepdims=True))
    return out, jnp.sum(grad_in * normed, axis=0, keepdims=True)


def back_body(
    dh2, dgates, gates, cot, keep, middle, gain, router_t, h2_all, dm_all, dmid, smalls, acc, landing, dg_all, staged, *sems
):
    b = spot()
    greet([device(flip(b, ["h"]))] + cube_all(b))
    me = slot_of(b)
    copies = []
    for step, peer in enumerate(cube_all(b)):
        s = lax.rem(me + step + 1, 16)
        cp = remote(dgates.at[s], dg_all.at[me], sems[10].at[step], sems[11].at[step], peer)
        cp.start()
        copies.append(cp)
    dg_all[me] = dgates[me]
    scatter_cube(b, dh2, acc, landing, *sems[0:4])
    wait_small(b, dg_all, sems[10], sems[11], copies)
    level = lax.broadcasted_iota(jnp.int32, (8, 128), 0)
    dg = jnp.zeros((8, 128), F32)
    for e in range(4):
        total = dg_all[4 * e] + dg_all[4 * e + 1] + dg_all[4 * e + 2] + dg_all[4 * e + 3]
        dg = jnp.where(level == e, total, dg)
    g = gates[me]
    dl_t = g * (dg - jnp.sum(g * dg, axis=0, keepdims=True))
    dl = jnp.concatenate([dl_t, jnp.zeros((120, 128), F32)], axis=0).T
    d_h2 = acc[eighth(b)].astype(F32)
    for e in range(4):
        d_h2 = d_h2 + dl[:, e : e + 1] * router_t[e : e + 1]
    high = dl_t.astype(BF)
    rest = (dl_t - high.astype(F32)).astype(BF)
    h2 = h2_all[me]
    smalls[0:8] = jnp.dot(high, h2, preferred_element_type=F32) + jnp.dot(
        rest, h2, preferred_element_type=F32
    )
    grad_mid, grad_gain = norm_back_rows(middle[...], gain[...], d_h2)
    smalls[4:5] = grad_gain
    d_mid = cot[...].astype(F32) * keep[...] + grad_mid
    dmid[...] = d_mid
    staged[0] = d_mid[:64].astype(BF)
    staged[1] = d_mid[64:].astype(BF)
    gather_sequence(b, dm_all, staged, sems[4:8], sems[8], sems[9])


def attend_back_body(
    h1, dm, w_o, qs, ks, vs, out_t, lse, dist, packed, grads, sums, dos, k_t, delta, p_buf, s_buf, dq_t, dk, dv, near0, near1, left
):
    for i in range(8):
        rows = slice(i * TILE, (i + 1) * TILE)
        d = lax.dot_general(dm[rows], w_o[...], NT, preferred_element_type=F32).astype(BF)
        dos[rows] = d
        delta[:, rows] = jnp.broadcast_to(
            jnp.sum(d.astype(F32).T[:64] * out_t[:, rows], axis=0, keepdims=True), (8, TILE)
        )
        kt = ks[rows].astype(F32).T
        k_t[:, rows] = jnp.where(
            lax.broadcasted_iota(jnp.int32, (128, TILE), 0) == 64, 1.0, kt
        ).astype(BF)
    near = near_tiles(dist[0:1])
    near0[...] = jnp.zeros_like(near0)
    near1[...] = jnp.zeros_like(near1)
    for i in range(8):
        cols = slice(i * TILE, (i + 1) * TILE)
        q = qs[cols]
        do = dos[cols]
        level = lse[0:1, cols]
        dl = delta[0:1, cols]
        for j in range(i + 1):
            rows = slice(j * TILE, (j + 1) * TILE)
            s = lax.dot_general(ks[rows], q, NT, preferred_element_type=F32)
            if i - j < 2:
                s = s + near[i - j]
            p = jnp.exp(s - level)
            dp = lax.dot_general(vs[rows], do, NT, preferred_element_type=F32)
            ds = (p * (dp - dl)).astype(BF)
            p_buf[rows] = p.astype(BF)
            s_buf[rows] = ds
            if i == j:
                near0[...] += ds.astype(F32)
            if i - j == 1:
                near1[...] += ds.astype(F32)
        n = (i + 1) * TILE
        dq_t[:, cols] = jnp.dot(k_t[:, :n], s_buf[:n], preferred_element_type=F32)
        new_v = jnp.dot(p_buf[:n], do, preferred_element_type=F32)
        new_k = jnp.dot(s_buf[:n], q, preferred_element_type=F32)
        if i > 0:
            dv[: n - TILE] += new_v[: n - TILE]
            dk[: n - TILE] += new_k[: n - TILE]
        dv[n - TILE : n] = new_v[n - TILE :]
        dk[n - TILE : n] = new_k[n - TILE :]
    total = jnp.sum(dq_t[64:65, :].reshape(1, 16, 128), axis=1)
    skew = jnp.concatenate([near0[...], near1[...]], axis=1)
    level_u = lax.broadcasted_iota(jnp.int32, (TILE, 2 * TILE), 0)
    for bit in range(8):
        moved = pltpu.roll(skew, 2 * TILE - (1 << bit), 1)
        skew = jnp.where((level_u // (1 << bit)) % 2 == 1, moved, skew)
    sums[0:1] = jnp.sum(skew, axis=0, keepdims=True)
    sums[1:2] = jnp.concatenate([total, jnp.zeros((1, 384), F32)], axis=1)
    for i in range(8):
        rows = slice(i * TILE, (i + 1) * TILE)
        dq = dq_t[:, rows] * 0.125
        vk = jnp.where(lane((TILE, 128)) < 64, dv[rows], pltpu.roll(dk[rows], 64, 1)).T
        left[0:64, rows] = dq[:64].astype(BF)
        left[64:128, rows] = vk[64:128].astype(BF)
        left[128:192, rows] = vk[0:64].astype(BF)
        left[192:256, rows] = out_t[:, rows].astype(BF)
        blocks = slice(4 * i, 4 * i + 4)
        packed[blocks, 0:32] = pack_halves(dq.T).astype(BF)
        packed[blocks, 32:64] = pack_halves(dk[rows]).astype(BF)
        packed[blocks, 64:96] = pack_halves(dv[rows]).astype(BF)
    qkv = jnp.dot(left[0:192], h1[...], preferred_element_type=F32).astype(BF)
    grads[0] = qkv[0:128]
    grads[1, 0:64] = qkv[128:192]
    grads[1, 64:128] = jnp.dot(left[192:256], dm[...], preferred_element_type=F32).astype(BF)


def last_body(
    packed, grads, tokens, dmid, gain, wq, wk, wv, part, dtokens, whole, smalls, land, other, joined, inbox, *sems
):
    b = spot()
    greet([peer for _, peer in world_all(b)[1]])
    partner = device(flip(b, ["h"]))
    h = b["h"]
    trade = remote(grads.at[1 - h], other, sems[8].at[0], sems[9].at[0], partner)
    trade.start()

    def at(j):
        return land.at[j]

    me, copies = everyone(b, packed, at, sems[10], sems[11])
    land[me] = packed[me]
    trade.wait()
    me_slot = slot_of(b)
    whole[h, me_slot] = (grads[h].astype(F32) + other[...].astype(F32)).astype(BF)
    share = remote(
        whole.at[h, me_slot], whole.at[h, me_slot], sems[8].at[1], sems[9].at[1], partner
    )
    share.start()

    def view_of(side):
        def view(v, p):
            c0, cn = COLUMNS[p]
            return whole.at[side, slot_of(v), :, pl.ds(c0, cn)]

        return view

    gather_cube(b, view_of(h), *sems[0:4])
    theirs = whole.at[1 - h, me_slot]
    share.wait_send()
    remote(theirs, theirs, sems[8].at[1], sems[9].at[1], partner).wait_recv()
    gather_cube(b, view_of(1 - h), *sems[4:8])
    everyone_wait(b, me, at, sems[10], sems[11], copies)
    for kind in range(3):
        for s in range(2):
            for pair in range(8):
                first, second = 2 * pair, 2 * pair + 1
                j0 = (first // 4) * 8 + s * 4 + first % 4
                j1 = (second // 4) * 8 + s * 4 + second % 4
                span = slice(kind * 32, kind * 32 + 32)
                top, bottom = unpack_halves(land[j0, span], land[j1, span])
                cols = slice(pair * 128, pair * 128 + 128)
                joined[kind, s * 64 : s * 64 + 32, cols] = top
                joined[kind, s * 64 + 32 : s * 64 + 64, cols] = bottom
    d_h1 = (
        lax.dot_general(joined[0], wq[...], NT, preferred_element_type=F32)
        + lax.dot_general(joined[1], wk[...], NT, preferred_element_type=F32)
        + lax.dot_general(joined[2], wv[...], NT, preferred_element_type=F32)
    )
    grad_in, grad_gain = norm_back_rows(tokens[...].astype(F32), gain[...], d_h1)
    dtokens[...] = dmid[...] + grad_in
    smalls[...] = part[...]
    smalls[5:6] = grad_gain
    for step, name in enumerate(("k", "x", "y", "l", "h")):
        cp = remote(
            smalls, inbox.at[step], sems[12].at[step], sems[13].at[step], device(flip(b, [name]))
        )
        cp.start()
        cp.wait()
        smalls[...] = smalls[...] + inbox[step]


def routed_body(routed, middle, keep, gwg, gwu, gwd, result, down, wide, acc, landing, inbox_w, inbox_d, half, *sems):
    b = spot()
    h = b["h"]
    col = col_of(b)
    partner = device(flip(b, ["h"]))
    around = []
    for names in (["x"], ["l"], ["x", "l"]):
        around.append(flip(b, names))
    greet([partner] + cube_peers(b) + [device(around[2])])
    trades = [
        remote(gwg.at[1 - h], inbox_w.at[0], sems[4].at[0], sems[5].at[0], partner),
        remote(gwu.at[1 - h], inbox_w.at[1], sems[4].at[1], sems[5].at[1], partner),
        remote(gwd.at[1 - h], inbox_d, sems[4].at[2], sems[5].at[2], partner),
    ]
    for cp in trades:
        cp.start()
    scatter_cube(b, routed, acc, landing, *sems[0:4])
    result[...] = (
        (middle[...] + acc[eighth(b)].astype(F32)) * keep[...]
    ).astype(BF)
    started = []
    for n, g in enumerate((gwg, gwu)):
        trades[n].wait()
        half[n] = (g[h].astype(F32) + inbox_w[n].astype(F32)).astype(BF)
        for i, there in enumerate(around):
            cp = remote(
                half.at[n, col_of(there)],
                wide.at[n, col],
                sems[6].at[3 * n + i],
                sems[7].at[3 * n + i],
                device(there),
            )
            cp.start()
            started.append(cp)
        wide[n, col] = half[n, col]
    trades[2].wait()
    down[...] = gwd[h].astype(F32) + inbox_d[...].astype(F32)
    for n in range(2):
        for i, there in enumerate(around):
            ref = wide.at[n, col_of(there)]
            remote(ref, ref, sems[6].at[3 * n + i], sems[7].at[3 * n + i], device(there)).wait_recv()
    for cp in started:
        cp.wait_send()


def distance_buckets():
    table = []
    for distance in range(2 * TILE):
        table.append(bucket_of(distance, 32, MAXDIST))
    return np.array(table, np.int32)


def on_device_fast(
    tokens,
    lengths,
    expert_index,
    cotangent,
    norm_attn,
    w_query,
    w_key,
    w_value,
    w_out,
    rel_bias,
    norm_ffn,
    router,
    w_gate,
    w_up,
    w_down,
):
    dma = pltpu.SemaphoreType.DMA
    b = spot()
    head = slot_of(b)
    col = col_of(b)
    device_at = lax.axis_index(("experts", "context"))
    positions = device_at * 64 + jnp.arange(64, dtype=jnp.int32)
    live = positions[None, :] < lengths[:, None]
    keep = live.reshape(128, 1).astype(F32)
    picks = jnp.where(live[:, :, None], expert_index, -1).astype(F32).reshape(128, 2).T
    picks = jnp.concatenate([picks, jnp.zeros((6, 128), F32)], axis=0)
    gain_attn = norm_attn.reshape(1, 1024)
    gain_ffn = norm_ffn.reshape(1, 1024)
    flat = tokens.reshape(128, 1024)
    cot = cotangent.reshape(128, 1024)

    def head_columns(w):
        return jnp.pad(lax.dynamic_slice_in_dim(w, head * 64, 64, 1), ((0, 0), (0, 64)))

    w3 = jnp.concatenate([head_columns(w_query), head_columns(w_key), head_columns(w_value)], axis=1)
    w_o = jnp.pad(lax.dynamic_slice_in_dim(w_out, head * 64, 64, 0), ((0, 64), (0, 0)))
    buckets = distance_buckets()
    onehot = np.zeros((2 * TILE, 32), np.float32)
    onehot[np.arange(2 * TILE), buckets] = 1.0
    bias = lax.dynamic_slice_in_dim(rel_bias, head, 1, 1)[:, 0]
    by_distance = jnp.dot(jnp.asarray(onehot), bias - bias[31], precision=highest)
    dist = jnp.broadcast_to(by_distance[None], (8, 2 * TILE))
    mine = lax.dynamic_slice_in_dim(lengths, b["h"], 1, 0)

    def columns_share(w):
        return lax.dynamic_index_in_dim(
            w[0].reshape(1024, 2, 4, 352), col, 2, keepdims=False
        ).reshape(1024, SHARE)

    wg = columns_share(w_gate)
    wu = columns_share(w_up)
    wd = lax.dynamic_index_in_dim(
        w_down[0].reshape(2, 4, 352, 1024), col, 1, keepdims=False
    ).reshape(SHARE, 1024)
    high = router.astype(BF)
    rest = router - high.astype(F32)
    mid = rest.astype(BF)
    lo = (rest - mid.astype(F32)).astype(BF)
    router3 = jnp.concatenate(
        [jnp.pad(r, ((0, 0), (0, 4))) for r in (high, mid, lo)] + [jnp.zeros((1024, 104), BF)], axis=1
    )
    router_t = jnp.pad(router.T, ((0, 4), (0, 0)))

    h1, dy_all, picks_all = call(
        first_body,
        [shape((4, 2, 4, 64, 1024)), shape((16, 128, 1024)), shape((16, 8, 128), F32)],
        [VMEM((2, 64, 1024), BF)] + CUBE_SEMS + CUBE_SEMS + [dma(()), dma(()), dma((15,)), dma((15,))],
        1,
        tokens,
        cot,
        gain_attn,
        picks,
    )
    h1 = h1.reshape(2048, 1024)
    packed, out_t, qs, ks, vs, lse = pl.pallas_call(
        attend_body,
        out_shape=[
            shape((32, 32, 128)),
            shape((64, 2048), F32),
            shape((2048, 128)),
            shape((2048, 128)),
            shape((2048, 128)),
            shape((8, 2048), F32),
        ],
        in_specs=[pl.BlockSpec(memory_space=pltpu.SMEM)] + [pl.BlockSpec(memory_space=VMEM)] * 3,
        out_specs=[pl.BlockSpec(memory_space=VMEM)] * 6,
        scratch_shapes=[VMEM((2048, TILE), F32), VMEM((128, 2048), BF), VMEM((2048, TILE), BF)],
        compiler_params=params(),
    )(mine, h1, w3, dist)
    middle, h2_all, gates_all = call(
        middle_body,
        [shape((128, 1024), F32), shape((16, 128, 1024)), shape((16, 8, 128), F32)],
        [VMEM((32, 32, 128), BF), VMEM((128, 1024), BF), VMEM((8, 128), F32)]
        + CUBE_SEMS
        + [dma((31,)), dma((31,)), dma((15,)), dma((15,))],
        2,
        packed,
        flat,
        w_out,
        gain_ffn,
        router3,
    )
    routed, dh2, dgates, gwg, gwu, gwd = call(
        expert_body,
        [
            shape((16, 128, 1024)),
            shape((16, 128, 1024)),
            shape((16, 8, 128), F32),
            shape((1024, SHARE)),
            shape((1024, SHARE)),
            shape((SHARE, 1024)),
        ],
        [VMEM((1280, 1024), BF)] * 3
        + [VMEM((1280, 128), F32)]
        + [VMEM((1280, SHARE), BF)] * 3
        + [VMEM((1280, 1024), BF)] * 2
        + [VMEM((1280, 128), F32)],
        None,
        h2_all,
        dy_all,
        gates_all,
        picks_all,
        wg,
        wu,
        wd,
    )
    dm_all, dmid, smalls = call(
        back_body,
        [shape((4, 2, 4, 64, 1024)), shape((128, 1024), F32), shape((8, 1024), F32)],
        [
            VMEM((8, 128, 1024), BF),
            VMEM((8, 128, 1024), BF),
            VMEM((16, 8, 128), F32),
            VMEM((2, 64, 1024), BF),
        ]
        + CUBE_SEMS
        + CUBE_SEMS
        + [dma(()), dma(()), dma((15,)), dma((15,))],
        3,
        dh2,
        dgates,
        gates_all,
        cot,
        keep,
        middle,
        gain_ffn,
        router_t,
        h2_all,
    )
    packed_back, grads, sums = call(
        attend_back_body,
        [shape((32, 96, 128)), shape((2, 128, 1024)), shape((8, 512), F32)],
        [
            VMEM((2048, 128), BF),
            VMEM((128, 2048), BF),
            VMEM((8, 2048), F32),
            VMEM((2048, TILE), BF),
            VMEM((2048, TILE), BF),
            VMEM((128, 2048), F32),
            VMEM((2048, 128), F32),
            VMEM((2048, 128), F32),
            VMEM((TILE, TILE), F32),
            VMEM((TILE, TILE), F32),
            VMEM((256, 2048), BF),
        ],
        None,
        h1,
        dm_all.reshape(2048, 1024),
        w_o,
        qs,
        ks,
        vs,
        out_t,
        lse,
        dist,
    )
    table = jnp.dot(sums[0], jnp.asarray(onehot), precision=highest)
    table = table.at[31].set(jnp.sum(sums[1]) - jnp.sum(table[:31]))
    row = lax.dynamic_update_slice_in_dim(jnp.zeros((1024,), F32), table, head * 32, 0)
    smalls = jnp.concatenate([smalls[:6], row[None], jnp.zeros((1, 1024), F32)], axis=0)
    dtokens, whole, smalls = call(
        last_body,
        [shape((128, 1024), F32), shape((2, 16, 128, 1024)), shape((8, 1024), F32)],
        [
            VMEM((32, 96, 128), BF),
            VMEM((128, 1024), BF),
            VMEM((3, 128, 1024), BF),
            VMEM((5, 8, 1024), F32),
        ]
        + CUBE_SEMS
        + CUBE_SEMS
        + [dma((2,)), dma((2,)), dma((31,)), dma((31,)), dma((5,)), dma((5,))],
        4,
        packed_back,
        grads,
        flat,
        dmid,
        gain_attn,
        w_query,
        w_key,
        w_value,
        smalls,
    )
    result, down, wide = call(
        routed_body,
        [shape((128, 1024)), shape((352, 1024), F32), shape((2, 4, 128, SHARE))],
        [
            VMEM((8, 128, 1024), BF),
            VMEM((8, 128, 1024), BF),
            VMEM((2, 4, 128, SHARE), BF),
            VMEM((352, 1024), BF),
            VMEM((2, 4, 128, SHARE), BF),
        ]
        + CUBE_SEMS
        + [dma((3,)), dma((3,)), dma((6,)), dma((6,))],
        5,
        routed,
        middle,
        keep,
        gwg.reshape(2, 4, 128, SHARE),
        gwu.reshape(2, 4, 128, SHARE),
        gwd.reshape(2, 352, 1024),
    )

    def widen(w):
        return (
            w.reshape(4, 128, 2, 352).transpose(1, 2, 0, 3).reshape(1, 128, 2816).astype(F32)
        )

    def dense(rows):
        return rows.reshape(1024, 1024).astype(F32)

    return (
        result.reshape(2, 64, 1024),
        dtokens.reshape(2, 64, 1024),
        smalls[5],
        dense(whole[0, :, 0:64]).T,
        dense(whole[0, :, 64:128]).T,
        dense(whole[1, :, 0:64]).T,
        dense(whole[1, :, 64:128]),
        smalls[6, :512].reshape(16, 32).T,
        smalls[4],
        smalls[0:4].T,
        widen(wide[0]),
        widen(wide[1]),
        down[None],
    )


def solution(mesh):
    sizes = dict(mesh.shape)
    fits = sizes == {"experts": 4, "context": 8}
    placed = (
        P(None, ("experts", "context"), None),
        P(),
        P(None, ("experts", "context"), None),
        P(None, ("experts", "context"), None),
        P(),
        P(),
        P(),
        P(),
        P(),
        P(),
        P(),
        P(),
        P("experts", None, None),
        P("experts", None, None),
        P("experts", None, None),
    )
    return jax.shard_map(
        on_device_fast if fits else on_device,
        mesh=mesh,
        in_specs=placed,
        out_specs=(
            P(None, ("experts", "context"), None),
            P(None, ("experts", "context"), None),
            P(),
            P(),
            P(),
            P(),
            P(),
            P(),
            P(),
            P(),
            P("experts", "context", None),
            P("experts", "context", None),
            P("experts", "context", None),
        ),
        check_vma=False,
    )
```

```python
import math

import jax
import jax.numpy as jnp
import numpy as np
from jax import lax
from jax.experimental import pallas as pl
from jax.experimental.pallas import tpu as pltpu
from jax.sharding import PartitionSpec as P

MAXDIST = 128


norm_epsilon = 1e-06
mask_fill = -1e30
highest = lax.Precision.HIGHEST


def bucket_of(distance, bucket_count, reach):
    exact = bucket_count // 2
    if distance < exact:
        return distance
    level = exact + int(
        math.log(distance / exact) / math.log(reach / exact) * (bucket_count - exact)
    )
    return min(level, bucket_count - 1)


def bucket_edges(bucket_count, reach):
    edges = []
    for level in range(1, bucket_count):
        distance = 0
        while bucket_of(distance, bucket_count, reach) < level:
            distance += 1
        edges.append(distance)
    return edges


def relative_bucket(query_pos, key_pos, bucket_count):
    distance = jnp.maximum(query_pos[:, None] - key_pos[None, :], 0)
    bucket = jnp.zeros(distance.shape, jnp.int32)
    for edge in bucket_edges(bucket_count, MAXDIST):
        bucket = bucket + (distance >= edge).astype(jnp.int32)
    return bucket


def rms_norm(values, gain):
    inverse = lax.rsqrt(jnp.mean(values * values, axis=-1, keepdims=True) + norm_epsilon)
    return values * inverse * gain


def norm_back(values, gain, grad_in):
    inverse = lax.rsqrt(jnp.mean(values * values, axis=-1, keepdims=True) + norm_epsilon)
    normed = values * inverse
    grad_normed = grad_in * gain
    grad_values = inverse * (
        grad_normed - normed * jnp.mean(grad_normed * normed, axis=-1, keepdims=True)
    )
    return (grad_values, jnp.sum(grad_in * normed, 0))


def score_block(query_rows, key_rows, rel_bias, query_pos, key_pos, lengths, score_scale):
    raw_scores = (
        jnp.einsum("sqhd,skhd->sqhk", query_rows, key_rows, preferred_element_type=jnp.float32)
        * score_scale
    )
    bucket = relative_bucket(query_pos, key_pos, rel_bias.shape[0])
    onehot = (bucket[:, :, None] == jnp.arange(rel_bias.shape[0], dtype=jnp.int32)).astype(
        jnp.float32
    )
    bias_rows = jnp.einsum("qkb,bh->qhk", onehot, rel_bias, precision=highest)
    causal = (key_pos[None, :] <= query_pos[:, None])[None]
    inside = key_pos[None, None, :] < lengths[:, None, None]
    allowed = (causal & inside)[:, :, None, :]
    return (raw_scores + bias_rows[None], allowed, onehot)


def pair_grads(query_set, key_set, rel_bias, lengths, score_scale):
    query_rows, grad_rows, log_total, delta, query_pos = query_set
    key_rows, value_rows, key_pos = key_set
    scores, allowed, onehot = score_block(
        query_rows, key_rows, rel_bias, query_pos, key_pos, lengths, score_scale
    )
    weights = jnp.where(allowed, jnp.exp(scores - log_total[..., None]), 0.0)
    grad_value = jnp.einsum(
        "sqhk,sqhd->skhd",
        weights.astype(jnp.bfloat16),
        grad_rows,
        preferred_element_type=jnp.float32,
    )
    grad_weights = jnp.einsum(
        "sqhd,skhd->sqhk", grad_rows, value_rows, preferred_element_type=jnp.float32
    )
    grad_scores = (weights * (grad_weights - delta[..., None])).astype(jnp.bfloat16)
    grad_query = score_scale * jnp.einsum(
        "sqhk,skhd->sqhd", grad_scores, key_rows, preferred_element_type=jnp.float32
    )
    grad_key = score_scale * jnp.einsum(
        "sqhk,sqhd->skhd", grad_scores, query_rows, preferred_element_type=jnp.float32
    )
    grad_table = jnp.einsum(
        "sqhk,qkb->bh", grad_scores, onehot.astype(jnp.bfloat16), preferred_element_type=jnp.float32
    )
    return (grad_query, grad_key, grad_value, grad_table)


def dispatch_table(expert_index, live_rows, expert_count, capacity):
    picked = expert_index.reshape(-1)
    live_pairs = jnp.broadcast_to(live_rows[:, :, None], expert_index.shape).reshape(-1)
    chosen = (
        (picked[:, None] == jnp.arange(expert_count, dtype=jnp.int32)[None, :])
        & live_pairs[:, None]
    ).astype(jnp.int32)
    earlier = jnp.cumsum(chosen, axis=0) - chosen
    position_in = jnp.sum(earlier * chosen, -1)
    kept_pairs = live_pairs & (position_in < capacity)
    slot_of = jnp.where(kept_pairs, picked * capacity + position_in, -1)
    matches = slot_of[None, :] == jnp.arange(expert_count * capacity, dtype=jnp.int32)[:, None]
    table = jnp.any(matches.reshape(expert_count * capacity, -1, 2), -1).astype(jnp.float32)
    slot_ids = jnp.arange(expert_count * capacity, dtype=jnp.int32) // capacity
    slot_expert = (slot_ids[:, None] == jnp.arange(expert_count, dtype=jnp.int32)[None, :]).astype(
        jnp.float32
    )
    return (table, slot_expert)


def on_device(
    tokens,
    lengths,
    expert_index,
    cotangent,
    norm_attn,
    w_query,
    w_key,
    w_value,
    w_out,
    rel_bias,
    norm_ffn,
    router,
    w_gate,
    w_up,
    w_down,
):
    slot_count, per_slot, model_width = tokens.shape
    head_count = rel_bias.shape[1]
    head_size = model_width // head_count
    expert_count = router.shape[1]
    capacity = (10 * slot_count * per_slot + 4 * expert_count - 1) // (4 * expert_count)
    score_scale = head_size ** (-0.5)
    row_count = slot_count * per_slot
    shape_four = (slot_count, per_slot, head_count, head_size)
    shape_three = (slot_count, per_slot, model_width)
    device_at = lax.axis_index(("experts", "context"))
    positions = device_at * per_slot + jnp.arange(per_slot, dtype=jnp.int32)
    live_rows = positions[None, :] < lengths[:, None]
    keep_mask = live_rows.reshape(row_count, 1).astype(jnp.float32)
    inputs = tokens.reshape(row_count, model_width).astype(jnp.float32)
    normed = rms_norm(inputs, norm_attn).astype(jnp.bfloat16)
    query_flat = jnp.dot(normed, w_query, preferred_element_type=jnp.float32).astype(jnp.bfloat16)
    key_flat = jnp.dot(normed, w_key, preferred_element_type=jnp.float32).astype(jnp.bfloat16)
    value_flat = jnp.dot(normed, w_value, preferred_element_type=jnp.float32).astype(jnp.bfloat16)
    query_four = query_flat.reshape(shape_four)
    key_four = key_flat.reshape(shape_four)
    value_four = value_flat.reshape(shape_four)
    key_three = key_flat.reshape(shape_three)
    value_three = value_flat.reshape(shape_three)
    start_state = (
        jnp.zeros(shape_four, jnp.float32),
        jnp.full((slot_count, per_slot, head_count), mask_fill, jnp.float32),
        jnp.zeros((slot_count, per_slot, head_count), jnp.float32),
    )
    offset = jnp.int32(0)
    key_all = lax.all_gather(key_three, ("experts", "context"), axis=1, tiled=True)
    value_all = lax.all_gather(value_three, ("experts", "context"), axis=1, tiled=True)
    piece_rows = key_all.shape[1]
    block_rows = math.gcd(piece_rows, 8 * per_slot)

    def forward_visit(carried, block_id):
        running, running_max, denominator = carried
        local_at = block_id * block_rows
        key_rows = lax.dynamic_slice_in_dim(key_all, local_at, block_rows, 1).reshape(
            slot_count, block_rows, head_count, head_size
        )
        value_rows = lax.dynamic_slice_in_dim(value_all, local_at, block_rows, 1).reshape(
            slot_count, block_rows, head_count, head_size
        )
        key_pos = offset + local_at + jnp.arange(block_rows, dtype=jnp.int32)
        scores, allowed, _ = score_block(
            query_four, key_rows, rel_bias, positions, key_pos, lengths, score_scale
        )
        scores = jnp.where(allowed, scores, mask_fill)
        new_max = jnp.maximum(running_max, jnp.max(scores, -1))
        factor = jnp.exp(running_max - new_max)
        weights = jnp.where(allowed, jnp.exp(scores - new_max[..., None]), 0.0)
        denominator = denominator * factor + jnp.sum(weights, -1)
        running = running * factor[..., None] + jnp.einsum(
            "sqhk,skhd->sqhd",
            weights.astype(jnp.bfloat16),
            value_rows,
            preferred_element_type=jnp.float32,
        )
        return ((running, new_max, denominator), None)

    carried, _ = lax.scan(
        forward_visit, start_state, jnp.arange(piece_rows // block_rows, dtype=jnp.int32)
    )
    running, running_max, denominator = carried
    attended = running / denominator[..., None]
    log_total = running_max + jnp.log(denominator)
    attended_low = attended.reshape(row_count, model_width).astype(jnp.bfloat16)
    middle = inputs + jnp.dot(attended_low, w_out, preferred_element_type=jnp.float32)
    second_low = rms_norm(middle, norm_ffn).astype(jnp.bfloat16)
    second_wide = second_low.astype(jnp.float32)
    logits = jnp.dot(second_wide, router, precision=highest)
    gates = jax.nn.softmax(logits, axis=-1)
    table, slot_expert = dispatch_table(expert_index, live_rows, expert_count, capacity)
    table_low = table.astype(jnp.bfloat16)
    dispatched = jnp.dot(table_low, second_low, preferred_element_type=jnp.float32).astype(
        jnp.bfloat16
    )
    arrived = lax.all_to_all(
        dispatched.reshape(expert_count, capacity, model_width),
        "experts",
        split_axis=0,
        concat_axis=1,
        tiled=True,
    )[0]
    gate_pre = jnp.dot(arrived, w_gate[0], preferred_element_type=jnp.float32)
    up_pre = jnp.dot(arrived, w_up[0], preferred_element_type=jnp.float32)
    hidden_low = (jax.nn.gelu(gate_pre, approximate=True) * up_pre).astype(jnp.bfloat16)
    produced = jnp.dot(hidden_low, w_down[0], preferred_element_type=jnp.float32).astype(
        jnp.bfloat16
    )
    returned = lax.all_to_all(
        produced[None], "experts", split_axis=1, concat_axis=0, tiled=True
    ).reshape(expert_count * capacity, model_width)
    returned_wide = returned.astype(jnp.float32)
    slot_weight = jnp.sum(jnp.dot(table, gates, precision=highest) * slot_expert, -1)
    routed = jnp.dot(table.T, slot_weight[:, None] * returned_wide, precision=highest)
    result = ((middle + routed) * keep_mask).astype(jnp.bfloat16).reshape(shape_three)
    grad_result = cotangent.reshape(row_count, model_width).astype(jnp.float32) * keep_mask
    gathered_grad = jnp.dot(table, grad_result, precision=highest)
    grad_produced = (
        (slot_weight[:, None] * gathered_grad)
        .astype(jnp.bfloat16)
        .reshape(expert_count, capacity, model_width)
    )
    grad_arrived_out = lax.all_to_all(
        grad_produced, "experts", split_axis=0, concat_axis=1, tiled=True
    )[0]
    grad_slot_weight = jnp.sum(gathered_grad * returned_wide, -1)
    grad_hidden = jnp.dot(grad_arrived_out, w_down[0].T, preferred_element_type=jnp.float32)
    grad_w_down = jnp.dot(hidden_low.T, grad_arrived_out, preferred_element_type=jnp.float32)

    def activation(gate_in, up_in):
        return jax.nn.gelu(gate_in, approximate=True) * up_in

    _, activation_back = jax.vjp(activation, gate_pre, up_pre)
    grad_gate_pre, grad_up_pre = activation_back(grad_hidden)
    grad_gate_low = grad_gate_pre.astype(jnp.bfloat16)
    grad_up_low = grad_up_pre.astype(jnp.bfloat16)
    grad_w_gate = jnp.dot(arrived.T, grad_gate_low, preferred_element_type=jnp.float32)
    grad_w_up = jnp.dot(arrived.T, grad_up_low, preferred_element_type=jnp.float32)
    grad_arrived = (
        jnp.dot(grad_gate_low, w_gate[0].T, preferred_element_type=jnp.float32)
        + jnp.dot(grad_up_low, w_up[0].T, preferred_element_type=jnp.float32)
    ).astype(jnp.bfloat16)
    grad_returned = lax.all_to_all(
        grad_arrived[None], "experts", split_axis=1, concat_axis=0, tiled=True
    ).reshape(expert_count * capacity, model_width)
    expert_sums = (
        lax.psum_scatter(
            grad_w_gate[None].astype(jnp.bfloat16), "context", scatter_dimension=1, tiled=True
        ).astype(jnp.float32),
        lax.psum_scatter(
            grad_w_up[None].astype(jnp.bfloat16), "context", scatter_dimension=1, tiled=True
        ).astype(jnp.float32),
        lax.psum_scatter(
            grad_w_down[None].astype(jnp.bfloat16), "context", scatter_dimension=1, tiled=True
        ).astype(jnp.float32),
    )
    grad_second = jnp.dot(table_low.T, grad_returned, preferred_element_type=jnp.float32)
    grad_gates = jnp.dot(table.T, grad_slot_weight[:, None] * slot_expert, precision=highest)
    grad_logits = gates * (grad_gates - jnp.sum(gates * grad_gates, -1, keepdims=True))
    grad_router = jnp.dot(second_wide.T, grad_logits, precision=highest)
    grad_second = grad_second + jnp.dot(grad_logits, router.T, precision=highest)
    grad_middle_norm, grad_norm_ffn = norm_back(middle, norm_ffn, grad_second)
    grad_middle = grad_result + grad_middle_norm
    grad_middle_low = grad_middle.astype(jnp.bfloat16)
    grad_w_out = jnp.dot(attended_low.T, grad_middle_low, preferred_element_type=jnp.float32)
    grad_attended_low = jnp.dot(
        grad_middle_low, w_out.T, preferred_element_type=jnp.float32
    ).astype(jnp.bfloat16)
    grad_attended_four = grad_attended_low.reshape(shape_four)
    grad_attended_three = grad_attended_low.reshape(shape_three)
    delta = jnp.sum(grad_attended_four.astype(jnp.float32) * attended, -1)
    local_queries = (query_four, grad_attended_four, log_total, delta, positions)
    grad_start = (jnp.zeros(shape_four, jnp.float32), jnp.zeros(rel_bias.shape, jnp.float32))
    query_offset = jnp.int32(0)
    query_key_all = lax.all_gather(key_three, ("experts", "context"), axis=1, tiled=True)
    query_value_all = lax.all_gather(value_three, ("experts", "context"), axis=1, tiled=True)
    piece_rows = query_key_all.shape[1]
    query_block_rows = math.gcd(piece_rows, 8 * per_slot)

    def query_visit(carried, block_id):
        local_at = block_id * query_block_rows
        key_rows = lax.dynamic_slice_in_dim(query_key_all, local_at, query_block_rows, 1).reshape(
            slot_count, query_block_rows, head_count, head_size
        )
        value_rows = lax.dynamic_slice_in_dim(
            query_value_all, local_at, query_block_rows, 1
        ).reshape(slot_count, query_block_rows, head_count, head_size)
        key_pos = query_offset + local_at + jnp.arange(query_block_rows, dtype=jnp.int32)
        grad_query, _, _, grad_table = pair_grads(
            local_queries, (key_rows, value_rows, key_pos), rel_bias, lengths, score_scale
        )
        return ((carried[0] + grad_query, carried[1] + grad_table), None)

    carried, _ = lax.scan(
        query_visit, grad_start, jnp.arange(piece_rows // query_block_rows, dtype=jnp.int32)
    )
    grad_query_four, grad_table = carried
    log_whole, delta_whole = (
        lax.all_gather(log_total, ("experts", "context"), axis=1, tiled=True),
        lax.all_gather(delta, ("experts", "context"), axis=1, tiled=True),
    )
    local_keys = (key_four, value_four, positions)
    zero_four = jnp.zeros(shape_four, jnp.float32)
    key_offset = jnp.int32(0)
    query_all = lax.all_gather(
        query_flat.reshape(shape_three), ("experts", "context"), axis=1, tiled=True
    )
    grad_all = lax.all_gather(grad_attended_three, ("experts", "context"), axis=1, tiled=True)
    piece_rows = query_all.shape[1]
    key_block_rows = math.gcd(piece_rows, 8 * per_slot)

    def key_visit(carried, block_id):
        local_at = block_id * key_block_rows
        whole_at = key_offset + local_at
        query_rows = lax.dynamic_slice_in_dim(query_all, local_at, key_block_rows, 1).reshape(
            slot_count, key_block_rows, head_count, head_size
        )
        grad_rows = lax.dynamic_slice_in_dim(grad_all, local_at, key_block_rows, 1).reshape(
            slot_count, key_block_rows, head_count, head_size
        )
        log_rows = lax.dynamic_slice_in_dim(log_whole, whole_at, key_block_rows, 1)
        delta_rows = lax.dynamic_slice_in_dim(delta_whole, whole_at, key_block_rows, 1)
        query_pos = whole_at + jnp.arange(key_block_rows, dtype=jnp.int32)
        _, grad_key, grad_value, _ = pair_grads(
            (query_rows, grad_rows, log_rows, delta_rows, query_pos),
            local_keys,
            rel_bias,
            lengths,
            score_scale,
        )
        return ((carried[0] + grad_key, carried[1] + grad_value), None)

    carried, _ = lax.scan(
        key_visit, (zero_four, zero_four), jnp.arange(piece_rows // key_block_rows, dtype=jnp.int32)
    )
    grad_key_four, grad_value_four = carried
    grad_query_low = grad_query_four.reshape(row_count, model_width).astype(jnp.bfloat16)
    grad_key_low = grad_key_four.reshape(row_count, model_width).astype(jnp.bfloat16)
    grad_value_low = grad_value_four.reshape(row_count, model_width).astype(jnp.bfloat16)
    grad_w_query = jnp.dot(normed.T, grad_query_low, preferred_element_type=jnp.float32)
    grad_w_key = jnp.dot(normed.T, grad_key_low, preferred_element_type=jnp.float32)
    grad_w_value = jnp.dot(normed.T, grad_value_low, preferred_element_type=jnp.float32)
    grad_normed = (
        jnp.dot(grad_query_low, w_query.T, preferred_element_type=jnp.float32)
        + jnp.dot(grad_key_low, w_key.T, preferred_element_type=jnp.float32)
        + jnp.dot(grad_value_low, w_value.T, preferred_element_type=jnp.float32)
    )
    grad_input_norm, grad_norm_attn = norm_back(inputs, norm_attn, grad_normed)
    grad_tokens = (grad_middle + grad_input_norm).reshape(shape_three)
    dense = lax.psum(
        (
            grad_norm_attn,
            grad_w_query,
            grad_w_key,
            grad_w_value,
            grad_w_out,
            grad_table,
            grad_norm_ffn,
            grad_router,
        ),
        ("experts", "context"),
    )
    return (
        result,
        grad_tokens,
        dense[0],
        dense[1],
        dense[2],
        dense[3],
        dense[4],
        dense[5],
        dense[6],
        dense[7],
        expert_sums[0],
        expert_sums[1],
        expert_sums[2],
    )


MESH = pl.DeviceIdType.MESH
BF = jnp.bfloat16
F32 = jnp.float32
VMEM = pltpu.VMEM
ORDERS = (("x", "y", "l"), ("y", "l", "x"), ("l", "x", "y"))
COLUMNS = ((0, 384), (384, 384), (768, 256))
BIG = -1e30
TILE = 256
PLACES = 80
SHARE = 704
UP_FIRST = 192
UP_SECOND = 224
NT = (((1,), (1,)), ((), ()))
TN = (((0,), (0,)), ((), ()))
CUBE_SEMS = [pltpu.SemaphoreType.DMA((3, 8))] * 4


def spot():
    e = lax.axis_index("experts")
    c = lax.axis_index("context")
    return dict(k=lax.rem(e, 2), y=e // 2, x=lax.rem(c, 2), l=lax.rem(c // 2, 2), h=c // 4)


def flip(b, names):
    return {n: (1 - v if n in names else v) for n, v in b.items()}


def device(b):
    return {"experts": b["y"] * 2 + b["k"], "context": b["h"] * 4 + b["l"] * 2 + b["x"]}


def row_of(b):
    return b["y"] * 2 + b["k"]


def col_of(b):
    return b["l"] * 2 + b["x"]


def slot_of(b):
    return row_of(b) * 4 + col_of(b)


def greet(peers):
    barrier = pltpu.get_barrier_semaphore()
    for peer in peers:
        pl.semaphore_signal(barrier, inc=1, device_id=peer, device_id_type=MESH)
    pl.semaphore_wait(barrier, len(peers))


def cube_peers(b):
    return [device(flip(b, [n])) for n in ("x", "y", "l", "k")]


def cube_all(b):
    peers = []
    for step in range(1, 16):
        s = lax.rem(slot_of(b) + step, 16)
        peers.append({"experts": s // 4, "context": b["h"] * 4 + lax.rem(s, 4)})
    return peers


def world_all(b):
    me = row_of(b) * 8 + b["h"] * 4 + col_of(b)
    peers = []
    for step in range(1, 32):
        j = lax.rem(me + step, 32)
        peers.append((j, {"experts": j // 8, "context": lax.rem(j, 8)}))
    return me, peers


def remote(src, dst, ssem, rsem, peer):
    return pltpu.make_async_remote_copy(
        src_ref=src, dst_ref=dst, send_sem=ssem, recv_sem=rsem, device_id=peer, device_id_type=MESH
    )


def names_of(order, t):
    return [order[i] for i in range(3) if (t >> i) & 1]


def gather_steps(b, view, ss, rs, cs, cr):
    started = []
    core = device(flip(b, ["k"]))

    def link(p, t, i):
        ref = view(flip(b, names_of(ORDERS[p], t)), p)
        n = t | (1 << i)
        cp = remote(ref, ref, ss.at[p, n], rs.at[p, n], device(flip(b, [ORDERS[p][i]])))
        cp.start()
        started.append(cp)

    def across(p, t):
        ref = view(flip(b, names_of(ORDERS[p], t)), p)
        cp = remote(ref, ref, cs.at[p, t], cr.at[p, t], core)
        cp.start()
        started.append(cp)

    for i in range(3):
        for p in range(3):
            link(p, 0, i)
    for p in range(3):
        across(p, 0)
    yield
    for t in range(1, 8):
        for p in range(3):
            ref = view(flip(b, names_of(ORDERS[p], t)), p)
            remote(ref, ref, ss.at[p, t], rs.at[p, t], core).wait_recv()
            for i in range(t.bit_length(), 3):
                link(p, t, i)
            across(p, t)
        yield
    for cp in started:
        cp.wait_send()
    for p in range(3):
        for t in range(8):
            ref = view(flip(b, names_of(ORDERS[p], t) + ["k"]), p)
            remote(ref, ref, cs.at[p, t], cr.at[p, t], core).wait_recv()
    yield


def gather_cube(*args):
    for _ in gather_steps(*args):
        pass


def eighth(b):
    return b["y"] * 4 + b["l"] * 2 + b["x"]


def scatter_steps(b, parts, acc, landing, ss, rs, cs, cr):
    started = []
    core = device(flip(b, ["k"]))
    order = sorted(range(8), key=lambda t: -bin(t).count("1"))

    def bits_t(t):
        return flip(b, [n for i, n in enumerate(("x", "y", "l")) if (t >> i) & 1])

    for t in order:
        there = flip(bits_t(t), ["k"])
        cp = remote(parts.at[slot_of(there)], acc.at[eighth(there)], cs.at[0, t], cr.at[0, t], core)
        cp.start()
        started.append(cp)
    yield
    for t in order:
        here = bits_t(t)
        n = eighth(here)
        remote(parts.at[slot_of(here)], acc.at[n], cs.at[0, t], cr.at[0, t], core).wait_recv()
        acc[n] = (acc[n].astype(F32) + parts[slot_of(here)].astype(F32)).astype(BF)
    for step in range(3):
        rest = 2 - step
        count = 1 << rest
        for p in range(3):
            c0, cn = COLUMNS[p]
            first = ORDERS[p][step]
            others = ORDERS[p][step + 1 :]
            for t in range(count - 1, -1, -1):
                there = flip(b, [first] + [others[i] for i in range(rest) if (t >> i) & 1])
                n = count + t
                cp = remote(
                    acc.at[eighth(there), :, pl.ds(c0, cn)],
                    landing.at[n, :, pl.ds(c0, cn)],
                    ss.at[p, n],
                    rs.at[p, n],
                    device(flip(b, [first])),
                )
                cp.start()
                started.append(cp)
        yield
        for p in range(3):
            c0, cn = COLUMNS[p]
            others = ORDERS[p][step + 1 :]
            for t in range(count - 1, -1, -1):
                here = flip(b, [others[i] for i in range(rest) if (t >> i) & 1])
                n = count + t
                target = eighth(here)
                ref = landing.at[n, :, pl.ds(c0, cn)]
                remote(ref, ref, ss.at[p, n], rs.at[p, n], core).wait_recv()
                acc[target, :, c0 : c0 + cn] = (
                    acc[target, :, c0 : c0 + cn].astype(F32)
                    + landing[n, :, c0 : c0 + cn].astype(F32)
                ).astype(BF)
    for cp in started:
        cp.wait_send()
    yield


def scatter_cube(*args):
    for _ in scatter_steps(*args):
        pass


def params(cid=None, mib=60):
    if cid is None:
        return pltpu.CompilerParams(vmem_limit_bytes=mib * 2**20)
    return pltpu.CompilerParams(
        collective_id=cid, has_side_effects=True, vmem_limit_bytes=mib * 2**20
    )


def call(body, outs, scratch, cid, *args, anywhere=(), outs_anywhere=(), scalars=()):
    def spec(i, listed):
        if i in listed:
            return pl.BlockSpec(memory_space=pl.ANY)
        return pl.BlockSpec(memory_space=VMEM)

    return pl.pallas_call(
        body,
        out_shape=outs,
        in_specs=[
            pl.BlockSpec(memory_space=pltpu.SMEM) if i in scalars else spec(i, anywhere)
            for i in range(len(args))
        ],
        out_specs=[spec(i, outs_anywhere) for i in range(len(outs))],
        scratch_shapes=scratch,
        compiler_params=params(cid),
    )(*args)


def shape(dims, kind=BF):
    return jax.ShapeDtypeStruct(dims, kind)


def gather_sequence(b, whole, staged, sems, hs, hr, after=()):
    partner = device(flip(b, ["h"]))
    mine = whole.at[row_of(b), b["h"], col_of(b)]
    cp = remote(staged.at[1 - b["h"]], mine, hs, hr, partner)
    cp.start()
    for later in after:
        later.start()
    whole[row_of(b), b["h"], col_of(b)] = staged[b["h"]]
    theirs = whole.at[row_of(b), 1 - b["h"], col_of(b)]
    remote(theirs, theirs, hs, hr, partner).wait_recv()

    def view(v, p):
        c0, cn = COLUMNS[p]
        return whole.at[row_of(v), :, col_of(v), :, pl.ds(c0, cn)]

    gather_cube(b, view, *sems)
    cp.wait_send()


def group_view(ref, r0=0, rn=128):
    def view(v, p):
        c0, cn = COLUMNS[p]
        return ref.at[slot_of(v), pl.ds(r0, rn), pl.ds(c0, cn)]

    return view


def send_small(b, src, into, ss, rs):
    copies = []
    for step, peer in enumerate(cube_all(b)):
        cp = remote(src, into.at[slot_of(b)], ss.at[step], rs.at[step], peer)
        cp.start()
        copies.append(cp)
    return copies


def wait_small(b, into, ss, rs, copies):
    me = slot_of(b)
    for step in range(15):
        came = into.at[lax.rem(me + 15 - step, 16)]
        remote(came, came, ss.at[step], rs.at[step], device(b)).wait_recv()
    for cp in copies:
        cp.wait_send()


def inverse_rms(values):
    return lax.rsqrt(jnp.mean(values * values, axis=-1, keepdims=True) + norm_epsilon)


def first_body(tokens, gain, picks, h1, picks_all, staged, *sems):
    b = spot()
    greet([device(flip(b, ["h"]))] + cube_all(b))
    copies = send_small(b, picks, picks_all, sems[6], sems[7])
    picks_all[slot_of(b)] = picks[...]
    for s in range(2):
        rows = tokens[s].astype(F32)
        staged[s] = (rows * inverse_rms(rows) * gain[...]).astype(BF)
    gather_sequence(b, h1, staged, sems[0:4], sems[4], sems[5])
    wait_small(b, picks_all, sems[6], sems[7], copies)


def lane(shape_, dim=1):
    return lax.broadcasted_iota(jnp.int32, shape_, dim)


def near_tiles(row):
    wide = jnp.broadcast_to(row, (TILE, 2 * TILE))
    wide = pltpu.roll(wide, 0, 1, stride=1, stride_axis=0)
    later = lax.broadcasted_iota(jnp.int32, (TILE, TILE), 0) > lane((TILE, TILE))
    return [jnp.where(later, BIG, wide[:, :TILE]), wide[:, TILE:]]


def pack_halves(rows):
    n = rows.shape[0] // 64
    four = rows.reshape(n, 2, 32, 128)
    return jnp.where(
        lax.broadcasted_iota(jnp.int32, (n, 32, 128), 2) < 64,
        four[:, 0],
        pltpu.roll(four[:, 1].reshape(n * 32, 128), 64, 1).reshape(n, 32, 128),
    )


def attend_body(length, h1, w3, dist, cot, packed, out_t, qs, ks, vs, lse, dy, strip, v_t, weights, *sems):
    b = spot()
    greet(cube_peers(b))
    dy[slot_of(b)] = cot[...]
    steps = gather_steps(b, group_view(dy, 0, 64), *sems)
    next(steps)
    limit = length[0]
    for i in range(8):
        rows = slice(i * TILE, (i + 1) * TILE)
        p = jnp.dot(h1[rows], w3[...], preferred_element_type=F32)
        spot_lane = lane((TILE, 128))
        where_at = lax.broadcasted_iota(jnp.int32, (TILE, 128), 0) + i * TILE
        one = spot_lane == 64
        qs[rows] = jnp.where(one, 1.0, p[:, :128] * 0.125).astype(BF)
        ks[rows] = jnp.where(one & (where_at >= limit), BIG, p[:, 128:256]).astype(BF)
        v = jnp.where(one, 1.0, p[:, 256:]).astype(BF)
        vs[rows] = v
        v_t[:, rows] = v.astype(F32).T.astype(BF)
    near = near_tiles(dist[0:1])
    for i in range(8):
        cols = slice(i * TILE, (i + 1) * TILE)
        q = qs[cols]
        top = None
        for j in range(i + 1):
            rows = slice(j * TILE, (j + 1) * TILE)
            s = lax.dot_general(ks[rows], q, NT, preferred_element_type=F32)
            if i - j < 2:
                s = s + near[i - j]
            strip[rows] = s
            m = jnp.max(s, axis=0, keepdims=True)
            top = m if top is None else jnp.maximum(top, m)
        for j in range(i + 1):
            rows = slice(j * TILE, (j + 1) * TILE)
            weights[rows] = jnp.exp(strip[rows] - top).astype(BF)
        n = (i + 1) * TILE
        o = jnp.dot(v_t[:, :n], weights[:n], preferred_element_type=F32)
        total = o[64:65]
        o = o / total
        lse[:, cols] = jnp.broadcast_to(top + jnp.log(total), (8, TILE))
        out_t[:, cols] = o[:64]
        packed[4 * i : 4 * i + 4] = pack_halves(o.T).astype(BF)
        next(steps)


def unpack_halves(first, second):
    a = first.astype(F32)
    c = second.astype(F32)
    left = lane((32, 128)) < 64
    top = jnp.where(left, a, pltpu.roll(c, 64, 1))
    bottom = jnp.where(left, pltpu.roll(a, 64, 1), c)
    return top.astype(BF), bottom.astype(BF)


def everyone(b, src, dst_at, ss, rs):
    me, peers = world_all(b)
    copies = []
    for step, (j, peer) in enumerate(peers):
        cp = remote(src.at[j], dst_at(me), ss.at[step], rs.at[step], peer)
        cp.start()
        copies.append(cp)
    return me, copies


def everyone_wait(b, me, dst_at, ss, rs, copies):
    for step in range(31):
        came = dst_at(lax.rem(me + 31 - step, 32))
        remote(came, came, ss.at[step], rs.at[step], device(b)).wait_recv()
    for cp in copies:
        cp.wait_send()


def middle_body(packed, tokens, w_out, gain, router3, middle, h2_all, gates_all, land, joined, gates, *sems):
    b = spot()
    greet([peer for _, peer in world_all(b)[1]])

    def at(j):
        return land.at[j]

    me, copies = everyone(b, packed, at, sems[4], sems[5])
    land[me] = packed[me]
    everyone_wait(b, me, at, sems[4], sems[5], copies)
    for s in range(2):
        for pair in range(8):
            first, second = 2 * pair, 2 * pair + 1
            j0 = (first // 4) * 8 + s * 4 + first % 4
            j1 = (second // 4) * 8 + s * 4 + second % 4
            top, bottom = unpack_halves(land[j0], land[j1])
            cols = slice(pair * 128, pair * 128 + 128)
            joined[s * 64 : s * 64 + 32, cols] = top
            joined[s * 64 + 32 : s * 64 + 64, cols] = bottom
    x = tokens[...].astype(F32)
    mid = x + jnp.dot(joined[...], w_out[...], preferred_element_type=F32)
    middle[...] = mid
    h2 = (mid * inverse_rms(mid) * gain[...]).astype(BF)
    h2_all[slot_of(b)] = h2
    gather_half = group_view(h2_all)
    logits = jnp.dot(h2, router3[...], preferred_element_type=F32).T
    logits = logits[0:8] + logits[8:16] + logits[16:24]
    real = lax.broadcasted_iota(jnp.int32, (8, 128), 0) < 4
    logits = jnp.where(real, logits, BIG)
    g = jnp.exp(logits - jnp.max(logits, axis=0, keepdims=True))
    gates[...] = g / jnp.sum(g, axis=0, keepdims=True)
    small = send_small(b, gates, gates_all, sems[6], sems[7])
    gates_all[slot_of(b)] = gates[...]
    gather_cube(b, gather_half, *sems[0:4])
    wait_small(b, gates_all, sems[6], sems[7], small)


def expert_body(
    h2, dy0, cot, gates, picks, wg, wu, wd, routed, dh2, dgates, near_g, near_u, near_d, far_g, far_u, far_d, dy, rows, grad, dexp, weight, hid, dgs, dus, acts, slopes, outs, drs, dws, load, *sems
):
    b = spot()
    greet(cube_peers(b))
    fetch = pltpu.make_async_copy(dy0, dy.at[:, pl.ds(0, 64)], load)
    fetch.start()
    dy[slot_of(b), 64:128] = cot[...]
    steps = gather_steps(b, group_view(dy, 64, 64), *sems)
    next(steps)
    mine = row_of(b)
    mine_f = mine.astype(F32)
    first = picks[:, 0, :]
    second = picks[:, 1, :]
    chosen = jnp.where((first == mine_f) | (second == mine_f), 1.0, 0.0)
    earlier = jnp.where(
        lax.broadcasted_iota(jnp.int32, (128, 128), 0) < lane((128, 128)), 1.0, 0.0
    )
    place = jnp.dot(chosen.astype(BF), earlier.astype(BF), preferred_element_type=F32)
    place = jnp.where((chosen > 0.5) & (place < PLACES), place, -1.0)
    place_t = jnp.concatenate([place, jnp.full((112, 128), -1.0, F32)], axis=0).T
    level = lax.broadcasted_iota(jnp.int32, (PLACES, 128), 0).astype(F32)
    level_t = lane((128, PLACES)).astype(F32)
    is_mine = lax.broadcasted_iota(jnp.int32, (8, 128), 0) == mine
    for m in range(16):
        at = slice(m * PLACES, (m + 1) * PLACES)
        hit = jnp.where(level == place[m : m + 1], 1.0, 0.0)
        rows[at] = jnp.dot(hit.astype(BF), h2[m], preferred_element_type=F32).astype(BF)
        gate_row = jnp.sum(jnp.where(is_mine, gates[m], 0.0), axis=0, keepdims=True)
        w = jnp.sum(hit * gate_row, axis=1, keepdims=True)
        weight[at] = jnp.broadcast_to(w, (PLACES, 128))
        if m % 8 == 7:
            next(steps)
    c0 = math.sqrt(2.0 / math.pi)
    c1 = 0.044715
    for i in range(5):
        at = slice(i * TILE, (i + 1) * TILE)
        r = rows[at]
        gp = jnp.dot(r, wg[...], preferred_element_type=F32)
        up = jnp.dot(r, wu[...], preferred_element_type=F32)
        sq = gp * gp
        th = jnp.tanh(c0 * gp * (1.0 + c1 * sq))
        half = 0.5 * (1.0 + th)
        act = gp * half
        slope = half + 0.5 * gp * (1.0 - th * th) * (c0 * (1.0 + 3.0 * c1 * sq))
        acts[at] = act
        slopes[at] = up * slope
        h = (act * up).astype(BF)
        hid[at] = h
        outs[at] = jnp.dot(h, wd[...], preferred_element_type=F32).astype(BF)
        next(steps)
    next(steps)
    fetch.wait()
    for m in range(16):
        at = slice(m * PLACES, (m + 1) * PLACES)
        hit = jnp.where(level == place[m : m + 1], 1.0, 0.0).astype(BF)
        g = jnp.dot(hit, dy[m], preferred_element_type=F32)
        grad[at] = g.astype(BF)
        dexp[at] = (weight[at, 0:1] * g).astype(BF)
    for i in range(5):
        at = slice(i * TILE, (i + 1) * TILE)
        o = outs[at].astype(F32)
        dws[at] = jnp.broadcast_to(
            jnp.sum(grad[at].astype(F32) * o, axis=1, keepdims=True), (TILE, 128)
        )
        outs[at] = (weight[at, 0:1] * o).astype(BF)
        dh = lax.dot_general(dexp[at], wd[...], NT, preferred_element_type=F32)
        dg = (dh * slopes[at]).astype(BF)
        du = (dh * acts[at]).astype(BF)
        dgs[at] = dg
        dus[at] = du
        drs[at] = (
            lax.dot_general(dg, wg[...], NT, preferred_element_type=F32)
            + lax.dot_general(du, wu[...], NT, preferred_element_type=F32)
        ).astype(BF)
    for m in range(16):
        at = slice(m * PLACES, (m + 1) * PLACES)
        back = jnp.where(place_t[:, m : m + 1] == level_t, 1.0, 0.0).astype(BF)
        routed[m] = jnp.dot(back, outs[at], preferred_element_type=F32).astype(BF)
        dh2[m] = jnp.dot(back, drs[at], preferred_element_type=F32).astype(BF)
        hit = jnp.where(level == place[m : m + 1], 1.0, 0.0)
        dgates[m] = jnp.broadcast_to(
            jnp.sum(hit * dws[at], axis=0, keepdims=True), (8, 128)
        )
    h = b["h"]
    for side, g_out, u_out in ((1 - h, far_g, far_u), (h, near_g, near_u)):
        part = rows[:, pl.ds(pl.multiple_of(side * 512, 512), 512)]
        g_out[...] = lax.dot_general(part, dgs[...], TN, preferred_element_type=F32).astype(BF)
        u_out[...] = lax.dot_general(part, dus[...], TN, preferred_element_type=F32).astype(BF)
    down = lax.dot_general(hid[...], dexp[...], TN, preferred_element_type=F32).astype(BF)
    upper = h == 1
    near_d[...] = jnp.where(upper, down[352:], down[:352])
    far_d[...] = jnp.where(upper, down[:352], down[352:])


def norm_back_rows(values, gain, grad_in):
    inverse = inverse_rms(values)
    normed = values * inverse
    scaled = grad_in * gain
    out = inverse * (scaled - normed * jnp.mean(scaled * normed, axis=-1, keepdims=True))
    return out, jnp.sum(grad_in * normed, axis=0, keepdims=True)


def back_body(
    dh2, dgates, gates, cot, keep, middle, gain, router_t, h2_all, far_g, far_u, dm_all, dmid, smalls, got_g, got_u, acc, landing, dg_all, staged, *sems
):
    b = spot()
    greet([device(flip(b, ["h"]))] + cube_all(b))
    me = slot_of(b)
    partner = device(flip(b, ["h"]))
    trades = [
        remote(far_g.at[pl.ds(0, 384)], got_g.at[pl.ds(0, 384)], sems[12].at[0], sems[13].at[0], partner),
        remote(far_g.at[pl.ds(384, 128)], got_g.at[pl.ds(384, 128)], sems[12].at[1], sems[13].at[1], partner),
        remote(far_u.at[pl.ds(0, UP_FIRST)], got_u, sems[12].at[2], sems[13].at[2], partner),
    ]
    trades[0].start()
    copies = []
    for step, peer in enumerate(cube_all(b)):
        s = lax.rem(me + step + 1, 16)
        cp = remote(dgates.at[s], dg_all.at[me], sems[10].at[step], sems[11].at[step], peer)
        cp.start()
        copies.append(cp)
    dg_all[me] = dgates[me]
    scatter_cube(b, dh2, acc, landing, *sems[0:4])
    wait_small(b, dg_all, sems[10], sems[11], copies)
    level = lax.broadcasted_iota(jnp.int32, (8, 128), 0)
    dg = jnp.zeros((8, 128), F32)
    for e in range(4):
        total = dg_all[4 * e] + dg_all[4 * e + 1] + dg_all[4 * e + 2] + dg_all[4 * e + 3]
        dg = jnp.where(level == e, total, dg)
    g = gates[me]
    dl_t = g * (dg - jnp.sum(g * dg, axis=0, keepdims=True))
    dl = jnp.concatenate([dl_t, jnp.zeros((120, 128), F32)], axis=0).T
    d_h2 = acc[eighth(b)].astype(F32)
    for e in range(4):
        d_h2 = d_h2 + dl[:, e : e + 1] * router_t[e : e + 1]
    high = dl_t.astype(BF)
    rest = (dl_t - high.astype(F32)).astype(BF)
    h2 = h2_all[me]
    smalls[0:8] = jnp.dot(high, h2, preferred_element_type=F32) + jnp.dot(
        rest, h2, preferred_element_type=F32
    )
    grad_mid, grad_gain = norm_back_rows(middle[...], gain[...], d_h2)
    smalls[4:5] = grad_gain
    d_mid = cot[...].astype(F32) * keep[...] + grad_mid
    dmid[...] = d_mid
    staged[0] = d_mid[:64].astype(BF)
    staged[1] = d_mid[64:].astype(BF)
    gather_sequence(b, dm_all, staged, sems[4:8], sems[8], sems[9], trades[1:])
    for cp in trades:
        cp.wait()


def attend_back_body(
    h1, dm, w_o, qs, ks, vs, out_t, lse, dist, onehot, routed, middle, keep, far_u, packed, grads, table, result, got_u, dos, k_t, delta, p_buf, s_buf, dq_t, dk, dv, near0, near1, left, acc, landing, *sems
):
    b = spot()
    partner = device(flip(b, ["h"]))
    greet([partner] + cube_peers(b))
    trade = remote(
        far_u.at[pl.ds(UP_FIRST, UP_SECOND)], got_u, sems[4], sems[5], partner
    )
    trade.start()
    steps = scatter_steps(b, routed, acc, landing, *sems[0:4])
    next(steps)
    for i in range(8):
        rows = slice(i * TILE, (i + 1) * TILE)
        d = lax.dot_general(dm[rows], w_o[...], NT, preferred_element_type=F32).astype(BF)
        dos[rows] = d
        delta[:, rows] = jnp.broadcast_to(
            jnp.sum(d.astype(F32).T[:64] * out_t[:, rows], axis=0, keepdims=True), (8, TILE)
        )
        kt = ks[rows].astype(F32).T
        k_t[:, rows] = jnp.where(
            lax.broadcasted_iota(jnp.int32, (128, TILE), 0) == 64, 1.0, kt
        ).astype(BF)
    next(steps)
    near = near_tiles(dist[0:1])
    near0[...] = jnp.zeros_like(near0)
    near1[...] = jnp.zeros_like(near1)
    for i in range(8):
        cols = slice(i * TILE, (i + 1) * TILE)
        q = qs[cols]
        do = dos[cols]
        level = lse[0:1, cols]
        dl = delta[0:1, cols]
        for j in range(i + 1):
            rows = slice(j * TILE, (j + 1) * TILE)
            s = lax.dot_general(ks[rows], q, NT, preferred_element_type=F32)
            if i - j < 2:
                s = s + near[i - j]
            p = jnp.exp(s - level)
            dp = lax.dot_general(vs[rows], do, NT, preferred_element_type=F32)
            ds = (p * (dp - dl)).astype(BF)
            p_buf[rows] = p.astype(BF)
            s_buf[rows] = ds
            if i == j:
                near0[...] += ds.astype(F32)
            if i - j == 1:
                near1[...] += ds.astype(F32)
        n = (i + 1) * TILE
        dq_t[:, cols] = jnp.dot(k_t[:, :n], s_buf[:n], preferred_element_type=F32)
        new_v = jnp.dot(p_buf[:n], do, preferred_element_type=F32)
        new_k = jnp.dot(s_buf[:n], q, preferred_element_type=F32)
        if i > 0:
            dv[: n - TILE] += new_v[: n - TILE]
            dk[: n - TILE] += new_k[: n - TILE]
        dv[n - TILE : n] = new_v[n - TILE :]
        dk[n - TILE : n] = new_k[n - TILE :]
        if i in (4, 6, 7):
            next(steps)
    total = jnp.sum(dq_t[64:65, :].reshape(1, 16, 128), axis=1)
    skew = jnp.concatenate([near0[...], near1[...]], axis=1)
    level_u = lax.broadcasted_iota(jnp.int32, (TILE, 2 * TILE), 0)
    for bit in range(8):
        moved = pltpu.roll(skew, 2 * TILE - (1 << bit), 1)
        skew = jnp.where((level_u // (1 << bit)) % 2 == 1, moved, skew)
    by_distance = jnp.broadcast_to(jnp.sum(skew, axis=0, keepdims=True), (8, 2 * TILE))
    buckets = jnp.dot(by_distance, onehot[...], precision=highest)
    spot_lane = lane((8, 128))
    others = jnp.sum(jnp.where(spot_lane < 31, buckets, 0.0), axis=1, keepdims=True)
    whole_sum = jnp.sum(total, axis=1, keepdims=True)
    buckets = jnp.where(spot_lane == 31, whole_sum - others, buckets)
    row = jnp.concatenate([buckets, jnp.zeros((8, 384), F32)], axis=1)
    table[...] = pltpu.roll(row, slot_of(b) * 32, 1)
    for i in range(8):
        rows = slice(i * TILE, (i + 1) * TILE)
        dq = dq_t[:, rows] * 0.125
        vk = jnp.where(lane((TILE, 128)) < 64, dv[rows], pltpu.roll(dk[rows], 64, 1)).T
        left[0:64, rows] = dq[:64].astype(BF)
        left[64:128, rows] = vk[64:128].astype(BF)
        left[128:192, rows] = vk[0:64].astype(BF)
        left[192:256, rows] = out_t[:, rows].astype(BF)
        blocks = slice(4 * i, 4 * i + 4)
        packed[blocks, 0:32] = pack_halves(dq.T).astype(BF)
        packed[blocks, 32:64] = pack_halves(dk[rows]).astype(BF)
        packed[blocks, 64:96] = pack_halves(dv[rows]).astype(BF)
    qkv = jnp.dot(left[0:192], h1[...], preferred_element_type=F32).astype(BF)
    grads[0] = qkv[0:128]
    grads[1, 0:64] = qkv[128:192]
    grads[1, 64:128] = jnp.dot(left[192:256], dm[...], preferred_element_type=F32).astype(BF)
    result[...] = ((middle[...] + acc[eighth(b)].astype(F32)) * keep[...]).astype(BF)
    trade.wait()


def last_body(
    packed, grads, tokens, dmid, gain, wq, wk, wv, part, table, near_g, got_g, near_u, got_u1, got_u2, near_d, far_u, far_d, dtokens, whole, smalls, wide, down, land, other, joined, inbox, half, pieces, got_u3, got_d, *sems
):
    b = spot()
    greet([peer for _, peer in world_all(b)[1]])
    partner = device(flip(b, ["h"]))
    h = b["h"]
    col = col_of(b)
    around = [flip(b, names) for names in (["x", "l"], ["x"], ["l"])]
    started = []

    def spread_out(n):
        for i, there in enumerate(around):
            cp = remote(
                half.at[n, col_of(there)],
                pieces.at[n, col],
                sems[14].at[3 * n + i],
                sems[15].at[3 * n + i],
                device(there),
            )
            cp.start()
            started.append(cp)
        pieces[n, col] = half[n, col]

    trade = remote(grads.at[1 - h], other, sems[8].at[0], sems[9].at[0], partner)
    trade.start()
    half[0] = (near_g[...].astype(F32) + got_g[...].astype(F32)).astype(BF)
    spread_out(0)
    ends = [0, UP_FIRST, UP_FIRST + UP_SECOND, 512]
    for got, lo, hi in ((got_u1, 0, 1), (got_u2, 1, 2)):
        near_rows = near_u[ends[lo] : ends[hi]].astype(F32)
        for blk in range(4):
            at0, at1 = max(ends[lo], blk * 128), min(ends[hi], blk * 128 + 128)
            if at0 < at1:
                half[1, blk, at0 - blk * 128 : at1 - blk * 128] = (
                    near_rows[at0 - ends[lo] : at1 - ends[lo]]
                    + got[at0 - ends[lo] : at1 - ends[lo]].astype(F32)
                ).astype(BF)

    def at(j):
        return land.at[j]

    trade.wait()
    me_slot = slot_of(b)
    whole[h, me_slot] = (grads[h].astype(F32) + other[...].astype(F32)).astype(BF)
    share = remote(
        whole.at[h, me_slot], whole.at[h, me_slot], sems[8].at[1], sems[9].at[1], partner
    )
    share.start()

    def view_of(side):
        def view(v, p):
            c0, cn = COLUMNS[p]
            return whole.at[side, slot_of(v), :, pl.ds(c0, cn)]

        return view

    near = gather_steps(b, view_of(h), *sems[0:4])
    far = gather_steps(b, view_of(1 - h), *sems[4:8])
    next(near)
    rest_u = remote(far_u.at[pl.ds(ends[2], 512 - ends[2])], got_u3, sems[16].at[0], sems[17].at[0], partner)
    rest_u.start()
    me, copies = everyone(b, packed, at, sems[10], sems[11])
    land[me] = packed[me]
    trade_d = remote(far_d, got_d, sems[16].at[1], sems[17].at[1], partner)
    trade_d.start()
    next(near)
    next(near)
    theirs = whole.at[1 - h, me_slot]
    remote(theirs, theirs, sems[8].at[1], sems[9].at[1], partner).wait_recv()
    next(far)
    next(near)
    rest_u.wait()
    half[1, 3, ends[2] - 384 : 128] = (
        near_u[ends[2] : 512].astype(F32) + got_u3[...].astype(F32)
    ).astype(BF)
    spread_out(1)
    for _ in range(4):
        next(near)
        next(far)
    next(near)
    everyone_wait(b, me, at, sems[10], sems[11], copies)
    for kind in range(3):
        for s in range(2):
            for pair in range(8):
                first, second = 2 * pair, 2 * pair + 1
                j0 = (first // 4) * 8 + s * 4 + first % 4
                j1 = (second // 4) * 8 + s * 4 + second % 4
                span = slice(kind * 32, kind * 32 + 32)
                top, bottom = unpack_halves(land[j0, span], land[j1, span])
                cols = slice(pair * 128, pair * 128 + 128)
                joined[kind, s * 64 : s * 64 + 32, cols] = top
                joined[kind, s * 64 + 32 : s * 64 + 64, cols] = bottom
    d_h1 = (
        lax.dot_general(joined[0], wq[...], NT, preferred_element_type=F32)
        + lax.dot_general(joined[1], wk[...], NT, preferred_element_type=F32)
        + lax.dot_general(joined[2], wv[...], NT, preferred_element_type=F32)
    )
    grad_in, grad_gain = norm_back_rows(tokens[...].astype(F32), gain[...], d_h1)
    dtokens[...] = dmid[...] + grad_in
    smalls[...] = part[...]
    smalls[5:6] = grad_gain
    smalls[6:8] = jnp.concatenate([table[0:2], jnp.zeros((2, 512), F32)], axis=1)
    for step, name in enumerate(("k", "x", "y", "l", "h")):
        cp = remote(
            smalls, inbox.at[step], sems[12].at[step], sems[13].at[step], device(flip(b, [name]))
        )
        cp.start()
        if step < 4:
            next(far)
        cp.wait()
        smalls[...] = smalls[...] + inbox[step]
    share.wait_send()
    for n in range(2):
        for i, there in enumerate(around):
            ref = pieces.at[n, col_of(there)]
            remote(ref, ref, sems[14].at[3 * n + i], sems[15].at[3 * n + i], device(there)).wait_recv()
    for cp in started:
        cp.wait_send()
    for n in range(2):
        for i in range(4):
            wide[n, :, i * 352 : i * 352 + 352] = pieces[n, i, :, 0:352]
            wide[n, :, (4 + i) * 352 : (4 + i) * 352 + 352] = pieces[n, i, :, 352:704]
    trade_d.wait()
    down[...] = (near_d[...].astype(F32) + got_d[...].astype(F32)).astype(BF)


def dense_body(whole, grad_q, grad_k, grad_v, grad_o):
    for out, side, at in ((grad_q, 0, 0), (grad_k, 0, 64), (grad_v, 1, 0)):
        rows = whole[side, :, at : at + 64, :].reshape(128, 1024).astype(F32)
        for c in range(0, 1024, 128):
            out[c : c + 128, :] = rows[:, c : c + 128].T
    grad_o[...] = whole[1, :, 64:128, :].reshape(128, 1024).astype(F32)


def distance_buckets():
    table = []
    for distance in range(2 * TILE):
        table.append(bucket_of(distance, 32, MAXDIST))
    return np.array(table, np.int32)


def on_device_fast(
    tokens,
    lengths,
    expert_index,
    cotangent,
    norm_attn,
    w_query,
    w_key,
    w_value,
    w_out,
    rel_bias,
    norm_ffn,
    router,
    w_gate,
    w_up,
    w_down,
):
    dma = pltpu.SemaphoreType.DMA
    b = spot()
    head = slot_of(b)
    col = col_of(b)
    device_at = lax.axis_index(("experts", "context"))
    positions = device_at * 64 + jnp.arange(64, dtype=jnp.int32)
    live = positions[None, :] < lengths[:, None]
    keep = live.reshape(128, 1).astype(F32)
    picks = jnp.where(live[:, :, None], expert_index, -1).astype(F32).reshape(128, 2).T
    picks = jnp.concatenate([picks, jnp.zeros((6, 128), F32)], axis=0)
    gain_attn = norm_attn.reshape(1, 1024)
    gain_ffn = norm_ffn.reshape(1, 1024)
    flat = tokens.reshape(128, 1024)
    cot = cotangent.reshape(128, 1024)

    def head_columns(w):
        return jnp.pad(lax.dynamic_slice_in_dim(w, head * 64, 64, 1), ((0, 0), (0, 64)))

    w3 = jnp.concatenate([head_columns(w_query), head_columns(w_key), head_columns(w_value)], axis=1)
    w_o = jnp.pad(lax.dynamic_slice_in_dim(w_out, head * 64, 64, 0), ((0, 64), (0, 0)))
    buckets = distance_buckets()
    onehot = np.zeros((2 * TILE, 32), np.float32)
    onehot[np.arange(2 * TILE), buckets] = 1.0
    bias = lax.dynamic_slice_in_dim(rel_bias, head, 1, 1)[:, 0]
    by_distance = jnp.dot(jnp.asarray(onehot), bias - bias[31], precision=highest)
    dist = jnp.broadcast_to(by_distance[None], (8, 2 * TILE))
    mine = lax.dynamic_slice_in_dim(lengths, b["h"], 1, 0)

    def columns_share(w):
        return jnp.concatenate(
            [lax.dynamic_slice_in_dim(w[0], (4 * n + col) * 352, 352, 1) for n in range(2)], axis=1
        )

    wg = columns_share(w_gate)
    wu = columns_share(w_up)
    wd = jnp.concatenate(
        [lax.dynamic_slice_in_dim(w_down[0], (4 * n + col) * 352, 352, 0) for n in range(2)], axis=0
    )
    high = router.astype(BF)
    rest = router - high.astype(F32)
    mid = rest.astype(BF)
    lo = (rest - mid.astype(F32)).astype(BF)
    router3 = jnp.concatenate(
        [jnp.pad(r, ((0, 0), (0, 4))) for r in (high, mid, lo)] + [jnp.zeros((1024, 104), BF)], axis=1
    )
    router_t = jnp.pad(router.T, ((0, 4), (0, 0)))

    h1, picks_all = call(
        first_body,
        [shape((4, 2, 4, 64, 1024)), shape((16, 8, 128), F32)],
        [VMEM((2, 64, 1024), BF)] + CUBE_SEMS + [dma(()), dma(()), dma((15,)), dma((15,))],
        1,
        tokens,
        gain_attn,
        picks,
    )
    h1 = h1.reshape(2048, 1024)
    packed, out_t, qs, ks, vs, lse, dy0 = call(
        attend_body,
        [
            shape((32, 32, 128)),
            shape((64, 2048), F32),
            shape((2048, 128)),
            shape((2048, 128)),
            shape((2048, 128)),
            shape((8, 2048), F32),
            shape((16, 64, 1024)),
        ],
        [VMEM((2048, TILE), F32), VMEM((128, 2048), BF), VMEM((2048, TILE), BF)] + CUBE_SEMS,
        2,
        mine,
        h1,
        w3,
        dist,
        cot[:64],
        scalars=(0,),
    )
    middle, h2_all, gates_all = call(
        middle_body,
        [shape((128, 1024), F32), shape((16, 128, 1024)), shape((16, 8, 128), F32)],
        [VMEM((32, 32, 128), BF), VMEM((128, 1024), BF), VMEM((8, 128), F32)]
        + CUBE_SEMS
        + [dma((31,)), dma((31,)), dma((15,)), dma((15,))],
        3,
        packed,
        flat,
        w_out,
        gain_ffn,
        router3,
    )
    routed, dh2, dgates, near_g, near_u, near_d, far_g, far_u, far_d = call(
        expert_body,
        [
            shape((16, 128, 1024)),
            shape((16, 128, 1024)),
            shape((16, 8, 128), F32),
            shape((512, SHARE)),
            shape((512, SHARE)),
            shape((352, 1024)),
            shape((512, SHARE)),
            shape((512, SHARE)),
            shape((352, 1024)),
        ],
        [VMEM((16, 128, 1024), BF)]
        + [VMEM((1280, 1024), BF)] * 3
        + [VMEM((1280, 128), F32)]
        + [VMEM((1280, SHARE), BF)] * 3
        + [VMEM((1280, SHARE), F32)] * 2
        + [VMEM((1280, 1024), BF)] * 2
        + [VMEM((1280, 128), F32)]
        + [dma(())]
        + CUBE_SEMS,
        4,
        h2_all,
        dy0,
        cot[64:],
        gates_all,
        picks_all,
        wg,
        wu,
        wd,
        anywhere=(1,),
    )
    dm_all, dmid, smalls, got_g, got_u1 = call(
        back_body,
        [
            shape((4, 2, 4, 64, 1024)),
            shape((128, 1024), F32),
            shape((8, 1024), F32),
            shape((512, SHARE)),
            shape((UP_FIRST, SHARE)),
        ],
        [
            VMEM((8, 128, 1024), BF),
            VMEM((8, 128, 1024), BF),
            VMEM((16, 8, 128), F32),
            VMEM((2, 64, 1024), BF),
        ]
        + CUBE_SEMS
        + CUBE_SEMS
        + [dma(()), dma(()), dma((15,)), dma((15,)), dma((3,)), dma((3,))],
        5,
        dh2,
        dgates,
        gates_all,
        cot,
        keep,
        middle,
        gain_ffn,
        router_t,
        h2_all,
        far_g,
        far_u,
        anywhere=(9, 10),
        outs_anywhere=(3, 4),
    )
    packed_back, grads, table, result, got_u2 = call(
        attend_back_body,
        [
            shape((32, 96, 128)),
            shape((2, 128, 1024)),
            shape((8, 512), F32),
            shape((128, 1024)),
            shape((UP_SECOND, SHARE)),
        ],
        [
            VMEM((2048, 128), BF),
            VMEM((128, 2048), BF),
            VMEM((8, 2048), F32),
            VMEM((2048, TILE), BF),
            VMEM((2048, TILE), BF),
            VMEM((128, 2048), F32),
            VMEM((2048, 128), F32),
            VMEM((2048, 128), F32),
            VMEM((TILE, TILE), F32),
            VMEM((TILE, TILE), F32),
            VMEM((256, 2048), BF),
            VMEM((8, 128, 1024), BF),
            VMEM((8, 128, 1024), BF),
        ]
        + CUBE_SEMS
        + [dma(()), dma(())],
        6,
        h1,
        dm_all.reshape(2048, 1024),
        w_o,
        qs,
        ks,
        vs,
        out_t,
        lse,
        dist,
        jnp.asarray(np.pad(onehot, ((0, 0), (0, 96)))),
        routed,
        middle,
        keep,
        far_u,
        anywhere=(13,),
        outs_anywhere=(4,),
    )
    dtokens, whole, smalls, wide, down = call(
        last_body,
        [
            shape((128, 1024), F32),
            shape((2, 16, 128, 1024)),
            shape((8, 1024), F32),
            shape((2, 128, 2816)),
            shape((352, 1024)),
        ],
        [
            VMEM((32, 96, 128), BF),
            VMEM((128, 1024), BF),
            VMEM((3, 128, 1024), BF),
            VMEM((5, 8, 1024), F32),
            VMEM((2, 4, 128, SHARE), BF),
            VMEM((2, 4, 128, SHARE), BF),
            VMEM((512 - UP_FIRST - UP_SECOND, SHARE), BF),
            VMEM((352, 1024), BF),
        ]
        + CUBE_SEMS
        + CUBE_SEMS
        + [dma((2,)), dma((2,)), dma((31,)), dma((31,)), dma((5,)), dma((5,)), dma((6,)), dma((6,))]
        + [dma((2,)), dma((2,))],
        7,
        packed_back,
        grads,
        flat,
        dmid,
        gain_attn,
        w_query,
        w_key,
        w_value,
        smalls,
        table,
        near_g.reshape(4, 128, SHARE),
        got_g.reshape(4, 128, SHARE),
        near_u,
        got_u1,
        got_u2,
        near_d,
        far_u,
        far_d,
    )
    grad_q, grad_k, grad_v, grad_o = pl.pallas_call(
        dense_body,
        grid=(8,),
        out_shape=[shape((1024, 1024), F32)] * 4,
        in_specs=[pl.BlockSpec((2, 2, 128, 1024), lambda i: (0, i, 0, 0))],
        out_specs=[pl.BlockSpec((1024, 128), lambda i: (0, i))] * 3
        + [pl.BlockSpec((128, 1024), lambda i: (i, 0))],
        compiler_params=params(),
        cost_estimate=pl.CostEstimate(flops=0, bytes_accessed=25 * 2**20, transcendentals=0),
    )(whole)
    return (
        result.reshape(2, 64, 1024),
        dtokens.reshape(2, 64, 1024),
        smalls[5],
        grad_q,
        grad_k,
        grad_v,
        grad_o,
        smalls[6, :512].reshape(16, 32).T,
        smalls[4],
        smalls[0:4].T,
        wide[0:1].astype(F32),
        wide[1:2].astype(F32),
        down[None].astype(F32),
    )


def solution(mesh):
    sizes = dict(mesh.shape)
    fits = sizes == {"experts": 4, "context": 8}
    placed = (
        P(None, ("experts", "context"), None),
        P(),
        P(None, ("experts", "context"), None),
        P(None, ("experts", "context"), None),
        P(),
        P(),
        P(),
        P(),
        P(),
        P(),
        P(),
        P(),
        P("experts", None, None),
        P("experts", None, None),
        P("experts", None, None),
    )
    return jax.shard_map(
        on_device_fast if fits else on_device,
        mesh=mesh,
        in_specs=placed,
        out_specs=(
            P(None, ("experts", "context"), None),
            P(None, ("experts", "context"), None),
            P(),
            P(),
            P(),
            P(),
            P(),
            P(),
            P(),
            P(),
            P("experts", "context", None),
            P("experts", "context", None),
            P("experts", "context", None),
        ),
        check_vma=False,
    )
```

```python
import math

import jax
import jax.numpy as jnp
import numpy as np
from jax import lax
from jax.experimental import pallas as pl
from jax.experimental.pallas import tpu as pltpu
from jax.sharding import PartitionSpec as P

MAXDIST = 128


norm_epsilon = 1e-06
mask_fill = -1e30
highest = lax.Precision.HIGHEST


def bucket_of(distance, bucket_count, reach):
    exact = bucket_count // 2
    if distance < exact:
        return distance
    level = exact + int(
        math.log(distance / exact) / math.log(reach / exact) * (bucket_count - exact)
    )
    return min(level, bucket_count - 1)


def bucket_edges(bucket_count, reach):
    edges = []
    for level in range(1, bucket_count):
        distance = 0
        while bucket_of(distance, bucket_count, reach) < level:
            distance += 1
        edges.append(distance)
    return edges


def relative_bucket(query_pos, key_pos, bucket_count):
    distance = jnp.maximum(query_pos[:, None] - key_pos[None, :], 0)
    bucket = jnp.zeros(distance.shape, jnp.int32)
    for edge in bucket_edges(bucket_count, MAXDIST):
        bucket = bucket + (distance >= edge).astype(jnp.int32)
    return bucket


def rms_norm(values, gain):
    inverse = lax.rsqrt(jnp.mean(values * values, axis=-1, keepdims=True) + norm_epsilon)
    return values * inverse * gain


def norm_back(values, gain, grad_in):
    inverse = lax.rsqrt(jnp.mean(values * values, axis=-1, keepdims=True) + norm_epsilon)
    normed = values * inverse
    grad_normed = grad_in * gain
    grad_values = inverse * (
        grad_normed - normed * jnp.mean(grad_normed * normed, axis=-1, keepdims=True)
    )
    return (grad_values, jnp.sum(grad_in * normed, 0))


def score_block(query_rows, key_rows, rel_bias, query_pos, key_pos, lengths, score_scale):
    raw_scores = (
        jnp.einsum("sqhd,skhd->sqhk", query_rows, key_rows, preferred_element_type=jnp.float32)
        * score_scale
    )
    bucket = relative_bucket(query_pos, key_pos, rel_bias.shape[0])
    onehot = (bucket[:, :, None] == jnp.arange(rel_bias.shape[0], dtype=jnp.int32)).astype(
        jnp.float32
    )
    bias_rows = jnp.einsum("qkb,bh->qhk", onehot, rel_bias, precision=highest)
    causal = (key_pos[None, :] <= query_pos[:, None])[None]
    inside = key_pos[None, None, :] < lengths[:, None, None]
    allowed = (causal & inside)[:, :, None, :]
    return (raw_scores + bias_rows[None], allowed, onehot)


def pair_grads(query_set, key_set, rel_bias, lengths, score_scale):
    query_rows, grad_rows, log_total, delta, query_pos = query_set
    key_rows, value_rows, key_pos = key_set
    scores, allowed, onehot = score_block(
        query_rows, key_rows, rel_bias, query_pos, key_pos, lengths, score_scale
    )
    weights = jnp.where(allowed, jnp.exp(scores - log_total[..., None]), 0.0)
    grad_value = jnp.einsum(
        "sqhk,sqhd->skhd",
        weights.astype(jnp.bfloat16),
        grad_rows,
        preferred_element_type=jnp.float32,
    )
    grad_weights = jnp.einsum(
        "sqhd,skhd->sqhk", grad_rows, value_rows, preferred_element_type=jnp.float32
    )
    grad_scores = (weights * (grad_weights - delta[..., None])).astype(jnp.bfloat16)
    grad_query = score_scale * jnp.einsum(
        "sqhk,skhd->sqhd", grad_scores, key_rows, preferred_element_type=jnp.float32
    )
    grad_key = score_scale * jnp.einsum(
        "sqhk,sqhd->skhd", grad_scores, query_rows, preferred_element_type=jnp.float32
    )
    grad_table = jnp.einsum(
        "sqhk,qkb->bh", grad_scores, onehot.astype(jnp.bfloat16), preferred_element_type=jnp.float32
    )
    return (grad_query, grad_key, grad_value, grad_table)


def dispatch_table(expert_index, live_rows, expert_count, capacity):
    picked = expert_index.reshape(-1)
    live_pairs = jnp.broadcast_to(live_rows[:, :, None], expert_index.shape).reshape(-1)
    chosen = (
        (picked[:, None] == jnp.arange(expert_count, dtype=jnp.int32)[None, :])
        & live_pairs[:, None]
    ).astype(jnp.int32)
    earlier = jnp.cumsum(chosen, axis=0) - chosen
    position_in = jnp.sum(earlier * chosen, -1)
    kept_pairs = live_pairs & (position_in < capacity)
    slot_of = jnp.where(kept_pairs, picked * capacity + position_in, -1)
    matches = slot_of[None, :] == jnp.arange(expert_count * capacity, dtype=jnp.int32)[:, None]
    table = jnp.any(matches.reshape(expert_count * capacity, -1, 2), -1).astype(jnp.float32)
    slot_ids = jnp.arange(expert_count * capacity, dtype=jnp.int32) // capacity
    slot_expert = (slot_ids[:, None] == jnp.arange(expert_count, dtype=jnp.int32)[None, :]).astype(
        jnp.float32
    )
    return (table, slot_expert)


def on_device(
    tokens,
    lengths,
    expert_index,
    cotangent,
    norm_attn,
    w_query,
    w_key,
    w_value,
    w_out,
    rel_bias,
    norm_ffn,
    router,
    w_gate,
    w_up,
    w_down,
):
    slot_count, per_slot, model_width = tokens.shape
    head_count = rel_bias.shape[1]
    head_size = model_width // head_count
    expert_count = router.shape[1]
    capacity = (10 * slot_count * per_slot + 4 * expert_count - 1) // (4 * expert_count)
    score_scale = head_size ** (-0.5)
    row_count = slot_count * per_slot
    shape_four = (slot_count, per_slot, head_count, head_size)
    shape_three = (slot_count, per_slot, model_width)
    device_at = lax.axis_index(("experts", "context"))
    positions = device_at * per_slot + jnp.arange(per_slot, dtype=jnp.int32)
    live_rows = positions[None, :] < lengths[:, None]
    keep_mask = live_rows.reshape(row_count, 1).astype(jnp.float32)
    inputs = tokens.reshape(row_count, model_width).astype(jnp.float32)
    normed = rms_norm(inputs, norm_attn).astype(jnp.bfloat16)
    query_flat = jnp.dot(normed, w_query, preferred_element_type=jnp.float32).astype(jnp.bfloat16)
    key_flat = jnp.dot(normed, w_key, preferred_element_type=jnp.float32).astype(jnp.bfloat16)
    value_flat = jnp.dot(normed, w_value, preferred_element_type=jnp.float32).astype(jnp.bfloat16)
    query_four = query_flat.reshape(shape_four)
    key_four = key_flat.reshape(shape_four)
    value_four = value_flat.reshape(shape_four)
    key_three = key_flat.reshape(shape_three)
    value_three = value_flat.reshape(shape_three)
    start_state = (
        jnp.zeros(shape_four, jnp.float32),
        jnp.full((slot_count, per_slot, head_count), mask_fill, jnp.float32),
        jnp.zeros((slot_count, per_slot, head_count), jnp.float32),
    )
    offset = jnp.int32(0)
    key_all = lax.all_gather(key_three, ("experts", "context"), axis=1, tiled=True)
    value_all = lax.all_gather(value_three, ("experts", "context"), axis=1, tiled=True)
    piece_rows = key_all.shape[1]
    block_rows = math.gcd(piece_rows, 8 * per_slot)

    def forward_visit(carried, block_id):
        running, running_max, denominator = carried
        local_at = block_id * block_rows
        key_rows = lax.dynamic_slice_in_dim(key_all, local_at, block_rows, 1).reshape(
            slot_count, block_rows, head_count, head_size
        )
        value_rows = lax.dynamic_slice_in_dim(value_all, local_at, block_rows, 1).reshape(
            slot_count, block_rows, head_count, head_size
        )
        key_pos = offset + local_at + jnp.arange(block_rows, dtype=jnp.int32)
        scores, allowed, _ = score_block(
            query_four, key_rows, rel_bias, positions, key_pos, lengths, score_scale
        )
        scores = jnp.where(allowed, scores, mask_fill)
        new_max = jnp.maximum(running_max, jnp.max(scores, -1))
        factor = jnp.exp(running_max - new_max)
        weights = jnp.where(allowed, jnp.exp(scores - new_max[..., None]), 0.0)
        denominator = denominator * factor + jnp.sum(weights, -1)
        running = running * factor[..., None] + jnp.einsum(
            "sqhk,skhd->sqhd",
            weights.astype(jnp.bfloat16),
            value_rows,
            preferred_element_type=jnp.float32,
        )
        return ((running, new_max, denominator), None)

    carried, _ = lax.scan(
        forward_visit, start_state, jnp.arange(piece_rows // block_rows, dtype=jnp.int32)
    )
    running, running_max, denominator = carried
    attended = running / denominator[..., None]
    log_total = running_max + jnp.log(denominator)
    attended_low = attended.reshape(row_count, model_width).astype(jnp.bfloat16)
    middle = inputs + jnp.dot(attended_low, w_out, preferred_element_type=jnp.float32)
    second_low = rms_norm(middle, norm_ffn).astype(jnp.bfloat16)
    second_wide = second_low.astype(jnp.float32)
    logits = jnp.dot(second_wide, router, precision=highest)
    gates = jax.nn.softmax(logits, axis=-1)
    table, slot_expert = dispatch_table(expert_index, live_rows, expert_count, capacity)
    table_low = table.astype(jnp.bfloat16)
    dispatched = jnp.dot(table_low, second_low, preferred_element_type=jnp.float32).astype(
        jnp.bfloat16
    )
    arrived = lax.all_to_all(
        dispatched.reshape(expert_count, capacity, model_width),
        "experts",
        split_axis=0,
        concat_axis=1,
        tiled=True,
    )[0]
    gate_pre = jnp.dot(arrived, w_gate[0], preferred_element_type=jnp.float32)
    up_pre = jnp.dot(arrived, w_up[0], preferred_element_type=jnp.float32)
    hidden_low = (jax.nn.gelu(gate_pre, approximate=True) * up_pre).astype(jnp.bfloat16)
    produced = jnp.dot(hidden_low, w_down[0], preferred_element_type=jnp.float32).astype(
        jnp.bfloat16
    )
    returned = lax.all_to_all(
        produced[None], "experts", split_axis=1, concat_axis=0, tiled=True
    ).reshape(expert_count * capacity, model_width)
    returned_wide = returned.astype(jnp.float32)
    slot_weight = jnp.sum(jnp.dot(table, gates, precision=highest) * slot_expert, -1)
    routed = jnp.dot(table.T, slot_weight[:, None] * returned_wide, precision=highest)
    result = ((middle + routed) * keep_mask).astype(jnp.bfloat16).reshape(shape_three)
    grad_result = cotangent.reshape(row_count, model_width).astype(jnp.float32) * keep_mask
    gathered_grad = jnp.dot(table, grad_result, precision=highest)
    grad_produced = (
        (slot_weight[:, None] * gathered_grad)
        .astype(jnp.bfloat16)
        .reshape(expert_count, capacity, model_width)
    )
    grad_arrived_out = lax.all_to_all(
        grad_produced, "experts", split_axis=0, concat_axis=1, tiled=True
    )[0]
    grad_slot_weight = jnp.sum(gathered_grad * returned_wide, -1)
    grad_hidden = jnp.dot(grad_arrived_out, w_down[0].T, preferred_element_type=jnp.float32)
    grad_w_down = jnp.dot(hidden_low.T, grad_arrived_out, preferred_element_type=jnp.float32)

    def activation(gate_in, up_in):
        return jax.nn.gelu(gate_in, approximate=True) * up_in

    _, activation_back = jax.vjp(activation, gate_pre, up_pre)
    grad_gate_pre, grad_up_pre = activation_back(grad_hidden)
    grad_gate_low = grad_gate_pre.astype(jnp.bfloat16)
    grad_up_low = grad_up_pre.astype(jnp.bfloat16)
    grad_w_gate = jnp.dot(arrived.T, grad_gate_low, preferred_element_type=jnp.float32)
    grad_w_up = jnp.dot(arrived.T, grad_up_low, preferred_element_type=jnp.float32)
    grad_arrived = (
        jnp.dot(grad_gate_low, w_gate[0].T, preferred_element_type=jnp.float32)
        + jnp.dot(grad_up_low, w_up[0].T, preferred_element_type=jnp.float32)
    ).astype(jnp.bfloat16)
    grad_returned = lax.all_to_all(
        grad_arrived[None], "experts", split_axis=1, concat_axis=0, tiled=True
    ).reshape(expert_count * capacity, model_width)
    expert_sums = (
        lax.psum_scatter(
            grad_w_gate[None].astype(jnp.bfloat16), "context", scatter_dimension=1, tiled=True
        ).astype(jnp.float32),
        lax.psum_scatter(
            grad_w_up[None].astype(jnp.bfloat16), "context", scatter_dimension=1, tiled=True
        ).astype(jnp.float32),
        lax.psum_scatter(
            grad_w_down[None].astype(jnp.bfloat16), "context", scatter_dimension=1, tiled=True
        ).astype(jnp.float32),
    )
    grad_second = jnp.dot(table_low.T, grad_returned, preferred_element_type=jnp.float32)
    grad_gates = jnp.dot(table.T, grad_slot_weight[:, None] * slot_expert, precision=highest)
    grad_logits = gates * (grad_gates - jnp.sum(gates * grad_gates, -1, keepdims=True))
    grad_router = jnp.dot(second_wide.T, grad_logits, precision=highest)
    grad_second = grad_second + jnp.dot(grad_logits, router.T, precision=highest)
    grad_middle_norm, grad_norm_ffn = norm_back(middle, norm_ffn, grad_second)
    grad_middle = grad_result + grad_middle_norm
    grad_middle_low = grad_middle.astype(jnp.bfloat16)
    grad_w_out = jnp.dot(attended_low.T, grad_middle_low, preferred_element_type=jnp.float32)
    grad_attended_low = jnp.dot(
        grad_middle_low, w_out.T, preferred_element_type=jnp.float32
    ).astype(jnp.bfloat16)
    grad_attended_four = grad_attended_low.reshape(shape_four)
    grad_attended_three = grad_attended_low.reshape(shape_three)
    delta = jnp.sum(grad_attended_four.astype(jnp.float32) * attended, -1)
    local_queries = (query_four, grad_attended_four, log_total, delta, positions)
    grad_start = (jnp.zeros(shape_four, jnp.float32), jnp.zeros(rel_bias.shape, jnp.float32))
    query_offset = jnp.int32(0)
    query_key_all = lax.all_gather(key_three, ("experts", "context"), axis=1, tiled=True)
    query_value_all = lax.all_gather(value_three, ("experts", "context"), axis=1, tiled=True)
    piece_rows = query_key_all.shape[1]
    query_block_rows = math.gcd(piece_rows, 8 * per_slot)

    def query_visit(carried, block_id):
        local_at = block_id * query_block_rows
        key_rows = lax.dynamic_slice_in_dim(query_key_all, local_at, query_block_rows, 1).reshape(
            slot_count, query_block_rows, head_count, head_size
        )
        value_rows = lax.dynamic_slice_in_dim(
            query_value_all, local_at, query_block_rows, 1
        ).reshape(slot_count, query_block_rows, head_count, head_size)
        key_pos = query_offset + local_at + jnp.arange(query_block_rows, dtype=jnp.int32)
        grad_query, _, _, grad_table = pair_grads(
            local_queries, (key_rows, value_rows, key_pos), rel_bias, lengths, score_scale
        )
        return ((carried[0] + grad_query, carried[1] + grad_table), None)

    carried, _ = lax.scan(
        query_visit, grad_start, jnp.arange(piece_rows // query_block_rows, dtype=jnp.int32)
    )
    grad_query_four, grad_table = carried
    log_whole, delta_whole = (
        lax.all_gather(log_total, ("experts", "context"), axis=1, tiled=True),
        lax.all_gather(delta, ("experts", "context"), axis=1, tiled=True),
    )
    local_keys = (key_four, value_four, positions)
    zero_four = jnp.zeros(shape_four, jnp.float32)
    key_offset = jnp.int32(0)
    query_all = lax.all_gather(
        query_flat.reshape(shape_three), ("experts", "context"), axis=1, tiled=True
    )
    grad_all = lax.all_gather(grad_attended_three, ("experts", "context"), axis=1, tiled=True)
    piece_rows = query_all.shape[1]
    key_block_rows = math.gcd(piece_rows, 8 * per_slot)

    def key_visit(carried, block_id):
        local_at = block_id * key_block_rows
        whole_at = key_offset + local_at
        query_rows = lax.dynamic_slice_in_dim(query_all, local_at, key_block_rows, 1).reshape(
            slot_count, key_block_rows, head_count, head_size
        )
        grad_rows = lax.dynamic_slice_in_dim(grad_all, local_at, key_block_rows, 1).reshape(
            slot_count, key_block_rows, head_count, head_size
        )
        log_rows = lax.dynamic_slice_in_dim(log_whole, whole_at, key_block_rows, 1)
        delta_rows = lax.dynamic_slice_in_dim(delta_whole, whole_at, key_block_rows, 1)
        query_pos = whole_at + jnp.arange(key_block_rows, dtype=jnp.int32)
        _, grad_key, grad_value, _ = pair_grads(
            (query_rows, grad_rows, log_rows, delta_rows, query_pos),
            local_keys,
            rel_bias,
            lengths,
            score_scale,
        )
        return ((carried[0] + grad_key, carried[1] + grad_value), None)

    carried, _ = lax.scan(
        key_visit, (zero_four, zero_four), jnp.arange(piece_rows // key_block_rows, dtype=jnp.int32)
    )
    grad_key_four, grad_value_four = carried
    grad_query_low = grad_query_four.reshape(row_count, model_width).astype(jnp.bfloat16)
    grad_key_low = grad_key_four.reshape(row_count, model_width).astype(jnp.bfloat16)
    grad_value_low = grad_value_four.reshape(row_count, model_width).astype(jnp.bfloat16)
    grad_w_query = jnp.dot(normed.T, grad_query_low, preferred_element_type=jnp.float32)
    grad_w_key = jnp.dot(normed.T, grad_key_low, preferred_element_type=jnp.float32)
    grad_w_value = jnp.dot(normed.T, grad_value_low, preferred_element_type=jnp.float32)
    grad_normed = (
        jnp.dot(grad_query_low, w_query.T, preferred_element_type=jnp.float32)
        + jnp.dot(grad_key_low, w_key.T, preferred_element_type=jnp.float32)
        + jnp.dot(grad_value_low, w_value.T, preferred_element_type=jnp.float32)
    )
    grad_input_norm, grad_norm_attn = norm_back(inputs, norm_attn, grad_normed)
    grad_tokens = (grad_middle + grad_input_norm).reshape(shape_three)
    dense = lax.psum(
        (
            grad_norm_attn,
            grad_w_query,
            grad_w_key,
            grad_w_value,
            grad_w_out,
            grad_table,
            grad_norm_ffn,
            grad_router,
        ),
        ("experts", "context"),
    )
    return (
        result,
        grad_tokens,
        dense[0],
        dense[1],
        dense[2],
        dense[3],
        dense[4],
        dense[5],
        dense[6],
        dense[7],
        expert_sums[0],
        expert_sums[1],
        expert_sums[2],
    )


MESH = pl.DeviceIdType.MESH
BF = jnp.bfloat16
F32 = jnp.float32
VMEM = pltpu.VMEM
THREE = (
    (("x", "y", "l"), 0, 384),
    (("y", "l", "x"), 384, 384),
    (("l", "x", "y"), 768, 256),
)
TWO = ((("l", "x", "y"), 0, 512), (("l", "y", "x"), 512, 512))
LATE = ((("x", "y", "l"), 0, 512), (("y", "x", "l"), 512, 512))
BY_Y = ((("l", "x", "y"), 0, 1024),)
BY_X = ((("l", "y", "x"), 0, 1024),)
BIG = -1e30
TILE = 256
PLACES = 80
SHARE = 704
GATE_FIRST = 384
UP_FIRST = 320
DOWN_FIRST = 192
TOKENS_AT = 3
UP_AT = 4
NT = (((1,), (1,)), ((), ()))
TN = (((0,), (0,)), ((), ()))
CUBE_SEMS = [pltpu.SemaphoreType.DMA((3, 8))] * 4
ONE_SEMS = [pltpu.SemaphoreType.DMA((1, 8))] * 4


def spot():
    e = lax.axis_index("experts")
    c = lax.axis_index("context")
    return dict(k=lax.rem(e, 2), y=e // 2, x=lax.rem(c, 2), l=lax.rem(c // 2, 2), h=c // 4)


def flip(b, names):
    return {n: (1 - v if n in names else v) for n, v in b.items()}


def device(b):
    return {"experts": b["y"] * 2 + b["k"], "context": b["h"] * 4 + b["l"] * 2 + b["x"]}


def row_of(b):
    return b["y"] * 2 + b["k"]


def col_of(b):
    return b["l"] * 2 + b["x"]


def slot_of(b):
    return row_of(b) * 4 + col_of(b)


def greet(peers):
    barrier = pltpu.get_barrier_semaphore()
    for peer in peers:
        pl.semaphore_signal(barrier, inc=1, device_id=peer, device_id_type=MESH)
    pl.semaphore_wait(barrier, len(peers))


def cube_peers(b):
    return [device(flip(b, [n])) for n in ("x", "y", "l", "k")]


def cube_all(b):
    peers = []
    for step in range(1, 16):
        s = lax.rem(slot_of(b) + step, 16)
        peers.append({"experts": s // 4, "context": b["h"] * 4 + lax.rem(s, 4)})
    return peers


def world_all(b):
    me = row_of(b) * 8 + b["h"] * 4 + col_of(b)
    peers = []
    for step in range(1, 32):
        j = lax.rem(me + step, 32)
        peers.append((j, {"experts": j // 8, "context": lax.rem(j, 8)}))
    return me, peers


def remote(src, dst, ssem, rsem, peer):
    return pltpu.make_async_remote_copy(
        src_ref=src, dst_ref=dst, send_sem=ssem, recv_sem=rsem, device_id=peer, device_id_type=MESH
    )


def names_of(order, t):
    return [order[i] for i in range(3) if (t >> i) & 1]


def gather_steps(b, view, ss, rs, cs, cr, parts=THREE):
    started = []
    core = device(flip(b, ["k"]))
    every = range(len(parts))

    def piece(p, t, more=()):
        order, c0, cn = parts[p]
        return view(flip(b, names_of(order, t) + list(more)), c0, cn)

    def link(p, t, i):
        ref = piece(p, t)
        n = t | (1 << i)
        cp = remote(ref, ref, ss.at[p, n], rs.at[p, n], device(flip(b, [parts[p][0][i]])))
        cp.start()
        started.append(cp)

    def across(p, t):
        ref = piece(p, t)
        cp = remote(ref, ref, cs.at[p, t], cr.at[p, t], core)
        cp.start()
        started.append(cp)

    for i in range(3):
        for p in every:
            link(p, 0, i)
    for p in every:
        across(p, 0)
    yield
    for t in range(1, 8):
        for p in every:
            ref = piece(p, t)
            remote(ref, ref, ss.at[p, t], rs.at[p, t], core).wait_recv()
            for i in range(t.bit_length(), 3):
                link(p, t, i)
            across(p, t)
        yield
    for cp in started:
        cp.wait_send()
    for p in every:
        for t in range(8):
            ref = piece(p, t, ["k"])
            remote(ref, ref, cs.at[p, t], cr.at[p, t], core).wait_recv()
    yield


def gather_cube(*args):
    for _ in gather_steps(*args):
        pass


def eighth(b):
    return b["y"] * 4 + b["l"] * 2 + b["x"]


def scatter_steps(b, parts, acc, landing, ss, rs, cs, cr, cuts=THREE):
    started = []
    core = device(flip(b, ["k"]))
    dims = ("x", "y", "l")
    order = sorted(range(8), key=lambda t: -bin(t).count("1"))

    def set_of(t):
        return [n for i, n in enumerate(dims) if (t >> i) & 1]

    def push(p, step, others_set):
        dims_in_order, c0, cn = cuts[p]
        first = dims_in_order[step]
        others = dims_in_order[step + 1 :]
        there = flip(b, [first] + others_set)
        n = (1 << len(others)) + sum(1 << i for i, name in enumerate(others) if name in others_set)
        cp = remote(
            acc.at[eighth(there), :, pl.ds(c0, cn)],
            landing.at[n, :, pl.ds(c0, cn)],
            ss.at[p, n],
            rs.at[p, n],
            device(flip(b, [first])),
        )
        cp.start()
        started.append(cp)

    for t in order:
        there = flip(b, set_of(t) + ["k"])
        cp = remote(parts.at[slot_of(there)], acc.at[eighth(there)], cs.at[0, t], cr.at[0, t], core)
        cp.start()
        started.append(cp)
    yield
    for t in order:
        here = flip(b, set_of(t))
        n = eighth(here)
        remote(parts.at[slot_of(here)], acc.at[n], cs.at[0, t], cr.at[0, t], core).wait_recv()
        acc[n] = (acc[n].astype(F32) + parts[slot_of(here)].astype(F32)).astype(BF)
        for p in range(len(cuts)):
            first = cuts[p][0][0]
            if first in set_of(t):
                push(p, 0, [name for name in set_of(t) if name != first])
    yield
    for step in range(3):
        rest = 2 - step
        count = 1 << rest
        for t in range(count - 1, -1, -1):
            for p in range(len(cuts)):
                dims_in_order, c0, cn = cuts[p]
                others = dims_in_order[step + 1 :]
                names = [others[i] for i in range(rest) if (t >> i) & 1]
                target = eighth(flip(b, names))
                n = count + t
                ref = landing.at[n, :, pl.ds(c0, cn)]
                remote(ref, ref, ss.at[p, n], rs.at[p, n], core).wait_recv()
                acc[target, :, c0 : c0 + cn] = (
                    acc[target, :, c0 : c0 + cn].astype(F32)
                    + landing[n, :, c0 : c0 + cn].astype(F32)
                ).astype(BF)
                if rest and others[0] in names:
                    push(p, step + 1, [name for name in names if name != others[0]])
        yield
    for cp in started:
        cp.wait_send()
    yield


def scatter_cube(*args):
    for _ in scatter_steps(*args):
        pass


def params(cid=None, mib=60):
    if cid is None:
        return pltpu.CompilerParams(vmem_limit_bytes=mib * 2**20)
    return pltpu.CompilerParams(
        collective_id=cid, has_side_effects=True, vmem_limit_bytes=mib * 2**20
    )


def call(body, outs, scratch, cid, *args, anywhere=(), outs_anywhere=(), scalars=()):
    def spec(i, listed):
        if i in listed:
            return pl.BlockSpec(memory_space=pl.ANY)
        return pl.BlockSpec(memory_space=VMEM)

    return pl.pallas_call(
        body,
        out_shape=outs,
        in_specs=[
            pl.BlockSpec(memory_space=pltpu.SMEM) if i in scalars else spec(i, anywhere)
            for i in range(len(args))
        ],
        out_specs=[spec(i, outs_anywhere) for i in range(len(outs))],
        scratch_shapes=scratch,
        compiler_params=params(cid),
    )(*args)


def shape(dims, kind=BF):
    return jax.ShapeDtypeStruct(dims, kind)


def sequence_steps(b, whole, staged, sems, hs, hr):
    partner = device(flip(b, ["h"]))
    mine = whole.at[row_of(b), b["h"], col_of(b)]
    cp = remote(staged.at[1 - b["h"]], mine, hs, hr, partner)
    cp.start()
    whole[row_of(b), b["h"], col_of(b)] = staged[b["h"]]
    yield
    theirs = whole.at[row_of(b), 1 - b["h"], col_of(b)]
    remote(theirs, theirs, hs, hr, partner).wait_recv()

    def view(v, c0, cn):
        return whole.at[row_of(v), :, col_of(v), :, pl.ds(c0, cn)]

    for _ in gather_steps(b, view, *sems):
        yield
    cp.wait_send()
    yield


def group_view(ref, r0=0, rn=128):
    def view(v, c0, cn):
        return ref.at[slot_of(v), pl.ds(r0, rn), pl.ds(c0, cn)]

    return view


def send_small(b, src, into, ss, rs):
    copies = []
    for step, peer in enumerate(cube_all(b)):
        cp = remote(src, into.at[slot_of(b)], ss.at[step], rs.at[step], peer)
        cp.start()
        copies.append(cp)
    return copies


def wait_small(b, into, ss, rs, copies):
    me = slot_of(b)
    for step in range(15):
        came = into.at[lax.rem(me + 15 - step, 16)]
        remote(came, came, ss.at[step], rs.at[step], device(b)).wait_recv()
    for cp in copies:
        cp.wait_send()


def inverse_rms(values):
    return lax.rsqrt(jnp.mean(values * values, axis=-1, keepdims=True) + norm_epsilon)


def first_body(
    tokens, gain, picks, w_query, w_key, w_value, w_gate, w_up, bias_t, onehot_t, h1, picks_all, w3, wg, wu, dist, staged, heads, wide, *sems
):
    b = spot()
    head = slot_of(b)
    loads = []
    for n, w in enumerate((w_query, w_key, w_value)):
        at = pl.multiple_of((head // 2) * 128, 128)
        loads.append(pltpu.make_async_copy(w.at[:, pl.ds(at, 128)], heads.at[n], sems[8].at[n]))
    offsets = []
    for n, w in enumerate((w_gate, w_gate, w_up, w_up)):
        share = 4 * (n % 2) + col_of(b)
        block = (share * 352) // 128 - share // 7
        offsets.append(share * 352 - block * 128)
        at = pl.multiple_of(block * 128, 128)
        loads.append(
            pltpu.make_async_copy(w.at[:, pl.ds(at, 512)], wide.at[n], sems[8].at[3 + n])
        )
    for cp in loads:
        cp.start()
    for s in range(2):
        rows = tokens[s].astype(F32)
        staged[s] = (rows * inverse_rms(rows) * gain[...]).astype(BF)
    greet([device(flip(b, ["h"]))] + cube_all(b))
    steps = sequence_steps(b, h1, staged, sems[0:4], sems[4], sems[5])
    next(steps)
    copies = send_small(b, picks, picks_all, sems[6], sems[7])
    picks_all[slot_of(b)] = picks[...]
    row = jnp.broadcast_to(bias_t[pl.ds(head, 1)], (8, 128))
    row = row - row[:, 31:32]
    dist[...] = jnp.dot(row, onehot_t[...], precision=highest)
    for cp in loads:
        cp.wait()
    next(steps)
    left = lane((1024, 128)) < 64
    for n in range(3):
        turned = pltpu.roll(heads[n].astype(F32), lax.rem(head, 2) * 64, 1)
        w3[:, n * 128 : n * 128 + 128] = jnp.where(left, turned, 0.0).astype(BF)
        next(steps)
    for n in range(4):
        out = wg if n < 2 else wu
        for r in range(0, 1024, 256):
            turned = pltpu.roll(wide[n, r : r + 256].astype(F32), 512 - offsets[n], 1)
            at = (n % 2) * 352
            out[r : r + 256, at : at + 352] = turned[:, :352].astype(BF)
        next(steps)
    for _ in range(3):
        next(steps, None)
    wait_small(b, picks_all, sems[6], sems[7], copies)


def lane(shape_, dim=1):
    return lax.broadcasted_iota(jnp.int32, shape_, dim)


def near_tiles(row):
    wide = jnp.broadcast_to(row, (TILE, 2 * TILE))
    wide = pltpu.roll(wide, 0, 1, stride=1, stride_axis=0)
    later = lax.broadcasted_iota(jnp.int32, (TILE, TILE), 0) > lane((TILE, TILE))
    return [jnp.where(later, BIG, wide[:, :TILE]), wide[:, TILE:]]


def pack_halves(rows):
    n = rows.shape[0] // 64
    four = rows.reshape(n, 2, 32, 128)
    return jnp.where(
        lax.broadcasted_iota(jnp.int32, (n, 32, 128), 2) < 64,
        four[:, 0],
        pltpu.roll(four[:, 1].reshape(n * 32, 128), 64, 1).reshape(n, 32, 128),
    )


def attend_body(length, h1, w3, dist, cot, packed, out_t, qs, ks, vs, lse, dy, strip, v_t, weights, *sems):
    b = spot()
    dy[slot_of(b)] = cot[...]
    greet(cube_peers(b))
    steps = gather_steps(b, group_view(dy, 0, 64), *sems, parts=BY_Y)
    next(steps)
    limit = length[b["h"]]
    for i in range(8):
        rows = slice(i * TILE, (i + 1) * TILE)
        p = jnp.dot(h1[rows], w3[...], preferred_element_type=F32)
        spot_lane = lane((TILE, 128))
        where_at = lax.broadcasted_iota(jnp.int32, (TILE, 128), 0) + i * TILE
        one = spot_lane == 64
        qs[rows] = jnp.where(one, 1.0, p[:, :128] * 0.125).astype(BF)
        ks[rows] = jnp.where(one & (where_at >= limit), BIG, p[:, 128:256]).astype(BF)
        v = jnp.where(one, 1.0, p[:, 256:]).astype(BF)
        vs[rows] = v
        v_t[:, rows] = v.astype(F32).T.astype(BF)
    next(steps)
    near = near_tiles(dist[0:1])
    for i in range(8):
        cols = slice(i * TILE, (i + 1) * TILE)
        q = qs[cols]
        top = None
        for j in range(i + 1):
            rows = slice(j * TILE, (j + 1) * TILE)
            s = lax.dot_general(ks[rows], q, NT, preferred_element_type=F32)
            if i - j < 2:
                s = s + near[i - j]
            strip[rows] = s
            m = jnp.max(s, axis=0, keepdims=True)
            top = m if top is None else jnp.maximum(top, m)
        for j in range(i + 1):
            rows = slice(j * TILE, (j + 1) * TILE)
            weights[rows] = jnp.exp(strip[rows] - top).astype(BF)
        n = (i + 1) * TILE
        o = jnp.dot(v_t[:, :n], weights[:n], preferred_element_type=F32)
        total = o[64:65]
        o = o / total
        lse[:, cols] = jnp.broadcast_to(top + jnp.log(total), (8, TILE))
        out_t[:, cols] = o[:64]
        packed[4 * i : 4 * i + 4] = pack_halves(o.T).astype(BF)
        for _ in range((0, 0, 1, 1, 1, 1, 2, 1)[i]):
            next(steps)


def unpack_halves(first, second):
    a = first.astype(F32)
    c = second.astype(F32)
    left = lane((32, 128)) < 64
    top = jnp.where(left, a, pltpu.roll(c, 64, 1))
    bottom = jnp.where(left, pltpu.roll(a, 64, 1), c)
    return top.astype(BF), bottom.astype(BF)


def everyone(b, src, dst_at, ss, rs):
    me, peers = world_all(b)
    copies = []
    for step, (j, peer) in enumerate(peers):
        cp = remote(src.at[j], dst_at(me), ss.at[step], rs.at[step], peer)
        cp.start()
        copies.append(cp)
    return me, copies


def everyone_wait(b, me, dst_at, ss, rs, copies):
    for step in range(31):
        came = dst_at(lax.rem(me + 31 - step, 32))
        remote(came, came, ss.at[step], rs.at[step], device(b)).wait_recv()
    for cp in copies:
        cp.wait_send()


def middle_body(packed, tokens, w_out, gain, router3, middle, h2_all, gates_all, joined, land, gates, *sems):
    b = spot()
    greet([peer for _, peer in world_all(b)[1]])

    def at(j):
        return land.at[j]

    me, copies = everyone(b, packed, at, sems[4], sems[5])
    land[me] = packed[me]
    everyone_wait(b, me, at, sems[4], sems[5], copies)
    for s in range(2):
        for pair in range(8):
            first, second = 2 * pair, 2 * pair + 1
            j0 = (first // 4) * 8 + s * 4 + first % 4
            j1 = (second // 4) * 8 + s * 4 + second % 4
            top, bottom = unpack_halves(land[j0], land[j1])
            cols = slice(pair * 128, pair * 128 + 128)
            joined[s * 64 : s * 64 + 32, cols] = top
            joined[s * 64 + 32 : s * 64 + 64, cols] = bottom
    x = tokens[...].astype(F32)
    mid = x + jnp.dot(joined[...], w_out[...], preferred_element_type=F32)
    middle[...] = mid
    h2 = (mid * inverse_rms(mid) * gain[...]).astype(BF)
    h2_all[slot_of(b)] = h2
    gather_half = group_view(h2_all)
    logits = jnp.dot(h2, router3[...], preferred_element_type=F32).T
    logits = logits[0:8] + logits[8:16] + logits[16:24]
    real = lax.broadcasted_iota(jnp.int32, (8, 128), 0) < 4
    logits = jnp.where(real, logits, BIG)
    g = jnp.exp(logits - jnp.max(logits, axis=0, keepdims=True))
    gates[...] = g / jnp.sum(g, axis=0, keepdims=True)
    small = send_small(b, gates, gates_all, sems[6], sems[7])
    gates_all[slot_of(b)] = gates[...]
    gather_cube(b, gather_half, *sems[0:4])
    wait_small(b, gates_all, sems[6], sems[7], small)


def expert_body(
    h2, dy0, cot, gates, picks, wg, wu, w_down, routed, dh2, dgates, near_g, near_u, near_d, far_g, far_u, far_d, got_d, dy, rows, grad, dexp, weight, hid, dgs, dus, acts, slopes, outs, drs, dws, wd, load, *sems
):
    b = spot()
    h = b["h"]
    partner = device(flip(b, ["h"]))
    fetches = [pltpu.make_async_copy(dy0, dy.at[:, pl.ds(0, 64)], load.at[0])]
    for n in range(2):
        at = pl.multiple_of((4 * n + col_of(b)) * 352, 32)
        fetches.append(
            pltpu.make_async_copy(
                w_down.at[pl.ds(at, 352)], wd.at[pl.ds(n * 352, 352)], load.at[1 + n]
            )
        )
    for cp in fetches:
        cp.start()
    dy[slot_of(b), 64:128] = cot[...]
    greet([partner] + cube_peers(b))
    steps = gather_steps(b, group_view(dy, 64, 64), *sems[0:4], parts=BY_X)
    next(steps)
    mine = row_of(b)
    mine_f = mine.astype(F32)
    first = picks[:, 0, :]
    second = picks[:, 1, :]
    chosen = jnp.where((first == mine_f) | (second == mine_f), 1.0, 0.0)
    earlier = jnp.where(
        lax.broadcasted_iota(jnp.int32, (128, 128), 0) < lane((128, 128)), 1.0, 0.0
    )
    place = jnp.dot(chosen.astype(BF), earlier.astype(BF), preferred_element_type=F32)
    place = jnp.where((chosen > 0.5) & (place < PLACES), place, -1.0)
    place_t = jnp.concatenate([place, jnp.full((112, 128), -1.0, F32)], axis=0).T
    level = lax.broadcasted_iota(jnp.int32, (PLACES, 128), 0).astype(F32)
    level_t = lane((128, PLACES)).astype(F32)
    is_mine = lax.broadcasted_iota(jnp.int32, (8, 128), 0) == mine
    for m in range(16):
        at = slice(m * PLACES, (m + 1) * PLACES)
        hit = jnp.where(level == place[m : m + 1], 1.0, 0.0)
        rows[at] = jnp.dot(hit.astype(BF), h2[m], preferred_element_type=F32).astype(BF)
        gate_row = jnp.sum(jnp.where(is_mine, gates[m], 0.0), axis=0, keepdims=True)
        w = jnp.sum(hit * gate_row, axis=1, keepdims=True)
        weight[at] = jnp.broadcast_to(w, (PLACES, 128))
    for cp in fetches:
        cp.wait()
    next(steps)
    c0 = math.sqrt(2.0 / math.pi)
    c1 = 0.044715
    for i in range(5):
        at = slice(i * TILE, (i + 1) * TILE)
        r = rows[at]
        gp = jnp.dot(r, wg[...], preferred_element_type=F32)
        up = jnp.dot(r, wu[...], preferred_element_type=F32)
        sq = gp * gp
        th = jnp.tanh(c0 * gp * (1.0 + c1 * sq))
        half = 0.5 * (1.0 + th)
        act = gp * half
        slope = half + 0.5 * gp * (1.0 - th * th) * (c0 * (1.0 + 3.0 * c1 * sq))
        acts[at] = act
        slopes[at] = up * slope
        hd = (act * up).astype(BF)
        hid[at] = hd
        outs[at] = jnp.dot(hd, wd[...], preferred_element_type=F32).astype(BF)
        for _ in range((1, 1, 2, 2, 1)[i]):
            next(steps)
    for m in range(16):
        at = slice(m * PLACES, (m + 1) * PLACES)
        hit = jnp.where(level == place[m : m + 1], 1.0, 0.0).astype(BF)
        g = jnp.dot(hit, dy[m], preferred_element_type=F32)
        grad[at] = g.astype(BF)
        dexp[at] = (weight[at, 0:1] * g).astype(BF)
    down = lax.dot_general(hid[...], dexp[...], TN, preferred_element_type=F32).astype(BF)
    upper = h == 1
    far_d[...] = jnp.where(upper, down[:352], down[352:])
    near_d[...] = jnp.where(upper, down[352:], down[:352])
    trade = remote(far_d.at[pl.ds(0, DOWN_FIRST)], got_d, load.at[3], load.at[4], partner)
    trade.start()
    for i in range(5):
        at = slice(i * TILE, (i + 1) * TILE)
        o = outs[at].astype(F32)
        dws[at] = jnp.broadcast_to(
            jnp.sum(grad[at].astype(F32) * o, axis=1, keepdims=True), (TILE, 128)
        )
        outs[at] = (weight[at, 0:1] * o).astype(BF)
        dh = lax.dot_general(dexp[at], wd[...], NT, preferred_element_type=F32)
        dg = (dh * slopes[at]).astype(BF)
        du = (dh * acts[at]).astype(BF)
        dgs[at] = dg
        dus[at] = du
        drs[at] = (
            lax.dot_general(dg, wg[...], NT, preferred_element_type=F32)
            + lax.dot_general(du, wu[...], NT, preferred_element_type=F32)
        ).astype(BF)
    for m in range(16):
        at = slice(m * PLACES, (m + 1) * PLACES)
        back = jnp.where(place_t[:, m : m + 1] == level_t, 1.0, 0.0).astype(BF)
        dh2[m] = jnp.dot(back, drs[at], preferred_element_type=F32).astype(BF)
        routed[m] = jnp.dot(back, outs[at], preferred_element_type=F32).astype(BF)
        hit = jnp.where(level == place[m : m + 1], 1.0, 0.0)
        dgates[m] = jnp.broadcast_to(
            jnp.sum(hit * dws[at], axis=0, keepdims=True), (8, 128)
        )
    for side, g_out, u_out in ((1 - h, far_g, far_u), (h, near_g, near_u)):
        part = rows[:, pl.ds(pl.multiple_of(side * 512, 512), 512)]
        g_out[...] = lax.dot_general(part, dgs[...], TN, preferred_element_type=F32).astype(BF)
        u_out[...] = lax.dot_general(part, dus[...], TN, preferred_element_type=F32).astype(BF)
    trade.wait()


def norm_back_rows(values, gain, grad_in):
    inverse = inverse_rms(values)
    normed = values * inverse
    scaled = grad_in * gain
    out = inverse * (scaled - normed * jnp.mean(scaled * normed, axis=-1, keepdims=True))
    return out, jnp.sum(grad_in * normed, axis=0, keepdims=True)


def split_halves(rows):
    top, bottom = rows[:32], rows[32:]
    left = lane((32, 128)) < 64
    first = jnp.where(left, top, pltpu.roll(bottom, 64, 1))
    second = jnp.where(left, pltpu.roll(top, 64, 1), bottom)
    return first.astype(BF), second.astype(BF)


def device_of(s, head):
    return (head // 4) * 8 + s * 4 + head % 4


def back_body(
    dh2, dgates, gates, cot, keep, middle, gain, router_t, h2_all, far_g, joined, w_out, do_all, dmid, smalls, got_g, gwo, acc, landing, dg_all, parcels, *sems
):
    b = spot()
    partner = device(flip(b, ["h"]))
    greet([peer for _, peer in world_all(b)[1]])
    steps = scatter_steps(b, dh2, acc, landing, *sems[0:4])
    next(steps)
    trades = [
        remote(
            far_g.at[pl.ds(r0, rn)], got_g.at[pl.ds(r0, rn)], sems[8].at[n], sems[9].at[n], partner
        )
        for n, (r0, rn) in enumerate(((0, GATE_FIRST), (GATE_FIRST, 512 - GATE_FIRST)))
    ]
    trades[0].start()
    me = slot_of(b)
    copies = []
    for step, peer in enumerate(cube_all(b)):
        s = lax.rem(me + step + 1, 16)
        cp = remote(dgates.at[s], dg_all.at[me], sems[6].at[step], sems[7].at[step], peer)
        cp.start()
        copies.append(cp)
    dg_all[me] = dgates[me]
    for _ in range(5):
        next(steps)
    wait_small(b, dg_all, sems[6], sems[7], copies)
    level = lax.broadcasted_iota(jnp.int32, (8, 128), 0)
    dg = jnp.zeros((8, 128), F32)
    for e in range(4):
        total = dg_all[4 * e] + dg_all[4 * e + 1] + dg_all[4 * e + 2] + dg_all[4 * e + 3]
        dg = jnp.where(level == e, total, dg)
    g = gates[me]
    dl_t = g * (dg - jnp.sum(g * dg, axis=0, keepdims=True))
    dl = jnp.concatenate([dl_t, jnp.zeros((120, 128), F32)], axis=0).T
    d_h2 = acc[eighth(b)].astype(F32)
    for e in range(4):
        d_h2 = d_h2 + dl[:, e : e + 1] * router_t[e : e + 1]
    grad_mid, grad_gain = norm_back_rows(middle[...], gain[...], d_h2)
    d_mid = cot[...].astype(F32) * keep[...] + grad_mid
    d_low = d_mid.astype(BF)
    d_o = lax.dot_general(d_low, w_out[...], NT, preferred_element_type=F32)
    for s in range(2):
        for pair in range(8):
            rows = d_o[s * 64 : s * 64 + 64, pair * 128 : pair * 128 + 128]
            one, two = split_halves(rows)
            parcels[device_of(s, 2 * pair)] = one
            parcels[device_of(s, 2 * pair + 1)] = two

    def at(j):
        return do_all.at[j]

    whoami, sent = everyone(b, parcels, at, sems[4], sems[5])
    trades[1].start()
    do_all[whoami] = parcels[whoami]
    dmid[...] = d_mid
    high = dl_t.astype(BF)
    rest = (dl_t - high.astype(F32)).astype(BF)
    h2 = h2_all[me]
    smalls[0:8] = jnp.dot(high, h2, preferred_element_type=F32) + jnp.dot(
        rest, h2, preferred_element_type=F32
    )
    smalls[4:5] = grad_gain
    grad_out = lax.dot_general(joined[...], d_low, TN, preferred_element_type=F32).astype(BF)
    gwo[...] = grad_out.reshape(16, 64, 1024)
    everyone_wait(b, whoami, at, sems[4], sems[5], sent)
    for cp in trades:
        cp.wait()


def attend_back_body(
    h1, do_all, qs, ks, vs, out_t, lse, dist, onehot, gwo, far_u, packed, grads, table, wo, got_u, dos, k_t, delta, p_buf, s_buf, dq_t, dk, dv, near0, near1, left, acc, landing, *sems
):
    b = spot()
    partner = device(flip(b, ["h"]))
    greet([partner] + cube_peers(b))
    steps = scatter_steps(b, gwo, acc, landing, *sems[0:4])
    next(steps)
    trade = remote(far_u.at[pl.ds(0, UP_FIRST)], got_u, sems[4], sems[5], partner)
    trade.start()
    live = lax.broadcasted_iota(jnp.int32, (4, 32, 128), 2) < 64
    for i in range(8):
        rows = slice(i * TILE, (i + 1) * TILE)
        both = do_all[4 * i : 4 * i + 4].astype(F32)
        turned = pltpu.roll(both.reshape(128, 128), 64, 1).reshape(4, 32, 128)
        d = jnp.concatenate(
            [jnp.where(live, both, 0.0)[:, None], jnp.where(live, turned, 0.0)[:, None]], axis=1
        ).reshape(TILE, 128)
        dos[rows] = d.astype(BF)
        delta[:, rows] = jnp.broadcast_to(
            jnp.sum(d.T[:64] * out_t[:, rows], axis=0, keepdims=True), (8, TILE)
        )
        kt = ks[rows].astype(F32).T
        k_t[:, rows] = jnp.where(
            lax.broadcasted_iota(jnp.int32, (128, TILE), 0) == 64, 1.0, kt
        ).astype(BF)
    next(steps)
    near = near_tiles(dist[0:1])
    near0[...] = jnp.zeros_like(near0)
    near1[...] = jnp.zeros_like(near1)
    for i in range(8):
        cols = slice(i * TILE, (i + 1) * TILE)
        q = qs[cols]
        do = dos[cols]
        level = lse[0:1, cols]
        dl = delta[0:1, cols]
        for j in range(i + 1):
            rows = slice(j * TILE, (j + 1) * TILE)
            s = lax.dot_general(ks[rows], q, NT, preferred_element_type=F32)
            if i - j < 2:
                s = s + near[i - j]
            p = jnp.exp(s - level)
            dp = lax.dot_general(vs[rows], do, NT, preferred_element_type=F32)
            ds = (p * (dp - dl)).astype(BF)
            p_buf[rows] = p.astype(BF)
            s_buf[rows] = ds
            if i == j:
                near0[...] += ds.astype(F32)
            if i - j == 1:
                near1[...] += ds.astype(F32)
        n = (i + 1) * TILE
        dq_t[:, cols] = jnp.dot(k_t[:, :n], s_buf[:n], preferred_element_type=F32)
        new_v = jnp.dot(p_buf[:n], do, preferred_element_type=F32)
        new_k = jnp.dot(s_buf[:n], q, preferred_element_type=F32)
        if i > 0:
            dv[: n - TILE] += new_v[: n - TILE]
            dk[: n - TILE] += new_k[: n - TILE]
        dv[n - TILE : n] = new_v[n - TILE :]
        dk[n - TILE : n] = new_k[n - TILE :]
        if i in (3, 5, 6, 7):
            next(steps)
    total = jnp.sum(dq_t[64:65, :].reshape(1, 16, 128), axis=1)
    skew = jnp.concatenate([near0[...], near1[...]], axis=1)
    level_u = lax.broadcasted_iota(jnp.int32, (TILE, 2 * TILE), 0)
    for bit in range(8):
        moved = pltpu.roll(skew, 2 * TILE - (1 << bit), 1)
        skew = jnp.where((level_u // (1 << bit)) % 2 == 1, moved, skew)
    by_distance = jnp.broadcast_to(jnp.sum(skew, axis=0, keepdims=True), (8, 2 * TILE))
    buckets = jnp.dot(by_distance, onehot[...], precision=highest)
    spot_lane = lane((8, 128))
    others = jnp.sum(jnp.where(spot_lane < 31, buckets, 0.0), axis=1, keepdims=True)
    whole_sum = jnp.sum(total, axis=1, keepdims=True)
    buckets = jnp.where(spot_lane == 31, whole_sum - others, buckets)
    row = jnp.concatenate([buckets, jnp.zeros((8, 384), F32)], axis=1)
    table[...] = pltpu.roll(row, slot_of(b) * 32, 1)
    for i in range(8):
        rows = slice(i * TILE, (i + 1) * TILE)
        dq = dq_t[:, rows] * 0.125
        vk = jnp.where(lane((TILE, 128)) < 64, dv[rows], pltpu.roll(dk[rows], 64, 1)).T
        left[0:64, rows] = dq[:64].astype(BF)
        left[64:128, rows] = vk[64:128].astype(BF)
        left[128:192, rows] = vk[0:64].astype(BF)
        blocks = slice(4 * i, 4 * i + 4)
        packed[blocks, 0:32] = pack_halves(dq.T).astype(BF)
        packed[blocks, 32:64] = pack_halves(dk[rows]).astype(BF)
        packed[blocks, 64:96] = pack_halves(dv[rows]).astype(BF)
    grads[...] = (
        jnp.dot(left[...], h1[...], preferred_element_type=F32).astype(BF).reshape(2, 96, 1024)
    )
    wo[...] = acc[eighth(b)]
    trade.wait()


def last_body(
    packed, grads, wo, tokens, dmid, gain, wq, wk, wv, part, table, near_g, got_g, near_u, got_u1, near_d, got_d1, far_u, far_d, routed, middle, keep, dtokens, result, whole, whole_o, smalls, gain_out, wide, down, land, other, other_o, joined, inbox, crowd, mine, half, pieces, got_u2, got_d2, acc, landing, *sems
):
    b = spot()
    greet([peer for _, peer in world_all(b)[1]])
    partner = device(flip(b, ["h"]))
    h = b["h"]
    col = col_of(b)
    around = [flip(b, names) for names in (["x", "l"], ["x"], ["l"])]
    started = []

    def spread_out(n):
        for i, there in enumerate(around):
            cp = remote(
                half.at[n, col_of(there)],
                pieces.at[n, col],
                sems[14].at[3 * n + i],
                sems[15].at[3 * n + i],
                device(there),
            )
            cp.start()
            started.append(cp)
        pieces[n, col] = half[n, col]

    def at(j):
        return land.at[j]

    def view_of(side):
        def view(v, c0, cn):
            return whole.at[side, slot_of(v), :, pl.ds(c0, cn)]

        return view

    trade = remote(grads.at[1 - h], other, sems[8].at[0], sems[9].at[0], partner)
    trade.start()
    trade_o = remote(wo, other_o, sems[8].at[2], sems[9].at[2], partner)
    trade_o.start()
    me_slot = slot_of(b)
    smalls[...] = part[...]
    smalls[5:8] = jnp.concatenate([table[0:3], jnp.zeros((3, 512), F32)], axis=1)

    def add_small():
        for step, name in enumerate(("k", "x", "y", "l", "h")):
            cp = remote(
                smalls, inbox.at[step], sems[12].at[step], sems[13].at[step], device(flip(b, [name]))
            )
            cp.start()
            yield
            cp.wait()
            smalls[...] = smalls[...] + inbox[step]
        yield

    tokens_back = scatter_steps(b, routed, acc, landing, *sems[24:28], cuts=LATE)
    next(tokens_back)
    rounds = add_small()
    next(rounds)
    half[0] = (near_g[...].astype(F32) + got_g[...].astype(F32)).astype(BF)
    spread_out(0)
    next(tokens_back)
    next(rounds)
    trade.wait()
    whole[h, me_slot] = (grads[h].astype(F32) + other[...].astype(F32)).astype(BF)
    share = remote(
        whole.at[h, me_slot], whole.at[h, me_slot], sems[8].at[1], sems[9].at[1], partner
    )
    share.start()
    near = gather_steps(b, view_of(h), *sems[0:4], parts=TWO)
    next(near)
    me, copies = everyone(b, packed, at, sems[10], sems[11])
    trades = [
        remote(far_u.at[pl.ds(UP_FIRST, 512 - UP_FIRST)], got_u2, sems[16].at[0], sems[17].at[0], partner),
        remote(far_d.at[pl.ds(DOWN_FIRST, 352 - DOWN_FIRST)], got_d2, sems[16].at[1], sems[17].at[1], partner),
    ]
    for cp in trades:
        cp.start()
    land[me] = packed[me]
    next(rounds)
    next(near)
    trade_o.wait()
    whole_o[me_slot] = (wo[...].astype(F32) + other_o[...].astype(F32)).astype(BF)
    outs = gather_steps(b, group_view(whole_o, 0, 64), *sems[18:22], parts=BY_Y)
    next(outs)
    next(near)
    next(rounds)
    theirs = whole.at[1 - h, me_slot]
    remote(theirs, theirs, sems[8].at[1], sems[9].at[1], partner).wait_recv()
    far = gather_steps(b, view_of(1 - h), *sems[4:8], parts=TWO)
    next(far)
    ends = [0, UP_FIRST, 512]

    def tokens_done():
        everyone_wait(b, me, at, sems[10], sems[11], copies)
        for kind in range(3):
            for s in range(2):
                for pair in range(8):
                    j0, j1 = device_of(s, 2 * pair), device_of(s, 2 * pair + 1)
                    span = slice(kind * 32, kind * 32 + 32)
                    top, bottom = unpack_halves(land[j0, span], land[j1, span])
                    cols = slice(pair * 128, pair * 128 + 128)
                    joined[kind, s * 64 : s * 64 + 32, cols] = top
                    joined[kind, s * 64 + 32 : s * 64 + 64, cols] = bottom
        d_h1 = (
            lax.dot_general(joined[0], wq[...], NT, preferred_element_type=F32)
            + lax.dot_general(joined[1], wk[...], NT, preferred_element_type=F32)
            + lax.dot_general(joined[2], wv[...], NT, preferred_element_type=F32)
        )
        grad_in, grad_gain = norm_back_rows(tokens[...].astype(F32), gain[...], d_h1)
        dtokens[...] = dmid[...] + grad_in
        mine[...] = grad_gain.reshape(8, 128)
        sent = []
        for step, (j, peer) in enumerate(world_all(b)[1]):
            cp = remote(mine, crowd.at[me], sems[22].at[step], sems[23].at[step], peer)
            cp.start()
            sent.append(cp)
        crowd[me] = mine[...]
        return sent

    def up_done():
        trades[0].wait()
        for got, lo in ((got_u1, 0), (got_u2, 1)):
            for blk in range(4):
                at0, at1 = max(ends[lo], blk * 128), min(ends[lo + 1], blk * 128 + 128)
                if at0 < at1:
                    half[1, blk, at0 - blk * 128 : at1 - blk * 128] = (
                        near_u[at0:at1].astype(F32)
                        + got[at0 - ends[lo] : at1 - ends[lo]].astype(F32)
                    ).astype(BF)
        spread_out(1)

    def widen(n):
        for i, there in enumerate(around):
            ref = pieces.at[n, col_of(there)]
            remote(ref, ref, sems[14].at[3 * n + i], sems[15].at[3 * n + i], device(there)).wait_recv()
        for i in range(4):
            wide[n, :, i * 352 : i * 352 + 352] = pieces[n, i, :, 0:352]
            wide[n, :, (4 + i) * 352 : (4 + i) * 352 + 352] = pieces[n, i, :, 352:704]

    sent = []
    for n in range(7):
        if n % 2 == 0:
            next(tokens_back)
        next(near, None)
        next(outs)
        next(far)
        if n == 2:
            widen(0)
        if n == 3:
            next(rounds)
        if n == TOKENS_AT:
            sent = tokens_done()
        if n == UP_AT:
            up_done()
    next(outs)
    next(far)
    next(rounds)
    share.wait_send()
    result[...] = ((middle[...] + acc[eighth(b)].astype(F32)) * keep[...]).astype(BF)
    everyone_wait(b, me, lambda j: crowd.at[j], sems[22], sems[23], sent)
    gain_out[...] = jnp.sum(crowd[...], axis=0)
    widen(1)
    trades[1].wait()
    down[:DOWN_FIRST] = (near_d[:DOWN_FIRST].astype(F32) + got_d1[...].astype(F32)).astype(BF)
    down[DOWN_FIRST:] = (near_d[DOWN_FIRST:].astype(F32) + got_d2[...].astype(F32)).astype(BF)
    for cp in started:
        cp.wait_send()


def dense_body(whole, whole_o, grad_q, grad_k, grad_v, grad_o):
    sides = (whole[0].astype(F32), whole[1].astype(F32))
    spans = (
        (grad_q, ((0, 0, 64),)),
        (grad_k, ((0, 64, 96), (1, 0, 32))),
        (grad_v, ((1, 32, 96),)),
    )
    for out, parts in spans:
        pieces = []
        for head in range(2):
            for side, lo, hi in parts:
                pieces.append(sides[side][head, lo:hi])
        rows = jnp.concatenate(pieces, axis=0)
        for c in range(0, 1024, 128):
            out[c : c + 128, :] = rows[:, c : c + 128].T
    grad_o[...] = whole_o[...].reshape(128, 1024).astype(F32)


def distance_buckets():
    table = []
    for distance in range(2 * TILE):
        table.append(bucket_of(distance, 32, MAXDIST))
    return np.array(table, np.int32)


def on_device_fast(
    tokens,
    lengths,
    expert_index,
    cotangent,
    norm_attn,
    w_query,
    w_key,
    w_value,
    w_out,
    rel_bias,
    norm_ffn,
    router,
    w_gate,
    w_up,
    w_down,
):
    dma = pltpu.SemaphoreType.DMA
    b = spot()
    head = slot_of(b)
    col = col_of(b)
    device_at = lax.axis_index(("experts", "context"))
    positions = device_at * 64 + jnp.arange(64, dtype=jnp.int32)
    live = positions[None, :] < lengths[:, None]
    keep = live.reshape(128, 1).astype(F32)
    picks = jnp.where(live[:, :, None], expert_index, -1).astype(F32).reshape(128, 2).T
    picks = jnp.concatenate([picks, jnp.zeros((6, 128), F32)], axis=0)
    gain_attn = norm_attn.reshape(1, 1024)
    gain_ffn = norm_ffn.reshape(1, 1024)
    flat = tokens.reshape(128, 1024)
    cot = cotangent.reshape(128, 1024)

    buckets = distance_buckets()
    onehot = np.zeros((2 * TILE, 128), np.float32)
    onehot[np.arange(2 * TILE), buckets] = 1.0
    bias_t = jnp.pad(rel_bias.T, ((0, 0), (0, 96)))
    high = router.astype(BF)
    rest = router - high.astype(F32)
    mid = rest.astype(BF)
    lo = (rest - mid.astype(F32)).astype(BF)
    router3 = jnp.concatenate(
        [jnp.pad(r, ((0, 0), (0, 4))) for r in (high, mid, lo)] + [jnp.zeros((1024, 104), BF)], axis=1
    )
    router_t = jnp.pad(router.T, ((0, 4), (0, 0)))

    h1, picks_all, w3, wg, wu, dist = call(
        first_body,
        [
            shape((4, 2, 4, 64, 1024)),
            shape((16, 8, 128), F32),
            shape((1024, 384)),
            shape((1024, SHARE)),
            shape((1024, SHARE)),
            shape((8, 2 * TILE), F32),
        ],
        [VMEM((2, 64, 1024), BF), VMEM((3, 1024, 128), BF), VMEM((4, 1024, 512), BF)]
        + CUBE_SEMS
        + [dma(()), dma(()), dma((15,)), dma((15,)), dma((7,))],
        1,
        tokens,
        gain_attn,
        picks,
        w_query,
        w_key,
        w_value,
        w_gate[0],
        w_up[0],
        bias_t,
        jnp.asarray(onehot.T),
        anywhere=(3, 4, 5, 6, 7),
    )
    h1 = h1.reshape(2048, 1024)
    packed, out_t, qs, ks, vs, lse, dy0 = call(
        attend_body,
        [
            shape((32, 32, 128)),
            shape((64, 2048), F32),
            shape((2048, 128)),
            shape((2048, 128)),
            shape((2048, 128)),
            shape((8, 2048), F32),
            shape((16, 64, 1024)),
        ],
        [VMEM((2048, TILE), F32), VMEM((128, 2048), BF), VMEM((2048, TILE), BF)] + ONE_SEMS,
        2,
        lengths,
        h1,
        w3,
        dist,
        cot[:64],
        scalars=(0,),
    )
    middle, h2_all, gates_all, joined = call(
        middle_body,
        [
            shape((128, 1024), F32),
            shape((16, 128, 1024)),
            shape((16, 8, 128), F32),
            shape((128, 1024)),
        ],
        [VMEM((32, 32, 128), BF), VMEM((8, 128), F32)]
        + CUBE_SEMS
        + [dma((31,)), dma((31,)), dma((15,)), dma((15,))],
        3,
        packed,
        flat,
        w_out,
        gain_ffn,
        router3,
    )
    routed, dh2, dgates, near_g, near_u, near_d, far_g, far_u, far_d, got_d = call(
        expert_body,
        [
            shape((16, 128, 1024)),
            shape((16, 128, 1024)),
            shape((16, 8, 128), F32),
            shape((512, SHARE)),
            shape((512, SHARE)),
            shape((352, 1024)),
            shape((512, SHARE)),
            shape((512, SHARE)),
            shape((352, 1024)),
            shape((DOWN_FIRST, 1024)),
        ],
        [VMEM((16, 128, 1024), BF)]
        + [VMEM((1280, 1024), BF)] * 3
        + [VMEM((1280, 128), F32)]
        + [VMEM((1280, SHARE), BF)] * 3
        + [VMEM((1280, SHARE), F32)] * 2
        + [VMEM((1280, 1024), BF)] * 2
        + [VMEM((1280, 128), F32)]
        + [VMEM((SHARE, 1024), BF)]
        + [dma((5,))]
        + ONE_SEMS,
        4,
        h2_all,
        dy0,
        cot[64:],
        gates_all,
        picks_all,
        wg,
        wu,
        w_down[0],
        anywhere=(1, 7),
    )
    do_all, dmid, smalls, got_g, gwo = call(
        back_body,
        [
            shape((32, 32, 128)),
            shape((128, 1024), F32),
            shape((8, 1024), F32),
            shape((512, SHARE)),
            shape((16, 64, 1024)),
        ],
        [
            VMEM((8, 128, 1024), BF),
            VMEM((8, 128, 1024), BF),
            VMEM((16, 8, 128), F32),
            VMEM((32, 32, 128), BF),
        ]
        + CUBE_SEMS
        + [dma((31,)), dma((31,)), dma((15,)), dma((15,)), dma((2,)), dma((2,))],
        5,
        dh2,
        dgates,
        gates_all,
        cot,
        keep,
        middle,
        gain_ffn,
        router_t,
        h2_all,
        far_g,
        joined,
        w_out,
        anywhere=(9,),
        outs_anywhere=(3,),
    )
    packed_back, grads, table, wo, got_u = call(
        attend_back_body,
        [
            shape((32, 96, 128)),
            shape((2, 96, 1024)),
            shape((8, 512), F32),
            shape((64, 1024)),
            shape((UP_FIRST, SHARE)),
        ],
        [
            VMEM((2048, 128), BF),
            VMEM((128, 2048), BF),
            VMEM((8, 2048), F32),
            VMEM((2048, TILE), BF),
            VMEM((2048, TILE), BF),
            VMEM((128, 2048), F32),
            VMEM((2048, 128), F32),
            VMEM((2048, 128), F32),
            VMEM((TILE, TILE), F32),
            VMEM((TILE, TILE), F32),
            VMEM((192, 2048), BF),
            VMEM((8, 64, 1024), BF),
            VMEM((8, 64, 1024), BF),
        ]
        + CUBE_SEMS
        + [dma(()), dma(())],
        6,
        h1,
        do_all,
        qs,
        ks,
        vs,
        out_t,
        lse,
        dist,
        jnp.asarray(onehot),
        gwo,
        far_u,
        anywhere=(10,),
        outs_anywhere=(4,),
    )
    dtokens, result, whole, whole_o, smalls, gain_out, wide, down = call(
        last_body,
        [
            shape((128, 1024), F32),
            shape((128, 1024)),
            shape((2, 16, 96, 1024)),
            shape((16, 64, 1024)),
            shape((8, 1024), F32),
            shape((8, 128), F32),
            shape((2, 128, 2816)),
            shape((352, 1024)),
        ],
        [
            VMEM((32, 96, 128), BF),
            VMEM((96, 1024), BF),
            VMEM((64, 1024), BF),
            VMEM((3, 128, 1024), BF),
            VMEM((5, 8, 1024), F32),
            VMEM((32, 8, 128), F32),
            VMEM((8, 128), F32),
            VMEM((2, 4, 128, SHARE), BF),
            VMEM((2, 4, 128, SHARE), BF),
            VMEM((512 - UP_FIRST, SHARE), BF),
            VMEM((352 - DOWN_FIRST, 1024), BF),
            VMEM((8, 128, 1024), BF),
            VMEM((8, 128, 1024), BF),
        ]
        + CUBE_SEMS
        + CUBE_SEMS
        + [dma((3,)), dma((3,)), dma((31,)), dma((31,)), dma((5,)), dma((5,)), dma((6,)), dma((6,))]
        + [dma((2,)), dma((2,))]
        + ONE_SEMS
        + [dma((31,)), dma((31,))]
        + CUBE_SEMS,
        7,
        packed_back,
        grads,
        wo,
        flat,
        dmid,
        gain_attn,
        w_query,
        w_key,
        w_value,
        smalls,
        table,
        near_g.reshape(4, 128, SHARE),
        got_g.reshape(4, 128, SHARE),
        near_u,
        got_u,
        near_d,
        got_d,
        far_u,
        far_d,
        routed,
        middle,
        keep,
    )
    grad_q, grad_k, grad_v, grad_o = pl.pallas_call(
        dense_body,
        grid=(8,),
        out_shape=[shape((1024, 1024), F32)] * 4,
        in_specs=[
            pl.BlockSpec((2, 2, 96, 1024), lambda i: (0, i, 0, 0)),
            pl.BlockSpec((2, 64, 1024), lambda i: (i, 0, 0)),
        ],
        out_specs=[pl.BlockSpec((1024, 128), lambda i: (0, i))] * 3
        + [pl.BlockSpec((128, 1024), lambda i: (i, 0))],
        compiler_params=params(),
        cost_estimate=pl.CostEstimate(flops=0, bytes_accessed=25 * 2**20, transcendentals=0),
    )(whole, whole_o)
    return (
        result.reshape(2, 64, 1024),
        dtokens.reshape(2, 64, 1024),
        gain_out.reshape(1024),
        grad_q,
        grad_k,
        grad_v,
        grad_o,
        smalls[5, :512].reshape(16, 32).T,
        smalls[4],
        smalls[0:4].T,
        wide[0:1].astype(F32),
        wide[1:2].astype(F32),
        down[None].astype(F32),
    )


def solution(mesh):
    sizes = dict(mesh.shape)
    fits = sizes == {"experts": 4, "context": 8}
    placed = (
        P(None, ("experts", "context"), None),
        P(),
        P(None, ("experts", "context"), None),
        P(None, ("experts", "context"), None),
        P(),
        P(),
        P(),
        P(),
        P(),
        P(),
        P(),
        P(),
        P("experts", None, None),
        P("experts", None, None),
        P("experts", None, None),
    )
    return jax.shard_map(
        on_device_fast if fits else on_device,
        mesh=mesh,
        in_specs=placed,
        out_specs=(
            P(None, ("experts", "context"), None),
            P(None, ("experts", "context"), None),
            P(),
            P(),
            P(),
            P(),
            P(),
            P(),
            P(),
            P(),
            P("experts", "context", None),
            P("experts", "context", None),
            P("experts", "context", None),
        ),
        check_vma=False,
    )
```

```python
import math

import jax
import jax.numpy as jnp
import numpy as np
from jax import lax
from jax.experimental import pallas as pl
from jax.experimental.pallas import tpu as pltpu
from jax.sharding import PartitionSpec as P

MAXDIST = 128


norm_epsilon = 1e-06
mask_fill = -1e30
highest = lax.Precision.HIGHEST


def bucket_of(distance, bucket_count, reach):
    exact = bucket_count // 2
    if distance < exact:
        return distance
    level = exact + int(
        math.log(distance / exact) / math.log(reach / exact) * (bucket_count - exact)
    )
    return min(level, bucket_count - 1)


def bucket_edges(bucket_count, reach):
    edges = []
    for level in range(1, bucket_count):
        distance = 0
        while bucket_of(distance, bucket_count, reach) < level:
            distance += 1
        edges.append(distance)
    return edges


def relative_bucket(query_pos, key_pos, bucket_count):
    distance = jnp.maximum(query_pos[:, None] - key_pos[None, :], 0)
    bucket = jnp.zeros(distance.shape, jnp.int32)
    for edge in bucket_edges(bucket_count, MAXDIST):
        bucket = bucket + (distance >= edge).astype(jnp.int32)
    return bucket


def rms_norm(values, gain):
    inverse = lax.rsqrt(jnp.mean(values * values, axis=-1, keepdims=True) + norm_epsilon)
    return values * inverse * gain


def norm_back(values, gain, grad_in):
    inverse = lax.rsqrt(jnp.mean(values * values, axis=-1, keepdims=True) + norm_epsilon)
    normed = values * inverse
    grad_normed = grad_in * gain
    grad_values = inverse * (
        grad_normed - normed * jnp.mean(grad_normed * normed, axis=-1, keepdims=True)
    )
    return (grad_values, jnp.sum(grad_in * normed, 0))


def score_block(query_rows, key_rows, rel_bias, query_pos, key_pos, lengths, score_scale):
    raw_scores = (
        jnp.einsum("sqhd,skhd->sqhk", query_rows, key_rows, preferred_element_type=jnp.float32)
        * score_scale
    )
    bucket = relative_bucket(query_pos, key_pos, rel_bias.shape[0])
    onehot = (bucket[:, :, None] == jnp.arange(rel_bias.shape[0], dtype=jnp.int32)).astype(
        jnp.float32
    )
    bias_rows = jnp.einsum("qkb,bh->qhk", onehot, rel_bias, precision=highest)
    causal = (key_pos[None, :] <= query_pos[:, None])[None]
    inside = key_pos[None, None, :] < lengths[:, None, None]
    allowed = (causal & inside)[:, :, None, :]
    return (raw_scores + bias_rows[None], allowed, onehot)


def pair_grads(query_set, key_set, rel_bias, lengths, score_scale):
    query_rows, grad_rows, log_total, delta, query_pos = query_set
    key_rows, value_rows, key_pos = key_set
    scores, allowed, onehot = score_block(
        query_rows, key_rows, rel_bias, query_pos, key_pos, lengths, score_scale
    )
    weights = jnp.where(allowed, jnp.exp(scores - log_total[..., None]), 0.0)
    grad_value = jnp.einsum(
        "sqhk,sqhd->skhd",
        weights.astype(jnp.bfloat16),
        grad_rows,
        preferred_element_type=jnp.float32,
    )
    grad_weights = jnp.einsum(
        "sqhd,skhd->sqhk", grad_rows, value_rows, preferred_element_type=jnp.float32
    )
    grad_scores = (weights * (grad_weights - delta[..., None])).astype(jnp.bfloat16)
    grad_query = score_scale * jnp.einsum(
        "sqhk,skhd->sqhd", grad_scores, key_rows, preferred_element_type=jnp.float32
    )
    grad_key = score_scale * jnp.einsum(
        "sqhk,sqhd->skhd", grad_scores, query_rows, preferred_element_type=jnp.float32
    )
    grad_table = jnp.einsum(
        "sqhk,qkb->bh", grad_scores, onehot.astype(jnp.bfloat16), preferred_element_type=jnp.float32
    )
    return (grad_query, grad_key, grad_value, grad_table)


def dispatch_table(expert_index, live_rows, expert_count, capacity):
    picked = expert_index.reshape(-1)
    live_pairs = jnp.broadcast_to(live_rows[:, :, None], expert_index.shape).reshape(-1)
    chosen = (
        (picked[:, None] == jnp.arange(expert_count, dtype=jnp.int32)[None, :])
        & live_pairs[:, None]
    ).astype(jnp.int32)
    earlier = jnp.cumsum(chosen, axis=0) - chosen
    position_in = jnp.sum(earlier * chosen, -1)
    kept_pairs = live_pairs & (position_in < capacity)
    slot_of = jnp.where(kept_pairs, picked * capacity + position_in, -1)
    matches = slot_of[None, :] == jnp.arange(expert_count * capacity, dtype=jnp.int32)[:, None]
    table = jnp.any(matches.reshape(expert_count * capacity, -1, 2), -1).astype(jnp.float32)
    slot_ids = jnp.arange(expert_count * capacity, dtype=jnp.int32) // capacity
    slot_expert = (slot_ids[:, None] == jnp.arange(expert_count, dtype=jnp.int32)[None, :]).astype(
        jnp.float32
    )
    return (table, slot_expert)


def on_device(
    tokens,
    lengths,
    expert_index,
    cotangent,
    norm_attn,
    w_query,
    w_key,
    w_value,
    w_out,
    rel_bias,
    norm_ffn,
    router,
    w_gate,
    w_up,
    w_down,
):
    slot_count, per_slot, model_width = tokens.shape
    head_count = rel_bias.shape[1]
    head_size = model_width // head_count
    expert_count = router.shape[1]
    capacity = (10 * slot_count * per_slot + 4 * expert_count - 1) // (4 * expert_count)
    score_scale = head_size ** (-0.5)
    row_count = slot_count * per_slot
    shape_four = (slot_count, per_slot, head_count, head_size)
    shape_three = (slot_count, per_slot, model_width)
    device_at = lax.axis_index(("experts", "context"))
    positions = device_at * per_slot + jnp.arange(per_slot, dtype=jnp.int32)
    live_rows = positions[None, :] < lengths[:, None]
    keep_mask = live_rows.reshape(row_count, 1).astype(jnp.float32)
    inputs = tokens.reshape(row_count, model_width).astype(jnp.float32)
    normed = rms_norm(inputs, norm_attn).astype(jnp.bfloat16)
    query_flat = jnp.dot(normed, w_query, preferred_element_type=jnp.float32).astype(jnp.bfloat16)
    key_flat = jnp.dot(normed, w_key, preferred_element_type=jnp.float32).astype(jnp.bfloat16)
    value_flat = jnp.dot(normed, w_value, preferred_element_type=jnp.float32).astype(jnp.bfloat16)
    query_four = query_flat.reshape(shape_four)
    key_four = key_flat.reshape(shape_four)
    value_four = value_flat.reshape(shape_four)
    key_three = key_flat.reshape(shape_three)
    value_three = value_flat.reshape(shape_three)
    start_state = (
        jnp.zeros(shape_four, jnp.float32),
        jnp.full((slot_count, per_slot, head_count), mask_fill, jnp.float32),
        jnp.zeros((slot_count, per_slot, head_count), jnp.float32),
    )
    offset = jnp.int32(0)
    key_all = lax.all_gather(key_three, ("experts", "context"), axis=1, tiled=True)
    value_all = lax.all_gather(value_three, ("experts", "context"), axis=1, tiled=True)
    piece_rows = key_all.shape[1]
    block_rows = math.gcd(piece_rows, 8 * per_slot)

    def forward_visit(carried, block_id):
        running, running_max, denominator = carried
        local_at = block_id * block_rows
        key_rows = lax.dynamic_slice_in_dim(key_all, local_at, block_rows, 1).reshape(
            slot_count, block_rows, head_count, head_size
        )
        value_rows = lax.dynamic_slice_in_dim(value_all, local_at, block_rows, 1).reshape(
            slot_count, block_rows, head_count, head_size
        )
        key_pos = offset + local_at + jnp.arange(block_rows, dtype=jnp.int32)
        scores, allowed, _ = score_block(
            query_four, key_rows, rel_bias, positions, key_pos, lengths, score_scale
        )
        scores = jnp.where(allowed, scores, mask_fill)
        new_max = jnp.maximum(running_max, jnp.max(scores, -1))
        factor = jnp.exp(running_max - new_max)
        weights = jnp.where(allowed, jnp.exp(scores - new_max[..., None]), 0.0)
        denominator = denominator * factor + jnp.sum(weights, -1)
        running = running * factor[..., None] + jnp.einsum(
            "sqhk,skhd->sqhd",
            weights.astype(jnp.bfloat16),
            value_rows,
            preferred_element_type=jnp.float32,
        )
        return ((running, new_max, denominator), None)

    carried, _ = lax.scan(
        forward_visit, start_state, jnp.arange(piece_rows // block_rows, dtype=jnp.int32)
    )
    running, running_max, denominator = carried
    attended = running / denominator[..., None]
    log_total = running_max + jnp.log(denominator)
    attended_low = attended.reshape(row_count, model_width).astype(jnp.bfloat16)
    middle = inputs + jnp.dot(attended_low, w_out, preferred_element_type=jnp.float32)
    second_low = rms_norm(middle, norm_ffn).astype(jnp.bfloat16)
    second_wide = second_low.astype(jnp.float32)
    logits = jnp.dot(second_wide, router, precision=highest)
    gates = jax.nn.softmax(logits, axis=-1)
    table, slot_expert = dispatch_table(expert_index, live_rows, expert_count, capacity)
    table_low = table.astype(jnp.bfloat16)
    dispatched = jnp.dot(table_low, second_low, preferred_element_type=jnp.float32).astype(
        jnp.bfloat16
    )
    arrived = lax.all_to_all(
        dispatched.reshape(expert_count, capacity, model_width),
        "experts",
        split_axis=0,
        concat_axis=1,
        tiled=True,
    )[0]
    gate_pre = jnp.dot(arrived, w_gate[0], preferred_element_type=jnp.float32)
    up_pre = jnp.dot(arrived, w_up[0], preferred_element_type=jnp.float32)
    hidden_low = (jax.nn.gelu(gate_pre, approximate=True) * up_pre).astype(jnp.bfloat16)
    produced = jnp.dot(hidden_low, w_down[0], preferred_element_type=jnp.float32).astype(
        jnp.bfloat16
    )
    returned = lax.all_to_all(
        produced[None], "experts", split_axis=1, concat_axis=0, tiled=True
    ).reshape(expert_count * capacity, model_width)
    returned_wide = returned.astype(jnp.float32)
    slot_weight = jnp.sum(jnp.dot(table, gates, precision=highest) * slot_expert, -1)
    routed = jnp.dot(table.T, slot_weight[:, None] * returned_wide, precision=highest)
    result = ((middle + routed) * keep_mask).astype(jnp.bfloat16).reshape(shape_three)
    grad_result = cotangent.reshape(row_count, model_width).astype(jnp.float32) * keep_mask
    gathered_grad = jnp.dot(table, grad_result, precision=highest)
    grad_produced = (
        (slot_weight[:, None] * gathered_grad)
        .astype(jnp.bfloat16)
        .reshape(expert_count, capacity, model_width)
    )
    grad_arrived_out = lax.all_to_all(
        grad_produced, "experts", split_axis=0, concat_axis=1, tiled=True
    )[0]
    grad_slot_weight = jnp.sum(gathered_grad * returned_wide, -1)
    grad_hidden = jnp.dot(grad_arrived_out, w_down[0].T, preferred_element_type=jnp.float32)
    grad_w_down = jnp.dot(hidden_low.T, grad_arrived_out, preferred_element_type=jnp.float32)

    def activation(gate_in, up_in):
        return jax.nn.gelu(gate_in, approximate=True) * up_in

    _, activation_back = jax.vjp(activation, gate_pre, up_pre)
    grad_gate_pre, grad_up_pre = activation_back(grad_hidden)
    grad_gate_low = grad_gate_pre.astype(jnp.bfloat16)
    grad_up_low = grad_up_pre.astype(jnp.bfloat16)
    grad_w_gate = jnp.dot(arrived.T, grad_gate_low, preferred_element_type=jnp.float32)
    grad_w_up = jnp.dot(arrived.T, grad_up_low, preferred_element_type=jnp.float32)
    grad_arrived = (
        jnp.dot(grad_gate_low, w_gate[0].T, preferred_element_type=jnp.float32)
        + jnp.dot(grad_up_low, w_up[0].T, preferred_element_type=jnp.float32)
    ).astype(jnp.bfloat16)
    grad_returned = lax.all_to_all(
        grad_arrived[None], "experts", split_axis=1, concat_axis=0, tiled=True
    ).reshape(expert_count * capacity, model_width)
    expert_sums = (
        lax.psum_scatter(
            grad_w_gate[None].astype(jnp.bfloat16), "context", scatter_dimension=1, tiled=True
        ).astype(jnp.float32),
        lax.psum_scatter(
            grad_w_up[None].astype(jnp.bfloat16), "context", scatter_dimension=1, tiled=True
        ).astype(jnp.float32),
        lax.psum_scatter(
            grad_w_down[None].astype(jnp.bfloat16), "context", scatter_dimension=1, tiled=True
        ).astype(jnp.float32),
    )
    grad_second = jnp.dot(table_low.T, grad_returned, preferred_element_type=jnp.float32)
    grad_gates = jnp.dot(table.T, grad_slot_weight[:, None] * slot_expert, precision=highest)
    grad_logits = gates * (grad_gates - jnp.sum(gates * grad_gates, -1, keepdims=True))
    grad_router = jnp.dot(second_wide.T, grad_logits, precision=highest)
    grad_second = grad_second + jnp.dot(grad_logits, router.T, precision=highest)
    grad_middle_norm, grad_norm_ffn = norm_back(middle, norm_ffn, grad_second)
    grad_middle = grad_result + grad_middle_norm
    grad_middle_low = grad_middle.astype(jnp.bfloat16)
    grad_w_out = jnp.dot(attended_low.T, grad_middle_low, preferred_element_type=jnp.float32)
    grad_attended_low = jnp.dot(
        grad_middle_low, w_out.T, preferred_element_type=jnp.float32
    ).astype(jnp.bfloat16)
    grad_attended_four = grad_attended_low.reshape(shape_four)
    grad_attended_three = grad_attended_low.reshape(shape_three)
    delta = jnp.sum(grad_attended_four.astype(jnp.float32) * attended, -1)
    local_queries = (query_four, grad_attended_four, log_total, delta, positions)
    grad_start = (jnp.zeros(shape_four, jnp.float32), jnp.zeros(rel_bias.shape, jnp.float32))
    query_offset = jnp.int32(0)
    query_key_all = lax.all_gather(key_three, ("experts", "context"), axis=1, tiled=True)
    query_value_all = lax.all_gather(value_three, ("experts", "context"), axis=1, tiled=True)
    piece_rows = query_key_all.shape[1]
    query_block_rows = math.gcd(piece_rows, 8 * per_slot)

    def query_visit(carried, block_id):
        local_at = block_id * query_block_rows
        key_rows = lax.dynamic_slice_in_dim(query_key_all, local_at, query_block_rows, 1).reshape(
            slot_count, query_block_rows, head_count, head_size
        )
        value_rows = lax.dynamic_slice_in_dim(
            query_value_all, local_at, query_block_rows, 1
        ).reshape(slot_count, query_block_rows, head_count, head_size)
        key_pos = query_offset + local_at + jnp.arange(query_block_rows, dtype=jnp.int32)
        grad_query, _, _, grad_table = pair_grads(
            local_queries, (key_rows, value_rows, key_pos), rel_bias, lengths, score_scale
        )
        return ((carried[0] + grad_query, carried[1] + grad_table), None)

    carried, _ = lax.scan(
        query_visit, grad_start, jnp.arange(piece_rows // query_block_rows, dtype=jnp.int32)
    )
    grad_query_four, grad_table = carried
    log_whole, delta_whole = (
        lax.all_gather(log_total, ("experts", "context"), axis=1, tiled=True),
        lax.all_gather(delta, ("experts", "context"), axis=1, tiled=True),
    )
    local_keys = (key_four, value_four, positions)
    zero_four = jnp.zeros(shape_four, jnp.float32)
    key_offset = jnp.int32(0)
    query_all = lax.all_gather(
        query_flat.reshape(shape_three), ("experts", "context"), axis=1, tiled=True
    )
    grad_all = lax.all_gather(grad_attended_three, ("experts", "context"), axis=1, tiled=True)
    piece_rows = query_all.shape[1]
    key_block_rows = math.gcd(piece_rows, 8 * per_slot)

    def key_visit(carried, block_id):
        local_at = block_id * key_block_rows
        whole_at = key_offset + local_at
        query_rows = lax.dynamic_slice_in_dim(query_all, local_at, key_block_rows, 1).reshape(
            slot_count, key_block_rows, head_count, head_size
        )
        grad_rows = lax.dynamic_slice_in_dim(grad_all, local_at, key_block_rows, 1).reshape(
            slot_count, key_block_rows, head_count, head_size
        )
        log_rows = lax.dynamic_slice_in_dim(log_whole, whole_at, key_block_rows, 1)
        delta_rows = lax.dynamic_slice_in_dim(delta_whole, whole_at, key_block_rows, 1)
        query_pos = whole_at + jnp.arange(key_block_rows, dtype=jnp.int32)
        _, grad_key, grad_value, _ = pair_grads(
            (query_rows, grad_rows, log_rows, delta_rows, query_pos),
            local_keys,
            rel_bias,
            lengths,
            score_scale,
        )
        return ((carried[0] + grad_key, carried[1] + grad_value), None)

    carried, _ = lax.scan(
        key_visit, (zero_four, zero_four), jnp.arange(piece_rows // key_block_rows, dtype=jnp.int32)
    )
    grad_key_four, grad_value_four = carried
    grad_query_low = grad_query_four.reshape(row_count, model_width).astype(jnp.bfloat16)
    grad_key_low = grad_key_four.reshape(row_count, model_width).astype(jnp.bfloat16)
    grad_value_low = grad_value_four.reshape(row_count, model_width).astype(jnp.bfloat16)
    grad_w_query = jnp.dot(normed.T, grad_query_low, preferred_element_type=jnp.float32)
    grad_w_key = jnp.dot(normed.T, grad_key_low, preferred_element_type=jnp.float32)
    grad_w_value = jnp.dot(normed.T, grad_value_low, preferred_element_type=jnp.float32)
    grad_normed = (
        jnp.dot(grad_query_low, w_query.T, preferred_element_type=jnp.float32)
        + jnp.dot(grad_key_low, w_key.T, preferred_element_type=jnp.float32)
        + jnp.dot(grad_value_low, w_value.T, preferred_element_type=jnp.float32)
    )
    grad_input_norm, grad_norm_attn = norm_back(inputs, norm_attn, grad_normed)
    grad_tokens = (grad_middle + grad_input_norm).reshape(shape_three)
    dense = lax.psum(
        (
            grad_norm_attn,
            grad_w_query,
            grad_w_key,
            grad_w_value,
            grad_w_out,
            grad_table,
            grad_norm_ffn,
            grad_router,
        ),
        ("experts", "context"),
    )
    return (
        result,
        grad_tokens,
        dense[0],
        dense[1],
        dense[2],
        dense[3],
        dense[4],
        dense[5],
        dense[6],
        dense[7],
        expert_sums[0],
        expert_sums[1],
        expert_sums[2],
    )


MESH = pl.DeviceIdType.MESH
BF = jnp.bfloat16
F32 = jnp.float32
VMEM = pltpu.VMEM
THREE = (
    (("x", "y", "l"), 0, 384),
    (("y", "l", "x"), 384, 384),
    (("l", "x", "y"), 768, 256),
)
TWO = ((("l", "x", "y"), 0, 512), (("l", "y", "x"), 512, 512))
LATE = ((("x", "y", "l"), 0, 512), (("y", "x", "l"), 512, 512))
BY_Y = ((("l", "x", "y"), 0, 1024),)
BY_X = ((("l", "y", "x"), 0, 1024),)
BIG = -1e30
TILE = 256
PLACES = 80
SHARE = 704
GATE_FIRST = 384
UP_FIRST = 256
DOWN_FIRST = 224
TOKENS_AT = 3
UP_AT = 4
NT = (((1,), (1,)), ((), ()))
TN = (((0,), (0,)), ((), ()))
CUBE_SEMS = [pltpu.SemaphoreType.DMA((3, 8))] * 4
TWO_SEMS = [pltpu.SemaphoreType.DMA((2, 8))] * 4
ONE_SEMS = [pltpu.SemaphoreType.DMA((1, 8))] * 4


def spot():
    e = lax.axis_index("experts")
    c = lax.axis_index("context")
    return dict(k=lax.rem(e, 2), y=e // 2, x=lax.rem(c, 2), l=lax.rem(c // 2, 2), h=c // 4)


def flip(b, names):
    return {n: (1 - v if n in names else v) for n, v in b.items()}


def device(b):
    return {"experts": b["y"] * 2 + b["k"], "context": b["h"] * 4 + b["l"] * 2 + b["x"]}


def row_of(b):
    return b["y"] * 2 + b["k"]


def col_of(b):
    return b["l"] * 2 + b["x"]


def slot_of(b):
    return row_of(b) * 4 + col_of(b)


def greet_start(peers):
    barrier = pltpu.get_barrier_semaphore()
    for peer in peers:
        pl.semaphore_signal(barrier, inc=1, device_id=peer, device_id_type=MESH)


def greet_end(count):
    pl.semaphore_wait(pltpu.get_barrier_semaphore(), count)


def greet(peers):
    greet_start(peers)
    greet_end(len(peers))


def cube_peers(b):
    return [device(flip(b, [n])) for n in ("x", "y", "l", "k")]


def cube_all(b):
    peers = []
    for step in range(1, 16):
        s = lax.rem(slot_of(b) + step, 16)
        peers.append({"experts": s // 4, "context": b["h"] * 4 + lax.rem(s, 4)})
    return peers


def world_all(b):
    me = row_of(b) * 8 + b["h"] * 4 + col_of(b)
    peers = []
    for step in range(1, 32):
        j = lax.rem(me + step, 32)
        peers.append((j, {"experts": j // 8, "context": lax.rem(j, 8)}))
    return me, peers


def remote(src, dst, ssem, rsem, peer):
    return pltpu.make_async_remote_copy(
        src_ref=src, dst_ref=dst, send_sem=ssem, recv_sem=rsem, device_id=peer, device_id_type=MESH
    )


def names_of(order, t):
    return [order[i] for i in range(3) if (t >> i) & 1]


def gather_steps(b, view, ss, rs, cs, cr, parts=THREE):
    started = []
    core = device(flip(b, ["k"]))
    every = range(len(parts))

    def piece(p, t, more=()):
        order, c0, cn = parts[p]
        return view(flip(b, names_of(order, t) + list(more)), c0, cn)

    def link(p, t, i):
        ref = piece(p, t)
        n = t | (1 << i)
        cp = remote(ref, ref, ss.at[p, n], rs.at[p, n], device(flip(b, [parts[p][0][i]])))
        cp.start()
        started.append(cp)

    def across(p, t):
        ref = piece(p, t)
        cp = remote(ref, ref, cs.at[p, t], cr.at[p, t], core)
        cp.start()
        started.append(cp)

    for i in range(3):
        for p in every:
            link(p, 0, i)
    for p in every:
        across(p, 0)
    yield
    for t in range(1, 8):
        for p in every:
            ref = piece(p, t)
            remote(ref, ref, ss.at[p, t], rs.at[p, t], core).wait_recv()
            for i in range(t.bit_length(), 3):
                link(p, t, i)
            across(p, t)
        yield
    for cp in started:
        cp.wait_send()
    for p in every:
        for t in range(8):
            ref = piece(p, t, ["k"])
            remote(ref, ref, cs.at[p, t], cr.at[p, t], core).wait_recv()
    yield


def gather_cube(*args):
    for _ in gather_steps(*args):
        pass


def eighth(b):
    return b["y"] * 4 + b["l"] * 2 + b["x"]


def scatter_steps(b, parts, acc, landing, ss, rs, cs, cr, cuts=THREE):
    started = []
    core = device(flip(b, ["k"]))
    dims = ("x", "y", "l")
    order = sorted(range(8), key=lambda t: -bin(t).count("1"))

    def set_of(t):
        return [n for i, n in enumerate(dims) if (t >> i) & 1]

    def push(p, step, others_set):
        dims_in_order, c0, cn = cuts[p]
        first = dims_in_order[step]
        others = dims_in_order[step + 1 :]
        there = flip(b, [first] + others_set)
        n = (1 << len(others)) + sum(1 << i for i, name in enumerate(others) if name in others_set)
        cp = remote(
            acc.at[eighth(there), :, pl.ds(c0, cn)],
            landing.at[n, :, pl.ds(c0, cn)],
            ss.at[p, n],
            rs.at[p, n],
            device(flip(b, [first])),
        )
        cp.start()
        started.append(cp)

    for t in order:
        there = flip(b, set_of(t) + ["k"])
        cp = remote(parts.at[slot_of(there)], acc.at[eighth(there)], cs.at[0, t], cr.at[0, t], core)
        cp.start()
        started.append(cp)
    yield
    for t in order:
        here = flip(b, set_of(t))
        n = eighth(here)
        remote(parts.at[slot_of(here)], acc.at[n], cs.at[0, t], cr.at[0, t], core).wait_recv()
        acc[n] = (acc[n].astype(F32) + parts[slot_of(here)].astype(F32)).astype(BF)
        for p in range(len(cuts)):
            first = cuts[p][0][0]
            if first in set_of(t):
                push(p, 0, [name for name in set_of(t) if name != first])
    yield
    for step in range(3):
        rest = 2 - step
        count = 1 << rest
        for t in range(count - 1, -1, -1):
            for p in range(len(cuts)):
                dims_in_order, c0, cn = cuts[p]
                others = dims_in_order[step + 1 :]
                names = [others[i] for i in range(rest) if (t >> i) & 1]
                target = eighth(flip(b, names))
                n = count + t
                ref = landing.at[n, :, pl.ds(c0, cn)]
                remote(ref, ref, ss.at[p, n], rs.at[p, n], core).wait_recv()
                acc[target, :, c0 : c0 + cn] = (
                    acc[target, :, c0 : c0 + cn].astype(F32)
                    + landing[n, :, c0 : c0 + cn].astype(F32)
                ).astype(BF)
                if rest and others[0] in names:
                    push(p, step + 1, [name for name in names if name != others[0]])
        yield
    for cp in started:
        cp.wait_send()
    yield


def scatter_cube(*args):
    for _ in scatter_steps(*args):
        pass


def params(cid=None, mib=60):
    if cid is None:
        return pltpu.CompilerParams(vmem_limit_bytes=mib * 2**20)
    return pltpu.CompilerParams(
        collective_id=cid, has_side_effects=True, vmem_limit_bytes=mib * 2**20
    )


def call(body, outs, scratch, cid, *args, anywhere=(), outs_anywhere=(), scalars=()):
    def spec(i, listed):
        if i in listed:
            return pl.BlockSpec(memory_space=pl.ANY)
        return pl.BlockSpec(memory_space=VMEM)

    return pl.pallas_call(
        body,
        out_shape=outs,
        in_specs=[
            pl.BlockSpec(memory_space=pltpu.SMEM) if i in scalars else spec(i, anywhere)
            for i in range(len(args))
        ],
        out_specs=[spec(i, outs_anywhere) for i in range(len(outs))],
        scratch_shapes=scratch,
        compiler_params=params(cid),
    )(*args)


def shape(dims, kind=BF):
    return jax.ShapeDtypeStruct(dims, kind)


def sequence_steps(b, whole, staged, sems, hs, hr):
    partner = device(flip(b, ["h"]))
    mine = whole.at[row_of(b), b["h"], col_of(b)]
    cp = remote(staged.at[1 - b["h"]], mine, hs, hr, partner)
    cp.start()
    whole[row_of(b), b["h"], col_of(b)] = staged[b["h"]]
    yield
    theirs = whole.at[row_of(b), 1 - b["h"], col_of(b)]
    remote(theirs, theirs, hs, hr, partner).wait_recv()

    def view(v, c0, cn):
        return whole.at[row_of(v), :, col_of(v), :, pl.ds(c0, cn)]

    for _ in gather_steps(b, view, *sems):
        yield
    cp.wait_send()
    yield


def group_view(ref, r0=0, rn=128):
    def view(v, c0, cn):
        return ref.at[slot_of(v), pl.ds(r0, rn), pl.ds(c0, cn)]

    return view


def send_small(b, src, into, ss, rs):
    copies = []
    for step, peer in enumerate(cube_all(b)):
        cp = remote(src, into.at[slot_of(b)], ss.at[step], rs.at[step], peer)
        cp.start()
        copies.append(cp)
    return copies


def wait_small(b, into, ss, rs, copies):
    me = slot_of(b)
    for step in range(15):
        came = into.at[lax.rem(me + 15 - step, 16)]
        remote(came, came, ss.at[step], rs.at[step], device(b)).wait_recv()
    for cp in copies:
        cp.wait_send()


def inverse_rms(values):
    return lax.rsqrt(jnp.mean(values * values, axis=-1, keepdims=True) + norm_epsilon)


def first_body(
    tokens, gain, picks, w_query, w_key, w_value, w_gate, w_up, bias_t, onehot_t, h1, picks_all, w3, wg, wu, dist, staged, heads, wide, *sems
):
    b = spot()
    head = slot_of(b)
    loads = []
    for n, w in enumerate((w_query, w_key, w_value)):
        at = pl.multiple_of((head // 2) * 128, 128)
        loads.append(pltpu.make_async_copy(w.at[:, pl.ds(at, 128)], heads.at[n], sems[8].at[n]))
    offsets = []
    for n, w in enumerate((w_gate, w_gate, w_up, w_up)):
        share = 4 * (n % 2) + col_of(b)
        block = (share * 352) // 128 - share // 7
        offsets.append(share * 352 - block * 128)
        at = pl.multiple_of(block * 128, 128)
        loads.append(
            pltpu.make_async_copy(w.at[:, pl.ds(at, 512)], wide.at[n], sems[8].at[3 + n])
        )
    for cp in loads:
        cp.start()
    for s in range(2):
        rows = tokens[s].astype(F32)
        staged[s] = (rows * inverse_rms(rows) * gain[...]).astype(BF)
    greet([device(flip(b, ["h"]))] + cube_all(b))
    steps = sequence_steps(b, h1, staged, sems[0:4], sems[4], sems[5])
    next(steps)
    copies = send_small(b, picks, picks_all, sems[6], sems[7])
    picks_all[slot_of(b)] = picks[...]
    row = jnp.broadcast_to(bias_t[pl.ds(head, 1)], (8, 128))
    row = row - row[:, 31:32]
    dist[...] = jnp.dot(row, onehot_t[...], precision=highest)
    for cp in loads:
        cp.wait()
    next(steps)
    left = lane((1024, 128)) < 64
    for n in range(3):
        turned = pltpu.roll(heads[n].astype(F32), lax.rem(head, 2) * 64, 1)
        w3[:, n * 128 : n * 128 + 128] = jnp.where(left, turned, 0.0).astype(BF)
        next(steps)
    for n in range(4):
        out = wg if n < 2 else wu
        for r in range(0, 1024, 256):
            turned = pltpu.roll(wide[n, r : r + 256].astype(F32), 512 - offsets[n], 1)
            at = (n % 2) * 352
            out[r : r + 256, at : at + 352] = turned[:, :352].astype(BF)
        next(steps)
    for _ in range(3):
        next(steps, None)
    wait_small(b, picks_all, sems[6], sems[7], copies)


def lane(shape_, dim=1):
    return lax.broadcasted_iota(jnp.int32, shape_, dim)


def near_tiles(row):
    wide = jnp.broadcast_to(row, (TILE, 2 * TILE))
    wide = pltpu.roll(wide, 0, 1, stride=1, stride_axis=0)
    later = lax.broadcasted_iota(jnp.int32, (TILE, TILE), 0) > lane((TILE, TILE))
    return [jnp.where(later, BIG, wide[:, :TILE]), wide[:, TILE:]]


def pack_halves(rows):
    n = rows.shape[0] // 64
    four = rows.reshape(n, 2, 32, 128)
    return jnp.where(
        lax.broadcasted_iota(jnp.int32, (n, 32, 128), 2) < 64,
        four[:, 0],
        pltpu.roll(four[:, 1].reshape(n * 32, 128), 64, 1).reshape(n, 32, 128),
    )


def device_of(s, head):
    return (head // 4) * 8 + s * 4 + head % 4


def unpack_halves(first, second):
    a = first.astype(F32)
    c = second.astype(F32)
    left = lane((32, 128)) < 64
    top = jnp.where(left, a, pltpu.roll(c, 64, 1))
    bottom = jnp.where(left, pltpu.roll(a, 64, 1), c)
    return top.astype(BF), bottom.astype(BF)


def everyone(b, src, dst_at, ss, rs):
    me, peers = world_all(b)
    copies = []
    for step, (j, peer) in enumerate(peers):
        cp = remote(src.at[j], dst_at(me), ss.at[step], rs.at[step], peer)
        cp.start()
        copies.append(cp)
    return me, copies


def everyone_wait(b, me, dst_at, ss, rs, copies):
    for step in range(31):
        came = dst_at(lax.rem(me + 31 - step, 32))
        remote(came, came, ss.at[step], rs.at[step], device(b)).wait_recv()
    for cp in copies:
        cp.wait_send()


def attend_body(
    length, h1, w3, dist, cot, tokens, w_out, gain, router3, out_t, qs, ks, vs, lse, dy, middle, h2_all, gates_all, joined, strip, v_t, weights, packed, land, gates, w_buf, load, *sems
):
    b = spot()
    me, peers = world_all(b)
    greet_start([peer for _, peer in peers])
    fetch = pltpu.make_async_copy(w_out, w_buf, load)
    fetch.start()
    dy[slot_of(b)] = cot[...]
    limit = length[b["h"]]
    for i in range(8):
        rows = slice(i * TILE, (i + 1) * TILE)
        p = jnp.dot(h1[rows], w3[...], preferred_element_type=F32)
        spot_lane = lane((TILE, 128))
        where_at = lax.broadcasted_iota(jnp.int32, (TILE, 128), 0) + i * TILE
        one = spot_lane == 64
        qs[rows] = jnp.where(one, 1.0, p[:, :128] * 0.125).astype(BF)
        ks[rows] = jnp.where(one & (where_at >= limit), BIG, p[:, 128:256]).astype(BF)
        v = jnp.where(one, 1.0, p[:, 256:]).astype(BF)
        vs[rows] = v
        v_t[:, rows] = v.astype(F32).T.astype(BF)
        if i == 3:
            greet_end(31)
            steps = gather_steps(b, group_view(dy, 0, 64), *sems[4:8], parts=TWO)
            next(steps)
    next(steps)
    near = near_tiles(dist[0:1])
    for i in range(8):
        cols = slice(i * TILE, (i + 1) * TILE)
        q = qs[cols]
        top = None
        for j in range(i + 1):
            rows = slice(j * TILE, (j + 1) * TILE)
            s = lax.dot_general(ks[rows], q, NT, preferred_element_type=F32)
            if i - j < 2:
                s = s + near[i - j]
            strip[rows] = s
            m = jnp.max(s, axis=0, keepdims=True)
            top = m if top is None else jnp.maximum(top, m)
        for j in range(i + 1):
            rows = slice(j * TILE, (j + 1) * TILE)
            weights[rows] = jnp.exp(strip[rows] - top).astype(BF)
        n = (i + 1) * TILE
        o = jnp.dot(v_t[:, :n], weights[:n], preferred_element_type=F32)
        total = o[64:65]
        o = o / total
        lse[:, cols] = jnp.broadcast_to(top + jnp.log(total), (8, TILE))
        out_t[:, cols] = o[:64]
        packed[4 * i : 4 * i + 4] = pack_halves(o.T).astype(BF)
        for j in range(4 * i, 4 * i + 4):

            @pl.when(me != j)
            def _(j=j):
                peer = {"experts": j // 8, "context": j % 8}
                remote(packed.at[j], land.at[me], sems[8].at[j], sems[9].at[me], peer).start()

        for _ in range((0, 0, 1, 1, 1, 1, 2, 1)[i]):
            next(steps)
    land[me] = packed[me]
    fetch.wait()
    for j in range(32):

        @pl.when(me != j)
        def _(j=j):
            peer = {"experts": j // 8, "context": j % 8}
            remote(packed.at[j], land.at[j], sems[8].at[j], sems[9].at[j], peer).wait()

    for s in range(2):
        for pair in range(8):
            top, bottom = unpack_halves(
                land[device_of(s, 2 * pair)], land[device_of(s, 2 * pair + 1)]
            )
            cols = slice(pair * 128, pair * 128 + 128)
            joined[s * 64 : s * 64 + 32, cols] = top
            joined[s * 64 + 32 : s * 64 + 64, cols] = bottom
    x = tokens[...].astype(F32)
    mid = x + jnp.dot(joined[...], w_buf[...], preferred_element_type=F32)
    h2 = (mid * inverse_rms(mid) * gain[...]).astype(BF)
    h2_all[slot_of(b)] = h2
    steps = gather_steps(b, group_view(h2_all), *sems[0:4])
    next(steps)
    middle[...] = mid
    logits = jnp.dot(h2, router3[...], preferred_element_type=F32).T
    logits = logits[0:8] + logits[8:16] + logits[16:24]
    real = lax.broadcasted_iota(jnp.int32, (8, 128), 0) < 4
    logits = jnp.where(real, logits, BIG)
    g = jnp.exp(logits - jnp.max(logits, axis=0, keepdims=True))
    gates[...] = g / jnp.sum(g, axis=0, keepdims=True)
    small = send_small(b, gates, gates_all, sems[10], sems[11])
    gates_all[slot_of(b)] = gates[...]
    for _ in steps:
        pass
    wait_small(b, gates_all, sems[10], sems[11], small)


def norm_back_rows(values, gain, grad_in):
    inverse = inverse_rms(values)
    normed = values * inverse
    scaled = grad_in * gain
    out = inverse * (scaled - normed * jnp.mean(scaled * normed, axis=-1, keepdims=True))
    return out, jnp.sum(grad_in * normed, axis=0, keepdims=True)


def split_halves(rows):
    top, bottom = rows[:32], rows[32:]
    left = lane((32, 128)) < 64
    first = jnp.where(left, top, pltpu.roll(bottom, 64, 1))
    second = jnp.where(left, pltpu.roll(top, 64, 1), bottom)
    return first.astype(BF), second.astype(BF)


def expert_body(
    h2, dy0, cot, gates, picks, wg, wu, w_down, keep, middle, gain, router_t, joined, w_out, routed, near_g, near_u, near_d, got_g, got_d, do_all, dmid, smalls, gwo, far_u, far_d, dy, rows, grad, dexp, weight, hid, dgs, dus, acts, slopes, outs, drs, dws, wd, w_buf, far_g, acc, landing, dgates, dg_all, parcels, load, *sems
):
    b = spot()
    h = b["h"]
    partner = device(flip(b, ["h"]))
    whoami, peers = world_all(b)
    greet_start([peer for _, peer in peers])
    fetches = [
        pltpu.make_async_copy(dy0, dy.at[:, pl.ds(0, 64)], load.at[0]),
        pltpu.make_async_copy(w_out, w_buf, load.at[3]),
    ]
    for n in range(2):
        at = pl.multiple_of((4 * n + col_of(b)) * 352, 32)
        fetches.append(
            pltpu.make_async_copy(
                w_down.at[pl.ds(at, 352)], wd.at[pl.ds(n * 352, 352)], load.at[1 + n]
            )
        )
    for cp in fetches:
        cp.start()
    dy[slot_of(b), 64:128] = cot[64:]
    mine = row_of(b)
    mine_f = mine.astype(F32)
    first = picks[:, 0, :]
    second = picks[:, 1, :]
    chosen = jnp.where((first == mine_f) | (second == mine_f), 1.0, 0.0)
    earlier = jnp.where(
        lax.broadcasted_iota(jnp.int32, (128, 128), 0) < lane((128, 128)), 1.0, 0.0
    )
    place = jnp.dot(chosen.astype(BF), earlier.astype(BF), preferred_element_type=F32)
    place = jnp.where((chosen > 0.5) & (place < PLACES), place, -1.0)
    place_t = jnp.concatenate([place, jnp.full((112, 128), -1.0, F32)], axis=0).T
    level = lax.broadcasted_iota(jnp.int32, (PLACES, 128), 0).astype(F32)
    level_t = lane((128, PLACES)).astype(F32)
    is_mine = lax.broadcasted_iota(jnp.int32, (8, 128), 0) == mine
    for m in range(16):
        at = slice(m * PLACES, (m + 1) * PLACES)
        hit = jnp.where(level == place[m : m + 1], 1.0, 0.0)
        rows[at] = jnp.dot(hit.astype(BF), h2[m], preferred_element_type=F32).astype(BF)
        gate_row = jnp.sum(jnp.where(is_mine, gates[m], 0.0), axis=0, keepdims=True)
        w = jnp.sum(hit * gate_row, axis=1, keepdims=True)
        weight[at] = jnp.broadcast_to(w, (PLACES, 128))
        if m == 7:
            greet_end(31)
            steps = gather_steps(b, group_view(dy, 64, 64), *sems[0:4], parts=TWO)
            next(steps)
    for cp in fetches:
        cp.wait()
    next(steps)
    c0 = math.sqrt(2.0 / math.pi)
    c1 = 0.044715
    for i in range(5):
        at = slice(i * TILE, (i + 1) * TILE)
        r = rows[at]
        gp = jnp.dot(r, wg[...], preferred_element_type=F32)
        up = jnp.dot(r, wu[...], preferred_element_type=F32)
        sq = gp * gp
        th = jnp.tanh(c0 * gp * (1.0 + c1 * sq))
        half = 0.5 * (1.0 + th)
        act = gp * half
        slope = half + 0.5 * gp * (1.0 - th * th) * (c0 * (1.0 + 3.0 * c1 * sq))
        acts[at] = act.astype(BF)
        slopes[at] = (up * slope).astype(BF)
        hd = (act * up).astype(BF)
        hid[at] = hd
        outs[at] = jnp.dot(hd, wd[...], preferred_element_type=F32).astype(BF)
        for _ in range((1, 1, 2, 2, 1)[i]):
            next(steps)
    for m in range(16):
        at = slice(m * PLACES, (m + 1) * PLACES)
        hit = jnp.where(level == place[m : m + 1], 1.0, 0.0).astype(BF)
        g = jnp.dot(hit, dy[m], preferred_element_type=F32)
        grad[at] = g.astype(BF)
        dexp[at] = (weight[at, 0:1] * g).astype(BF)
    down = lax.dot_general(hid[...], dexp[...], TN, preferred_element_type=F32).astype(BF)
    upper = h == 1
    far_d[...] = jnp.where(upper, down[:352], down[352:])
    near_d[...] = jnp.where(upper, down[352:], down[:352])
    trades = [
        remote(
            far_d.at[pl.ds(0, DOWN_FIRST)], got_d.at[pl.ds(0, DOWN_FIRST)], sems[16].at[0], sems[17].at[0], partner
        )
    ]
    for n, (r0, rn) in enumerate(((0, GATE_FIRST), (GATE_FIRST, 512 - GATE_FIRST))):
        trades.append(
            remote(
                far_g.at[pl.ds(r0, rn)], got_g.at[pl.ds(r0, rn)], sems[16].at[1 + n], sems[17].at[1 + n], partner
            )
        )
    trades[0].start()
    for i in range(5):
        at = slice(i * TILE, (i + 1) * TILE)
        o = outs[at].astype(F32)
        dws[at] = jnp.broadcast_to(
            jnp.sum(grad[at].astype(F32) * o, axis=1, keepdims=True), (TILE, 128)
        )
        outs[at] = (weight[at, 0:1] * o).astype(BF)
        dh = lax.dot_general(dexp[at], wd[...], NT, preferred_element_type=F32)
        dg = (dh * slopes[at].astype(F32)).astype(BF)
        du = (dh * acts[at].astype(F32)).astype(BF)
        dgs[at] = dg
        dus[at] = du
        drs[at] = (
            lax.dot_general(dg, wg[...], NT, preferred_element_type=F32)
            + lax.dot_general(du, wu[...], NT, preferred_element_type=F32)
        ).astype(BF)
    for m in range(16):
        at = slice(m * PLACES, (m + 1) * PLACES)
        back = jnp.where(place_t[:, m : m + 1] == level_t, 1.0, 0.0).astype(BF)
        dy[m] = jnp.dot(back, drs[at], preferred_element_type=F32).astype(BF)
        hit = jnp.where(level == place[m : m + 1], 1.0, 0.0)
        dgates[m] = jnp.broadcast_to(
            jnp.sum(hit * dws[at], axis=0, keepdims=True), (8, 128)
        )
    me = slot_of(b)
    steps = scatter_steps(b, dy, acc, landing, *sems[4:8])
    next(steps)
    copies = []
    for step, peer in enumerate(cube_all(b)):
        s = lax.rem(me + step + 1, 16)
        cp = remote(dgates.at[s], dg_all.at[me], sems[8].at[step], sems[9].at[step], peer)
        cp.start()
        copies.append(cp)
    dg_all[me] = dgates[me]
    part = rows[:, pl.ds(pl.multiple_of((1 - h) * 512, 512), 512)]
    far_g[...] = lax.dot_general(part, dgs[...], TN, preferred_element_type=F32).astype(BF)
    trades[1].start()
    next(steps)
    far_u[...] = lax.dot_general(part, dus[...], TN, preferred_element_type=F32).astype(BF)
    part = rows[:, pl.ds(pl.multiple_of(h * 512, 512), 512)]
    near_g[...] = lax.dot_general(part, dgs[...], TN, preferred_element_type=F32).astype(BF)
    next(steps)
    near_u[...] = lax.dot_general(part, dus[...], TN, preferred_element_type=F32).astype(BF)
    next(steps)
    for m in range(8):
        at = slice(m * PLACES, (m + 1) * PLACES)
        back = jnp.where(place_t[:, m : m + 1] == level_t, 1.0, 0.0).astype(BF)
        routed[m] = jnp.dot(back, outs[at], preferred_element_type=F32).astype(BF)
    next(steps)
    next(steps)
    wait_small(b, dg_all, sems[8], sems[9], copies)
    row_level = lax.broadcasted_iota(jnp.int32, (8, 128), 0)
    dg = jnp.zeros((8, 128), F32)
    for e in range(4):
        total = dg_all[4 * e] + dg_all[4 * e + 1] + dg_all[4 * e + 2] + dg_all[4 * e + 3]
        dg = jnp.where(row_level == e, total, dg)
    g = gates[me]
    dl_t = g * (dg - jnp.sum(g * dg, axis=0, keepdims=True))
    dl = jnp.concatenate([dl_t, jnp.zeros((120, 128), F32)], axis=0).T
    d_h2 = acc[eighth(b)].astype(F32)
    for e in range(4):
        d_h2 = d_h2 + dl[:, e : e + 1] * router_t[e : e + 1]
    grad_mid, grad_gain = norm_back_rows(middle[...], gain[...], d_h2)
    d_mid = cot[...].astype(F32) * keep[...] + grad_mid
    d_low = d_mid.astype(BF)
    d_o = lax.dot_general(d_low, w_buf[...], NT, preferred_element_type=F32)
    for s in range(2):
        for pair in range(8):
            rows_of = d_o[s * 64 : s * 64 + 64, pair * 128 : pair * 128 + 128]
            one, two = split_halves(rows_of)
            parcels[device_of(s, 2 * pair)] = one
            parcels[device_of(s, 2 * pair + 1)] = two

    def at_device(j):
        return do_all.at[j]

    whoami, sent = everyone(b, parcels, at_device, sems[10], sems[11])
    trades[2].start()
    do_all[whoami] = parcels[whoami]
    dmid[...] = d_mid
    high = dl_t.astype(BF)
    rest = (dl_t - high.astype(F32)).astype(BF)
    own = h2[me]
    smalls[0:8] = jnp.dot(high, own, preferred_element_type=F32) + jnp.dot(
        rest, own, preferred_element_type=F32
    )
    smalls[4:5] = grad_gain
    grad_out = lax.dot_general(joined[...], d_low, TN, preferred_element_type=F32).astype(BF)
    gwo[...] = grad_out.reshape(16, 64, 1024)
    for m in range(8, 16):
        at = slice(m * PLACES, (m + 1) * PLACES)
        back = jnp.where(place_t[:, m : m + 1] == level_t, 1.0, 0.0).astype(BF)
        routed[m] = jnp.dot(back, outs[at], preferred_element_type=F32).astype(BF)
    everyone_wait(b, whoami, at_device, sems[10], sems[11], sent)
    for cp in trades:
        cp.wait()


def back_body(
    h1, do_all, qs, ks, vs, out_t, lse, dist, onehot, gwo, tokens, dmid, gain, part, middle, keep, routed_in, near_g_in, near_u_in, near_d_in, got_g_in, got_d_in, far_u, far_d, w_query, w_key, w_value, dtokens, result, whole, whole_o, smalls, gain_out, wide, down, dos, k_t, delta, p_buf, s_buf, dq_t, dk, dv, near0, near1, left, acc_o, landing_o, packed, grads, table, wo, land, other, other_o, joined, inbox, crowd, mine, half, pieces, got_u, got_d2, acc, landing, routed, near_g, near_u, near_d, got_g, got_d1, wq, wk, wv, load, *sems
):
    b = spot()
    partner = device(flip(b, ["h"]))
    h = b["h"]
    col = col_of(b)
    me, peers = world_all(b)
    greet_start([peer for _, peer in peers])
    pairs = (
        (near_g_in, near_g),
        (got_g_in, got_g),
        (routed_in, routed),
        (near_u_in, near_u),
        (near_d_in, near_d),
        (got_d_in, got_d1),
        (w_query, wq),
        (w_key, wk),
        (w_value, wv),
    )
    loads = [pltpu.make_async_copy(src, dst, load.at[n]) for n, (src, dst) in enumerate(pairs)]
    for cp in loads:
        cp.start()
    around = [flip(b, names) for names in (["x", "l"], ["x"], ["l"])]
    started = []

    def spread_out(n):
        for i, there in enumerate(around):
            cp = remote(
                half.at[n, col_of(there)],
                pieces.at[n, col],
                sems[14].at[3 * n + i],
                sems[15].at[3 * n + i],
                device(there),
            )
            cp.start()
            started.append(cp)
        pieces[n, col] = half[n, col]

    live = lax.broadcasted_iota(jnp.int32, (4, 32, 128), 2) < 64
    for i in range(8):
        rows = slice(i * TILE, (i + 1) * TILE)
        both = do_all[4 * i : 4 * i + 4].astype(F32)
        turned = pltpu.roll(both.reshape(128, 128), 64, 1).reshape(4, 32, 128)
        d = jnp.concatenate(
            [jnp.where(live, both, 0.0)[:, None], jnp.where(live, turned, 0.0)[:, None]], axis=1
        ).reshape(TILE, 128)
        dos[rows] = d.astype(BF)
        delta[:, rows] = jnp.broadcast_to(
            jnp.sum(d.T[:64] * out_t[:, rows], axis=0, keepdims=True), (8, TILE)
        )
        kt = ks[rows].astype(F32).T
        k_t[:, rows] = jnp.where(
            lax.broadcasted_iota(jnp.int32, (128, TILE), 0) == 64, 1.0, kt
        ).astype(BF)
    greet_end(31)
    steps = scatter_steps(b, gwo, acc_o, landing_o, *sems[28:32])
    next(steps)
    trades = [
        remote(
            far_u.at[pl.ds(r0, rn)], got_u.at[pl.ds(r0, rn)], sems[16].at[n], sems[17].at[n], partner
        )
        for n, (r0, rn) in enumerate(((0, UP_FIRST), (UP_FIRST, 512 - UP_FIRST)))
    ]
    trades.append(
        remote(far_d.at[pl.ds(DOWN_FIRST, 352 - DOWN_FIRST)], got_d2, sems[16].at[2], sems[17].at[2], partner)
    )
    trades[0].start()
    loads[0].wait()
    loads[1].wait()
    half[0] = (near_g[...].astype(F32) + got_g[...].astype(F32)).astype(BF)
    spread_out(0)
    next(steps)
    near = near_tiles(dist[0:1])
    near0[...] = jnp.zeros_like(near0)
    near1[...] = jnp.zeros_like(near1)
    for i in range(8):
        cols = slice(i * TILE, (i + 1) * TILE)
        q = qs[cols]
        do = dos[cols]
        level = lse[0:1, cols]
        dl = delta[0:1, cols]
        for j in range(i + 1):
            rows = slice(j * TILE, (j + 1) * TILE)
            s = lax.dot_general(ks[rows], q, NT, preferred_element_type=F32)
            if i - j < 2:
                s = s + near[i - j]
            p = jnp.exp(s - level)
            dp = lax.dot_general(vs[rows], do, NT, preferred_element_type=F32)
            ds = (p * (dp - dl)).astype(BF)
            p_buf[rows] = p.astype(BF)
            s_buf[rows] = ds
            if i == j:
                near0[...] += ds.astype(F32)
            if i - j == 1:
                near1[...] += ds.astype(F32)
        n = (i + 1) * TILE
        dq_t[:, cols] = jnp.dot(k_t[:, :n], s_buf[:n], preferred_element_type=F32)
        new_v = jnp.dot(p_buf[:n], do, preferred_element_type=F32)
        new_k = jnp.dot(s_buf[:n], q, preferred_element_type=F32)
        if i > 0:
            dv[: n - TILE] += new_v[: n - TILE]
            dk[: n - TILE] += new_k[: n - TILE]
        dv[n - TILE : n] = new_v[n - TILE :]
        dk[n - TILE : n] = new_k[n - TILE :]
        if i in (3, 5, 6, 7):
            next(steps)
    total = jnp.sum(dq_t[64:65, :].reshape(1, 16, 128), axis=1)
    skew = jnp.concatenate([near0[...], near1[...]], axis=1)
    level_u = lax.broadcasted_iota(jnp.int32, (TILE, 2 * TILE), 0)
    for bit in range(8):
        moved = pltpu.roll(skew, 2 * TILE - (1 << bit), 1)
        skew = jnp.where((level_u // (1 << bit)) % 2 == 1, moved, skew)
    by_distance = jnp.broadcast_to(jnp.sum(skew, axis=0, keepdims=True), (8, 2 * TILE))
    buckets = jnp.dot(by_distance, onehot[...], precision=highest)
    spot_lane = lane((8, 128))
    others = jnp.sum(jnp.where(spot_lane < 31, buckets, 0.0), axis=1, keepdims=True)
    whole_sum = jnp.sum(total, axis=1, keepdims=True)
    buckets = jnp.where(spot_lane == 31, whole_sum - others, buckets)
    row = jnp.concatenate([buckets, jnp.zeros((8, 384), F32)], axis=1)
    table[...] = pltpu.roll(row, slot_of(b) * 32, 1)
    for i in range(8):
        rows = slice(i * TILE, (i + 1) * TILE)
        dq = dq_t[:, rows] * 0.125
        vk = jnp.where(lane((TILE, 128)) < 64, dv[rows], pltpu.roll(dk[rows], 64, 1)).T
        left[0:64, rows] = dq[:64].astype(BF)
        left[64:128, rows] = vk[64:128].astype(BF)
        left[128:192, rows] = vk[0:64].astype(BF)
        blocks = slice(4 * i, 4 * i + 4)
        packed[blocks, 0:32] = pack_halves(dq.T).astype(BF)
        packed[blocks, 32:64] = pack_halves(dk[rows]).astype(BF)
        packed[blocks, 64:96] = pack_halves(dv[rows]).astype(BF)
    grads[...] = (
        jnp.dot(left[...], h1[...], preferred_element_type=F32).astype(BF).reshape(2, 96, 1024)
    )
    trade = remote(grads.at[1 - h], other, sems[8].at[0], sems[9].at[0], partner)
    trade.start()
    wo[...] = acc_o[eighth(b)]
    trade_o = remote(wo, other_o, sems[8].at[2], sems[9].at[2], partner)
    trade_o.start()

    def at(j):
        return land.at[j]

    def view_of(side):
        def view(v, c0, cn):
            return whole.at[side, slot_of(v), :, pl.ds(c0, cn)]

        return view

    me_slot = slot_of(b)
    smalls[...] = part[...]
    smalls[5:8] = jnp.concatenate([table[0:3], jnp.zeros((3, 512), F32)], axis=1)

    def add_small():
        for step, name in enumerate(("k", "x", "y", "l", "h")):
            cp = remote(
                smalls, inbox.at[step], sems[12].at[step], sems[13].at[step], device(flip(b, [name]))
            )
            cp.start()
            yield
            cp.wait()
            smalls[...] = smalls[...] + inbox[step]
        yield

    for cp in loads[2:]:
        cp.wait()
    tokens_back = scatter_steps(b, routed, acc, landing, *sems[24:28], cuts=LATE)
    next(tokens_back)
    rounds = add_small()
    next(rounds)
    next(tokens_back)
    next(rounds)
    trade.wait()
    whole[h, me_slot] = (grads[h].astype(F32) + other[...].astype(F32)).astype(BF)
    share = remote(
        whole.at[h, me_slot], whole.at[h, me_slot], sems[8].at[1], sems[9].at[1], partner
    )
    share.start()
    near = gather_steps(b, view_of(h), *sems[0:4], parts=TWO)
    next(near)
    me, copies = everyone(b, packed, at, sems[10], sems[11])
    for cp in trades[1:]:
        cp.start()
    land[me] = packed[me]
    next(rounds)
    next(near)
    trade_o.wait()
    whole_o[me_slot] = (wo[...].astype(F32) + other_o[...].astype(F32)).astype(BF)
    outs = gather_steps(b, group_view(whole_o, 0, 64), *sems[18:22], parts=BY_Y)
    next(outs)
    next(near)
    next(rounds)
    theirs = whole.at[1 - h, me_slot]
    remote(theirs, theirs, sems[8].at[1], sems[9].at[1], partner).wait_recv()
    far = gather_steps(b, view_of(1 - h), *sems[4:8], parts=TWO)
    next(far)
    def tokens_done():
        everyone_wait(b, me, at, sems[10], sems[11], copies)
        for kind in range(3):
            for s in range(2):
                for pair in range(8):
                    j0, j1 = device_of(s, 2 * pair), device_of(s, 2 * pair + 1)
                    span = slice(kind * 32, kind * 32 + 32)
                    top, bottom = unpack_halves(land[j0, span], land[j1, span])
                    cols = slice(pair * 128, pair * 128 + 128)
                    joined[kind, s * 64 : s * 64 + 32, cols] = top
                    joined[kind, s * 64 + 32 : s * 64 + 64, cols] = bottom
        d_h1 = (
            lax.dot_general(joined[0], wq[...], NT, preferred_element_type=F32)
            + lax.dot_general(joined[1], wk[...], NT, preferred_element_type=F32)
            + lax.dot_general(joined[2], wv[...], NT, preferred_element_type=F32)
        )
        grad_in, grad_gain = norm_back_rows(tokens[...].astype(F32), gain[...], d_h1)
        dtokens[...] = dmid[...] + grad_in
        mine[...] = grad_gain.reshape(8, 128)
        sent = []
        for step, (j, peer) in enumerate(world_all(b)[1]):
            cp = remote(mine, crowd.at[me], sems[22].at[step], sems[23].at[step], peer)
            cp.start()
            sent.append(cp)
        crowd[me] = mine[...]
        return sent

    def up_done():
        trades[0].wait()
        trades[1].wait()
        half[1] = (near_u[...].astype(F32) + got_u[...].reshape(4, 128, SHARE).astype(F32)).astype(BF)
        spread_out(1)

    def widen(n):
        for i, there in enumerate(around):
            ref = pieces.at[n, col_of(there)]
            remote(ref, ref, sems[14].at[3 * n + i], sems[15].at[3 * n + i], device(there)).wait_recv()
        for i in range(4):
            wide[n, :, i * 352 : i * 352 + 352] = pieces[n, i, :, 0:352]
            wide[n, :, (4 + i) * 352 : (4 + i) * 352 + 352] = pieces[n, i, :, 352:704]

    sent = []
    for n in range(7):
        if n % 2 == 0:
            next(tokens_back)
        next(near, None)
        next(outs)
        next(far)
        if n == 2:
            widen(0)
        if n == 3:
            next(rounds)
        if n == TOKENS_AT:
            sent = tokens_done()
        if n == UP_AT:
            up_done()
    next(outs)
    next(far)
    next(rounds)
    share.wait_send()
    result[...] = ((middle[...] + acc[eighth(b)].astype(F32)) * keep[...]).astype(BF)
    everyone_wait(b, me, lambda j: crowd.at[j], sems[22], sems[23], sent)
    gain_out[...] = jnp.sum(crowd[...], axis=0)
    widen(1)
    trades[2].wait()
    down[:DOWN_FIRST] = (near_d[:DOWN_FIRST].astype(F32) + got_d1[:DOWN_FIRST].astype(F32)).astype(BF)
    down[DOWN_FIRST:] = (near_d[DOWN_FIRST:].astype(F32) + got_d2[...].astype(F32)).astype(BF)
    for cp in started:
        cp.wait_send()


def dense_body(whole, whole_o, grad_q, grad_k, grad_v, grad_o):
    sides = (whole[0].astype(F32), whole[1].astype(F32))
    spans = (
        (grad_q, ((0, 0, 64),)),
        (grad_k, ((0, 64, 96), (1, 0, 32))),
        (grad_v, ((1, 32, 96),)),
    )
    for out, parts in spans:
        pieces = []
        for head in range(2):
            for side, lo, hi in parts:
                pieces.append(sides[side][head, lo:hi])
        rows = jnp.concatenate(pieces, axis=0)
        for c in range(0, 1024, 128):
            out[c : c + 128, :] = rows[:, c : c + 128].T
    grad_o[...] = whole_o[...].reshape(128, 1024).astype(F32)


def distance_buckets():
    table = []
    for distance in range(2 * TILE):
        table.append(bucket_of(distance, 32, MAXDIST))
    return np.array(table, np.int32)


def on_device_fast(
    tokens,
    lengths,
    expert_index,
    cotangent,
    norm_attn,
    w_query,
    w_key,
    w_value,
    w_out,
    rel_bias,
    norm_ffn,
    router,
    w_gate,
    w_up,
    w_down,
):
    dma = pltpu.SemaphoreType.DMA
    b = spot()
    head = slot_of(b)
    col = col_of(b)
    device_at = lax.axis_index(("experts", "context"))
    positions = device_at * 64 + jnp.arange(64, dtype=jnp.int32)
    live = positions[None, :] < lengths[:, None]
    keep = live.reshape(128, 1).astype(F32)
    picks = jnp.where(live[:, :, None], expert_index, -1).astype(F32).reshape(128, 2).T
    picks = jnp.concatenate([picks, jnp.zeros((6, 128), F32)], axis=0)
    gain_attn = norm_attn.reshape(1, 1024)
    gain_ffn = norm_ffn.reshape(1, 1024)
    flat = tokens.reshape(128, 1024)
    cot = cotangent.reshape(128, 1024)

    buckets = distance_buckets()
    onehot = np.zeros((2 * TILE, 128), np.float32)
    onehot[np.arange(2 * TILE), buckets] = 1.0
    bias_t = jnp.pad(rel_bias.T, ((0, 0), (0, 96)))
    high = router.astype(BF)
    rest = router - high.astype(F32)
    mid = rest.astype(BF)
    lo = (rest - mid.astype(F32)).astype(BF)
    router3 = jnp.concatenate(
        [jnp.pad(r, ((0, 0), (0, 4))) for r in (high, mid, lo)] + [jnp.zeros((1024, 104), BF)], axis=1
    )
    router_t = jnp.pad(router.T, ((0, 4), (0, 0)))

    h1, picks_all, w3, wg, wu, dist = call(
        first_body,
        [
            shape((4, 2, 4, 64, 1024)),
            shape((16, 8, 128), F32),
            shape((1024, 384)),
            shape((1024, SHARE)),
            shape((1024, SHARE)),
            shape((8, 2 * TILE), F32),
        ],
        [VMEM((2, 64, 1024), BF), VMEM((3, 1024, 128), BF), VMEM((4, 1024, 512), BF)]
        + CUBE_SEMS
        + [dma(()), dma(()), dma((15,)), dma((15,)), dma((7,))],
        1,
        tokens,
        gain_attn,
        picks,
        w_query,
        w_key,
        w_value,
        w_gate[0],
        w_up[0],
        bias_t,
        jnp.asarray(onehot.T),
        anywhere=(3, 4, 5, 6, 7),
    )
    h1 = h1.reshape(2048, 1024)
    out_t, qs, ks, vs, lse, dy0, middle, h2_all, gates_all, joined = call(
        attend_body,
        [
            shape((64, 2048), F32),
            shape((2048, 128)),
            shape((2048, 128)),
            shape((2048, 128)),
            shape((8, 2048), F32),
            shape((16, 64, 1024)),
            shape((128, 1024), F32),
            shape((16, 128, 1024)),
            shape((16, 8, 128), F32),
            shape((128, 1024)),
        ],
        [
            VMEM((2048, TILE), F32),
            VMEM((128, 2048), BF),
            VMEM((2048, TILE), BF),
            VMEM((32, 32, 128), BF),
            VMEM((32, 32, 128), BF),
            VMEM((8, 128), F32),
            VMEM((1024, 1024), BF),
            dma(()),
        ]
        + CUBE_SEMS
        + TWO_SEMS
        + [dma((32,)), dma((32,)), dma((15,)), dma((15,))],
        2,
        lengths,
        h1,
        w3,
        dist,
        cot[:64],
        flat,
        w_out,
        gain_ffn,
        router3,
        scalars=(0,),
        anywhere=(6,),
    )
    routed, near_g, near_u, near_d, got_g, got_d, do_all, dmid, smalls, gwo, far_u, far_d = call(
        expert_body,
        [
            shape((16, 128, 1024)),
            shape((512, SHARE)),
            shape((512, SHARE)),
            shape((352, 1024)),
            shape((512, SHARE)),
            shape((352, 1024)),
            shape((32, 32, 128)),
            shape((128, 1024), F32),
            shape((8, 1024), F32),
            shape((16, 64, 1024)),
            shape((512, SHARE)),
            shape((352, 1024)),
        ],
        [VMEM((16, 128, 1024), BF)]
        + [VMEM((1280, 1024), BF)] * 3
        + [VMEM((1280, 128), F32)]
        + [VMEM((1280, SHARE), BF)] * 5
        + [VMEM((1280, 1024), BF)] * 2
        + [VMEM((1280, 128), F32)]
        + [VMEM((SHARE, 1024), BF), VMEM((1024, 1024), BF), VMEM((512, SHARE), BF)]
        + [VMEM((8, 128, 1024), BF)] * 2
        + [VMEM((16, 8, 128), F32)] * 2
        + [VMEM((32, 32, 128), BF)]
        + [dma((4,))]
        + TWO_SEMS
        + CUBE_SEMS
        + [dma((15,)), dma((15,)), dma((31,)), dma((31,))]
        + [dma(())] * 4
        + [dma((3,)), dma((3,))],
        3,
        h2_all,
        dy0,
        cot,
        gates_all,
        picks_all,
        wg,
        wu,
        w_down[0],
        keep,
        middle,
        gain_ffn,
        router_t,
        joined,
        w_out,
        anywhere=(1, 7, 13),
        outs_anywhere=(4, 5),
    )
    dtokens, result, whole, whole_o, smalls, gain_out, wide, down = call(
        back_body,
        [
            shape((128, 1024), F32),
            shape((128, 1024)),
            shape((2, 16, 96, 1024)),
            shape((16, 64, 1024)),
            shape((8, 1024), F32),
            shape((8, 128), F32),
            shape((2, 128, 2816)),
            shape((352, 1024)),
        ],
        [
            VMEM((2048, 128), BF),
            VMEM((128, 2048), BF),
            VMEM((8, 2048), F32),
            VMEM((2048, TILE), BF),
            VMEM((2048, TILE), BF),
            VMEM((128, 2048), F32),
            VMEM((2048, 128), F32),
            VMEM((2048, 128), F32),
            VMEM((TILE, TILE), F32),
            VMEM((TILE, TILE), F32),
            VMEM((192, 2048), BF),
            VMEM((8, 64, 1024), BF),
            VMEM((8, 64, 1024), BF),
            VMEM((32, 96, 128), BF),
            VMEM((2, 96, 1024), BF),
            VMEM((8, 512), F32),
            VMEM((64, 1024), BF),
            VMEM((32, 96, 128), BF),
            VMEM((96, 1024), BF),
            VMEM((64, 1024), BF),
            VMEM((3, 128, 1024), BF),
            VMEM((5, 8, 1024), F32),
            VMEM((32, 8, 128), F32),
            VMEM((8, 128), F32),
            VMEM((2, 4, 128, SHARE), BF),
            VMEM((2, 4, 128, SHARE), BF),
            VMEM((512, SHARE), BF),
            VMEM((352 - DOWN_FIRST, 1024), BF),
            VMEM((8, 128, 1024), BF),
            VMEM((8, 128, 1024), BF),
            VMEM((16, 128, 1024), BF),
            VMEM((4, 128, SHARE), BF),
            VMEM((4, 128, SHARE), BF),
            VMEM((352, 1024), BF),
            VMEM((4, 128, SHARE), BF),
            VMEM((352, 1024), BF),
            VMEM((1024, 1024), BF),
            VMEM((1024, 1024), BF),
            VMEM((1024, 1024), BF),
            dma((9,)),
        ]
        + CUBE_SEMS
        + CUBE_SEMS
        + [dma((3,)), dma((3,)), dma((31,)), dma((31,)), dma((5,)), dma((5,)), dma((6,)), dma((6,))]
        + [dma((3,)), dma((3,))]
        + ONE_SEMS
        + [dma((31,)), dma((31,))]
        + CUBE_SEMS
        + CUBE_SEMS,
        4,
        h1,
        do_all,
        qs,
        ks,
        vs,
        out_t,
        lse,
        dist,
        jnp.asarray(onehot),
        gwo,
        flat,
        dmid,
        gain_attn,
        smalls,
        middle,
        keep,
        routed,
        near_g.reshape(4, 128, SHARE),
        near_u.reshape(4, 128, SHARE),
        near_d,
        got_g.reshape(4, 128, SHARE),
        got_d,
        far_u,
        far_d,
        w_query,
        w_key,
        w_value,
        anywhere=tuple(range(16, 27)),
    )
    grad_q, grad_k, grad_v, grad_o = pl.pallas_call(
        dense_body,
        grid=(8,),
        out_shape=[shape((1024, 1024), F32)] * 4,
        in_specs=[
            pl.BlockSpec((2, 2, 96, 1024), lambda i: (0, i, 0, 0)),
            pl.BlockSpec((2, 64, 1024), lambda i: (i, 0, 0)),
        ],
        out_specs=[pl.BlockSpec((1024, 128), lambda i: (0, i))] * 3
        + [pl.BlockSpec((128, 1024), lambda i: (i, 0))],
        compiler_params=params(),
        cost_estimate=pl.CostEstimate(flops=0, bytes_accessed=25 * 2**20, transcendentals=0),
    )(whole, whole_o)
    return (
        result.reshape(2, 64, 1024),
        dtokens.reshape(2, 64, 1024),
        gain_out.reshape(1024),
        grad_q,
        grad_k,
        grad_v,
        grad_o,
        smalls[5, :512].reshape(16, 32).T,
        smalls[4],
        smalls[0:4].T,
        wide[0:1].astype(F32),
        wide[1:2].astype(F32),
        down[None].astype(F32),
    )


def solution(mesh):
    sizes = dict(mesh.shape)
    fits = sizes == {"experts": 4, "context": 8}
    placed = (
        P(None, ("experts", "context"), None),
        P(),
        P(None, ("experts", "context"), None),
        P(None, ("experts", "context"), None),
        P(),
        P(),
        P(),
        P(),
        P(),
        P(),
        P(),
        P(),
        P("experts", None, None),
        P("experts", None, None),
        P("experts", None, None),
    )
    return jax.shard_map(
        on_device_fast if fits else on_device,
        mesh=mesh,
        in_specs=placed,
        out_specs=(
            P(None, ("experts", "context"), None),
            P(None, ("experts", "context"), None),
            P(),
            P(),
            P(),
            P(),
            P(),
            P(),
            P(),
            P(),
            P("experts", "context", None),
            P("experts", "context", None),
            P("experts", "context", None),
        ),
        check_vma=False,
    )
```

```python
import math

import jax
import jax.numpy as jnp
import numpy as np
from jax import lax
from jax.experimental import pallas as pl
from jax.experimental.pallas import tpu as pltpu
from jax.sharding import PartitionSpec as P

MAXDIST = 128


norm_epsilon = 1e-06
mask_fill = -1e30
highest = lax.Precision.HIGHEST


def bucket_of(distance, bucket_count, reach):
    exact = bucket_count // 2
    if distance < exact:
        return distance
    level = exact + int(
        math.log(distance / exact) / math.log(reach / exact) * (bucket_count - exact)
    )
    return min(level, bucket_count - 1)


def bucket_edges(bucket_count, reach):
    edges = []
    for level in range(1, bucket_count):
        distance = 0
        while bucket_of(distance, bucket_count, reach) < level:
            distance += 1
        edges.append(distance)
    return edges


def relative_bucket(query_pos, key_pos, bucket_count):
    distance = jnp.maximum(query_pos[:, None] - key_pos[None, :], 0)
    bucket = jnp.zeros(distance.shape, jnp.int32)
    for edge in bucket_edges(bucket_count, MAXDIST):
        bucket = bucket + (distance >= edge).astype(jnp.int32)
    return bucket


def rms_norm(values, gain):
    inverse = lax.rsqrt(jnp.mean(values * values, axis=-1, keepdims=True) + norm_epsilon)
    return values * inverse * gain


def norm_back(values, gain, grad_in):
    inverse = lax.rsqrt(jnp.mean(values * values, axis=-1, keepdims=True) + norm_epsilon)
    normed = values * inverse
    grad_normed = grad_in * gain
    grad_values = inverse * (
        grad_normed - normed * jnp.mean(grad_normed * normed, axis=-1, keepdims=True)
    )
    return (grad_values, jnp.sum(grad_in * normed, 0))


def score_block(query_rows, key_rows, rel_bias, query_pos, key_pos, lengths, score_scale):
    raw_scores = (
        jnp.einsum("sqhd,skhd->sqhk", query_rows, key_rows, preferred_element_type=jnp.float32)
        * score_scale
    )
    bucket = relative_bucket(query_pos, key_pos, rel_bias.shape[0])
    onehot = (bucket[:, :, None] == jnp.arange(rel_bias.shape[0], dtype=jnp.int32)).astype(
        jnp.float32
    )
    bias_rows = jnp.einsum("qkb,bh->qhk", onehot, rel_bias, precision=highest)
    causal = (key_pos[None, :] <= query_pos[:, None])[None]
    inside = key_pos[None, None, :] < lengths[:, None, None]
    allowed = (causal & inside)[:, :, None, :]
    return (raw_scores + bias_rows[None], allowed, onehot)


def pair_grads(query_set, key_set, rel_bias, lengths, score_scale):
    query_rows, grad_rows, log_total, delta, query_pos = query_set
    key_rows, value_rows, key_pos = key_set
    scores, allowed, onehot = score_block(
        query_rows, key_rows, rel_bias, query_pos, key_pos, lengths, score_scale
    )
    weights = jnp.where(allowed, jnp.exp(scores - log_total[..., None]), 0.0)
    grad_value = jnp.einsum(
        "sqhk,sqhd->skhd",
        weights.astype(jnp.bfloat16),
        grad_rows,
        preferred_element_type=jnp.float32,
    )
    grad_weights = jnp.einsum(
        "sqhd,skhd->sqhk", grad_rows, value_rows, preferred_element_type=jnp.float32
    )
    grad_scores = (weights * (grad_weights - delta[..., None])).astype(jnp.bfloat16)
    grad_query = score_scale * jnp.einsum(
        "sqhk,skhd->sqhd", grad_scores, key_rows, preferred_element_type=jnp.float32
    )
    grad_key = score_scale * jnp.einsum(
        "sqhk,sqhd->skhd", grad_scores, query_rows, preferred_element_type=jnp.float32
    )
    grad_table = jnp.einsum(
        "sqhk,qkb->bh", grad_scores, onehot.astype(jnp.bfloat16), preferred_element_type=jnp.float32
    )
    return (grad_query, grad_key, grad_value, grad_table)


def dispatch_table(expert_index, live_rows, expert_count, capacity):
    picked = expert_index.reshape(-1)
    live_pairs = jnp.broadcast_to(live_rows[:, :, None], expert_index.shape).reshape(-1)
    chosen = (
        (picked[:, None] == jnp.arange(expert_count, dtype=jnp.int32)[None, :])
        & live_pairs[:, None]
    ).astype(jnp.int32)
    earlier = jnp.cumsum(chosen, axis=0) - chosen
    position_in = jnp.sum(earlier * chosen, -1)
    kept_pairs = live_pairs & (position_in < capacity)
    slot_of = jnp.where(kept_pairs, picked * capacity + position_in, -1)
    matches = slot_of[None, :] == jnp.arange(expert_count * capacity, dtype=jnp.int32)[:, None]
    table = jnp.any(matches.reshape(expert_count * capacity, -1, 2), -1).astype(jnp.float32)
    slot_ids = jnp.arange(expert_count * capacity, dtype=jnp.int32) // capacity
    slot_expert = (slot_ids[:, None] == jnp.arange(expert_count, dtype=jnp.int32)[None, :]).astype(
        jnp.float32
    )
    return (table, slot_expert)


def on_device(
    tokens,
    lengths,
    expert_index,
    cotangent,
    norm_attn,
    w_query,
    w_key,
    w_value,
    w_out,
    rel_bias,
    norm_ffn,
    router,
    w_gate,
    w_up,
    w_down,
):
    slot_count, per_slot, model_width = tokens.shape
    head_count = rel_bias.shape[1]
    head_size = model_width // head_count
    expert_count = router.shape[1]
    capacity = (10 * slot_count * per_slot + 4 * expert_count - 1) // (4 * expert_count)
    score_scale = head_size ** (-0.5)
    row_count = slot_count * per_slot
    shape_four = (slot_count, per_slot, head_count, head_size)
    shape_three = (slot_count, per_slot, model_width)
    device_at = lax.axis_index(("experts", "context"))
    positions = device_at * per_slot + jnp.arange(per_slot, dtype=jnp.int32)
    live_rows = positions[None, :] < lengths[:, None]
    keep_mask = live_rows.reshape(row_count, 1).astype(jnp.float32)
    inputs = tokens.reshape(row_count, model_width).astype(jnp.float32)
    normed = rms_norm(inputs, norm_attn).astype(jnp.bfloat16)
    query_flat = jnp.dot(normed, w_query, preferred_element_type=jnp.float32).astype(jnp.bfloat16)
    key_flat = jnp.dot(normed, w_key, preferred_element_type=jnp.float32).astype(jnp.bfloat16)
    value_flat = jnp.dot(normed, w_value, preferred_element_type=jnp.float32).astype(jnp.bfloat16)
    query_four = query_flat.reshape(shape_four)
    key_four = key_flat.reshape(shape_four)
    value_four = value_flat.reshape(shape_four)
    key_three = key_flat.reshape(shape_three)
    value_three = value_flat.reshape(shape_three)
    start_state = (
        jnp.zeros(shape_four, jnp.float32),
        jnp.full((slot_count, per_slot, head_count), mask_fill, jnp.float32),
        jnp.zeros((slot_count, per_slot, head_count), jnp.float32),
    )
    offset = jnp.int32(0)
    key_all = lax.all_gather(key_three, ("experts", "context"), axis=1, tiled=True)
    value_all = lax.all_gather(value_three, ("experts", "context"), axis=1, tiled=True)
    piece_rows = key_all.shape[1]
    block_rows = math.gcd(piece_rows, 8 * per_slot)

    def forward_visit(carried, block_id):
        running, running_max, denominator = carried
        local_at = block_id * block_rows
        key_rows = lax.dynamic_slice_in_dim(key_all, local_at, block_rows, 1).reshape(
            slot_count, block_rows, head_count, head_size
        )
        value_rows = lax.dynamic_slice_in_dim(value_all, local_at, block_rows, 1).reshape(
            slot_count, block_rows, head_count, head_size
        )
        key_pos = offset + local_at + jnp.arange(block_rows, dtype=jnp.int32)
        scores, allowed, _ = score_block(
            query_four, key_rows, rel_bias, positions, key_pos, lengths, score_scale
        )
        scores = jnp.where(allowed, scores, mask_fill)
        new_max = jnp.maximum(running_max, jnp.max(scores, -1))
        factor = jnp.exp(running_max - new_max)
        weights = jnp.where(allowed, jnp.exp(scores - new_max[..., None]), 0.0)
        denominator = denominator * factor + jnp.sum(weights, -1)
        running = running * factor[..., None] + jnp.einsum(
            "sqhk,skhd->sqhd",
            weights.astype(jnp.bfloat16),
            value_rows,
            preferred_element_type=jnp.float32,
        )
        return ((running, new_max, denominator), None)

    carried, _ = lax.scan(
        forward_visit, start_state, jnp.arange(piece_rows // block_rows, dtype=jnp.int32)
    )
    running, running_max, denominator = carried
    attended = running / denominator[..., None]
    log_total = running_max + jnp.log(denominator)
    attended_low = attended.reshape(row_count, model_width).astype(jnp.bfloat16)
    middle = inputs + jnp.dot(attended_low, w_out, preferred_element_type=jnp.float32)
    second_low = rms_norm(middle, norm_ffn).astype(jnp.bfloat16)
    second_wide = second_low.astype(jnp.float32)
    logits = jnp.dot(second_wide, router, precision=highest)
    gates = jax.nn.softmax(logits, axis=-1)
    table, slot_expert = dispatch_table(expert_index, live_rows, expert_count, capacity)
    table_low = table.astype(jnp.bfloat16)
    dispatched = jnp.dot(table_low, second_low, preferred_element_type=jnp.float32).astype(
        jnp.bfloat16
    )
    arrived = lax.all_to_all(
        dispatched.reshape(expert_count, capacity, model_width),
        "experts",
        split_axis=0,
        concat_axis=1,
        tiled=True,
    )[0]
    gate_pre = jnp.dot(arrived, w_gate[0], preferred_element_type=jnp.float32)
    up_pre = jnp.dot(arrived, w_up[0], preferred_element_type=jnp.float32)
    hidden_low = (jax.nn.gelu(gate_pre, approximate=True) * up_pre).astype(jnp.bfloat16)
    produced = jnp.dot(hidden_low, w_down[0], preferred_element_type=jnp.float32).astype(
        jnp.bfloat16
    )
    returned = lax.all_to_all(
        produced[None], "experts", split_axis=1, concat_axis=0, tiled=True
    ).reshape(expert_count * capacity, model_width)
    returned_wide = returned.astype(jnp.float32)
    slot_weight = jnp.sum(jnp.dot(table, gates, precision=highest) * slot_expert, -1)
    routed = jnp.dot(table.T, slot_weight[:, None] * returned_wide, precision=highest)
    result = ((middle + routed) * keep_mask).astype(jnp.bfloat16).reshape(shape_three)
    grad_result = cotangent.reshape(row_count, model_width).astype(jnp.float32) * keep_mask
    gathered_grad = jnp.dot(table, grad_result, precision=highest)
    grad_produced = (
        (slot_weight[:, None] * gathered_grad)
        .astype(jnp.bfloat16)
        .reshape(expert_count, capacity, model_width)
    )
    grad_arrived_out = lax.all_to_all(
        grad_produced, "experts", split_axis=0, concat_axis=1, tiled=True
    )[0]
    grad_slot_weight = jnp.sum(gathered_grad * returned_wide, -1)
    grad_hidden = jnp.dot(grad_arrived_out, w_down[0].T, preferred_element_type=jnp.float32)
    grad_w_down = jnp.dot(hidden_low.T, grad_arrived_out, preferred_element_type=jnp.float32)

    def activation(gate_in, up_in):
        return jax.nn.gelu(gate_in, approximate=True) * up_in

    _, activation_back = jax.vjp(activation, gate_pre, up_pre)
    grad_gate_pre, grad_up_pre = activation_back(grad_hidden)
    grad_gate_low = grad_gate_pre.astype(jnp.bfloat16)
    grad_up_low = grad_up_pre.astype(jnp.bfloat16)
    grad_w_gate = jnp.dot(arrived.T, grad_gate_low, preferred_element_type=jnp.float32)
    grad_w_up = jnp.dot(arrived.T, grad_up_low, preferred_element_type=jnp.float32)
    grad_arrived = (
        jnp.dot(grad_gate_low, w_gate[0].T, preferred_element_type=jnp.float32)
        + jnp.dot(grad_up_low, w_up[0].T, preferred_element_type=jnp.float32)
    ).astype(jnp.bfloat16)
    grad_returned = lax.all_to_all(
        grad_arrived[None], "experts", split_axis=1, concat_axis=0, tiled=True
    ).reshape(expert_count * capacity, model_width)
    expert_sums = (
        lax.psum_scatter(
            grad_w_gate[None].astype(jnp.bfloat16), "context", scatter_dimension=1, tiled=True
        ).astype(jnp.float32),
        lax.psum_scatter(
            grad_w_up[None].astype(jnp.bfloat16), "context", scatter_dimension=1, tiled=True
        ).astype(jnp.float32),
        lax.psum_scatter(
            grad_w_down[None].astype(jnp.bfloat16), "context", scatter_dimension=1, tiled=True
        ).astype(jnp.float32),
    )
    grad_second = jnp.dot(table_low.T, grad_returned, preferred_element_type=jnp.float32)
    grad_gates = jnp.dot(table.T, grad_slot_weight[:, None] * slot_expert, precision=highest)
    grad_logits = gates * (grad_gates - jnp.sum(gates * grad_gates, -1, keepdims=True))
    grad_router = jnp.dot(second_wide.T, grad_logits, precision=highest)
    grad_second = grad_second + jnp.dot(grad_logits, router.T, precision=highest)
    grad_middle_norm, grad_norm_ffn = norm_back(middle, norm_ffn, grad_second)
    grad_middle = grad_result + grad_middle_norm
    grad_middle_low = grad_middle.astype(jnp.bfloat16)
    grad_w_out = jnp.dot(attended_low.T, grad_middle_low, preferred_element_type=jnp.float32)
    grad_attended_low = jnp.dot(
        grad_middle_low, w_out.T, preferred_element_type=jnp.float32
    ).astype(jnp.bfloat16)
    grad_attended_four = grad_attended_low.reshape(shape_four)
    grad_attended_three = grad_attended_low.reshape(shape_three)
    delta = jnp.sum(grad_attended_four.astype(jnp.float32) * attended, -1)
    local_queries = (query_four, grad_attended_four, log_total, delta, positions)
    grad_start = (jnp.zeros(shape_four, jnp.float32), jnp.zeros(rel_bias.shape, jnp.float32))
    query_offset = jnp.int32(0)
    query_key_all = lax.all_gather(key_three, ("experts", "context"), axis=1, tiled=True)
    query_value_all = lax.all_gather(value_three, ("experts", "context"), axis=1, tiled=True)
    piece_rows = query_key_all.shape[1]
    query_block_rows = math.gcd(piece_rows, 8 * per_slot)

    def query_visit(carried, block_id):
        local_at = block_id * query_block_rows
        key_rows = lax.dynamic_slice_in_dim(query_key_all, local_at, query_block_rows, 1).reshape(
            slot_count, query_block_rows, head_count, head_size
        )
        value_rows = lax.dynamic_slice_in_dim(
            query_value_all, local_at, query_block_rows, 1
        ).reshape(slot_count, query_block_rows, head_count, head_size)
        key_pos = query_offset + local_at + jnp.arange(query_block_rows, dtype=jnp.int32)
        grad_query, _, _, grad_table = pair_grads(
            local_queries, (key_rows, value_rows, key_pos), rel_bias, lengths, score_scale
        )
        return ((carried[0] + grad_query, carried[1] + grad_table), None)

    carried, _ = lax.scan(
        query_visit, grad_start, jnp.arange(piece_rows // query_block_rows, dtype=jnp.int32)
    )
    grad_query_four, grad_table = carried
    log_whole, delta_whole = (
        lax.all_gather(log_total, ("experts", "context"), axis=1, tiled=True),
        lax.all_gather(delta, ("experts", "context"), axis=1, tiled=True),
    )
    local_keys = (key_four, value_four, positions)
    zero_four = jnp.zeros(shape_four, jnp.float32)
    key_offset = jnp.int32(0)
    query_all = lax.all_gather(
        query_flat.reshape(shape_three), ("experts", "context"), axis=1, tiled=True
    )
    grad_all = lax.all_gather(grad_attended_three, ("experts", "context"), axis=1, tiled=True)
    piece_rows = query_all.shape[1]
    key_block_rows = math.gcd(piece_rows, 8 * per_slot)

    def key_visit(carried, block_id):
        local_at = block_id * key_block_rows
        whole_at = key_offset + local_at
        query_rows = lax.dynamic_slice_in_dim(query_all, local_at, key_block_rows, 1).reshape(
            slot_count, key_block_rows, head_count, head_size
        )
        grad_rows = lax.dynamic_slice_in_dim(grad_all, local_at, key_block_rows, 1).reshape(
            slot_count, key_block_rows, head_count, head_size
        )
        log_rows = lax.dynamic_slice_in_dim(log_whole, whole_at, key_block_rows, 1)
        delta_rows = lax.dynamic_slice_in_dim(delta_whole, whole_at, key_block_rows, 1)
        query_pos = whole_at + jnp.arange(key_block_rows, dtype=jnp.int32)
        _, grad_key, grad_value, _ = pair_grads(
            (query_rows, grad_rows, log_rows, delta_rows, query_pos),
            local_keys,
            rel_bias,
            lengths,
            score_scale,
        )
        return ((carried[0] + grad_key, carried[1] + grad_value), None)

    carried, _ = lax.scan(
        key_visit, (zero_four, zero_four), jnp.arange(piece_rows // key_block_rows, dtype=jnp.int32)
    )
    grad_key_four, grad_value_four = carried
    grad_query_low = grad_query_four.reshape(row_count, model_width).astype(jnp.bfloat16)
    grad_key_low = grad_key_four.reshape(row_count, model_width).astype(jnp.bfloat16)
    grad_value_low = grad_value_four.reshape(row_count, model_width).astype(jnp.bfloat16)
    grad_w_query = jnp.dot(normed.T, grad_query_low, preferred_element_type=jnp.float32)
    grad_w_key = jnp.dot(normed.T, grad_key_low, preferred_element_type=jnp.float32)
    grad_w_value = jnp.dot(normed.T, grad_value_low, preferred_element_type=jnp.float32)
    grad_normed = (
        jnp.dot(grad_query_low, w_query.T, preferred_element_type=jnp.float32)
        + jnp.dot(grad_key_low, w_key.T, preferred_element_type=jnp.float32)
        + jnp.dot(grad_value_low, w_value.T, preferred_element_type=jnp.float32)
    )
    grad_input_norm, grad_norm_attn = norm_back(inputs, norm_attn, grad_normed)
    grad_tokens = (grad_middle + grad_input_norm).reshape(shape_three)
    dense = lax.psum(
        (
            grad_norm_attn,
            grad_w_query,
            grad_w_key,
            grad_w_value,
            grad_w_out,
            grad_table,
            grad_norm_ffn,
            grad_router,
        ),
        ("experts", "context"),
    )
    return (
        result,
        grad_tokens,
        dense[0],
        dense[1],
        dense[2],
        dense[3],
        dense[4],
        dense[5],
        dense[6],
        dense[7],
        expert_sums[0],
        expert_sums[1],
        expert_sums[2],
    )


MESH = pl.DeviceIdType.MESH
BF = jnp.bfloat16
F32 = jnp.float32
VMEM = pltpu.VMEM
THREE = (
    (("x", "y", "l"), 0, 384),
    (("y", "l", "x"), 384, 384),
    (("l", "x", "y"), 768, 256),
)
TWO = ((("l", "x", "y"), 0, 512), (("l", "y", "x"), 512, 512))
FOUR = tuple((("l", "x", "y") if n % 2 == 0 else ("l", "y", "x"), n * 256, 256) for n in range(4))
LATE = ((("x", "y", "l"), 0, 512), (("y", "x", "l"), 512, 512))
BY_Y = ((("l", "x", "y"), 0, 1024),)
BY_X = ((("l", "y", "x"), 0, 1024),)
BIG = -1e30
TILE = 256
PLACES = 80
SHARE = 704
TOKENS_AT = 3
NT = (((1,), (1,)), ((), ()))
TN = (((0,), (0,)), ((), ()))
CUBE_SEMS = [pltpu.SemaphoreType.DMA((3, 8))] * 4
FOUR_SEMS = [pltpu.SemaphoreType.DMA((4, 8))] * 4
TWO_SEMS = [pltpu.SemaphoreType.DMA((2, 8))] * 4
ONE_SEMS = [pltpu.SemaphoreType.DMA((1, 8))] * 4


def spot():
    e = lax.axis_index("experts")
    c = lax.axis_index("context")
    return dict(
        k=lax.rem(e, 2), y=e // 2, x=lax.rem(c, 2), l=lax.rem(c // 2, 2), h=c // 4, swap=False
    )


def expert_frame(b):
    return dict(b, l=b["h"], h=b["l"], swap=True)


def flip(b, names):
    return {n: (1 - v if n in names else v) for n, v in b.items()}


def device(b):
    high, low = (b["l"], b["h"]) if b["swap"] else (b["h"], b["l"])
    return {"experts": b["y"] * 2 + b["k"], "context": high * 4 + low * 2 + b["x"]}


def row_of(b):
    return b["y"] * 2 + b["k"]


def col_of(b):
    return b["l"] * 2 + b["x"]


def slot_of(b):
    return row_of(b) * 4 + col_of(b)


def greet_start(peers):
    barrier = pltpu.get_barrier_semaphore()
    for peer in peers:
        pl.semaphore_signal(barrier, inc=1, device_id=peer, device_id_type=MESH)


def greet_end(count):
    pl.semaphore_wait(pltpu.get_barrier_semaphore(), count)


def greet(peers):
    greet_start(peers)
    greet_end(len(peers))


def cube_peers(b):
    return [device(flip(b, [n])) for n in ("x", "y", "l", "k")]


def cube_all(b):
    peers = []
    for step in range(1, 16):
        s = lax.rem(slot_of(b) + step, 16)
        peers.append(
            device(
                dict(
                    b,
                    y=s // 8,
                    k=lax.rem(s // 4, 2),
                    l=lax.rem(s // 2, 2),
                    x=lax.rem(s, 2),
                )
            )
        )
    return peers


def cube_rest(b):
    peers = []
    for t in range(1, 16):
        names = [n for i, n in enumerate(("x", "y", "l", "k")) if (t >> i) & 1]
        if len(names) > 1:
            peers.append(device(flip(b, names)))
    return peers


def world_all(b):
    me = row_of(b) * 8 + device(b)["context"]
    peers = []
    for step in range(1, 32):
        j = lax.rem(me + step, 32)
        peers.append((j, {"experts": j // 8, "context": lax.rem(j, 8)}))
    return me, peers


def remote(src, dst, ssem, rsem, peer):
    return pltpu.make_async_remote_copy(
        src_ref=src, dst_ref=dst, send_sem=ssem, recv_sem=rsem, device_id=peer, device_id_type=MESH
    )


def names_of(order, t):
    return [order[i] for i in range(3) if (t >> i) & 1]


def gather_steps(b, view, ss, rs, cs, cr, parts=THREE):
    started = []
    core = device(flip(b, ["k"]))
    every = range(len(parts))

    def piece(p, t, more=()):
        order, c0, cn = parts[p]
        return view(flip(b, names_of(order, t) + list(more)), c0, cn)

    def link(p, t, i):
        ref = piece(p, t)
        n = t | (1 << i)
        cp = remote(ref, ref, ss.at[p, n], rs.at[p, n], device(flip(b, [parts[p][0][i]])))
        cp.start()
        started.append(cp)

    def across(p, t):
        ref = piece(p, t)
        cp = remote(ref, ref, cs.at[p, t], cr.at[p, t], core)
        cp.start()
        started.append(cp)

    for i in range(3):
        for p in every:
            link(p, 0, i)
    for p in every:
        across(p, 0)
    yield
    for t in range(1, 8):
        for p in every:
            ref = piece(p, t)
            remote(ref, ref, ss.at[p, t], rs.at[p, t], core).wait_recv()
            for i in range(t.bit_length(), 3):
                link(p, t, i)
            across(p, t)
        yield
    for cp in started:
        cp.wait_send()
    for p in every:
        for t in range(8):
            ref = piece(p, t, ["k"])
            remote(ref, ref, cs.at[p, t], cr.at[p, t], core).wait_recv()
    yield


def gather_cube(*args):
    for _ in gather_steps(*args):
        pass


def eighth(b):
    return b["y"] * 4 + b["l"] * 2 + b["x"]


def scatter_steps(b, parts, acc, landing, ss, rs, cs, cr, cuts=THREE):
    started = []
    core = device(flip(b, ["k"]))
    dims = ("x", "y", "l")
    order = sorted(range(8), key=lambda t: -bin(t).count("1"))

    def set_of(t):
        return [n for i, n in enumerate(dims) if (t >> i) & 1]

    def push(p, step, others_set):
        dims_in_order, c0, cn = cuts[p]
        first = dims_in_order[step]
        others = dims_in_order[step + 1 :]
        there = flip(b, [first] + others_set)
        n = (1 << len(others)) + sum(1 << i for i, name in enumerate(others) if name in others_set)
        cp = remote(
            acc.at[eighth(there), :, pl.ds(c0, cn)],
            landing.at[n, :, pl.ds(c0, cn)],
            ss.at[p, n],
            rs.at[p, n],
            device(flip(b, [first])),
        )
        cp.start()
        started.append(cp)

    for t in order:
        there = flip(b, set_of(t) + ["k"])
        cp = remote(parts.at[slot_of(there)], acc.at[eighth(there)], cs.at[0, t], cr.at[0, t], core)
        cp.start()
        started.append(cp)
    yield
    for t in order:
        here = flip(b, set_of(t))
        n = eighth(here)
        remote(parts.at[slot_of(here)], acc.at[n], cs.at[0, t], cr.at[0, t], core).wait_recv()
        acc[n] = (acc[n].astype(F32) + parts[slot_of(here)].astype(F32)).astype(BF)
        for p in range(len(cuts)):
            first = cuts[p][0][0]
            if first in set_of(t):
                push(p, 0, [name for name in set_of(t) if name != first])
    yield
    for step in range(3):
        rest = 2 - step
        count = 1 << rest
        for t in range(count - 1, -1, -1):
            for p in range(len(cuts)):
                dims_in_order, c0, cn = cuts[p]
                others = dims_in_order[step + 1 :]
                names = [others[i] for i in range(rest) if (t >> i) & 1]
                target = eighth(flip(b, names))
                n = count + t
                ref = landing.at[n, :, pl.ds(c0, cn)]
                remote(ref, ref, ss.at[p, n], rs.at[p, n], core).wait_recv()
                acc[target, :, c0 : c0 + cn] = (
                    acc[target, :, c0 : c0 + cn].astype(F32)
                    + landing[n, :, c0 : c0 + cn].astype(F32)
                ).astype(BF)
                if rest and others[0] in names:
                    push(p, step + 1, [name for name in names if name != others[0]])
        yield
    for cp in started:
        cp.wait_send()
    yield


def scatter_cube(*args):
    for _ in scatter_steps(*args):
        pass


def params(cid=None, mib=60):
    if cid is None:
        return pltpu.CompilerParams(vmem_limit_bytes=mib * 2**20)
    return pltpu.CompilerParams(
        collective_id=cid, has_side_effects=True, vmem_limit_bytes=mib * 2**20
    )


def call(body, outs, scratch, cid, *args, anywhere=(), outs_anywhere=(), scalars=()):
    def spec(i, listed):
        if i in listed:
            return pl.BlockSpec(memory_space=pl.ANY)
        return pl.BlockSpec(memory_space=VMEM)

    return pl.pallas_call(
        body,
        out_shape=outs,
        in_specs=[
            pl.BlockSpec(memory_space=pltpu.SMEM) if i in scalars else spec(i, anywhere)
            for i in range(len(args))
        ],
        out_specs=[spec(i, outs_anywhere) for i in range(len(outs))],
        scratch_shapes=scratch,
        compiler_params=params(cid),
    )(*args)


def shape(dims, kind=BF):
    return jax.ShapeDtypeStruct(dims, kind)


def sequence_steps(b, whole, staged, own_sems, other_sems, hs, hr):
    partner = device(flip(b, ["h"]))
    mine = whole.at[row_of(b), b["h"], col_of(b)]
    cp = remote(staged.at[1 - b["h"]], mine, hs, hr, partner)
    cp.start()
    whole[row_of(b), b["h"], col_of(b)] = staged[b["h"]]

    def view_of(side):
        def view(v, c0, cn):
            return whole.at[row_of(v), side, col_of(v), :, pl.ds(c0, cn)]

        return view

    own = gather_steps(b, view_of(b["h"]), *own_sems)
    next(own)
    yield
    next(own)
    next(own)
    yield
    theirs = whole.at[row_of(b), 1 - b["h"], col_of(b)]
    remote(theirs, theirs, hs, hr, partner).wait_recv()
    other = gather_steps(b, view_of(1 - b["h"]), *other_sems)
    next(other)
    yield
    for _ in range(5):
        next(own)
        next(other)
        yield
    next(own)
    for _ in range(3):
        next(other)
        yield
    cp.wait_send()
    yield


def group_view(ref, r0=0, rn=128):
    def view(v, c0, cn):
        return ref.at[slot_of(v), pl.ds(r0, rn), pl.ds(c0, cn)]

    return view


def send_small(b, src, into, ss, rs):
    copies = []
    for step, peer in enumerate(cube_all(b)):
        cp = remote(src, into.at[slot_of(b)], ss.at[step], rs.at[step], peer)
        cp.start()
        copies.append(cp)
    return copies


def wait_small(b, into, ss, rs, copies):
    me = slot_of(b)
    for step in range(15):
        came = into.at[lax.rem(me + 15 - step, 16)]
        remote(came, came, ss.at[step], rs.at[step], device(b)).wait_recv()
    for cp in copies:
        cp.wait_send()


def live_rows(b, length):
    row = lax.broadcasted_iota(jnp.int32, (128, 1), 0)
    start = (row_of(b) * 8 + device(b)["context"]) * 64
    limit = jnp.where(row < 64, length[0], length[1])
    return start + lax.rem(row, 64) < limit


def inverse_rms(values):
    return lax.rsqrt(jnp.mean(values * values, axis=-1, keepdims=True) + norm_epsilon)


def first_body(
    length, tokens, gain, index, w_query, w_key, w_value, w_gate, w_up, rel_bias, onehot_t, h1, picks_all, w3, wg, wu, dist, staged, heads, wide, picks, *sems
):
    b = spot()
    head = slot_of(b)
    loads = []
    for n, w in enumerate((w_query, w_key, w_value)):
        at = pl.multiple_of((head // 2) * 128, 128)
        loads.append(pltpu.make_async_copy(w.at[:, pl.ds(at, 128)], heads.at[n], sems[8].at[n]))
    offsets = []
    for n, w in enumerate((w_gate, w_gate, w_up, w_up)):
        share = b["h"] * 4 + (n % 2) * 2 + b["x"]
        block = (share * 352) // 128 - share // 7
        offsets.append(share * 352 - block * 128)
        at = pl.multiple_of(block * 128, 128)
        loads.append(
            pltpu.make_async_copy(w.at[:, pl.ds(at, 512)], wide.at[n], sems[8].at[3 + n])
        )
    for cp in loads:
        cp.start()
    for s in range(2):
        rows = tokens[s].astype(F32)
        staged[s] = (rows * inverse_rms(rows) * gain[...]).astype(BF)
    f = expert_frame(b)
    choices = jnp.where(live_rows(b, length), index[...].astype(F32), -1.0)
    at = lane((128, 128))
    choices = jnp.where(at == 0, choices[:, 0:1], jnp.where(at == 1, choices[:, 1:2], 0.0))
    picks[...] = choices.T[0:8]
    greet([device(flip(b, [n])) for n in ("h", "x", "y", "l", "k")] + cube_rest(f))
    steps = sequence_steps(b, h1, staged, sems[0:4], sems[9:13], sems[4], sems[5])
    next(steps)
    copies = send_small(f, picks, picks_all, sems[6], sems[7])
    picks_all[slot_of(f)] = picks[...]
    column = jnp.sum(jnp.where(lane((32, 16)) == head, rel_bias[...], 0.0), axis=1, keepdims=True)
    column = column - column[31:32]
    row = jnp.sum(column * onehot_t[...], axis=0, keepdims=True)
    dist[...] = jnp.broadcast_to(row, (8, 2 * TILE))
    for cp in loads:
        cp.wait()
    next(steps)
    left = lane((1024, 128)) < 64
    for n in range(3):
        turned = pltpu.roll(heads[n].astype(F32), lax.rem(head, 2) * 64, 1)
        w3[:, n * 128 : n * 128 + 128] = jnp.where(left, turned, 0.0).astype(BF)
        next(steps)
    for n in range(4):
        out = wg if n < 2 else wu
        for r in range(0, 1024, 256):
            turned = pltpu.roll(wide[n, r : r + 256].astype(F32), 512 - offsets[n], 1)
            at = (n % 2) * 352
            out[r : r + 256, at : at + 352] = turned[:, :352].astype(BF)
        next(steps)
    for _ in steps:
        pass
    wait_small(f, picks_all, sems[6], sems[7], copies)


def lane(shape_, dim=1):
    return lax.broadcasted_iota(jnp.int32, shape_, dim)


def near_tiles(row):
    wide = jnp.broadcast_to(row, (TILE, 2 * TILE))
    wide = pltpu.roll(wide, 0, 1, stride=1, stride_axis=0)
    later = lax.broadcasted_iota(jnp.int32, (TILE, TILE), 0) > lane((TILE, TILE))
    return [jnp.where(later, BIG, wide[:, :TILE]), wide[:, TILE:]]


def pack_halves(rows):
    n = rows.shape[0] // 64
    four = rows.reshape(n, 2, 32, 128)
    return jnp.where(
        lax.broadcasted_iota(jnp.int32, (n, 32, 128), 2) < 64,
        four[:, 0],
        pltpu.roll(four[:, 1].reshape(n * 32, 128), 64, 1).reshape(n, 32, 128),
    )


def device_of(s, head):
    return (head // 4) * 8 + s * 4 + head % 4


def unpack_halves(first, second):
    a = first.astype(F32)
    c = second.astype(F32)
    left = lane((32, 128)) < 64
    top = jnp.where(left, a, pltpu.roll(c, 64, 1))
    bottom = jnp.where(left, pltpu.roll(a, 64, 1), c)
    return top.astype(BF), bottom.astype(BF)


def everyone(b, src, dst_at, ss, rs):
    me, peers = world_all(b)
    copies = []
    for step, (j, peer) in enumerate(peers):
        cp = remote(src.at[j], dst_at(me), ss.at[step], rs.at[step], peer)
        cp.start()
        copies.append(cp)
    return me, copies


def everyone_wait(b, me, dst_at, ss, rs, copies):
    for step in range(31):
        came = dst_at(lax.rem(me + 31 - step, 32))
        remote(came, came, ss.at[step], rs.at[step], device(b)).wait_recv()
    for cp in copies:
        cp.wait_send()


def attend_body(
    length, h1, w3, dist, cot, tokens, w_out, gain, router, out_t, qs, ks, vs, lse, dy, middle, h2_all, gates_all, joined, strip, v_t, weights, packed, land, gates, w_buf, load, *sems
):
    b = spot()
    me, peers = world_all(b)
    greet_start([peer for _, peer in peers])
    fetch = pltpu.make_async_copy(w_out, w_buf, load)
    fetch.start()
    f = expert_frame(b)
    dy[slot_of(f)] = cot[0:64]
    limit = length[b["h"]]
    for i in range(8):
        rows = slice(i * TILE, (i + 1) * TILE)
        p = jnp.dot(h1[rows], w3[...], preferred_element_type=F32)
        spot_lane = lane((TILE, 128))
        where_at = lax.broadcasted_iota(jnp.int32, (TILE, 128), 0) + i * TILE
        one = spot_lane == 64
        qs[rows] = jnp.where(one, 1.0, p[:, :128] * 0.125).astype(BF)
        ks[rows] = jnp.where(one & (where_at >= limit), BIG, p[:, 128:256]).astype(BF)
        v = jnp.where(one, 1.0, p[:, 256:]).astype(BF)
        vs[rows] = v
        v_t[:, rows] = v.astype(F32).T.astype(BF)
        if i == 3:
            greet_end(31)
            steps = gather_steps(f, group_view(dy, 0, 64), *sems[4:8], parts=TWO)
            next(steps)
    next(steps)
    near = near_tiles(dist[0:1])
    for i in range(8):
        cols = slice(i * TILE, (i + 1) * TILE)
        q = qs[cols]
        top = None
        for j in range(i + 1):
            rows = slice(j * TILE, (j + 1) * TILE)
            s = lax.dot_general(ks[rows], q, NT, preferred_element_type=F32)
            if i - j < 2:
                s = s + near[i - j]
            strip[rows] = s
            m = jnp.max(s, axis=0, keepdims=True)
            top = m if top is None else jnp.maximum(top, m)
        for j in range(i + 1):
            rows = slice(j * TILE, (j + 1) * TILE)
            weights[rows] = jnp.exp(strip[rows] - top).astype(BF)
        n = (i + 1) * TILE
        o = jnp.dot(v_t[:, :n], weights[:n], preferred_element_type=F32)
        total = o[64:65]
        o = o / total
        lse[:, cols] = jnp.broadcast_to(top + jnp.log(total), (8, TILE))
        out_t[:, cols] = o[:64]
        packed[4 * i : 4 * i + 4] = pack_halves(o.T).astype(BF)
        for j in range(4 * i, 4 * i + 4):

            @pl.when(me != j)
            def _(j=j):
                peer = {"experts": j // 8, "context": j % 8}
                remote(packed.at[j], land.at[me], sems[8].at[j], sems[9].at[me], peer).start()

        for _ in range((0, 0, 1, 1, 1, 1, 2, 1)[i]):
            next(steps)
    land[me] = packed[me]
    fetch.wait()
    for j in range(32):

        @pl.when(me != j)
        def _(j=j):
            peer = {"experts": j // 8, "context": j % 8}
            remote(packed.at[j], land.at[j], sems[8].at[j], sems[9].at[j], peer).wait()

    for s in range(2):
        for pair in range(8):
            top, bottom = unpack_halves(
                land[device_of(s, 2 * pair)], land[device_of(s, 2 * pair + 1)]
            )
            cols = slice(pair * 128, pair * 128 + 128)
            joined[s * 64 : s * 64 + 32, cols] = top
            joined[s * 64 + 32 : s * 64 + 64, cols] = bottom
    x = tokens[...].astype(F32)
    mid = x + jnp.dot(joined[...], w_buf[...], preferred_element_type=F32)
    h2 = (mid * inverse_rms(mid) * gain[...]).astype(BF)
    h2_all[slot_of(f)] = h2
    steps = gather_steps(f, group_view(h2_all), *sems[0:4], parts=FOUR)
    next(steps)
    middle[...] = mid
    rest = router[...]
    logits = jnp.zeros((128, 4), F32)
    for _ in range(3):
        part = rest.astype(BF)
        rest = rest - part.astype(F32)
        logits = logits + jnp.dot(h2, part, preferred_element_type=F32)
    at = lane((128, 128))
    spread = jnp.zeros((128, 128), F32)
    for e in range(4):
        spread = jnp.where(at == e, logits[:, e : e + 1], spread)
    logits = spread.T[0:8]
    real = lax.broadcasted_iota(jnp.int32, (8, 128), 0) < 4
    logits = jnp.where(real, logits, BIG)
    g = jnp.exp(logits - jnp.max(logits, axis=0, keepdims=True))
    gates[...] = g / jnp.sum(g, axis=0, keepdims=True)
    small = send_small(f, gates, gates_all, sems[10], sems[11])
    gates_all[slot_of(f)] = gates[...]
    for _ in steps:
        pass
    wait_small(f, gates_all, sems[10], sems[11], small)


def spread_start(b, blocks, pieces, ss, rs):
    col = col_of(b)
    copies = []
    for i, names in enumerate((["x", "l"], ["x"], ["l"])):
        there = flip(b, names)
        cp = remote(blocks.at[col_of(there)], pieces.at[col], ss.at[i], rs.at[i], device(there))
        cp.start()
        copies.append(cp)
    pieces[col] = blocks[col]
    return copies


def spread_end(b, blocks, pieces, ss, rs, copies):
    for i, names in enumerate((["x", "l"], ["x"], ["l"])):
        there = flip(b, names)
        ref = pieces.at[col_of(there)]
        remote(ref, ref, ss.at[i], rs.at[i], device(there)).wait_recv()
    for cp in copies:
        cp.wait_send()


def norm_back_rows(values, gain, grad_in):
    inverse = inverse_rms(values)
    normed = values * inverse
    scaled = grad_in * gain
    out = inverse * (scaled - normed * jnp.mean(scaled * normed, axis=-1, keepdims=True))
    return out, jnp.sum(grad_in * normed, axis=0, keepdims=True)


def split_halves(rows):
    top, bottom = rows[:32], rows[32:]
    left = lane((32, 128)) < 64
    first = jnp.where(left, top, pltpu.roll(bottom, 64, 1))
    second = jnp.where(left, pltpu.roll(top, 64, 1), bottom)
    return first.astype(BF), second.astype(BF)


def expert_body(
    h2, dy0, cot, gates, picks, wg, wu, w_down, length, middle, gain, router_t, joined, w_out, routed, near_g, near_u, down, do_all, dmid, smalls, gwo, dy, rows, grad, dexp, weight, hid, dgs, dus, acts, slopes, outs, drs, dws, wd, w_buf, far_g, far_u, far_d, got_g, got_u, got_d, acc, landing, dgates, dg_all, parcels, load, *sems
):
    b = expert_frame(spot())
    h = b["h"]
    partner = device(flip(b, ["h"]))
    whoami, peers = world_all(b)
    greet_start([peer for _, peer in peers])
    fetches = [
        pltpu.make_async_copy(dy0, dy.at[:, pl.ds(0, 64)], load.at[0]),
        pltpu.make_async_copy(w_out, w_buf, load.at[3]),
    ]
    for n in range(2):
        at = pl.multiple_of((b["l"] * 4 + n * 2 + b["x"]) * 352, 32)
        fetches.append(
            pltpu.make_async_copy(
                w_down.at[pl.ds(at, 352)], wd.at[pl.ds(n * 352, 352)], load.at[1 + n]
            )
        )
    for cp in fetches:
        cp.start()
    dy[slot_of(b), 64:128] = cot[64:]
    mine = row_of(b)
    mine_f = mine.astype(F32)
    first = picks[:, 0, :]
    second = picks[:, 1, :]
    chosen = jnp.where((first == mine_f) | (second == mine_f), 1.0, 0.0)
    earlier = jnp.where(
        lax.broadcasted_iota(jnp.int32, (128, 128), 0) < lane((128, 128)), 1.0, 0.0
    )
    place = jnp.dot(chosen.astype(BF), earlier.astype(BF), preferred_element_type=F32)
    place = jnp.where((chosen > 0.5) & (place < PLACES), place, -1.0)
    place_t = jnp.concatenate([place, jnp.full((112, 128), -1.0, F32)], axis=0).T
    level = lax.broadcasted_iota(jnp.int32, (PLACES, 128), 0).astype(F32)
    level_t = lane((128, PLACES)).astype(F32)
    is_mine = lax.broadcasted_iota(jnp.int32, (8, 128), 0) == mine
    for m in range(16):
        at = slice(m * PLACES, (m + 1) * PLACES)
        hit = jnp.where(level == place[m : m + 1], 1.0, 0.0)
        rows[at] = jnp.dot(hit.astype(BF), h2[m], preferred_element_type=F32).astype(BF)
        gate_row = jnp.sum(jnp.where(is_mine, gates[m], 0.0), axis=0, keepdims=True)
        w = jnp.sum(hit * gate_row, axis=1, keepdims=True)
        weight[at] = jnp.broadcast_to(w, (PLACES, 128))
        if m == 7:
            greet_end(31)
            steps = gather_steps(b, group_view(dy, 64, 64), *sems[0:4], parts=TWO)
            next(steps)
    for cp in fetches:
        cp.wait()
    next(steps)
    c0 = math.sqrt(2.0 / math.pi)
    c1 = 0.044715
    for i in range(5):
        at = slice(i * TILE, (i + 1) * TILE)
        r = rows[at]
        gp = jnp.dot(r, wg[...], preferred_element_type=F32)
        up = jnp.dot(r, wu[...], preferred_element_type=F32)
        sq = gp * gp
        th = jnp.tanh(c0 * gp * (1.0 + c1 * sq))
        half = 0.5 * (1.0 + th)
        act = gp * half
        slope = half + 0.5 * gp * (1.0 - th * th) * (c0 * (1.0 + 3.0 * c1 * sq))
        acts[at] = act.astype(BF)
        slopes[at] = (up * slope).astype(BF)
        hd = (act * up).astype(BF)
        hid[at] = hd
        outs[at] = jnp.dot(hd, wd[...], preferred_element_type=F32).astype(BF)
        for _ in range((1, 1, 2, 2, 1)[i]):
            next(steps)
    for m in range(16):
        at = slice(m * PLACES, (m + 1) * PLACES)
        hit = jnp.where(level == place[m : m + 1], 1.0, 0.0).astype(BF)
        g = jnp.dot(hit, dy[m], preferred_element_type=F32)
        grad[at] = g.astype(BF)
        dexp[at] = (weight[at, 0:1] * g).astype(BF)
    whole_down = lax.dot_general(hid[...], dexp[...], TN, preferred_element_type=F32).astype(BF)
    upper = h == 1
    far_d[...] = jnp.where(upper, whole_down[:352], whole_down[352:])
    down[...] = jnp.where(upper, whole_down[352:], whole_down[:352])
    trades = [
        remote(src, dst, sems[16].at[n], sems[17].at[n], partner)
        for n, (src, dst) in enumerate(((far_d, got_d), (far_g, got_g), (far_u, got_u)))
    ]
    trades[0].start()
    for i in range(5):
        at = slice(i * TILE, (i + 1) * TILE)
        o = outs[at].astype(F32)
        dws[at] = jnp.broadcast_to(
            jnp.sum(grad[at].astype(F32) * o, axis=1, keepdims=True), (TILE, 128)
        )
        outs[at] = (weight[at, 0:1] * o).astype(BF)
        dh = lax.dot_general(dexp[at], wd[...], NT, preferred_element_type=F32)
        dg = (dh * slopes[at].astype(F32)).astype(BF)
        du = (dh * acts[at].astype(F32)).astype(BF)
        dgs[at] = dg
        dus[at] = du
        drs[at] = (
            lax.dot_general(dg, wg[...], NT, preferred_element_type=F32)
            + lax.dot_general(du, wu[...], NT, preferred_element_type=F32)
        ).astype(BF)
    for m in range(16):
        at = slice(m * PLACES, (m + 1) * PLACES)
        back = jnp.where(place_t[:, m : m + 1] == level_t, 1.0, 0.0).astype(BF)
        dy[m] = jnp.dot(back, drs[at], preferred_element_type=F32).astype(BF)
        hit = jnp.where(level == place[m : m + 1], 1.0, 0.0)
        dgates[m] = jnp.broadcast_to(
            jnp.sum(hit * dws[at], axis=0, keepdims=True), (8, 128)
        )
    me = slot_of(b)
    steps = scatter_steps(b, dy, acc, landing, *sems[4:8], cuts=LATE)
    next(steps)
    copies = []
    for step, peer in enumerate(cube_all(b)):
        s = lax.rem(me + step + 1, 16)
        cp = remote(dgates.at[s], dg_all.at[me], sems[8].at[step], sems[9].at[step], peer)
        cp.start()
        copies.append(cp)
    dg_all[me] = dgates[me]

    def weight_grad(side, grads_in):
        first = pl.multiple_of(side * 256, 256)
        second = pl.multiple_of(512 + side * 256, 256)
        return [
            lax.dot_general(rows[:, pl.ds(at, 256)], grads_in[...], TN, preferred_element_type=F32)
            .astype(BF)
            for at in (first, second)
        ]

    far_g[0:256], far_g[256:512] = weight_grad(1 - h, dgs)
    trades[1].start()
    next(steps)
    far_u[0:256], far_u[256:512] = weight_grad(1 - h, dus)
    trades[2].start()
    next(steps)
    near_g[0:256], near_g[256:512] = weight_grad(h, dgs)
    near_u[0:256], near_u[256:512] = weight_grad(h, dus)
    next(steps)
    for m in range(8):
        at = slice(m * PLACES, (m + 1) * PLACES)
        back = jnp.where(place_t[:, m : m + 1] == level_t, 1.0, 0.0).astype(BF)
        routed[m] = jnp.dot(back, outs[at], preferred_element_type=F32).astype(BF)
    next(steps)
    next(steps)
    wait_small(b, dg_all, sems[8], sems[9], copies)
    row_level = lax.broadcasted_iota(jnp.int32, (8, 128), 0)
    dg = jnp.zeros((8, 128), F32)
    for e in range(4):
        total = dg_all[4 * e] + dg_all[4 * e + 1] + dg_all[4 * e + 2] + dg_all[4 * e + 3]
        dg = jnp.where(row_level == e, total, dg)
    g = gates[me]
    dl_t = g * (dg - jnp.sum(g * dg, axis=0, keepdims=True))
    dl = jnp.concatenate([dl_t, jnp.zeros((120, 128), F32)], axis=0).T
    d_h2 = acc[eighth(b)].astype(F32)
    for e in range(4):
        d_h2 = d_h2 + dl[:, e : e + 1] * router_t[e : e + 1]
    grad_mid, grad_gain = norm_back_rows(middle[...], gain[...], d_h2)
    d_mid = jnp.where(live_rows(spot(), length), cot[...].astype(F32), 0.0) + grad_mid
    d_low = d_mid.astype(BF)
    d_o = lax.dot_general(d_low, w_buf[...], NT, preferred_element_type=F32)
    for s in range(2):
        for pair in range(8):
            rows_of = d_o[s * 64 : s * 64 + 64, pair * 128 : pair * 128 + 128]
            one, two = split_halves(rows_of)
            parcels[device_of(s, 2 * pair)] = one
            parcels[device_of(s, 2 * pair + 1)] = two

    def at_device(j):
        return do_all.at[j]

    whoami, sent = everyone(b, parcels, at_device, sems[10], sems[11])
    do_all[whoami] = parcels[whoami]
    dmid[...] = d_mid
    high = dl_t.astype(BF)
    rest = (dl_t - high.astype(F32)).astype(BF)
    own = h2[me]
    smalls[0:8] = jnp.dot(high, own, preferred_element_type=F32) + jnp.dot(
        rest, own, preferred_element_type=F32
    )
    smalls[4:5] = grad_gain
    grad_out = lax.dot_general(joined[...], d_low, TN, preferred_element_type=F32).astype(BF)
    gwo[...] = grad_out.reshape(16, 64, 1024)
    for m in range(8, 16):
        at = slice(m * PLACES, (m + 1) * PLACES)
        back = jnp.where(place_t[:, m : m + 1] == level_t, 1.0, 0.0).astype(BF)
        routed[m] = jnp.dot(back, outs[at], preferred_element_type=F32).astype(BF)
    everyone_wait(b, whoami, at_device, sems[10], sems[11], sent)
    for cp, own_part, came in zip(trades, (down, near_g, near_u), (got_d, got_g, got_u)):
        cp.wait()
        own_part[...] = (own_part[...].astype(F32) + came[...].astype(F32)).astype(BF)


def back_body(
    h1, do_all, qs, ks, vs, out_t, lse, dist, onehot, gwo, tokens, dmid, gain, part, middle, length, routed_in, half_g_in, half_u_in, w_query, w_key, w_value, dtokens, result, whole, whole_o, smalls, gain_out, wide_u, wide_g, dos, k_t, delta, p_buf, s_buf, dq_t, dk, dv, near0, near1, left, acc_o, landing_o, packed, grads, wo, land, other, other_o, joined, crowd, mine, half_g, half_u, pieces_g, pieces_u, acc, landing, routed, wq, wk, wv, load, *sems
):
    b = spot()
    partner = device(flip(b, ["h"]))
    h = b["h"]
    f = expert_frame(b)
    me, peers = world_all(b)
    greet_start([peer for _, peer in peers])
    pairs = (
        (half_g_in, half_g),
        (half_u_in, half_u),
        (routed_in, routed),
        (w_query, wq),
        (w_key, wk),
        (w_value, wv),
    )
    loads = [pltpu.make_async_copy(src, dst, load.at[n]) for n, (src, dst) in enumerate(pairs)]
    for cp in loads:
        cp.start()
    live = lax.broadcasted_iota(jnp.int32, (4, 32, 128), 2) < 64
    for i in range(8):
        rows = slice(i * TILE, (i + 1) * TILE)
        both = do_all[4 * i : 4 * i + 4].astype(F32)
        turned = pltpu.roll(both.reshape(128, 128), 64, 1).reshape(4, 32, 128)
        d = jnp.concatenate(
            [jnp.where(live, both, 0.0)[:, None], jnp.where(live, turned, 0.0)[:, None]], axis=1
        ).reshape(TILE, 128)
        dos[rows] = d.astype(BF)
        delta[:, rows] = jnp.broadcast_to(
            jnp.sum(d.T[:64] * out_t[:, rows], axis=0, keepdims=True), (8, TILE)
        )
        kt = ks[rows].astype(F32).T
        k_t[:, rows] = jnp.where(
            lax.broadcasted_iota(jnp.int32, (128, TILE), 0) == 64, 1.0, kt
        ).astype(BF)
    greet_end(31)
    steps = scatter_steps(b, gwo, acc_o, landing_o, *sems[28:32])
    next(steps)
    loads[0].wait()
    spread_g = spread_start(f, half_g, pieces_g, sems[14], sems[15])
    near = near_tiles(dist[0:1])
    near0[...] = jnp.zeros_like(near0)
    near1[...] = jnp.zeros_like(near1)
    for i in range(8):
        cols = slice(i * TILE, (i + 1) * TILE)
        q = qs[cols]
        do = dos[cols]
        level = lse[0:1, cols]
        dl = delta[0:1, cols]
        for j in range(i + 1):
            rows = slice(j * TILE, (j + 1) * TILE)
            s = lax.dot_general(ks[rows], q, NT, preferred_element_type=F32)
            if i - j < 2:
                s = s + near[i - j]
            p = jnp.exp(s - level)
            dp = lax.dot_general(vs[rows], do, NT, preferred_element_type=F32)
            ds = (p * (dp - dl)).astype(BF)
            p_buf[rows] = p.astype(BF)
            s_buf[rows] = ds
            if i == j:
                near0[...] += ds.astype(F32)
            if i - j == 1:
                near1[...] += ds.astype(F32)
        n = (i + 1) * TILE
        dq_t[:, cols] = jnp.dot(k_t[:, :n], s_buf[:n], preferred_element_type=F32)
        new_v = jnp.dot(p_buf[:n], do, preferred_element_type=F32)
        new_k = jnp.dot(s_buf[:n], q, preferred_element_type=F32)
        if i > 0:
            dv[: n - TILE] += new_v[: n - TILE]
            dk[: n - TILE] += new_k[: n - TILE]
        dv[n - TILE : n] = new_v[n - TILE :]
        dk[n - TILE : n] = new_k[n - TILE :]
        if i in (2, 5, 7):
            next(steps)
    total = jnp.sum(dq_t[64:65, :].reshape(1, 16, 128), axis=1)
    skew = jnp.concatenate([near0[...], near1[...]], axis=1)
    level_u = lax.broadcasted_iota(jnp.int32, (TILE, 2 * TILE), 0)
    for bit in range(8):
        moved = pltpu.roll(skew, 2 * TILE - (1 << bit), 1)
        skew = jnp.where((level_u // (1 << bit)) % 2 == 1, moved, skew)
    by_distance = jnp.broadcast_to(jnp.sum(skew, axis=0, keepdims=True), (8, 2 * TILE))
    buckets = jnp.dot(by_distance, onehot[...], precision=highest)
    spot_lane = lane((8, 128))
    others = jnp.sum(jnp.where(spot_lane < 31, buckets, 0.0), axis=1, keepdims=True)
    whole_sum = jnp.sum(total, axis=1, keepdims=True)
    buckets = jnp.where(spot_lane == 31, whole_sum - others, buckets)
    row = jnp.concatenate([buckets, jnp.zeros((8, 384), F32)], axis=1)
    row = pltpu.roll(row, slot_of(b) * 32, 1)
    small = jnp.concatenate(
        [part[0:5], jnp.concatenate([row[0:3], jnp.zeros((3, 512), F32)], axis=1)], axis=0
    )
    high = small.astype(BF)
    wo[64:72] = high
    wo[72:80] = (small - high.astype(F32)).astype(BF)
    for i in range(8):
        rows = slice(i * TILE, (i + 1) * TILE)
        dq = dq_t[:, rows] * 0.125
        vk = jnp.where(lane((TILE, 128)) < 64, dv[rows], pltpu.roll(dk[rows], 64, 1)).T
        left[0:64, rows] = dq[:64].astype(BF)
        left[64:128, rows] = vk[64:128].astype(BF)
        left[128:192, rows] = vk[0:64].astype(BF)
        blocks = slice(4 * i, 4 * i + 4)
        packed[blocks, 0:32] = pack_halves(dq.T).astype(BF)
        packed[blocks, 32:64] = pack_halves(dk[rows]).astype(BF)
        packed[blocks, 64:96] = pack_halves(dv[rows]).astype(BF)
    grads[...] = (
        jnp.dot(left[...], h1[...], preferred_element_type=F32).astype(BF).reshape(2, 96, 1024)
    )
    trade = remote(grads.at[1 - h], other, sems[8].at[0], sems[9].at[0], partner)
    trade.start()
    next(steps)

    def at(j):
        return land.at[j]

    def view_of(side):
        def view(v, c0, cn):
            return whole.at[side, slot_of(v), :, pl.ds(c0, cn)]

        return view

    me_slot = slot_of(b)
    next(steps)
    wo[0:64] = acc_o[eighth(b)]
    trade_o = remote(wo, other_o, sems[8].at[2], sems[9].at[2], partner)
    trade.wait()
    whole[h, me_slot] = (grads[h].astype(F32) + other[...].astype(F32)).astype(BF)
    share = remote(
        whole.at[h, me_slot], whole.at[h, me_slot], sems[8].at[1], sems[9].at[1], partner
    )
    share.start()
    trade_o.start()
    near = gather_steps(b, view_of(h), *sems[0:4])
    next(near)
    me, copies = everyone(b, packed, at, sems[10], sems[11])
    land[me] = packed[me]
    for cp in loads[1:]:
        cp.wait()
    spread_u = spread_start(f, half_u, pieces_u, sems[12], sems[13])
    tokens_back = scatter_steps(f, routed, acc, landing, *sems[24:28], cuts=LATE)
    next(tokens_back)
    next(near)
    spread_end(f, half_g, pieces_g, sems[14], sems[15], spread_g)
    for i in range(4):
        for side in range(2):
            at0 = ((i // 2) * 4 + side * 2 + i % 2) * 352
            wide_g[:, at0 : at0 + 352] = pieces_g[i, :, side * 352 : side * 352 + 352]
    next(near)
    theirs = whole.at[1 - h, me_slot]
    remote(theirs, theirs, sems[8].at[1], sems[9].at[1], partner).wait_recv()
    far = gather_steps(b, view_of(1 - h), *sems[4:8])
    next(far)
    trade_o.wait()
    whole_o[me_slot] = (wo[...].astype(F32) + other_o[...].astype(F32)).astype(BF)
    outs = gather_steps(b, group_view(whole_o, 0, 80), *sems[18:22])
    next(outs)

    def tokens_done():
        everyone_wait(b, me, at, sems[10], sems[11], copies)
        for kind in range(3):
            for s in range(2):
                for pair in range(8):
                    j0, j1 = device_of(s, 2 * pair), device_of(s, 2 * pair + 1)
                    span = slice(kind * 32, kind * 32 + 32)
                    top, bottom = unpack_halves(land[j0, span], land[j1, span])
                    cols = slice(pair * 128, pair * 128 + 128)
                    joined[kind, s * 64 : s * 64 + 32, cols] = top
                    joined[kind, s * 64 + 32 : s * 64 + 64, cols] = bottom
        d_h1 = (
            lax.dot_general(joined[0], wq[...], NT, preferred_element_type=F32)
            + lax.dot_general(joined[1], wk[...], NT, preferred_element_type=F32)
            + lax.dot_general(joined[2], wv[...], NT, preferred_element_type=F32)
        )
        grad_in, grad_gain = norm_back_rows(tokens[...].astype(F32), gain[...], d_h1)
        dtokens[...] = dmid[...] + grad_in
        mine[...] = grad_gain.reshape(8, 128)
        sent = []
        for step, (j, peer) in enumerate(world_all(b)[1]):
            cp = remote(mine, crowd.at[me], sems[22].at[step], sems[23].at[step], peer)
            cp.start()
            sent.append(cp)
        crowd[me] = mine[...]
        return sent

    sent = []
    for n in range(7):
        if n % 2 == 0:
            next(tokens_back)
        next(near, None)
        next(far)
        next(outs)
        if n == TOKENS_AT:
            sent = tokens_done()
    next(tokens_back)
    spread_end(f, half_u, pieces_u, sems[12], sems[13], spread_u)
    for i in range(4):
        for side in range(2):
            at0 = ((i // 2) * 4 + side * 2 + i % 2) * 352
            wide_u[:, at0 : at0 + 352] = pieces_u[i, :, side * 352 : side * 352 + 352]
    next(outs)
    next(far)
    total = whole_o[0, 64:80].astype(F32)
    for n in range(1, 16):
        total = total + whole_o[n, 64:80].astype(F32)
    smalls[...] = total[0:8] + total[8:16]
    share.wait_send()
    routed_rows = acc[eighth(f)].astype(F32)
    result[...] = jnp.where(live_rows(b, length), middle[...] + routed_rows, 0.0).astype(BF)
    everyone_wait(b, me, lambda j: crowd.at[j], sems[22], sems[23], sent)
    gain_out[...] = jnp.sum(crowd[...], axis=0)


def dense_body(whole, whole_o, grad_q, grad_k, grad_v, grad_o):
    sides = (whole[0].astype(F32), whole[1].astype(F32))
    spans = (
        (grad_q, ((0, 0, 64),)),
        (grad_k, ((0, 64, 96), (1, 0, 32))),
        (grad_v, ((1, 32, 96),)),
    )
    for out, parts in spans:
        pieces = []
        for head in range(2):
            for side, lo, hi in parts:
                pieces.append(sides[side][head, lo:hi])
        rows = jnp.concatenate(pieces, axis=0)
        for c in range(0, 1024, 128):
            out[c : c + 128, :] = rows[:, c : c + 128].T
    grad_o[...] = whole_o[:, 0:64, :].reshape(128, 1024).astype(F32)


def distance_buckets():
    table = []
    for distance in range(2 * TILE):
        table.append(bucket_of(distance, 32, MAXDIST))
    return np.array(table, np.int32)


def on_device_fast(
    tokens,
    lengths,
    expert_index,
    cotangent,
    norm_attn,
    w_query,
    w_key,
    w_value,
    w_out,
    rel_bias,
    norm_ffn,
    router,
    w_gate,
    w_up,
    w_down,
):
    dma = pltpu.SemaphoreType.DMA
    gain_attn = norm_attn.reshape(1, 1024)
    gain_ffn = norm_ffn.reshape(1, 1024)
    flat = tokens.reshape(128, 1024)
    cot = cotangent.reshape(128, 1024)

    buckets = distance_buckets()
    onehot = np.zeros((2 * TILE, 128), np.float32)
    onehot[np.arange(2 * TILE), buckets] = 1.0
    router_t = jnp.pad(router.T, ((0, 4), (0, 0)))

    h1, picks_all, w3, wg, wu, dist = call(
        first_body,
        [
            shape((4, 2, 4, 64, 1024)),
            shape((16, 8, 128), F32),
            shape((1024, 384)),
            shape((1024, SHARE)),
            shape((1024, SHARE)),
            shape((8, 2 * TILE), F32),
        ],
        [VMEM((2, 64, 1024), BF), VMEM((3, 1024, 128), BF), VMEM((4, 1024, 512), BF), VMEM((8, 128), F32)]
        + CUBE_SEMS
        + [dma(()), dma(()), dma((15,)), dma((15,)), dma((7,))]
        + CUBE_SEMS,
        1,
        lengths,
        tokens,
        gain_attn,
        expert_index.reshape(128, 2),
        w_query,
        w_key,
        w_value,
        w_gate[0],
        w_up[0],
        rel_bias,
        jnp.asarray(onehot.T[:32]),
        anywhere=(4, 5, 6, 7, 8),
        scalars=(0,),
    )
    h1 = h1.reshape(2048, 1024)
    out_t, qs, ks, vs, lse, dy0, middle, h2_all, gates_all, joined = call(
        attend_body,
        [
            shape((64, 2048), F32),
            shape((2048, 128)),
            shape((2048, 128)),
            shape((2048, 128)),
            shape((8, 2048), F32),
            shape((16, 64, 1024)),
            shape((128, 1024), F32),
            shape((16, 128, 1024)),
            shape((16, 8, 128), F32),
            shape((128, 1024)),
        ],
        [
            VMEM((2048, TILE), F32),
            VMEM((128, 2048), BF),
            VMEM((2048, TILE), BF),
            VMEM((32, 32, 128), BF),
            VMEM((32, 32, 128), BF),
            VMEM((8, 128), F32),
            VMEM((1024, 1024), BF),
            dma(()),
        ]
        + FOUR_SEMS
        + TWO_SEMS
        + [dma((32,)), dma((32,)), dma((15,)), dma((15,))],
        2,
        lengths,
        h1,
        w3,
        dist,
        cot,
        flat,
        w_out,
        gain_ffn,
        router,
        scalars=(0,),
        anywhere=(6,),
    )
    routed, near_g, near_u, down, do_all, dmid, smalls, gwo = call(
        expert_body,
        [
            shape((16, 128, 1024)),
            shape((512, SHARE)),
            shape((512, SHARE)),
            shape((352, 1024)),
            shape((32, 32, 128)),
            shape((128, 1024), F32),
            shape((8, 1024), F32),
            shape((16, 64, 1024)),
        ],
        [VMEM((16, 128, 1024), BF)]
        + [VMEM((1280, 1024), BF)] * 3
        + [VMEM((1280, 128), F32)]
        + [VMEM((1280, SHARE), BF)] * 5
        + [VMEM((1280, 1024), BF)] * 2
        + [VMEM((1280, 128), F32)]
        + [VMEM((SHARE, 1024), BF), VMEM((1024, 1024), BF)]
        + [VMEM((512, SHARE), BF), VMEM((512, SHARE), BF), VMEM((352, 1024), BF)] * 2
        + [VMEM((8, 128, 1024), BF)] * 2
        + [VMEM((16, 8, 128), F32)] * 2
        + [VMEM((32, 32, 128), BF)]
        + [dma((4,))]
        + TWO_SEMS
        + CUBE_SEMS
        + [dma((15,)), dma((15,)), dma((31,)), dma((31,))]
        + [dma(())] * 4
        + [dma((3,))] * 2,
        3,
        h2_all,
        dy0,
        cot,
        gates_all,
        picks_all,
        wg,
        wu,
        w_down[0],
        lengths,
        middle,
        gain_ffn,
        router_t,
        joined,
        w_out,
        anywhere=(1, 7, 13),
        scalars=(8,),
    )
    dtokens, result, whole, whole_o, smalls, gain_out, wide_u, wide_g = call(
        back_body,
        [
            shape((128, 1024), F32),
            shape((128, 1024)),
            shape((2, 16, 96, 1024)),
            shape((16, 80, 1024)),
            shape((8, 1024), F32),
            shape((8, 128), F32),
            shape((128, 2816)),
            shape((128, 2816)),
        ],
        [
            VMEM((2048, 128), BF),
            VMEM((128, 2048), BF),
            VMEM((8, 2048), F32),
            VMEM((2048, TILE), BF),
            VMEM((2048, TILE), BF),
            VMEM((128, 2048), F32),
            VMEM((2048, 128), F32),
            VMEM((2048, 128), F32),
            VMEM((TILE, TILE), F32),
            VMEM((TILE, TILE), F32),
            VMEM((192, 2048), BF),
            VMEM((8, 64, 1024), BF),
            VMEM((8, 64, 1024), BF),
            VMEM((32, 96, 128), BF),
            VMEM((2, 96, 1024), BF),
            VMEM((80, 1024), BF),
            VMEM((32, 96, 128), BF),
            VMEM((96, 1024), BF),
            VMEM((80, 1024), BF),
            VMEM((3, 128, 1024), BF),
            VMEM((32, 8, 128), F32),
            VMEM((8, 128), F32),
            VMEM((4, 128, SHARE), BF),
            VMEM((4, 128, SHARE), BF),
            VMEM((4, 128, SHARE), BF),
            VMEM((4, 128, SHARE), BF),
            VMEM((8, 128, 1024), BF),
            VMEM((8, 128, 1024), BF),
            VMEM((16, 128, 1024), BF),
            VMEM((1024, 1024), BF),
            VMEM((1024, 1024), BF),
            VMEM((1024, 1024), BF),
            dma((6,)),
        ]
        + CUBE_SEMS
        + CUBE_SEMS
        + [dma((3,)), dma((3,)), dma((31,)), dma((31,)), dma((5,)), dma((5,)), dma((6,)), dma((6,))]
        + [dma((3,)), dma((3,))]
        + CUBE_SEMS
        + [dma((31,)), dma((31,))]
        + CUBE_SEMS
        + CUBE_SEMS,
        4,
        h1,
        do_all,
        qs,
        ks,
        vs,
        out_t,
        lse,
        dist,
        jnp.asarray(onehot),
        gwo,
        flat,
        dmid,
        gain_attn,
        smalls,
        middle,
        lengths,
        routed,
        near_g.reshape(4, 128, SHARE),
        near_u.reshape(4, 128, SHARE),
        w_query,
        w_key,
        w_value,
        anywhere=tuple(range(16, 22)),
        scalars=(15,),
    )
    grad_q, grad_k, grad_v, grad_o = pl.pallas_call(
        dense_body,
        grid=(8,),
        out_shape=[shape((1024, 1024), F32)] * 4,
        in_specs=[
            pl.BlockSpec((2, 2, 96, 1024), lambda i: (0, i, 0, 0)),
            pl.BlockSpec((2, 80, 1024), lambda i: (i, 0, 0)),
        ],
        out_specs=[pl.BlockSpec((1024, 128), lambda i: (0, i))] * 3
        + [pl.BlockSpec((128, 1024), lambda i: (i, 0))],
        compiler_params=params(),
        cost_estimate=pl.CostEstimate(flops=0, bytes_accessed=25 * 2**20, transcendentals=0),
    )(whole, whole_o)
    return (
        result.reshape(2, 64, 1024),
        dtokens.reshape(2, 64, 1024),
        gain_out.reshape(1024),
        grad_q,
        grad_k,
        grad_v,
        grad_o,
        smalls[5, :512].reshape(16, 32).T,
        smalls[4],
        smalls[0:4].T,
        wide_g[None].astype(F32),
        wide_u[None].astype(F32),
        down[None].astype(F32),
    )


def solution(mesh):
    sizes = dict(mesh.shape)
    fits = sizes == {"experts": 4, "context": 8}
    placed = (
        P(None, ("experts", "context"), None),
        P(),
        P(None, ("experts", "context"), None),
        P(None, ("experts", "context"), None),
        P(),
        P(),
        P(),
        P(),
        P(),
        P(),
        P(),
        P(),
        P("experts", None, None),
        P("experts", None, None),
        P("experts", None, None),
    )
    return jax.shard_map(
        on_device_fast if fits else on_device,
        mesh=mesh,
        in_specs=placed,
        out_specs=(
            P(None, ("experts", "context"), None),
            P(None, ("experts", "context"), None),
            P(),
            P(),
            P(),
            P(),
            P(),
            P(),
            P(),
            P(),
            P("experts", "context", None),
            P("experts", "context", None),
            P("experts", "context", None),
        ),
        check_vma=False,
    )
```

```python
import math

import jax
import jax.numpy as jnp
import numpy as np
from jax import lax
from jax.experimental import pallas as pl
from jax.experimental.pallas import tpu as pltpu
from jax.sharding import PartitionSpec as P

MAXDIST = 128


norm_epsilon = 1e-06
mask_fill = -1e30
highest = lax.Precision.HIGHEST


def bucket_of(distance, bucket_count, reach):
    exact = bucket_count // 2
    if distance < exact:
        return distance
    level = exact + int(
        math.log(distance / exact) / math.log(reach / exact) * (bucket_count - exact)
    )
    return min(level, bucket_count - 1)


def bucket_edges(bucket_count, reach):
    edges = []
    for level in range(1, bucket_count):
        distance = 0
        while bucket_of(distance, bucket_count, reach) < level:
            distance += 1
        edges.append(distance)
    return edges


def relative_bucket(query_pos, key_pos, bucket_count):
    distance = jnp.maximum(query_pos[:, None] - key_pos[None, :], 0)
    bucket = jnp.zeros(distance.shape, jnp.int32)
    for edge in bucket_edges(bucket_count, MAXDIST):
        bucket = bucket + (distance >= edge).astype(jnp.int32)
    return bucket


def rms_norm(values, gain):
    inverse = lax.rsqrt(jnp.mean(values * values, axis=-1, keepdims=True) + norm_epsilon)
    return values * inverse * gain


def norm_back(values, gain, grad_in):
    inverse = lax.rsqrt(jnp.mean(values * values, axis=-1, keepdims=True) + norm_epsilon)
    normed = values * inverse
    grad_normed = grad_in * gain
    grad_values = inverse * (
        grad_normed - normed * jnp.mean(grad_normed * normed, axis=-1, keepdims=True)
    )
    return (grad_values, jnp.sum(grad_in * normed, 0))


def score_block(query_rows, key_rows, rel_bias, query_pos, key_pos, lengths, score_scale):
    raw_scores = (
        jnp.einsum("sqhd,skhd->sqhk", query_rows, key_rows, preferred_element_type=jnp.float32)
        * score_scale
    )
    bucket = relative_bucket(query_pos, key_pos, rel_bias.shape[0])
    onehot = (bucket[:, :, None] == jnp.arange(rel_bias.shape[0], dtype=jnp.int32)).astype(
        jnp.float32
    )
    bias_rows = jnp.einsum("qkb,bh->qhk", onehot, rel_bias, precision=highest)
    causal = (key_pos[None, :] <= query_pos[:, None])[None]
    inside = key_pos[None, None, :] < lengths[:, None, None]
    allowed = (causal & inside)[:, :, None, :]
    return (raw_scores + bias_rows[None], allowed, onehot)


def pair_grads(query_set, key_set, rel_bias, lengths, score_scale):
    query_rows, grad_rows, log_total, delta, query_pos = query_set
    key_rows, value_rows, key_pos = key_set
    scores, allowed, onehot = score_block(
        query_rows, key_rows, rel_bias, query_pos, key_pos, lengths, score_scale
    )
    weights = jnp.where(allowed, jnp.exp(scores - log_total[..., None]), 0.0)
    grad_value = jnp.einsum(
        "sqhk,sqhd->skhd",
        weights.astype(jnp.bfloat16),
        grad_rows,
        preferred_element_type=jnp.float32,
    )
    grad_weights = jnp.einsum(
        "sqhd,skhd->sqhk", grad_rows, value_rows, preferred_element_type=jnp.float32
    )
    grad_scores = (weights * (grad_weights - delta[..., None])).astype(jnp.bfloat16)
    grad_query = score_scale * jnp.einsum(
        "sqhk,skhd->sqhd", grad_scores, key_rows, preferred_element_type=jnp.float32
    )
    grad_key = score_scale * jnp.einsum(
        "sqhk,sqhd->skhd", grad_scores, query_rows, preferred_element_type=jnp.float32
    )
    grad_table = jnp.einsum(
        "sqhk,qkb->bh", grad_scores, onehot.astype(jnp.bfloat16), preferred_element_type=jnp.float32
    )
    return (grad_query, grad_key, grad_value, grad_table)


def dispatch_table(expert_index, live_rows, expert_count, capacity):
    picked = expert_index.reshape(-1)
    live_pairs = jnp.broadcast_to(live_rows[:, :, None], expert_index.shape).reshape(-1)
    chosen = (
        (picked[:, None] == jnp.arange(expert_count, dtype=jnp.int32)[None, :])
        & live_pairs[:, None]
    ).astype(jnp.int32)
    earlier = jnp.cumsum(chosen, axis=0) - chosen
    position_in = jnp.sum(earlier * chosen, -1)
    kept_pairs = live_pairs & (position_in < capacity)
    slot_of = jnp.where(kept_pairs, picked * capacity + position_in, -1)
    matches = slot_of[None, :] == jnp.arange(expert_count * capacity, dtype=jnp.int32)[:, None]
    table = jnp.any(matches.reshape(expert_count * capacity, -1, 2), -1).astype(jnp.float32)
    slot_ids = jnp.arange(expert_count * capacity, dtype=jnp.int32) // capacity
    slot_expert = (slot_ids[:, None] == jnp.arange(expert_count, dtype=jnp.int32)[None, :]).astype(
        jnp.float32
    )
    return (table, slot_expert)


def on_device(
    tokens,
    lengths,
    expert_index,
    cotangent,
    norm_attn,
    w_query,
    w_key,
    w_value,
    w_out,
    rel_bias,
    norm_ffn,
    router,
    w_gate,
    w_up,
    w_down,
):
    slot_count, per_slot, model_width = tokens.shape
    head_count = rel_bias.shape[1]
    head_size = model_width // head_count
    expert_count = router.shape[1]
    capacity = (10 * slot_count * per_slot + 4 * expert_count - 1) // (4 * expert_count)
    score_scale = head_size ** (-0.5)
    row_count = slot_count * per_slot
    shape_four = (slot_count, per_slot, head_count, head_size)
    shape_three = (slot_count, per_slot, model_width)
    device_at = lax.axis_index(("experts", "context"))
    positions = device_at * per_slot + jnp.arange(per_slot, dtype=jnp.int32)
    live_rows = positions[None, :] < lengths[:, None]
    keep_mask = live_rows.reshape(row_count, 1).astype(jnp.float32)
    inputs = tokens.reshape(row_count, model_width).astype(jnp.float32)
    normed = rms_norm(inputs, norm_attn).astype(jnp.bfloat16)
    query_flat = jnp.dot(normed, w_query, preferred_element_type=jnp.float32).astype(jnp.bfloat16)
    key_flat = jnp.dot(normed, w_key, preferred_element_type=jnp.float32).astype(jnp.bfloat16)
    value_flat = jnp.dot(normed, w_value, preferred_element_type=jnp.float32).astype(jnp.bfloat16)
    query_four = query_flat.reshape(shape_four)
    key_four = key_flat.reshape(shape_four)
    value_four = value_flat.reshape(shape_four)
    key_three = key_flat.reshape(shape_three)
    value_three = value_flat.reshape(shape_three)
    start_state = (
        jnp.zeros(shape_four, jnp.float32),
        jnp.full((slot_count, per_slot, head_count), mask_fill, jnp.float32),
        jnp.zeros((slot_count, per_slot, head_count), jnp.float32),
    )
    offset = jnp.int32(0)
    key_all = lax.all_gather(key_three, ("experts", "context"), axis=1, tiled=True)
    value_all = lax.all_gather(value_three, ("experts", "context"), axis=1, tiled=True)
    piece_rows = key_all.shape[1]
    block_rows = math.gcd(piece_rows, 8 * per_slot)

    def forward_visit(carried, block_id):
        running, running_max, denominator = carried
        local_at = block_id * block_rows
        key_rows = lax.dynamic_slice_in_dim(key_all, local_at, block_rows, 1).reshape(
            slot_count, block_rows, head_count, head_size
        )
        value_rows = lax.dynamic_slice_in_dim(value_all, local_at, block_rows, 1).reshape(
            slot_count, block_rows, head_count, head_size
        )
        key_pos = offset + local_at + jnp.arange(block_rows, dtype=jnp.int32)
        scores, allowed, _ = score_block(
            query_four, key_rows, rel_bias, positions, key_pos, lengths, score_scale
        )
        scores = jnp.where(allowed, scores, mask_fill)
        new_max = jnp.maximum(running_max, jnp.max(scores, -1))
        factor = jnp.exp(running_max - new_max)
        weights = jnp.where(allowed, jnp.exp(scores - new_max[..., None]), 0.0)
        denominator = denominator * factor + jnp.sum(weights, -1)
        running = running * factor[..., None] + jnp.einsum(
            "sqhk,skhd->sqhd",
            weights.astype(jnp.bfloat16),
            value_rows,
            preferred_element_type=jnp.float32,
        )
        return ((running, new_max, denominator), None)

    carried, _ = lax.scan(
        forward_visit, start_state, jnp.arange(piece_rows // block_rows, dtype=jnp.int32)
    )
    running, running_max, denominator = carried
    attended = running / denominator[..., None]
    log_total = running_max + jnp.log(denominator)
    attended_low = attended.reshape(row_count, model_width).astype(jnp.bfloat16)
    middle = inputs + jnp.dot(attended_low, w_out, preferred_element_type=jnp.float32)
    second_low = rms_norm(middle, norm_ffn).astype(jnp.bfloat16)
    second_wide = second_low.astype(jnp.float32)
    logits = jnp.dot(second_wide, router, precision=highest)
    gates = jax.nn.softmax(logits, axis=-1)
    table, slot_expert = dispatch_table(expert_index, live_rows, expert_count, capacity)
    table_low = table.astype(jnp.bfloat16)
    dispatched = jnp.dot(table_low, second_low, preferred_element_type=jnp.float32).astype(
        jnp.bfloat16
    )
    arrived = lax.all_to_all(
        dispatched.reshape(expert_count, capacity, model_width),
        "experts",
        split_axis=0,
        concat_axis=1,
        tiled=True,
    )[0]
    gate_pre = jnp.dot(arrived, w_gate[0], preferred_element_type=jnp.float32)
    up_pre = jnp.dot(arrived, w_up[0], preferred_element_type=jnp.float32)
    hidden_low = (jax.nn.gelu(gate_pre, approximate=True) * up_pre).astype(jnp.bfloat16)
    produced = jnp.dot(hidden_low, w_down[0], preferred_element_type=jnp.float32).astype(
        jnp.bfloat16
    )
    returned = lax.all_to_all(
        produced[None], "experts", split_axis=1, concat_axis=0, tiled=True
    ).reshape(expert_count * capacity, model_width)
    returned_wide = returned.astype(jnp.float32)
    slot_weight = jnp.sum(jnp.dot(table, gates, precision=highest) * slot_expert, -1)
    routed = jnp.dot(table.T, slot_weight[:, None] * returned_wide, precision=highest)
    result = ((middle + routed) * keep_mask).astype(jnp.bfloat16).reshape(shape_three)
    grad_result = cotangent.reshape(row_count, model_width).astype(jnp.float32) * keep_mask
    gathered_grad = jnp.dot(table, grad_result, precision=highest)
    grad_produced = (
        (slot_weight[:, None] * gathered_grad)
        .astype(jnp.bfloat16)
        .reshape(expert_count, capacity, model_width)
    )
    grad_arrived_out = lax.all_to_all(
        grad_produced, "experts", split_axis=0, concat_axis=1, tiled=True
    )[0]
    grad_slot_weight = jnp.sum(gathered_grad * returned_wide, -1)
    grad_hidden = jnp.dot(grad_arrived_out, w_down[0].T, preferred_element_type=jnp.float32)
    grad_w_down = jnp.dot(hidden_low.T, grad_arrived_out, preferred_element_type=jnp.float32)

    def activation(gate_in, up_in):
        return jax.nn.gelu(gate_in, approximate=True) * up_in

    _, activation_back = jax.vjp(activation, gate_pre, up_pre)
    grad_gate_pre, grad_up_pre = activation_back(grad_hidden)
    grad_gate_low = grad_gate_pre.astype(jnp.bfloat16)
    grad_up_low = grad_up_pre.astype(jnp.bfloat16)
    grad_w_gate = jnp.dot(arrived.T, grad_gate_low, preferred_element_type=jnp.float32)
    grad_w_up = jnp.dot(arrived.T, grad_up_low, preferred_element_type=jnp.float32)
    grad_arrived = (
        jnp.dot(grad_gate_low, w_gate[0].T, preferred_element_type=jnp.float32)
        + jnp.dot(grad_up_low, w_up[0].T, preferred_element_type=jnp.float32)
    ).astype(jnp.bfloat16)
    grad_returned = lax.all_to_all(
        grad_arrived[None], "experts", split_axis=1, concat_axis=0, tiled=True
    ).reshape(expert_count * capacity, model_width)
    expert_sums = (
        lax.psum_scatter(
            grad_w_gate[None].astype(jnp.bfloat16), "context", scatter_dimension=1, tiled=True
        ).astype(jnp.float32),
        lax.psum_scatter(
            grad_w_up[None].astype(jnp.bfloat16), "context", scatter_dimension=1, tiled=True
        ).astype(jnp.float32),
        lax.psum_scatter(
            grad_w_down[None].astype(jnp.bfloat16), "context", scatter_dimension=1, tiled=True
        ).astype(jnp.float32),
    )
    grad_second = jnp.dot(table_low.T, grad_returned, preferred_element_type=jnp.float32)
    grad_gates = jnp.dot(table.T, grad_slot_weight[:, None] * slot_expert, precision=highest)
    grad_logits = gates * (grad_gates - jnp.sum(gates * grad_gates, -1, keepdims=True))
    grad_router = jnp.dot(second_wide.T, grad_logits, precision=highest)
    grad_second = grad_second + jnp.dot(grad_logits, router.T, precision=highest)
    grad_middle_norm, grad_norm_ffn = norm_back(middle, norm_ffn, grad_second)
    grad_middle = grad_result + grad_middle_norm
    grad_middle_low = grad_middle.astype(jnp.bfloat16)
    grad_w_out = jnp.dot(attended_low.T, grad_middle_low, preferred_element_type=jnp.float32)
    grad_attended_low = jnp.dot(
        grad_middle_low, w_out.T, preferred_element_type=jnp.float32
    ).astype(jnp.bfloat16)
    grad_attended_four = grad_attended_low.reshape(shape_four)
    grad_attended_three = grad_attended_low.reshape(shape_three)
    delta = jnp.sum(grad_attended_four.astype(jnp.float32) * attended, -1)
    local_queries = (query_four, grad_attended_four, log_total, delta, positions)
    grad_start = (jnp.zeros(shape_four, jnp.float32), jnp.zeros(rel_bias.shape, jnp.float32))
    query_offset = jnp.int32(0)
    query_key_all = lax.all_gather(key_three, ("experts", "context"), axis=1, tiled=True)
    query_value_all = lax.all_gather(value_three, ("experts", "context"), axis=1, tiled=True)
    piece_rows = query_key_all.shape[1]
    query_block_rows = math.gcd(piece_rows, 8 * per_slot)

    def query_visit(carried, block_id):
        local_at = block_id * query_block_rows
        key_rows = lax.dynamic_slice_in_dim(query_key_all, local_at, query_block_rows, 1).reshape(
            slot_count, query_block_rows, head_count, head_size
        )
        value_rows = lax.dynamic_slice_in_dim(
            query_value_all, local_at, query_block_rows, 1
        ).reshape(slot_count, query_block_rows, head_count, head_size)
        key_pos = query_offset + local_at + jnp.arange(query_block_rows, dtype=jnp.int32)
        grad_query, _, _, grad_table = pair_grads(
            local_queries, (key_rows, value_rows, key_pos), rel_bias, lengths, score_scale
        )
        return ((carried[0] + grad_query, carried[1] + grad_table), None)

    carried, _ = lax.scan(
        query_visit, grad_start, jnp.arange(piece_rows // query_block_rows, dtype=jnp.int32)
    )
    grad_query_four, grad_table = carried
    log_whole, delta_whole = (
        lax.all_gather(log_total, ("experts", "context"), axis=1, tiled=True),
        lax.all_gather(delta, ("experts", "context"), axis=1, tiled=True),
    )
    local_keys = (key_four, value_four, positions)
    zero_four = jnp.zeros(shape_four, jnp.float32)
    key_offset = jnp.int32(0)
    query_all = lax.all_gather(
        query_flat.reshape(shape_three), ("experts", "context"), axis=1, tiled=True
    )
    grad_all = lax.all_gather(grad_attended_three, ("experts", "context"), axis=1, tiled=True)
    piece_rows = query_all.shape[1]
    key_block_rows = math.gcd(piece_rows, 8 * per_slot)

    def key_visit(carried, block_id):
        local_at = block_id * key_block_rows
        whole_at = key_offset + local_at
        query_rows = lax.dynamic_slice_in_dim(query_all, local_at, key_block_rows, 1).reshape(
            slot_count, key_block_rows, head_count, head_size
        )
        grad_rows = lax.dynamic_slice_in_dim(grad_all, local_at, key_block_rows, 1).reshape(
            slot_count, key_block_rows, head_count, head_size
        )
        log_rows = lax.dynamic_slice_in_dim(log_whole, whole_at, key_block_rows, 1)
        delta_rows = lax.dynamic_slice_in_dim(delta_whole, whole_at, key_block_rows, 1)
        query_pos = whole_at + jnp.arange(key_block_rows, dtype=jnp.int32)
        _, grad_key, grad_value, _ = pair_grads(
            (query_rows, grad_rows, log_rows, delta_rows, query_pos),
            local_keys,
            rel_bias,
            lengths,
            score_scale,
        )
        return ((carried[0] + grad_key, carried[1] + grad_value), None)

    carried, _ = lax.scan(
        key_visit, (zero_four, zero_four), jnp.arange(piece_rows // key_block_rows, dtype=jnp.int32)
    )
    grad_key_four, grad_value_four = carried
    grad_query_low = grad_query_four.reshape(row_count, model_width).astype(jnp.bfloat16)
    grad_key_low = grad_key_four.reshape(row_count, model_width).astype(jnp.bfloat16)
    grad_value_low = grad_value_four.reshape(row_count, model_width).astype(jnp.bfloat16)
    grad_w_query = jnp.dot(normed.T, grad_query_low, preferred_element_type=jnp.float32)
    grad_w_key = jnp.dot(normed.T, grad_key_low, preferred_element_type=jnp.float32)
    grad_w_value = jnp.dot(normed.T, grad_value_low, preferred_element_type=jnp.float32)
    grad_normed = (
        jnp.dot(grad_query_low, w_query.T, preferred_element_type=jnp.float32)
        + jnp.dot(grad_key_low, w_key.T, preferred_element_type=jnp.float32)
        + jnp.dot(grad_value_low, w_value.T, preferred_element_type=jnp.float32)
    )
    grad_input_norm, grad_norm_attn = norm_back(inputs, norm_attn, grad_normed)
    grad_tokens = (grad_middle + grad_input_norm).reshape(shape_three)
    dense = lax.psum(
        (
            grad_norm_attn,
            grad_w_query,
            grad_w_key,
            grad_w_value,
            grad_w_out,
            grad_table,
            grad_norm_ffn,
            grad_router,
        ),
        ("experts", "context"),
    )
    return (
        result,
        grad_tokens,
        dense[0],
        dense[1],
        dense[2],
        dense[3],
        dense[4],
        dense[5],
        dense[6],
        dense[7],
        expert_sums[0],
        expert_sums[1],
        expert_sums[2],
    )


MESH = pl.DeviceIdType.MESH
BF = jnp.bfloat16
F32 = jnp.float32
VMEM = pltpu.VMEM
THREE = (
    (("x", "y", "l"), 0, 384),
    (("y", "l", "x"), 384, 384),
    (("l", "x", "y"), 768, 256),
)
TWO = ((("l", "x", "y"), 0, 512), (("l", "y", "x"), 512, 512))
FOUR = tuple((("l", "x", "y") if n % 2 == 0 else ("l", "y", "x"), n * 256, 256) for n in range(4))
LAST_Y = ((("l", "x", "y"), 0, 512), (("x", "l", "y"), 512, 512))
LATE = ((("x", "y", "l"), 0, 512), (("y", "x", "l"), 512, 512))
BY_Y = ((("l", "x", "y"), 0, 1024),)
BY_X = ((("l", "y", "x"), 0, 1024),)
BIG = -1e30
TILE = 256
PLACES = 80
SHARE = 704
TOKENS_AT = 3
NT = (((1,), (1,)), ((), ()))
TN = (((0,), (0,)), ((), ()))
CUBE_SEMS = [pltpu.SemaphoreType.DMA((3, 8))] * 4
FOUR_SEMS = [pltpu.SemaphoreType.DMA((4, 8))] * 4
TWO_SEMS = [pltpu.SemaphoreType.DMA((2, 8))] * 4
ONE_SEMS = [pltpu.SemaphoreType.DMA((1, 8))] * 4


def spot():
    e = lax.axis_index("experts")
    c = lax.axis_index("context")
    return dict(
        k=lax.rem(e, 2), y=e // 2, x=lax.rem(c, 2), l=lax.rem(c // 2, 2), h=c // 4, swap=False
    )


def expert_frame(b):
    return dict(b, l=b["h"], h=b["l"], swap=True)


def flip(b, names):
    return {n: (1 - v if n in names else v) for n, v in b.items()}


def device(b):
    high, low = (b["l"], b["h"]) if b["swap"] else (b["h"], b["l"])
    return {"experts": b["y"] * 2 + b["k"], "context": high * 4 + low * 2 + b["x"]}


def row_of(b):
    return b["y"] * 2 + b["k"]


def col_of(b):
    return b["l"] * 2 + b["x"]


def slot_of(b):
    return row_of(b) * 4 + col_of(b)


def greet_start(peers):
    barrier = pltpu.get_barrier_semaphore()
    for peer in peers:
        pl.semaphore_signal(barrier, inc=1, device_id=peer, device_id_type=MESH)


def greet_end(count):
    pl.semaphore_wait(pltpu.get_barrier_semaphore(), count)


def greet(peers):
    greet_start(peers)
    greet_end(len(peers))


def cube_peers(b):
    return [device(flip(b, [n])) for n in ("x", "y", "l", "k")]


def cube_all(b):
    peers = []
    for step in range(1, 16):
        s = lax.rem(slot_of(b) + step, 16)
        peers.append(
            device(
                dict(
                    b,
                    y=s // 8,
                    k=lax.rem(s // 4, 2),
                    l=lax.rem(s // 2, 2),
                    x=lax.rem(s, 2),
                )
            )
        )
    return peers


def cube_rest(b):
    peers = []
    for t in range(1, 16):
        names = [n for i, n in enumerate(("x", "y", "l", "k")) if (t >> i) & 1]
        if len(names) > 1:
            peers.append(device(flip(b, names)))
    return peers


def world_all(b):
    me = row_of(b) * 8 + device(b)["context"]
    peers = []
    for step in range(1, 32):
        j = lax.rem(me + step, 32)
        peers.append((j, {"experts": j // 8, "context": lax.rem(j, 8)}))
    return me, peers


def remote(src, dst, ssem, rsem, peer):
    return pltpu.make_async_remote_copy(
        src_ref=src, dst_ref=dst, send_sem=ssem, recv_sem=rsem, device_id=peer, device_id_type=MESH
    )


def names_of(order, t):
    return [order[i] for i in range(3) if (t >> i) & 1]


def gather_steps(b, view, ss, rs, cs, cr, parts=THREE):
    started = []
    core = device(flip(b, ["k"]))
    every = range(len(parts))

    def piece(p, t, more=()):
        order, c0, cn = parts[p]
        return view(flip(b, names_of(order, t) + list(more)), c0, cn)

    def link(p, t, i):
        ref = piece(p, t)
        n = t | (1 << i)
        cp = remote(ref, ref, ss.at[p, n], rs.at[p, n], device(flip(b, [parts[p][0][i]])))
        cp.start()
        started.append(cp)

    def across(p, t):
        ref = piece(p, t)
        cp = remote(ref, ref, cs.at[p, t], cr.at[p, t], core)
        cp.start()
        started.append(cp)

    for i in range(3):
        for p in every:
            link(p, 0, i)
    for p in every:
        across(p, 0)
    yield
    for t in range(1, 8):
        for p in every:
            ref = piece(p, t)
            remote(ref, ref, ss.at[p, t], rs.at[p, t], core).wait_recv()
            for i in range(t.bit_length(), 3):
                link(p, t, i)
            across(p, t)
        yield
    for cp in started:
        cp.wait_send()
    for p in every:
        for t in range(8):
            ref = piece(p, t, ["k"])
            remote(ref, ref, cs.at[p, t], cr.at[p, t], core).wait_recv()
    yield


def gather_cube(*args):
    for _ in gather_steps(*args):
        pass


def eighth(b):
    return b["y"] * 4 + b["l"] * 2 + b["x"]


def scatter_steps(b, parts, acc, landing, ss, rs, cs, cr, cuts=THREE):
    started = []
    core = device(flip(b, ["k"]))
    dims = ("x", "y", "l")
    order = sorted(range(8), key=lambda t: -bin(t).count("1"))

    def set_of(t):
        return [n for i, n in enumerate(dims) if (t >> i) & 1]

    def push(p, step, others_set):
        dims_in_order, c0, cn = cuts[p]
        first = dims_in_order[step]
        others = dims_in_order[step + 1 :]
        there = flip(b, [first] + others_set)
        n = (1 << len(others)) + sum(1 << i for i, name in enumerate(others) if name in others_set)
        cp = remote(
            acc.at[eighth(there), :, pl.ds(c0, cn)],
            landing.at[n, :, pl.ds(c0, cn)],
            ss.at[p, n],
            rs.at[p, n],
            device(flip(b, [first])),
        )
        cp.start()
        started.append(cp)

    for t in order:
        there = flip(b, set_of(t) + ["k"])
        cp = remote(parts.at[slot_of(there)], acc.at[eighth(there)], cs.at[0, t], cr.at[0, t], core)
        cp.start()
        started.append(cp)
    yield
    for t in order:
        here = flip(b, set_of(t))
        n = eighth(here)
        remote(parts.at[slot_of(here)], acc.at[n], cs.at[0, t], cr.at[0, t], core).wait_recv()
        acc[n] = acc[n] + parts[slot_of(here)]
        for p in range(len(cuts)):
            first = cuts[p][0][0]
            if first in set_of(t):
                push(p, 0, [name for name in set_of(t) if name != first])
    yield
    for step in range(3):
        rest = 2 - step
        count = 1 << rest
        for t in range(count - 1, -1, -1):
            for p in range(len(cuts)):
                dims_in_order, c0, cn = cuts[p]
                others = dims_in_order[step + 1 :]
                names = [others[i] for i in range(rest) if (t >> i) & 1]
                target = eighth(flip(b, names))
                n = count + t
                ref = landing.at[n, :, pl.ds(c0, cn)]
                remote(ref, ref, ss.at[p, n], rs.at[p, n], core).wait_recv()
                acc[target, :, c0 : c0 + cn] = (
                    acc[target, :, c0 : c0 + cn] + landing[n, :, c0 : c0 + cn]
                )
                if rest and others[0] in names:
                    push(p, step + 1, [name for name in names if name != others[0]])
        yield
    for cp in started:
        cp.wait_send()
    yield


def scatter_cube(*args):
    for _ in scatter_steps(*args):
        pass


def params(cid=None, mib=60):
    if cid is None:
        return pltpu.CompilerParams(vmem_limit_bytes=mib * 2**20)
    return pltpu.CompilerParams(
        collective_id=cid, has_side_effects=True, vmem_limit_bytes=mib * 2**20
    )


def call(body, outs, scratch, cid, *args, anywhere=(), outs_anywhere=(), scalars=()):
    def spec(i, listed):
        if i in listed:
            return pl.BlockSpec(memory_space=pl.ANY)
        return pl.BlockSpec(memory_space=VMEM)

    return pl.pallas_call(
        body,
        out_shape=outs,
        in_specs=[
            pl.BlockSpec(memory_space=pltpu.SMEM) if i in scalars else spec(i, anywhere)
            for i in range(len(args))
        ],
        out_specs=[spec(i, outs_anywhere) for i in range(len(outs))],
        scratch_shapes=scratch,
        compiler_params=params(cid),
    )(*args)


def shape(dims, kind=BF):
    return jax.ShapeDtypeStruct(dims, kind)


def sequence_steps(b, whole, staged, own_sems, other_sems, hs, hr):
    partner = device(flip(b, ["h"]))
    mine = whole.at[row_of(b), b["h"], col_of(b)]
    cp = remote(staged.at[1 - b["h"]], mine, hs, hr, partner)
    cp.start()
    whole[row_of(b), b["h"], col_of(b)] = staged[b["h"]]

    def view_of(side):
        def view(v, c0, cn):
            return whole.at[row_of(v), side, col_of(v), :, pl.ds(c0, cn)]

        return view

    own = gather_steps(b, view_of(b["h"]), *own_sems)
    next(own)
    yield
    next(own)
    next(own)
    yield
    theirs = whole.at[row_of(b), 1 - b["h"], col_of(b)]
    remote(theirs, theirs, hs, hr, partner).wait_recv()
    other = gather_steps(b, view_of(1 - b["h"]), *other_sems)
    next(other)
    yield
    for _ in range(5):
        next(own)
        next(other)
        yield
    next(own)
    for _ in range(3):
        next(other)
        yield
    cp.wait_send()
    yield


def group_view(ref, r0=0, rn=128):
    def view(v, c0, cn):
        return ref.at[slot_of(v), pl.ds(r0, rn), pl.ds(c0, cn)]

    return view


def send_small(b, src, into, ss, rs):
    copies = []
    for step, peer in enumerate(cube_all(b)):
        cp = remote(src, into.at[slot_of(b)], ss.at[step], rs.at[step], peer)
        cp.start()
        copies.append(cp)
    return copies


def wait_small(b, into, ss, rs, copies):
    me = slot_of(b)
    for step in range(15):
        came = into.at[lax.rem(me + 15 - step, 16)]
        remote(came, came, ss.at[step], rs.at[step], device(b)).wait_recv()
    for cp in copies:
        cp.wait_send()


def live_rows(b, length):
    row = lax.broadcasted_iota(jnp.int32, (128, 1), 0)
    start = (row_of(b) * 8 + device(b)["context"]) * 64
    limit = jnp.where(row < 64, length[0], length[1])
    return start + lax.rem(row, 64) < limit


def inverse_rms(values):
    return lax.rsqrt(jnp.mean(values * values, axis=-1, keepdims=True) + norm_epsilon)


def first_body(
    length, tokens, gain, index, w_query, w_key, w_value, w_gate, w_up, rel_bias, onehot_t, h1, picks_all, w3, wg, wu, dist, staged, heads, wide, picks, *sems
):
    b = spot()
    head = slot_of(b)
    loads = []
    for n, w in enumerate((w_query, w_key, w_value)):
        at = pl.multiple_of((head // 2) * 128, 128)
        loads.append(pltpu.make_async_copy(w.at[:, pl.ds(at, 128)], heads.at[n], sems[8].at[n]))
    offsets = []
    for n, w in enumerate((w_gate, w_gate, w_up, w_up)):
        share = b["h"] * 4 + (n % 2) * 2 + b["x"]
        block = (share * 352) // 128 - share // 7
        offsets.append(share * 352 - block * 128)
        at = pl.multiple_of(block * 128, 128)
        loads.append(
            pltpu.make_async_copy(w.at[:, pl.ds(at, 512)], wide.at[n], sems[8].at[3 + n])
        )
    for cp in loads:
        cp.start()
    for s in range(2):
        rows = tokens[s].astype(F32)
        staged[s] = (rows * inverse_rms(rows) * gain[...]).astype(BF)
    f = expert_frame(b)
    choices = jnp.where(live_rows(b, length), index[...].astype(F32), -1.0)
    at = lane((128, 128))
    choices = jnp.where(at == 0, choices[:, 0:1], jnp.where(at == 1, choices[:, 1:2], 0.0))
    picks[...] = choices.T[0:8]
    greet([device(flip(b, [n])) for n in ("h", "x", "y", "l", "k")] + cube_rest(f))
    steps = sequence_steps(b, h1, staged, sems[0:4], sems[9:13], sems[4], sems[5])
    next(steps)
    copies = send_small(f, picks, picks_all, sems[6], sems[7])
    picks_all[slot_of(f)] = picks[...]
    column = jnp.sum(jnp.where(lane((32, 16)) == head, rel_bias[...], 0.0), axis=1, keepdims=True)
    column = column - column[31:32]
    row = jnp.sum(column * onehot_t[...], axis=0, keepdims=True)
    dist[...] = jnp.broadcast_to(row, (8, 2 * TILE))
    for cp in loads:
        cp.wait()
    next(steps)
    left = lane((1024, 128)) < 64
    for n in range(3):
        turned = pltpu.roll(heads[n].astype(F32), lax.rem(head, 2) * 64, 1)
        w3[:, n * 128 : n * 128 + 128] = jnp.where(left, turned, 0.0).astype(BF)
        next(steps)
    for n in range(4):
        out = wg if n < 2 else wu
        for r in range(0, 1024, 256):
            turned = pltpu.roll(wide[n, r : r + 256].astype(F32), 512 - offsets[n], 1)
            at = (n % 2) * 352
            out[r : r + 256, at : at + 352] = turned[:, :352].astype(BF)
        next(steps)
    for _ in steps:
        pass
    wait_small(f, picks_all, sems[6], sems[7], copies)


def lane(shape_, dim=1):
    return lax.broadcasted_iota(jnp.int32, shape_, dim)


def near_tiles(row):
    wide = jnp.broadcast_to(row, (TILE, 2 * TILE))
    wide = pltpu.roll(wide, 0, 1, stride=1, stride_axis=0)
    later = lax.broadcasted_iota(jnp.int32, (TILE, TILE), 0) > lane((TILE, TILE))
    return [jnp.where(later, BIG, wide[:, :TILE]), wide[:, TILE:]]


def pack_halves(rows):
    n = rows.shape[0] // 64
    four = rows.reshape(n, 2, 32, 128)
    return jnp.where(
        lax.broadcasted_iota(jnp.int32, (n, 32, 128), 2) < 64,
        four[:, 0],
        pltpu.roll(four[:, 1].reshape(n * 32, 128), 64, 1).reshape(n, 32, 128),
    )


def device_of(s, head):
    return (head // 4) * 8 + s * 4 + head % 4


def unpack_halves(first, second):
    a = first.astype(F32)
    c = second.astype(F32)
    left = lane((32, 128)) < 64
    top = jnp.where(left, a, pltpu.roll(c, 64, 1))
    bottom = jnp.where(left, pltpu.roll(a, 64, 1), c)
    return top.astype(BF), bottom.astype(BF)


def everyone(b, src, dst_at, ss, rs):
    me, peers = world_all(b)
    copies = []
    for step, (j, peer) in enumerate(peers):
        cp = remote(src.at[j], dst_at(me), ss.at[step], rs.at[step], peer)
        cp.start()
        copies.append(cp)
    return me, copies


def everyone_wait(b, me, dst_at, ss, rs, copies):
    for step in range(31):
        came = dst_at(lax.rem(me + 31 - step, 32))
        remote(came, came, ss.at[step], rs.at[step], device(b)).wait_recv()
    for cp in copies:
        cp.wait_send()


def attend_body(
    length, h1, w3, dist, cot, tokens, w_out, gain, router, out_t, qs, ks, vs, lse, dy, middle, h2_all, gates_all, joined, strip, v_t, weights, packed, land, gates, w_buf, load, *sems
):
    b = spot()
    me, peers = world_all(b)
    greet_start([peer for _, peer in peers])
    fetch = pltpu.make_async_copy(w_out, w_buf, load)
    fetch.start()
    f = expert_frame(b)
    dy[slot_of(f)] = cot[0:64]
    limit = length[b["h"]]
    for i in range(8):
        rows = slice(i * TILE, (i + 1) * TILE)
        p = jnp.dot(h1[rows], w3[...], preferred_element_type=F32)
        spot_lane = lane((TILE, 128))
        where_at = lax.broadcasted_iota(jnp.int32, (TILE, 128), 0) + i * TILE
        one = spot_lane == 64
        qs[rows] = jnp.where(one, 1.0, p[:, :128] * 0.125).astype(BF)
        ks[rows] = jnp.where(one & (where_at >= limit), BIG, p[:, 128:256]).astype(BF)
        v = jnp.where(one, 1.0, p[:, 256:]).astype(BF)
        vs[rows] = v
        v_t[:, rows] = v.astype(F32).T.astype(BF)
        if i == 3:
            greet_end(31)
            steps = gather_steps(f, group_view(dy, 0, 64), *sems[4:8], parts=TWO)
            next(steps)
    next(steps)
    near = near_tiles(dist[0:1])
    for i in range(8):
        cols = slice(i * TILE, (i + 1) * TILE)
        q = qs[cols]
        top = None
        for j in range(i + 1):
            rows = slice(j * TILE, (j + 1) * TILE)
            s = lax.dot_general(ks[rows], q, NT, preferred_element_type=F32)
            if i - j < 2:
                s = s + near[i - j]
            strip[rows] = s
            m = jnp.max(s, axis=0, keepdims=True)
            top = m if top is None else jnp.maximum(top, m)
        for j in range(i + 1):
            rows = slice(j * TILE, (j + 1) * TILE)
            weights[rows] = jnp.exp(strip[rows] - top).astype(BF)
        n = (i + 1) * TILE
        o = jnp.dot(v_t[:, :n], weights[:n], preferred_element_type=F32)
        total = o[64:65]
        o = o / total
        lse[:, cols] = jnp.broadcast_to(top + jnp.log(total), (8, TILE))
        out_t[:, cols] = o[:64]
        packed[4 * i : 4 * i + 4] = pack_halves(o.T).astype(BF)
        for j in range(4 * i, 4 * i + 4):

            @pl.when(me != j)
            def _(j=j):
                peer = {"experts": j // 8, "context": j % 8}
                remote(packed.at[j], land.at[me], sems[8].at[j], sems[9].at[me], peer).start()

        for _ in range((0, 0, 1, 1, 1, 1, 2, 1)[i]):
            next(steps)
    land[me] = packed[me]
    fetch.wait()
    for j in range(32):

        @pl.when(me != j)
        def _(j=j):
            peer = {"experts": j // 8, "context": j % 8}
            remote(packed.at[j], land.at[j], sems[8].at[j], sems[9].at[j], peer).wait()

    for s in range(2):
        for pair in range(8):
            top, bottom = unpack_halves(
                land[device_of(s, 2 * pair)], land[device_of(s, 2 * pair + 1)]
            )
            cols = slice(pair * 128, pair * 128 + 128)
            joined[s * 64 : s * 64 + 32, cols] = top
            joined[s * 64 + 32 : s * 64 + 64, cols] = bottom
    x = tokens[...].astype(F32)
    mid = x + jnp.dot(joined[...], w_buf[...], preferred_element_type=F32)
    h2 = (mid * inverse_rms(mid) * gain[...]).astype(BF)
    h2_all[slot_of(f)] = h2
    steps = gather_steps(f, group_view(h2_all), *sems[0:4], parts=FOUR)
    next(steps)
    middle[...] = mid
    rest = router[...]
    logits = jnp.zeros((128, 4), F32)
    for _ in range(3):
        part = rest.astype(BF)
        rest = rest - part.astype(F32)
        logits = logits + jnp.dot(h2, part, preferred_element_type=F32)
    at = lane((128, 128))
    spread = jnp.zeros((128, 128), F32)
    for e in range(4):
        spread = jnp.where(at == e, logits[:, e : e + 1], spread)
    logits = spread.T[0:8]
    real = lax.broadcasted_iota(jnp.int32, (8, 128), 0) < 4
    logits = jnp.where(real, logits, BIG)
    g = jnp.exp(logits - jnp.max(logits, axis=0, keepdims=True))
    gates[...] = g / jnp.sum(g, axis=0, keepdims=True)
    small = send_small(f, gates, gates_all, sems[10], sems[11])
    gates_all[slot_of(f)] = gates[...]
    for _ in steps:
        pass
    wait_small(f, gates_all, sems[10], sems[11], small)


def spread_start(b, blocks, pieces, ss, rs):
    col = col_of(b)
    copies = []
    for i, names in enumerate((["x", "l"], ["x"], ["l"])):
        there = flip(b, names)
        cp = remote(blocks.at[col_of(there)], pieces.at[col], ss.at[i], rs.at[i], device(there))
        cp.start()
        copies.append(cp)
    pieces[col] = blocks[col]
    return copies


def spread_end(b, blocks, pieces, ss, rs, copies):
    for i, names in enumerate((["x", "l"], ["x"], ["l"])):
        there = flip(b, names)
        ref = pieces.at[col_of(there)]
        remote(ref, ref, ss.at[i], rs.at[i], device(there)).wait_recv()
    for cp in copies:
        cp.wait_send()


def norm_back_rows(values, gain, grad_in):
    inverse = inverse_rms(values)
    normed = values * inverse
    scaled = grad_in * gain
    out = inverse * (scaled - normed * jnp.mean(scaled * normed, axis=-1, keepdims=True))
    return out, jnp.sum(grad_in * normed, axis=0, keepdims=True)


def split_halves(rows):
    top, bottom = rows[:32], rows[32:]
    left = lane((32, 128)) < 64
    first = jnp.where(left, top, pltpu.roll(bottom, 64, 1))
    second = jnp.where(left, pltpu.roll(top, 64, 1), bottom)
    return first.astype(BF), second.astype(BF)


def expert_body(
    h2, dy0, cot, gates, picks, wg, wu, w_down, length, middle, gain, router_t, joined, w_out, routed, near_g, near_u, down, do_all, dmid, smalls, gwo, dy, rows, grad, dexp, weight, hid, dgs, dus, acts, slopes, outs, drs, dws, wd, w_buf, far_g, far_u, far_d, got_g, got_u, got_d, acc, landing, dgates, dg_all, parcels, load, *sems
):
    b = expert_frame(spot())
    h = b["h"]
    partner = device(flip(b, ["h"]))
    whoami, peers = world_all(b)
    greet_start([peer for _, peer in peers])
    fetches = [
        pltpu.make_async_copy(dy0, dy.at[:, pl.ds(0, 64)], load.at[0]),
        pltpu.make_async_copy(w_out, w_buf, load.at[3]),
    ]
    for n in range(2):
        at = pl.multiple_of((b["l"] * 4 + n * 2 + b["x"]) * 352, 32)
        fetches.append(
            pltpu.make_async_copy(
                w_down.at[pl.ds(at, 352)], wd.at[pl.ds(n * 352, 352)], load.at[1 + n]
            )
        )
    for cp in fetches:
        cp.start()
    dy[slot_of(b), 64:128] = cot[64:]
    mine = row_of(b)
    mine_f = mine.astype(F32)
    first = picks[:, 0, :]
    second = picks[:, 1, :]
    chosen = jnp.where((first == mine_f) | (second == mine_f), 1.0, 0.0)
    earlier = jnp.where(
        lax.broadcasted_iota(jnp.int32, (128, 128), 0) < lane((128, 128)), 1.0, 0.0
    )
    place = jnp.dot(chosen.astype(BF), earlier.astype(BF), preferred_element_type=F32)
    place = jnp.where((chosen > 0.5) & (place < PLACES), place, -1.0)
    place_t = jnp.concatenate([place, jnp.full((112, 128), -1.0, F32)], axis=0).T
    level = lax.broadcasted_iota(jnp.int32, (PLACES, 128), 0).astype(F32)
    level_t = lane((128, PLACES)).astype(F32)
    is_mine = lax.broadcasted_iota(jnp.int32, (8, 128), 0) == mine
    for m in range(16):
        at = slice(m * PLACES, (m + 1) * PLACES)
        hit = jnp.where(level == place[m : m + 1], 1.0, 0.0)
        rows[at] = jnp.dot(hit.astype(BF), h2[m], preferred_element_type=F32).astype(BF)
        gate_row = jnp.sum(jnp.where(is_mine, gates[m], 0.0), axis=0, keepdims=True)
        w = jnp.sum(hit * gate_row, axis=1, keepdims=True)
        weight[at] = jnp.broadcast_to(w, (PLACES, 128))
        if m == 7:
            greet_end(31)
            steps = gather_steps(b, group_view(dy, 64, 64), *sems[0:4], parts=TWO)
            next(steps)
    for cp in fetches:
        cp.wait()
    next(steps)
    c0 = math.sqrt(2.0 / math.pi)
    c1 = 0.044715
    for i in range(5):
        at = slice(i * TILE, (i + 1) * TILE)
        r = rows[at]
        gp = jnp.dot(r, wg[...], preferred_element_type=F32)
        up = jnp.dot(r, wu[...], preferred_element_type=F32)
        sq = gp * gp
        th = jnp.tanh(c0 * gp * (1.0 + c1 * sq))
        half = 0.5 * (1.0 + th)
        act = gp * half
        slope = half + 0.5 * gp * (1.0 - th * th) * (c0 * (1.0 + 3.0 * c1 * sq))
        acts[at] = act.astype(BF)
        slopes[at] = (up * slope).astype(BF)
        hd = (act * up).astype(BF)
        hid[at] = hd
        outs[at] = jnp.dot(hd, wd[...], preferred_element_type=F32).astype(BF)
        for _ in range((1, 1, 2, 2, 1)[i]):
            next(steps)
    for m in range(16):
        at = slice(m * PLACES, (m + 1) * PLACES)
        hit = jnp.where(level == place[m : m + 1], 1.0, 0.0).astype(BF)
        g = jnp.dot(hit, dy[m], preferred_element_type=F32)
        grad[at] = g.astype(BF)
        dexp[at] = (weight[at, 0:1] * g).astype(BF)
    whole_down = lax.dot_general(hid[...], dexp[...], TN, preferred_element_type=F32).astype(BF)
    upper = h == 1
    far_d[...] = jnp.where(upper, whole_down[:352], whole_down[352:])
    down[...] = jnp.where(upper, whole_down[352:], whole_down[:352])
    trades = [
        remote(src, dst, sems[16].at[n], sems[17].at[n], partner)
        for n, (src, dst) in enumerate(((far_d, got_d), (far_g, got_g), (far_u, got_u)))
    ]
    trades[0].start()
    for i in range(5):
        at = slice(i * TILE, (i + 1) * TILE)
        o = outs[at].astype(F32)
        dws[at] = jnp.broadcast_to(
            jnp.sum(grad[at].astype(F32) * o, axis=1, keepdims=True), (TILE, 128)
        )
        outs[at] = (weight[at, 0:1] * o).astype(BF)
        dh = lax.dot_general(dexp[at], wd[...], NT, preferred_element_type=F32)
        dg = (dh * slopes[at].astype(F32)).astype(BF)
        du = (dh * acts[at].astype(F32)).astype(BF)
        dgs[at] = dg
        dus[at] = du
        drs[at] = (
            lax.dot_general(dg, wg[...], NT, preferred_element_type=F32)
            + lax.dot_general(du, wu[...], NT, preferred_element_type=F32)
        ).astype(BF)
    for m in range(16):
        at = slice(m * PLACES, (m + 1) * PLACES)
        back = jnp.where(place_t[:, m : m + 1] == level_t, 1.0, 0.0).astype(BF)
        dy[m] = jnp.dot(back, drs[at], preferred_element_type=F32).astype(BF)
        hit = jnp.where(level == place[m : m + 1], 1.0, 0.0)
        dgates[m] = jnp.broadcast_to(
            jnp.sum(hit * dws[at], axis=0, keepdims=True), (8, 128)
        )
    me = slot_of(b)
    steps = scatter_steps(b, dy, acc, landing, *sems[4:8], cuts=LATE)
    next(steps)
    copies = []
    for step, peer in enumerate(cube_all(b)):
        s = lax.rem(me + step + 1, 16)
        cp = remote(dgates.at[s], dg_all.at[me], sems[8].at[step], sems[9].at[step], peer)
        cp.start()
        copies.append(cp)
    dg_all[me] = dgates[me]

    def weight_grad(side, grads_in):
        first = pl.multiple_of(side * 256, 256)
        second = pl.multiple_of(512 + side * 256, 256)
        return [
            lax.dot_general(rows[:, pl.ds(at, 256)], grads_in[...], TN, preferred_element_type=F32)
            .astype(BF)
            for at in (first, second)
        ]

    far_g[0:256], far_g[256:512] = weight_grad(1 - h, dgs)
    trades[1].start()
    next(steps)
    far_u[0:256], far_u[256:512] = weight_grad(1 - h, dus)
    trades[2].start()
    next(steps)
    near_g[0:256], near_g[256:512] = weight_grad(h, dgs)
    near_u[0:256], near_u[256:512] = weight_grad(h, dus)
    next(steps)
    for m in range(8):
        at = slice(m * PLACES, (m + 1) * PLACES)
        back = jnp.where(place_t[:, m : m + 1] == level_t, 1.0, 0.0).astype(BF)
        routed[m] = jnp.dot(back, outs[at], preferred_element_type=F32).astype(BF)
    next(steps)
    next(steps)
    wait_small(b, dg_all, sems[8], sems[9], copies)
    row_level = lax.broadcasted_iota(jnp.int32, (8, 128), 0)
    dg = jnp.zeros((8, 128), F32)
    for e in range(4):
        total = dg_all[4 * e] + dg_all[4 * e + 1] + dg_all[4 * e + 2] + dg_all[4 * e + 3]
        dg = jnp.where(row_level == e, total, dg)
    g = gates[me]
    dl_t = g * (dg - jnp.sum(g * dg, axis=0, keepdims=True))
    dl = jnp.concatenate([dl_t, jnp.zeros((120, 128), F32)], axis=0).T
    d_h2 = acc[eighth(b)].astype(F32)
    for e in range(4):
        d_h2 = d_h2 + dl[:, e : e + 1] * router_t[e : e + 1]
    grad_mid, grad_gain = norm_back_rows(middle[...], gain[...], d_h2)
    d_mid = jnp.where(live_rows(spot(), length), cot[...].astype(F32), 0.0) + grad_mid
    d_low = d_mid.astype(BF)
    d_o = lax.dot_general(d_low, w_buf[...], NT, preferred_element_type=F32)
    for s in range(2):
        for pair in range(8):
            rows_of = d_o[s * 64 : s * 64 + 64, pair * 128 : pair * 128 + 128]
            one, two = split_halves(rows_of)
            parcels[device_of(s, 2 * pair)] = one
            parcels[device_of(s, 2 * pair + 1)] = two

    def at_device(j):
        return do_all.at[j]

    whoami, sent = everyone(b, parcels, at_device, sems[10], sems[11])
    do_all[whoami] = parcels[whoami]
    dmid[...] = d_mid
    high = dl_t.astype(BF)
    rest = (dl_t - high.astype(F32)).astype(BF)
    own = h2[me]
    smalls[0:8] = jnp.dot(high, own, preferred_element_type=F32) + jnp.dot(
        rest, own, preferred_element_type=F32
    )
    smalls[4:5] = grad_gain
    grad_out = lax.dot_general(joined[...], d_low, TN, preferred_element_type=F32).astype(BF)
    gwo[...] = grad_out.reshape(16, 64, 1024)
    for m in range(8, 16):
        at = slice(m * PLACES, (m + 1) * PLACES)
        back = jnp.where(place_t[:, m : m + 1] == level_t, 1.0, 0.0).astype(BF)
        routed[m] = jnp.dot(back, outs[at], preferred_element_type=F32).astype(BF)
    everyone_wait(b, whoami, at_device, sems[10], sems[11], sent)
    for cp, own_part, came in zip(trades, (down, near_g, near_u), (got_d, got_g, got_u)):
        cp.wait()
        own_part[...] = (own_part[...].astype(F32) + came[...].astype(F32)).astype(BF)


def back_body(
    h1, do_all, qs, ks, vs, out_t, lse, dist, onehot, gwo, tokens, dmid, gain, part, middle, length, routed_in, half_g_in, half_u_in, w_query, w_key, w_value, dtokens, result, whole, whole_o, smalls, gain_out, wide_u, wide_g, dos, k_t, delta, p_buf, s_buf, dq_t, dk, dv, near0, near1, left, acc_o, landing_o, packed, grads, wo, land, other, other_far, other_o, joined, crowd, mine, half_g, half_u, pieces_g, pieces_u, acc, landing, routed, wq, wk, wv, load, *sems
):
    b = spot()
    partner = device(flip(b, ["h"]))
    h = b["h"]
    f = expert_frame(b)
    me, peers = world_all(b)
    greet_start([peer for _, peer in peers])
    pairs = (
        (half_g_in, half_g),
        (half_u_in, half_u),
        (routed_in, routed),
        (w_query, wq),
        (w_key, wk),
        (w_value, wv),
    )
    loads = [pltpu.make_async_copy(src, dst, load.at[n]) for n, (src, dst) in enumerate(pairs)]
    for cp in loads:
        cp.start()
    live = lax.broadcasted_iota(jnp.int32, (4, 32, 128), 2) < 64
    for i in range(8):
        rows = slice(i * TILE, (i + 1) * TILE)
        both = do_all[4 * i : 4 * i + 4].astype(F32)
        turned = pltpu.roll(both.reshape(128, 128), 64, 1).reshape(4, 32, 128)
        d = jnp.concatenate(
            [jnp.where(live, both, 0.0)[:, None], jnp.where(live, turned, 0.0)[:, None]], axis=1
        ).reshape(TILE, 128)
        dos[rows] = d.astype(BF)
        delta[:, rows] = jnp.broadcast_to(
            jnp.sum(d.T[:64] * out_t[:, rows], axis=0, keepdims=True), (8, TILE)
        )
        kt = ks[rows].astype(F32).T
        k_t[:, rows] = jnp.where(
            lax.broadcasted_iota(jnp.int32, (128, TILE), 0) == 64, 1.0, kt
        ).astype(BF)
    greet_end(31)
    steps = scatter_steps(b, gwo, acc_o, landing_o, *sems[28:32])
    next(steps)
    loads[0].wait()
    spread_g = spread_start(f, half_g, pieces_g, sems[14], sems[15])
    near = near_tiles(dist[0:1])
    near0[...] = jnp.zeros_like(near0)
    near1[...] = jnp.zeros_like(near1)
    for i in range(8):
        cols = slice(i * TILE, (i + 1) * TILE)
        q = qs[cols]
        do = dos[cols]
        level = lse[0:1, cols]
        dl = delta[0:1, cols]
        for j in range(i + 1):
            rows = slice(j * TILE, (j + 1) * TILE)
            s = lax.dot_general(ks[rows], q, NT, preferred_element_type=F32)
            if i - j < 2:
                s = s + near[i - j]
            p = jnp.exp(s - level)
            dp = lax.dot_general(vs[rows], do, NT, preferred_element_type=F32)
            ds = (p * (dp - dl)).astype(BF)
            p_buf[rows] = p.astype(BF)
            s_buf[rows] = ds
            if i == j:
                near0[...] += ds.astype(F32)
            if i - j == 1:
                near1[...] += ds.astype(F32)
        n = (i + 1) * TILE
        dq_t[:, cols] = jnp.dot(k_t[:, :n], s_buf[:n], preferred_element_type=F32)
        new_v = jnp.dot(p_buf[:n], do, preferred_element_type=F32)
        new_k = jnp.dot(s_buf[:n], q, preferred_element_type=F32)
        if i > 0:
            dv[: n - TILE] += new_v[: n - TILE]
            dk[: n - TILE] += new_k[: n - TILE]
        dv[n - TILE : n] = new_v[n - TILE :]
        dk[n - TILE : n] = new_k[n - TILE :]
        if i in (2, 5, 7):
            next(steps)
    total = jnp.sum(dq_t[64:65, :].reshape(1, 16, 128), axis=1)
    skew = jnp.concatenate([near0[...], near1[...]], axis=1)
    level_u = lax.broadcasted_iota(jnp.int32, (TILE, 2 * TILE), 0)
    for bit in range(8):
        moved = pltpu.roll(skew, 2 * TILE - (1 << bit), 1)
        skew = jnp.where((level_u // (1 << bit)) % 2 == 1, moved, skew)
    by_distance = jnp.broadcast_to(jnp.sum(skew, axis=0, keepdims=True), (8, 2 * TILE))
    buckets = jnp.dot(by_distance, onehot[...], precision=highest)
    spot_lane = lane((8, 128))
    others = jnp.sum(jnp.where(spot_lane < 31, buckets, 0.0), axis=1, keepdims=True)
    whole_sum = jnp.sum(total, axis=1, keepdims=True)
    buckets = jnp.where(spot_lane == 31, whole_sum - others, buckets)
    row = jnp.concatenate([buckets, jnp.zeros((8, 384), F32)], axis=1)
    row = pltpu.roll(row, slot_of(b) * 32, 1)
    small = jnp.concatenate(
        [part[0:5], jnp.concatenate([row[0:3], jnp.zeros((3, 512), F32)], axis=1)], axis=0
    )
    high = small.astype(BF)
    wo[64:72] = high
    wo[72:80] = (small - high.astype(F32)).astype(BF)
    for i in range(8):
        rows = slice(i * TILE, (i + 1) * TILE)
        dq = dq_t[:, rows] * 0.125
        vk = jnp.where(lane((TILE, 128)) < 64, dv[rows], pltpu.roll(dk[rows], 64, 1)).T
        left[0:64, rows] = dq[:64].astype(BF)
        left[64:128, rows] = vk[64:128].astype(BF)
        left[128:192, rows] = vk[0:64].astype(BF)
        blocks = slice(4 * i, 4 * i + 4)
        packed[blocks, 0:32] = pack_halves(dq.T).astype(BF)
        packed[blocks, 32:64] = pack_halves(dk[rows]).astype(BF)
        packed[blocks, 64:96] = pack_halves(dv[rows]).astype(BF)
    grads[...] = (
        jnp.dot(left[...], h1[...], preferred_element_type=F32).astype(BF).reshape(2, 96, 1024)
    )
    trade = remote(grads.at[1 - h], other, sems[8].at[0], sems[9].at[0], partner)
    trade.start()
    trade_far = remote(grads.at[h], other_far, sems[8].at[1], sems[9].at[1], partner)
    trade_far.start()
    next(steps)

    def at(j):
        return land.at[j]

    def view_of(side):
        def view(v, c0, cn):
            return whole.at[side, slot_of(v), :, pl.ds(c0, cn)]

        return view

    me_slot = slot_of(b)
    next(steps)
    wo[0:64] = acc_o[eighth(b)]
    trade_o = remote(wo, other_o, sems[8].at[2], sems[9].at[2], partner)
    trade_o.start()
    trade.wait()
    whole[h, me_slot] = (grads[h].astype(F32) + other[...].astype(F32)).astype(BF)
    near = gather_steps(b, view_of(h), *sems[0:4])
    next(near)
    me, copies = everyone(b, packed, at, sems[10], sems[11])
    land[me] = packed[me]
    for cp in loads[1:]:
        cp.wait()
    spread_u = spread_start(f, half_u, pieces_u, sems[12], sems[13])
    tokens_back = scatter_steps(f, routed, acc, landing, *sems[24:28], cuts=LATE)
    next(tokens_back)
    next(near)
    spread_end(f, half_g, pieces_g, sems[14], sems[15], spread_g)
    for i in range(4):
        for side in range(2):
            at0 = ((i // 2) * 4 + side * 2 + i % 2) * 352
            wide_g[:, at0 : at0 + 352] = pieces_g[i, :, side * 352 : side * 352 + 352]
    next(near)
    trade_far.wait()
    whole[1 - h, me_slot] = (grads[1 - h].astype(F32) + other_far[...].astype(F32)).astype(BF)
    far = gather_steps(b, view_of(1 - h), *sems[4:8])
    next(far)
    trade_o.wait()
    whole_o[me_slot] = (wo[...].astype(F32) + other_o[...].astype(F32)).astype(BF)
    outs = gather_steps(b, group_view(whole_o, 0, 80), *sems[18:22], parts=LAST_Y)
    next(outs)

    def tokens_done():
        everyone_wait(b, me, at, sems[10], sems[11], copies)
        for kind in range(3):
            for s in range(2):
                for pair in range(8):
                    j0, j1 = device_of(s, 2 * pair), device_of(s, 2 * pair + 1)
                    span = slice(kind * 32, kind * 32 + 32)
                    top, bottom = unpack_halves(land[j0, span], land[j1, span])
                    cols = slice(pair * 128, pair * 128 + 128)
                    joined[kind, s * 64 : s * 64 + 32, cols] = top
                    joined[kind, s * 64 + 32 : s * 64 + 64, cols] = bottom
        d_h1 = (
            lax.dot_general(joined[0], wq[...], NT, preferred_element_type=F32)
            + lax.dot_general(joined[1], wk[...], NT, preferred_element_type=F32)
            + lax.dot_general(joined[2], wv[...], NT, preferred_element_type=F32)
        )
        grad_in, grad_gain = norm_back_rows(tokens[...].astype(F32), gain[...], d_h1)
        dtokens[...] = dmid[...] + grad_in
        mine[...] = grad_gain.reshape(8, 128)
        sent = []
        for step, (j, peer) in enumerate(world_all(b)[1]):
            cp = remote(mine, crowd.at[me], sems[22].at[step], sems[23].at[step], peer)
            cp.start()
            sent.append(cp)
        crowd[me] = mine[...]
        return sent

    sent = []
    for n in range(7):
        if n % 2 == 0:
            next(tokens_back)
        next(near, None)
        next(far)
        next(outs)
        if n == TOKENS_AT:
            sent = tokens_done()
    next(tokens_back)
    spread_end(f, half_u, pieces_u, sems[12], sems[13], spread_u)
    for i in range(4):
        for side in range(2):
            at0 = ((i // 2) * 4 + side * 2 + i % 2) * 352
            wide_u[:, at0 : at0 + 352] = pieces_u[i, :, side * 352 : side * 352 + 352]
    next(outs)
    next(far)
    total = whole_o[0, 64:80].astype(F32)
    for n in range(1, 16):
        total = total + whole_o[n, 64:80].astype(F32)
    smalls[...] = total[0:8] + total[8:16]
    routed_rows = acc[eighth(f)].astype(F32)
    result[...] = jnp.where(live_rows(b, length), middle[...] + routed_rows, 0.0).astype(BF)
    everyone_wait(b, me, lambda j: crowd.at[j], sems[22], sems[23], sent)
    gain_out[...] = jnp.sum(crowd[...], axis=0)


def dense_body(whole, whole_o, grad_q, grad_k, grad_v, grad_o):
    sides = (whole[0].astype(F32), whole[1].astype(F32))
    spans = (
        (grad_q, ((0, 0, 64),)),
        (grad_k, ((0, 64, 96), (1, 0, 32))),
        (grad_v, ((1, 32, 96),)),
    )
    for out, parts in spans:
        pieces = []
        for head in range(2):
            for side, lo, hi in parts:
                pieces.append(sides[side][head, lo:hi])
        rows = jnp.concatenate(pieces, axis=0)
        for c in range(0, 1024, 128):
            out[c : c + 128, :] = rows[:, c : c + 128].T
    grad_o[...] = whole_o[:, 0:64, :].reshape(128, 1024).astype(F32)


def distance_buckets():
    table = []
    for distance in range(2 * TILE):
        table.append(bucket_of(distance, 32, MAXDIST))
    return np.array(table, np.int32)


def on_device_fast(
    tokens,
    lengths,
    expert_index,
    cotangent,
    norm_attn,
    w_query,
    w_key,
    w_value,
    w_out,
    rel_bias,
    norm_ffn,
    router,
    w_gate,
    w_up,
    w_down,
):
    dma = pltpu.SemaphoreType.DMA
    gain_attn = norm_attn.reshape(1, 1024)
    gain_ffn = norm_ffn.reshape(1, 1024)
    flat = tokens.reshape(128, 1024)
    cot = cotangent.reshape(128, 1024)

    buckets = distance_buckets()
    onehot = np.zeros((2 * TILE, 128), np.float32)
    onehot[np.arange(2 * TILE), buckets] = 1.0
    router_t = jnp.pad(router.T, ((0, 4), (0, 0)))

    h1, picks_all, w3, wg, wu, dist = call(
        first_body,
        [
            shape((4, 2, 4, 64, 1024)),
            shape((16, 8, 128), F32),
            shape((1024, 384)),
            shape((1024, SHARE)),
            shape((1024, SHARE)),
            shape((8, 2 * TILE), F32),
        ],
        [VMEM((2, 64, 1024), BF), VMEM((3, 1024, 128), BF), VMEM((4, 1024, 512), BF), VMEM((8, 128), F32)]
        + CUBE_SEMS
        + [dma(()), dma(()), dma((15,)), dma((15,)), dma((7,))]
        + CUBE_SEMS,
        1,
        lengths,
        tokens,
        gain_attn,
        expert_index.reshape(128, 2),
        w_query,
        w_key,
        w_value,
        w_gate[0],
        w_up[0],
        rel_bias,
        jnp.asarray(onehot.T[:32]),
        anywhere=(4, 5, 6, 7, 8),
        scalars=(0,),
    )
    h1 = h1.reshape(2048, 1024)
    out_t, qs, ks, vs, lse, dy0, middle, h2_all, gates_all, joined = call(
        attend_body,
        [
            shape((64, 2048), F32),
            shape((2048, 128)),
            shape((2048, 128)),
            shape((2048, 128)),
            shape((8, 2048), F32),
            shape((16, 64, 1024)),
            shape((128, 1024), F32),
            shape((16, 128, 1024)),
            shape((16, 8, 128), F32),
            shape((128, 1024)),
        ],
        [
            VMEM((2048, TILE), F32),
            VMEM((128, 2048), BF),
            VMEM((2048, TILE), BF),
            VMEM((32, 32, 128), BF),
            VMEM((32, 32, 128), BF),
            VMEM((8, 128), F32),
            VMEM((1024, 1024), BF),
            dma(()),
        ]
        + FOUR_SEMS
        + TWO_SEMS
        + [dma((32,)), dma((32,)), dma((15,)), dma((15,))],
        2,
        lengths,
        h1,
        w3,
        dist,
        cot,
        flat,
        w_out,
        gain_ffn,
        router,
        scalars=(0,),
        anywhere=(6,),
    )
    routed, near_g, near_u, down, do_all, dmid, smalls, gwo = call(
        expert_body,
        [
            shape((16, 128, 1024)),
            shape((512, SHARE)),
            shape((512, SHARE)),
            shape((352, 1024)),
            shape((32, 32, 128)),
            shape((128, 1024), F32),
            shape((8, 1024), F32),
            shape((16, 64, 1024)),
        ],
        [VMEM((16, 128, 1024), BF)]
        + [VMEM((1280, 1024), BF)] * 3
        + [VMEM((1280, 128), F32)]
        + [VMEM((1280, SHARE), BF)] * 5
        + [VMEM((1280, 1024), BF)] * 2
        + [VMEM((1280, 128), F32)]
        + [VMEM((SHARE, 1024), BF), VMEM((1024, 1024), BF)]
        + [VMEM((512, SHARE), BF), VMEM((512, SHARE), BF), VMEM((352, 1024), BF)] * 2
        + [VMEM((8, 128, 1024), BF)] * 2
        + [VMEM((16, 8, 128), F32)] * 2
        + [VMEM((32, 32, 128), BF)]
        + [dma((4,))]
        + TWO_SEMS
        + CUBE_SEMS
        + [dma((15,)), dma((15,)), dma((31,)), dma((31,))]
        + [dma(())] * 4
        + [dma((3,))] * 2,
        3,
        h2_all,
        dy0,
        cot,
        gates_all,
        picks_all,
        wg,
        wu,
        w_down[0],
        lengths,
        middle,
        gain_ffn,
        router_t,
        joined,
        w_out,
        anywhere=(1, 7, 13),
        scalars=(8,),
    )
    dtokens, result, whole, whole_o, smalls, gain_out, wide_u, wide_g = call(
        back_body,
        [
            shape((128, 1024), F32),
            shape((128, 1024)),
            shape((2, 16, 96, 1024)),
            shape((16, 80, 1024)),
            shape((8, 1024), F32),
            shape((8, 128), F32),
            shape((128, 2816)),
            shape((128, 2816)),
        ],
        [
            VMEM((2048, 128), BF),
            VMEM((128, 2048), BF),
            VMEM((8, 2048), F32),
            VMEM((2048, TILE), BF),
            VMEM((2048, TILE), BF),
            VMEM((128, 2048), F32),
            VMEM((2048, 128), F32),
            VMEM((2048, 128), F32),
            VMEM((TILE, TILE), F32),
            VMEM((TILE, TILE), F32),
            VMEM((192, 2048), BF),
            VMEM((8, 64, 1024), BF),
            VMEM((8, 64, 1024), BF),
            VMEM((32, 96, 128), BF),
            VMEM((2, 96, 1024), BF),
            VMEM((80, 1024), BF),
            VMEM((32, 96, 128), BF),
            VMEM((96, 1024), BF),
            VMEM((96, 1024), BF),
            VMEM((80, 1024), BF),
            VMEM((3, 128, 1024), BF),
            VMEM((32, 8, 128), F32),
            VMEM((8, 128), F32),
            VMEM((4, 128, SHARE), BF),
            VMEM((4, 128, SHARE), BF),
            VMEM((4, 128, SHARE), BF),
            VMEM((4, 128, SHARE), BF),
            VMEM((8, 128, 1024), BF),
            VMEM((8, 128, 1024), BF),
            VMEM((16, 128, 1024), BF),
            VMEM((1024, 1024), BF),
            VMEM((1024, 1024), BF),
            VMEM((1024, 1024), BF),
            dma((6,)),
        ]
        + CUBE_SEMS
        + CUBE_SEMS
        + [dma((3,)), dma((3,)), dma((31,)), dma((31,)), dma((5,)), dma((5,)), dma((6,)), dma((6,))]
        + [dma((3,)), dma((3,))]
        + CUBE_SEMS
        + [dma((31,)), dma((31,))]
        + CUBE_SEMS
        + CUBE_SEMS,
        4,
        h1,
        do_all,
        qs,
        ks,
        vs,
        out_t,
        lse,
        dist,
        jnp.asarray(onehot),
        gwo,
        flat,
        dmid,
        gain_attn,
        smalls,
        middle,
        lengths,
        routed,
        near_g.reshape(4, 128, SHARE),
        near_u.reshape(4, 128, SHARE),
        w_query,
        w_key,
        w_value,
        anywhere=tuple(range(16, 22)),
        scalars=(15,),
    )
    grad_q, grad_k, grad_v, grad_o = pl.pallas_call(
        dense_body,
        grid=(8,),
        out_shape=[shape((1024, 1024), F32)] * 4,
        in_specs=[
            pl.BlockSpec((2, 2, 96, 1024), lambda i: (0, i, 0, 0)),
            pl.BlockSpec((2, 80, 1024), lambda i: (i, 0, 0)),
        ],
        out_specs=[pl.BlockSpec((1024, 128), lambda i: (0, i))] * 3
        + [pl.BlockSpec((128, 1024), lambda i: (i, 0))],
        compiler_params=params(),
        cost_estimate=pl.CostEstimate(flops=0, bytes_accessed=25 * 2**20, transcendentals=0),
    )(whole, whole_o)
    return (
        result.reshape(2, 64, 1024),
        dtokens.reshape(2, 64, 1024),
        gain_out.reshape(1024),
        grad_q,
        grad_k,
        grad_v,
        grad_o,
        smalls[5, :512].reshape(16, 32).T,
        smalls[4],
        smalls[0:4].T,
        wide_g[None].astype(F32),
        wide_u[None].astype(F32),
        down[None].astype(F32),
    )


def solution(mesh):
    sizes = dict(mesh.shape)
    fits = sizes == {"experts": 4, "context": 8}
    placed = (
        P(None, ("experts", "context"), None),
        P(),
        P(None, ("experts", "context"), None),
        P(None, ("experts", "context"), None),
        P(),
        P(),
        P(),
        P(),
        P(),
        P(),
        P(),
        P(),
        P("experts", None, None),
        P("experts", None, None),
        P("experts", None, None),
    )
    return jax.shard_map(
        on_device_fast if fits else on_device,
        mesh=mesh,
        in_specs=placed,
        out_specs=(
            P(None, ("experts", "context"), None),
            P(None, ("experts", "context"), None),
            P(),
            P(),
            P(),
            P(),
            P(),
            P(),
            P(),
            P(),
            P("experts", "context", None),
            P("experts", "context", None),
            P("experts", "context", None),
        ),
        check_vma=False,
    )
```
